32 devices in a mesh: wide: 8 (over z, x), narrow: 4 (over y, core).
Axes of the slice: x: 2, y: 2, z: 4, core: 2. Of those that a mesh axis runs over, the one named last changes fastest.
Arguments:
- tokens: bfloat16 [32768, 768], P(('narrow', 'wide')), may hold values from -15 to 15
- cotangent: bfloat16 [32768, 768], P(('narrow', 'wide')), may hold values from -15 to 15
- lengths: int32 [32, 24], P(('narrow', 'wide')), may hold values from 1 to 202, 1024 in all within a row
- projection: float32 [64, 32], replicated, may hold values from -4 to 4
- inward: float32 [3, 768, 768], P(None, 'wide'), may hold values from -0.21875 to 0.21875
- outward: float32 [768, 768], P('wide'), may hold values from -0.875 to 0.875
- expand: float32 [768, 3072], P('wide'), may hold values from -0.21875 to 0.21875
- shrink: float32 [3072, 768], P('wide'), may hold values from -0.109375 to 0.109375
- vectors: float32 [13, 768], replicated, may hold values from -1.2 to 2
- inward_rows: float32 [3, 768], P(None, 'wide'), may hold values from 2293.76 to 62259.2
- inward_columns: float32 [3, 768], replicated, may hold values from 12451.84 to 49152
- outward_rows: float32 [768], P('wide'), may hold values from 294.912 to 7536.64
- outward_columns: float32 [768], replicated, may hold values from 1540.096 to 6225.92
- expand_rows: float32 [768], P('wide'), may hold values from 229.376 to 5898.24
- expand_columns: float32 [3072], replicated, may hold values from 1179.648 to 4587.52
- shrink_rows: float32 [3072], P('wide'), may hold values from 720.896 to 19005.44
- shrink_columns: float32 [768], replicated, may hold values from 3833.856 to 15400.96
- vector_state: float32 [13, 768], replicated, may hold values from 983.04 to 124518.4
Outputs:
- block_out: float32 [32768, 768], P(('narrow', 'wide'))
- input_grad: float32 [32768, 768], P(('narrow', 'wide'))
- inward_grad: float32 [3, 768, 768], P(None, 'wide')
- outward_grad: float32 [768, 768], P('wide')
- expand_grad: float32 [768, 3072], P('wide')
- shrink_grad: float32 [3072, 768], P('wide')
- vector_grad: float32 [13, 768], replicated
- inward_rows_next: float32 [3, 768], P(None, 'wide')
- inward_columns_next: float32 [3, 768], replicated
- outward_rows_next: float32 [768], P('wide')
- outward_columns_next: float32 [768], replicated
- expand_rows_next: float32 [768], P('wide')
- expand_columns_next: float32 [3072], replicated
- shrink_rows_next: float32 [3072], P('wide')
- shrink_columns_next: float32 [768], replicated
- vector_state_next: float32 [13, 768], replicated
- inward_next: float32 [3, 768, 768], P(None, 'wide')
- outward_next: float32 [768, 768], P('wide')
- expand_next: float32 [768, 3072], P('wide')
- shrink_next: float32 [3072, 768], P('wide')
- vectors_next: float32 [13, 768], replicated
The draws below stay inside these ranges and needn't reach their ends.
Inputs may be any that keep to these rules, and one draw needn't show every extreme that they name: `lengths`: each row holds the token counts of the molecules of one sequence in order; a row sums to 1024 and its largest entry is 202.
All inputs are finite; a program needn't handle non-finite values.
Results may differ from the reference program's by a relative error of at most 0.008.
The reference program's roundings to bfloat16 on the way count: a program that leaves them out, or rounds other values in their place, can miss the bound.
Values may be sent and summed in bfloat16 or wider, within the bound.
No kernel may reach another device: no remote copies, remote signals or barrier semaphores. Data moves between devices by JAX's collectives and lax.ppermute only.
A program may use at most 112 MiB of HBM per device.

```python
import math
import jax
import jax.numpy as jnp
import numpy as np
from jax import lax

D = 768
HEADS = 12
HD = 64
FF = 3072
FEAT = 32
LEN = 1024
SEQ_DEV = 1
NSEG = 24
MOST = 202
STEP = 10
VROWS = 13
WIDE_SPAN = 8
NARROW_SPAN = 4
SEQS = 32
TOKENS = 32768


def draw_tokens(key, part):
    key = jax.random.fold_in(key, 7)
    first, second = jax.random.split(key, 2)
    row_scale = jnp.exp(jax.random.uniform(first, (TOKENS, 1), jnp.float32, math.log(0.3), math.log(3.0)))
    base = jnp.clip(jax.random.normal(second, (TOKENS, D), jnp.float32), -5.0, 5.0)
    return (base * row_scale).astype(jnp.bfloat16)


def draw_cotangent(key, part):
    key = jax.random.fold_in(key, 11)
    device_rows = jnp.arange(TOKENS, dtype=jnp.int32) // (SEQ_DEV * LEN)
    across = (device_rows % WIDE_SPAN).astype(jnp.float32) / max(WIDE_SPAN - 1, 1)
    downward = (device_rows // WIDE_SPAN).astype(jnp.float32) / max(NARROW_SPAN - 1, 1)
    growth = math.log(3.0)
    base = jnp.clip(jax.random.normal(key, (TOKENS, D), jnp.float32), -5.0, 5.0)
    row_scale = jnp.exp(growth * (0.5 * across + 0.5 * downward - 0.5))
    return (base * row_scale[:, None]).astype(jnp.bfloat16)


def draw_vectors(key, part):
    key = jax.random.fold_in(key, 13)
    first, second = jax.random.split(key)
    place = jnp.arange(D, dtype=jnp.float32) / D
    slope = 0.6 + 0.5 * place
    rough = jnp.exp(jax.random.uniform(first, (VROWS, D), jnp.float32, -0.35, 0.35))
    shifts = 0.3 * jnp.clip(jax.random.normal(second, (VROWS, D), jnp.float32), -4.0, 4.0)
    gains = slope[None, :] * rough
    row_ids = jnp.arange(VROWS, dtype=jnp.int32)
    is_gain = (row_ids == 0) | (row_ids == 2)
    return jnp.where(is_gain[:, None], gains, shifts)


def draw_vector_state(key, part):
    key = jax.random.fold_in(key, 17)
    row_scales = jnp.concatenate([jnp.array([5.0, 5.0, 0.64, 0.64, 1.7, 1.7, 1.7, 2.1, 1.5], jnp.float32), jnp.full((VROWS - 9,), 0.16, jnp.float32)])
    factor = jnp.exp(jax.random.uniform(key, (VROWS, D), jnp.float32, 0.0, math.log(4.0)))
    return 0.188 * TOKENS * row_scales[:, None] * factor


def falling_rows(key, lead, count, floor, last_level):
    place = jnp.arange(count, dtype=jnp.float32) / max(count - 1, 1)
    level = 4.0 * (last_level / 4.0) ** place
    factor = jnp.exp(jax.random.uniform(key, (lead, count), jnp.float32, -0.2, 0.2))
    return floor * level[None, :] * factor


def draw_inward_rows(key, part):
    key = jax.random.fold_in(key, 23)
    last_level = 0.5
    return falling_rows(key, 3, D, 0.38 * TOKENS, last_level)


def draw_outward_rows(key, part):
    key = jax.random.fold_in(key, 29)
    last_level = 0.5
    return falling_rows(key, 1, D, 0.047 * TOKENS, last_level)[0]


def draw_expand_rows(key, part):
    key = jax.random.fold_in(key, 31)
    last_level = 0.5
    return falling_rows(key, 1, D, 0.036 * TOKENS, last_level)[0]


def draw_shrink_rows(key, part):
    key = jax.random.fold_in(key, 37)
    last_level = 0.5
    return falling_rows(key, 1, FF, 0.117 * TOKENS, last_level)[0]


def block_scale(key, dims, pieces, least, top_value):
    level, own = 1.0, jax.random.fold_in(key, 6)
    for dim, blocks in pieces:
        draws = jnp.exp(jax.random.uniform(jax.random.fold_in(own, dim), (blocks,), jnp.float32, least / len(pieces), top_value / len(pieces)))
        level = level * jnp.repeat(draws, dims[dim] // blocks).reshape([-1 if axis == dim else 1 for axis in range(len(dims))])
    return level


def length_profile(number_of, total, most, skew):
    portions = [(1 << 20) // math.isqrt(standing ** skew) + 1 for standing in range(2, number_of + 1)]
    rest, holding = total - most - (number_of - 1), [1] * (number_of - 1)
    while rest > 0:
        free = [i for i in range(number_of - 1) if holding[i] < most]
        whole, budget = sum([portions[i] for i in free]), rest
        for i in free:
            more = min(most - holding[i], max(1, budget * portions[i] // whole), rest)
            holding[i] = holding[i] + more
            rest = rest - more
    return np.array([most] + holding)


def uneven(stream_key, number_of, total, bound, skew):
    if number_of == 2:
        one = jax.random.randint(stream_key, (), max(1, total - bound), min(bound, total - 1) + 1)
        return jnp.stack([one, total - one])
    tallies = jnp.asarray(length_profile(number_of, total, bound, skew), jnp.int32)
    pairs = (number_of - 1) // 2
    donor, receiver = tallies[1:1 + 2 * pairs:2], tallies[2:2 + 2 * pairs:2]
    room = jnp.minimum(donor - 1, bound - receiver)
    passed = jax.random.randint(jax.random.fold_in(stream_key, 1), (pairs,), 0, 1 << 20) % (room + 1)
    tallies = tallies.at[1:1 + 2 * pairs:2].set(donor - passed).at[2:2 + 2 * pairs:2].set(receiver + passed)
    return tallies[jax.random.permutation(jax.random.fold_in(stream_key, 2), number_of)]


def centred(stream_key, shape, scale, reach, pieces=(), held_as=jnp.bfloat16):
    result = scale * jax.random.normal(stream_key, shape, jnp.float32)
    if pieces:
        result = result * block_scale(stream_key, shape, pieces, -0.22, 0.18)
    return jnp.clip(result, -reach, reach).astype(held_as)


def setup_inputs(seed: int = 0) -> dict:
    splits = jax.random.split(jax.random.key(seed), 19)
    tokens = draw_tokens(jax.random.fold_in(splits[18], 71), 0)
    cotangent = draw_cotangent(jax.random.fold_in(splits[18], 71), 0)
    lengths = jax.vmap(lambda own: uneven(own, NSEG, LEN, MOST, 1))(jax.random.split(splits[2], SEQS)).reshape((SEQS, NSEG)).astype(jnp.int32)
    projection = centred(splits[3], (HD, FEAT), 1.0, 4.0, (), jnp.float32)
    inward = centred(splits[4], (3, D, D), D ** -0.5, 0.21875, ((1, 8),), jnp.float32)
    outward = centred(splits[5], (D, D), (D // 16) ** -0.5, 0.875, ((0, 8),), jnp.float32)
    expand = centred(splits[6], (D, FF), D ** -0.5, 0.21875, ((0, 8),), jnp.float32)
    shrink = centred(splits[7], (FF, D), FF ** -0.5, 0.109375, ((0, 8),), jnp.float32)
    vectors = draw_vectors(jax.random.fold_in(splits[18], 71), 0)
    inward_rows = draw_inward_rows(jax.random.fold_in(splits[18], 71), 0)
    inward_columns = jnp.clip(jnp.exp(jax.random.uniform(splits[10], (3, D), jnp.float32, math.log(12451.84), math.log(49152.0))), 12451.84, 49152.0)
    outward_rows = draw_outward_rows(jax.random.fold_in(splits[18], 71), 0)
    outward_columns = jnp.clip(jnp.exp(jax.random.uniform(splits[12], (D,), jnp.float32, math.log(1540.096), math.log(6225.92))), 1540.096, 6225.92)
    expand_rows = draw_expand_rows(jax.random.fold_in(splits[18], 71), 0)
    expand_columns = jnp.clip(jnp.exp(jax.random.uniform(splits[14], (FF,), jnp.float32, math.log(1179.648), math.log(4587.52))), 1179.648, 4587.52)
    shrink_rows = draw_shrink_rows(jax.random.fold_in(splits[18], 71), 0)
    shrink_columns = jnp.clip(jnp.exp(jax.random.uniform(splits[16], (D,), jnp.float32, math.log(3833.856), math.log(15400.96))), 3833.856, 15400.96)
    vector_state = draw_vector_state(jax.random.fold_in(splits[18], 71), 0)
    return {"tokens": tokens, "cotangent": cotangent, "lengths": lengths, "projection": projection, "inward": inward, "outward": outward, "expand": expand, "shrink": shrink, "vectors": vectors, "inward_rows": inward_rows, "inward_columns": inward_columns, "outward_rows": outward_rows, "outward_columns": outward_columns, "expand_rows": expand_rows, "expand_columns": expand_columns, "shrink_rows": shrink_rows, "shrink_columns": shrink_columns, "vector_state": vector_state}


@jax.custom_vjp
def low(v):
    return lax.optimization_barrier(v.astype(jnp.bfloat16)).astype(jnp.float32)

@jax.custom_vjp
def low_back(v):
    return v

def low_keep(v):
    return (low(v), None)

def low_pass(kept, grad):
    return (grad,)

def back_keep(v):
    return (v, None)

def back_low(kept, grad):
    return (low(grad),)
low.defvjp(low_keep, low_pass)
low_back.defvjp(back_keep, back_low)
HIGHEST = lax.Precision.HIGHEST
norm_eps = 1e-05
square_eps = 1e-30
clip_level = 1.0

def layer_norm(values, gain, shift):
    centre = values - lax.optimization_barrier(jnp.mean(values, axis=-1, keepdims=True))
    spread = lax.optimization_barrier(jnp.mean(centre * centre, axis=-1, keepdims=True))
    return centre * lax.rsqrt(spread + norm_eps) * gain + shift

def exact_gelu(values):
    return jax.nn.gelu(values, approximate=False)

def segment_tables(length_row, seq_len):
    ends_at = jnp.cumsum(length_row).astype(jnp.int32)
    starts_at = (ends_at - length_row).astype(jnp.int32)
    places = jnp.arange(seq_len, dtype=jnp.int32)
    member = (places[:, None] >= starts_at[None, :]) & (places[:, None] < ends_at[None, :])
    offsets = lax.optimization_barrier(jnp.sum(jnp.where(member, starts_at[None, :], 0), axis=1)).astype(jnp.int32)
    return (member.astype(jnp.float32), (places - offsets).astype(jnp.float32))

def rotate_half(values, positions):
    half_dim = values.shape[-1] // 2
    freq_table = 10000.0 ** (-jnp.arange(half_dim, dtype=jnp.float32) / half_dim)
    angles = positions[:, None] * freq_table[None, :]
    cosine = jnp.cos(angles)
    sine = jnp.sin(angles)
    first_half = values[:, :half_dim]
    second_half = values[:, half_dim:]
    return jnp.concatenate([first_half * cosine - second_half * sine, second_half * cosine + first_half * sine], axis=1)

def feature_map(values, projection):
    scaled = values * values.shape[-1] ** (-0.25)
    logits = jnp.dot(scaled, projection, precision=HIGHEST, preferred_element_type=jnp.float32)
    return jnp.exp(logits - 0.5 * lax.optimization_barrier(jnp.sum(scaled * scaled, axis=-1, keepdims=True))) * projection.shape[1] ** (-0.5)

def head_attention(q_head, k_head, v_head, onehot, positions, projection):
    seq_len, seg_count = onehot.shape
    q_feat = feature_map(rotate_half(q_head, positions), projection)
    k_feat = feature_map(rotate_half(k_head, positions), projection)
    feat_dim = q_feat.shape[1]
    q_spread = (onehot[:, :, None] * q_feat[:, None, :]).reshape(seq_len, seg_count * feat_dim)
    k_spread = (onehot[:, :, None] * k_feat[:, None, :]).reshape(seq_len, seg_count * feat_dim)
    kv_state = lax.dot_general(k_spread, v_head, (((0,), (0,)), ((), ())), precision=HIGHEST, preferred_element_type=jnp.float32)
    k_total = lax.optimization_barrier(jnp.sum(k_spread, axis=0))
    numerator = jnp.dot(q_spread, kv_state, precision=HIGHEST, preferred_element_type=jnp.float32)
    denominator = jnp.dot(q_spread, k_total, precision=HIGHEST, preferred_element_type=jnp.float32)
    return numerator / denominator[:, None]

def sequence_attention(q_seq, k_seq, v_seq, onehot, positions, projection):
    seq_len = q_seq.shape[0]

    def split_heads(values):
        return jnp.transpose(values.reshape(seq_len, HEADS, -1), (1, 0, 2))

    def one_head(triple):
        return jax.checkpoint(head_attention)(triple[0], triple[1], triple[2], onehot, positions, projection)
    mixed = lax.map(one_head, (split_heads(q_seq), split_heads(k_seq), split_heads(v_seq)))
    return jnp.transpose(mixed, (1, 0, 2)).reshape(seq_len, -1)

def local_attention(q_all, k_all, v_all, onehots, positions, projection):
    seq_count, seq_len = (onehots.shape[0], onehots.shape[1])

    def shaped(values):
        return values.reshape(seq_count, seq_len, -1)

    def one_sequence(bundle):
        return sequence_attention(bundle[0], bundle[1], bundle[2], bundle[3], bundle[4], projection)
    mixed = lax.map(one_sequence, (shaped(q_all), shaped(k_all), shaped(v_all), onehots, positions))
    return mixed.reshape(seq_count * seq_len, -1)

def factored_step(weight, grad, rows_old, columns_old, rate):
    decay = 1.0 - STEP ** (-0.8)
    squares = grad * grad + square_eps
    rows_new = decay * rows_old + (1.0 - decay) * lax.optimization_barrier(jnp.mean(squares, axis=1))
    columns_new = decay * columns_old + (1.0 - decay) * lax.optimization_barrier(jnp.mean(squares, axis=0))
    scaled = grad * lax.rsqrt(rows_new / jnp.mean(rows_new))[:, None] * lax.rsqrt(columns_new)[None, :]
    rms_value = jnp.sqrt(jnp.mean(scaled * scaled))
    return (weight - rate * scaled / jnp.maximum(1.0, rms_value / clip_level), rows_new, columns_new)

def reference(tokens, cotangent, lengths, projection, inward, outward, expand, shrink, vectors, inward_rows, inward_columns, outward_rows, outward_columns, expand_rows, expand_columns, shrink_rows, shrink_columns, vector_state):
    onehots, positions = jax.vmap(lambda length_row: segment_tables(length_row, LEN))(lengths)

    def forward(residual_in, in_weight, out_weight, up_weight, down_weight, table):
        low_in = low(in_weight)
        low_out = low(out_weight)
        low_up = low(up_weight)
        low_down = low(down_weight)
        normed = low(layer_norm(residual_in, table[0], table[1]))
        qkv_all = jnp.einsum('td,kde->tke', normed, low_in, precision=HIGHEST) + table[4:7][None]
        q_all = low_back(qkv_all[:, 0])
        k_all = low_back(qkv_all[:, 1])
        v_all = low_back(qkv_all[:, 2])
        mixed = low(local_attention(q_all, k_all, v_all, onehots, positions, projection))
        residual_mid = residual_in + low_back(jnp.dot(mixed, low_out, precision=HIGHEST, preferred_element_type=jnp.float32) + table[7])
        normed_two = low(layer_norm(residual_mid, table[2], table[3]))
        hidden = low_back(jnp.dot(normed_two, low_up, precision=HIGHEST, preferred_element_type=jnp.float32) + table[9:].reshape(-1))
        activated = low(exact_gelu(hidden))
        return residual_mid + low_back(jnp.dot(activated, low_down, precision=HIGHEST, preferred_element_type=jnp.float32) + table[8])
    residual_in = tokens.astype(jnp.float32)
    block_out, pullback = jax.vjp(forward, residual_in, inward, outward, expand, shrink, vectors)
    input_grad, inward_grad, outward_grad, expand_grad, shrink_grad, vector_grad = pullback(cotangent.astype(jnp.float32))
    inward_next, inward_rows_next, inward_columns_next = jax.vmap(factored_step, in_axes=(0, 0, 0, 0, None))(inward, inward_grad, inward_rows, inward_columns, 0.3 * D ** (-0.5))
    outward_next, outward_rows_next, outward_columns_next = factored_step(outward, outward_grad, outward_rows, outward_columns, 1.2 * D ** (-0.5))
    expand_next, expand_rows_next, expand_columns_next = factored_step(expand, expand_grad, expand_rows, expand_columns, 0.3 * D ** (-0.5))
    shrink_next, shrink_rows_next, shrink_columns_next = factored_step(shrink, shrink_grad, shrink_rows, shrink_columns, 0.3 * FF ** (-0.5))
    decay = 1.0 - STEP ** (-0.8)
    vector_state_next = decay * vector_state + (1.0 - decay) * (vector_grad * vector_grad + square_eps)
    vector_update = vector_grad * lax.rsqrt(vector_state_next)
    vector_rms = jnp.sqrt(jnp.mean(vector_update * vector_update))
    vectors_next = vectors - 0.25 * vector_update / jnp.maximum(1.0, vector_rms / clip_level)
    return (block_out, input_grad, inward_grad, outward_grad, expand_grad, shrink_grad, vector_grad, inward_rows_next, inward_columns_next, outward_rows_next, outward_columns_next, expand_rows_next, expand_columns_next, shrink_rows_next, shrink_columns_next, vector_state_next, inward_next, outward_next, expand_next, shrink_next, vectors_next)
```

```python
import jax
import jax.numpy as jnp
from jax import lax
from jax.sharding import PartitionSpec as P

D = 768
HEADS = 12
FF = 3072
STEP = 10


HIGHEST = lax.Precision.HIGHEST
norm_eps = 1e-05
square_eps = 1e-30
clip_level = 1.0


def layer_norm(values, gain, shift):
    centre = values - jnp.mean(values, axis=-1, keepdims=True)
    spread = jnp.mean(centre * centre, axis=-1, keepdims=True)
    return centre * lax.rsqrt(spread + norm_eps) * gain + shift


def exact_gelu(values):
    return jax.nn.gelu(values, approximate=False)


def segment_tables(length_row, seq_len):
    ends_at = jnp.cumsum(length_row)
    starts_at = ends_at - length_row
    places = jnp.arange(seq_len, dtype=jnp.int32)
    member = (places[:, None] >= starts_at[None, :]) & (places[:, None] < ends_at[None, :])
    offsets = jnp.sum(jnp.where(member, starts_at[None, :], 0), axis=1)
    return (member.astype(jnp.float32), (places - offsets).astype(jnp.float32))


def rotate_half(values, positions):
    half_dim = values.shape[-1] // 2
    freq_table = 10000.0 ** (-jnp.arange(half_dim, dtype=jnp.float32) / half_dim)
    angles = positions[:, None] * freq_table[None, :]
    cosine = jnp.cos(angles)
    sine = jnp.sin(angles)
    first_half = values[:, :half_dim]
    second_half = values[:, half_dim:]
    return jnp.concatenate(
        [first_half * cosine - second_half * sine, second_half * cosine + first_half * sine], axis=1
    )


def feature_map(values, projection):
    scaled = values * values.shape[-1] ** (-0.25)
    logits = jnp.dot(scaled, projection, precision=HIGHEST, preferred_element_type=jnp.float32)
    return jnp.exp(
        logits - 0.5 * jnp.sum(scaled * scaled, axis=-1, keepdims=True)
    ) * projection.shape[1] ** (-0.5)


def head_attention(q_head, k_head, v_head, onehot, positions, projection):
    seq_len, seg_count = onehot.shape
    q_feat = feature_map(rotate_half(q_head, positions), projection)
    k_feat = feature_map(rotate_half(k_head, positions), projection)
    feat_dim = q_feat.shape[1]
    q_spread = (onehot[:, :, None] * q_feat[:, None, :]).reshape(seq_len, seg_count * feat_dim)
    k_spread = (onehot[:, :, None] * k_feat[:, None, :]).reshape(seq_len, seg_count * feat_dim)
    kv_state = lax.dot_general(
        k_spread,
        v_head,
        (((0,), (0,)), ((), ())),
        precision=HIGHEST,
        preferred_element_type=jnp.float32,
    )
    k_total = jnp.sum(k_spread, axis=0)
    numerator = jnp.dot(q_spread, kv_state, precision=HIGHEST, preferred_element_type=jnp.float32)
    denominator = jnp.dot(q_spread, k_total, precision=HIGHEST, preferred_element_type=jnp.float32)
    return numerator / denominator[:, None]


def sequence_attention(q_seq, k_seq, v_seq, onehot, positions, projection):
    seq_len = q_seq.shape[0]

    def split_heads(values):
        return jnp.transpose(values.reshape(seq_len, HEADS, -1), (1, 0, 2))

    def one_head(triple):
        return jax.checkpoint(head_attention)(
            triple[0], triple[1], triple[2], onehot, positions, projection
        )

    mixed = lax.map(one_head, (split_heads(q_seq), split_heads(k_seq), split_heads(v_seq)))
    return jnp.transpose(mixed, (1, 0, 2)).reshape(seq_len, -1)


def local_attention(q_all, k_all, v_all, onehots, positions, projection):
    seq_count, seq_len = (onehots.shape[0], onehots.shape[1])

    def shaped(values):
        return values.reshape(seq_count, seq_len, -1)

    def one_sequence(bundle):
        return sequence_attention(bundle[0], bundle[1], bundle[2], bundle[3], bundle[4], projection)

    mixed = lax.map(one_sequence, (shaped(q_all), shaped(k_all), shaped(v_all), onehots, positions))
    return mixed.reshape(seq_count * seq_len, -1)


UNITS = 12


def wide_perm(shift_z, flip_x):
    pairs = []
    for z in range(4):
        for x in range(2):
            target_x = 1 - x if flip_x else x
            pairs.append((2 * z + x, 2 * ((z + shift_z) % 4) + target_x))
    return pairs


def narrow_perm(flip_y, flip_core):
    pairs = []
    for y in range(2):
        for core in range(2):
            pairs.append(
                (2 * y + core, 2 * (1 - y if flip_y else y) + (1 - core if flip_core else core))
            )
    return pairs


def pick(values, index, axis):
    return lax.dynamic_index_in_dim(values, index, axis, keepdims=False)


def to_units(inward, outward, expand, shrink):
    rows = outward.shape[0]
    return [
        inward,
        jnp.concatenate(
            [outward[None], jnp.transpose(expand.reshape(rows, 4, D), (1, 0, 2))], axis=0
        ),
        shrink.reshape(4, rows, D),
    ]


def places():
    wide = lax.axis_index("wide")
    narrow = lax.axis_index("narrow")
    return wide // 2, wide % 2, narrow // 2, narrow % 2


def special():
    return lax.axis_size("wide") == 8 and lax.axis_size("narrow") == 4


def gather_group(shard):
    if not special():
        return lax.all_gather(shard, "wide", axis=1, tiled=True)
    z, x, y, core = places()
    count = shard.shape[0]
    pieces = pick(shard.reshape(count, 2, 3, 16, D), core, 1)
    mine = jnp.stack([pick(pieces, y, 1), pieces[:, 2]], axis=0)
    along_z = [mine] + [lax.ppermute(mine, "wide", wide_perm(s, False)) for s in (1, 2, 3)]
    own_x = jnp.stack(along_z, axis=0)
    other_x = lax.ppermute(own_x, "wide", wide_perm(0, True))
    both = jnp.where(x == 0, jnp.stack([own_x, other_x]), jnp.stack([other_x, own_x]))
    other_y = lax.ppermute(both[:, :, 0], "narrow", narrow_perm(True, False))
    own_y = both[:, :, 0]
    half = jnp.stack(
        [jnp.where(y == 0, own_y, other_y), jnp.where(y == 0, other_y, own_y), both[:, :, 1]],
        axis=3,
    )
    other_half = lax.ppermute(half, "narrow", narrow_perm(False, True))
    full = jnp.where(
        core == 0, jnp.stack([half, other_half], axis=3), jnp.stack([other_half, half], axis=3)
    )
    order = (z - jnp.arange(4)) % 4
    full = jnp.take(full, order, axis=1)
    return jnp.transpose(full, (2, 1, 0, 3, 4, 5, 6)).reshape(count, D, D)


def reduce_group(local):
    if not special():
        part = lax.psum_scatter(
            local.astype(jnp.bfloat16), "wide", scatter_dimension=1, tiled=True
        )
        return lax.psum(part.astype(jnp.float32), "narrow")
    z, x, y, core = places()
    count = local.shape[0]
    low = local.astype(jnp.bfloat16).reshape(count, 4, 2, 2, 3, 16, D)
    got = lax.ppermute(pick(low, 1 - core, 3), "narrow", narrow_perm(False, True))
    chip = (pick(low, core, 3).astype(jnp.float32) + got.astype(jnp.float32)).astype(jnp.bfloat16)
    got = lax.ppermute(pick(chip, 1 - y, 3), "narrow", narrow_perm(True, False))
    own = (pick(chip, y, 3).astype(jnp.float32) + got.astype(jnp.float32)).astype(jnp.bfloat16)
    pair = jnp.stack([own, chip[:, :, :, 2]], axis=3)
    got = lax.ppermute(pick(pair, 1 - x, 2), "wide", wide_perm(0, True))
    line = (pick(pair, x, 2).astype(jnp.float32) + got.astype(jnp.float32)).astype(jnp.bfloat16)
    total = pick(line, z, 1).astype(jnp.float32)
    for s in (1, 2, 3):
        got = lax.ppermute(pick(line, (z + s) % 4, 1), "wide", wide_perm(s, False))
        total = total + got.astype(jnp.float32)
    mine = total.astype(jnp.bfloat16)
    got = lax.ppermute(mine, "narrow", narrow_perm(True, False))
    centre = (mine[:, 1].astype(jnp.float32) + got[:, 1].astype(jnp.float32)).astype(jnp.bfloat16)
    half = jnp.stack(
        [
            jnp.where(y == 0, mine[:, 0], got[:, 0]),
            jnp.where(y == 0, got[:, 0], mine[:, 0]),
            centre,
        ],
        axis=1,
    )
    other = lax.ppermute(half, "narrow", narrow_perm(False, True))
    full = jnp.where(core == 0, jnp.stack([half, other], 1), jnp.stack([other, half], 1))
    return full.astype(jnp.float32).reshape(count, 96, D)


def sum_wide(values):
    if not special():
        return lax.psum(values, "wide")
    for perm in (wide_perm(0, True), [(w, w ^ 2) for w in range(8)], [(w, w ^ 4) for w in range(8)]):
        values = values + lax.ppermute(values, "wide", perm)
    return values


def sum_narrow(values):
    if not special():
        return lax.psum(values, "narrow")
    for perm in (narrow_perm(False, True), narrow_perm(True, False)):
        values = values + lax.ppermute(values, "narrow", perm)
    return values


def shards(
    tokens,
    cotangent,
    lengths,
    projection,
    inward,
    outward,
    expand,
    shrink,
    vectors,
    inward_rows,
    inward_columns,
    outward_rows,
    outward_columns,
    expand_rows,
    expand_columns,
    shrink_rows,
    shrink_columns,
    vector_state,
):
    seq_count = lengths.shape[0]
    seq_len = tokens.shape[0] // seq_count
    model_dim = tokens.shape[1]
    onehots, positions = jax.vmap(lambda length_row: segment_tables(length_row, seq_len))(lengths)
    gain_one, shift_one, gain_two, shift_two = (vectors[0], vectors[1], vectors[2], vectors[3])
    bias_qkv = vectors[4:7]
    bias_out = vectors[7]
    bias_down = vectors[8]
    bias_up = vectors[9:].reshape(-1)
    groups = to_units(inward, outward, expand, shrink)
    gathered = [gather_group(group.astype(jnp.bfloat16)) for group in groups]
    full_in = gathered[0]
    full_out = gathered[1][0]
    full_up = jnp.transpose(gathered[1][1:], (1, 0, 2)).reshape(D, FF)
    full_down = jnp.transpose(gathered[2].reshape(4, lax.axis_size("wide"), -1, D), (1, 0, 2, 3)).reshape(FF, D)
    residual_in = tokens.astype(jnp.float32)
    normed_one, norm_one_back = jax.vjp(layer_norm, residual_in, gain_one, shift_one)
    normed_low = normed_one.astype(jnp.bfloat16)
    qkv_all = (
        jnp.einsum("td,kde->tke", normed_low, full_in, preferred_element_type=jnp.float32)
        + bias_qkv[None]
    )
    q_all, k_all, v_all = (qkv_all[:, 0], qkv_all[:, 1], qkv_all[:, 2])

    def attend(q_in, k_in, v_in):
        return local_attention(q_in, k_in, v_in, onehots, positions, projection)

    mixed, attend_back = jax.vjp(attend, q_all, k_all, v_all)
    mixed_low = mixed.astype(jnp.bfloat16)
    residual_mid = residual_in + (
        jnp.dot(mixed_low, full_out, preferred_element_type=jnp.float32) + bias_out
    )
    normed_two, norm_two_back = jax.vjp(layer_norm, residual_mid, gain_two, shift_two)
    normed_two_low = normed_two.astype(jnp.bfloat16)
    hidden = jnp.dot(normed_two_low, full_up, preferred_element_type=jnp.float32) + bias_up
    activated, gelu_back = jax.vjp(exact_gelu, hidden)
    activated_low = activated.astype(jnp.bfloat16)
    block_out = residual_mid + (
        jnp.dot(activated_low, full_down, preferred_element_type=jnp.float32) + bias_down
    )
    back_in, back_out, back_up, back_down = (full_in, full_out, full_up, full_down)
    out_grad_wide = cotangent.astype(jnp.float32)
    bias_down_grad = jnp.sum(cotangent, axis=0, dtype=jnp.float32)
    shrink_local = jnp.einsum(
        "tf,td->fd", activated_low, cotangent, preferred_element_type=jnp.float32
    )
    act_grad = jnp.einsum("td,fd->tf", cotangent, back_down, preferred_element_type=jnp.float32)
    hidden_grad = gelu_back(act_grad)[0].astype(jnp.bfloat16)
    bias_up_grad = jnp.sum(hidden_grad, axis=0, dtype=jnp.float32)
    expand_local = jnp.einsum(
        "td,tf->df", normed_two_low, hidden_grad, preferred_element_type=jnp.float32
    )
    normed_two_grad = jnp.einsum(
        "tf,df->td", hidden_grad, back_up, preferred_element_type=jnp.float32
    )
    mid_from_norm, gain_two_grad, shift_two_grad = norm_two_back(normed_two_grad)
    mid_grad = out_grad_wide + mid_from_norm
    branch_grad = mid_grad.astype(jnp.bfloat16)
    bias_out_grad = jnp.sum(branch_grad, axis=0, dtype=jnp.float32)
    outward_local = jnp.einsum(
        "td,te->de", mixed_low, branch_grad, preferred_element_type=jnp.float32
    )
    mixed_grad = jnp.einsum("te,de->td", branch_grad, back_out, preferred_element_type=jnp.float32)
    q_grad, k_grad, v_grad = attend_back(mixed_grad)
    qkv_grad = jnp.stack([q_grad, k_grad, v_grad], axis=1).astype(jnp.bfloat16)
    bias_qkv_grad = jnp.sum(qkv_grad, axis=0, dtype=jnp.float32)
    inward_local = jnp.einsum(
        "td,tke->kde", normed_low, qkv_grad, preferred_element_type=jnp.float32
    )
    normed_one_grad = jnp.einsum(
        "tke,kde->td", qkv_grad, back_in, preferred_element_type=jnp.float32
    )
    in_from_norm, gain_one_grad, shift_one_grad = norm_one_back(normed_one_grad)
    input_grad = mid_grad + in_from_norm
    vector_local = jnp.concatenate(
        [
            gain_one_grad[None],
            shift_one_grad[None],
            gain_two_grad[None],
            shift_two_grad[None],
            bias_qkv_grad,
            bias_out_grad[None],
            bias_down_grad[None],
            bias_up_grad.reshape(-1, model_dim),
        ],
        axis=0,
    )
    reduced = [
        reduce_group(part)
        for part in (
            jnp.transpose(
                shrink_local.reshape(lax.axis_size("wide"), 4, -1, D), (1, 0, 2, 3)
            ).reshape(4, D, D),
            jnp.concatenate(
                [outward_local[None], jnp.transpose(expand_local.reshape(D, 4, D), (1, 0, 2))]
            ),
            inward_local,
        )
    ]
    shrink_grad = reduced[0].reshape(-1, D)
    outward_grad = reduced[1][0]
    expand_grad = jnp.transpose(reduced[1][1:], (1, 0, 2)).reshape(-1, FF)
    inward_grad = reduced[2]
    vector_part = sum_narrow(vector_local)
    decay = 1.0 - STEP ** (-0.8)
    wide_count = lax.axis_size("wide")
    grads_list = [inward_grad, outward_grad[None], expand_grad[None], shrink_grad[None]]
    rows_old = [inward_rows, outward_rows[None], expand_rows[None], shrink_rows[None]]
    columns_old = [
        inward_columns,
        outward_columns[None],
        expand_columns[None],
        shrink_columns[None],
    ]
    weights_old = [inward, outward[None], expand[None], shrink[None]]
    rates = [0.3 * D ** (-0.5), 1.2 * D ** (-0.5), 0.3 * D ** (-0.5), 0.3 * FF ** (-0.5)]
    bounds = [0, 3, 4, 5, 6]
    rows_next = []
    column_parts = []
    for member in range(4):
        squares = grads_list[member] * grads_list[member] + square_eps
        rows_next.append(decay * rows_old[member] + (1.0 - decay) * jnp.mean(squares, axis=-1))
        column_parts.append(jnp.sum(squares, axis=-2))
    row_totals = jnp.concatenate([jnp.sum(entry, axis=-1) for entry in rows_next])
    shapes = [part.shape for part in column_parts] + [row_totals.shape, vector_part.shape]
    flat = jnp.concatenate(
        [part.reshape(-1) for part in column_parts + [row_totals, vector_part]]
    )
    flat = jnp.pad(flat, (0, -flat.shape[0] % 1024)).reshape(-1, 128)
    flat = sum_wide(flat).reshape(-1)
    summed = []
    offset = 0
    for shape in shapes:
        size = 1
        for extent in shape:
            size *= extent
        summed.append(flat[offset : offset + size].reshape(shape))
        offset += size
    column_sums = list(summed[0:4])
    totals_sum = summed[4]
    vector_grad = summed[5]
    columns_next = []
    scaled_list = []
    row_means = []
    sizes_full = []
    for member in range(4):
        grad_now = grads_list[member]
        rows_full = grad_now.shape[-2] * wide_count
        sizes_full.append(rows_full * grad_now.shape[-1])
        columns_next.append(
            decay * columns_old[member] + (1.0 - decay) * column_sums[member] / rows_full
        )
        row_mean = totals_sum[bounds[member] : bounds[member + 1]] / rows_full
        row_means.append(row_mean)
        scaled_list.append(
            grad_now
            * lax.rsqrt(rows_next[member] / row_mean[:, None])[..., None]
            * lax.rsqrt(columns_next[member])[:, None, :]
        )
    partial_squares = jnp.concatenate(
        [jnp.sum(entry * entry, axis=(-2, -1)) for entry in scaled_list]
    )
    total_squares = sum_wide(jnp.pad(partial_squares, (0, 122)).reshape(1, 128))[0, :6]
    rms_list = [
        jnp.sqrt(total_squares[bounds[member] : bounds[member + 1]] / sizes_full[member])
        for member in range(4)
    ]
    weights_next = []
    for member in range(4):
        limiter = jnp.maximum(1.0, rms_list[member] / clip_level)
        weights_next.append(
            weights_old[member] - rates[member] * scaled_list[member] / limiter[:, None, None]
        )
    vector_state_next = decay * vector_state + (1.0 - decay) * (
        vector_grad * vector_grad + square_eps
    )
    vector_update = vector_grad * lax.rsqrt(vector_state_next)
    vector_rms = jnp.sqrt(jnp.mean(vector_update * vector_update))
    vectors_next = vectors - 0.25 * vector_update / jnp.maximum(1.0, vector_rms / clip_level)
    return (
        block_out,
        input_grad,
        inward_grad,
        outward_grad,
        expand_grad,
        shrink_grad,
        vector_grad,
        rows_next[0],
        columns_next[0],
        rows_next[1][0],
        columns_next[1][0],
        rows_next[2][0],
        columns_next[2][0],
        rows_next[3][0],
        columns_next[3][0],
        vector_state_next,
        weights_next[0],
        weights_next[1][0],
        weights_next[2][0],
        weights_next[3][0],
        vectors_next,
    )


def solution(mesh):
    placed = (
        P(("narrow", "wide"), None),
        P(("narrow", "wide"), None),
        P(("narrow", "wide"), None),
        P(),
        P(None, "wide", None),
        P("wide", None),
        P("wide", None),
        P("wide", None),
        P(),
        P(None, "wide"),
        P(),
        P("wide"),
        P(),
        P("wide"),
        P(),
        P("wide"),
        P(),
        P(),
    )
    return jax.shard_map(
        shards,
        mesh=mesh,
        in_specs=placed,
        out_specs=(
            P(("narrow", "wide"), None),
            P(("narrow", "wide"), None),
            P(None, "wide", None),
            P("wide", None),
            P("wide", None),
            P("wide", None),
            P(),
            P(None, "wide"),
            P(),
            P("wide"),
            P(),
            P("wide"),
            P(),
            P("wide"),
            P(),
            P(),
            P(None, "wide", None),
            P("wide", None),
            P("wide", None),
            P("wide", None),
            P(),
        ),
        check_vma=False,
    )
```

```python
import functools

import jax
import jax.numpy as jnp
import numpy as np
from jax import lax
from jax.experimental import pallas as pl
from jax.experimental.pallas import tpu as pltpu
from jax.sharding import PartitionSpec as P

D = 768
HEADS = 12
HD = 64
FF = 3072
FEAT = 32
STEP = 10
LEN = 1024
SPAN = 256
CHUNKS = 3
GROUPS = 3
WIDTH = 256
FFC = FF // CHUNKS

norm_eps = 1e-05
square_eps = 1e-30
clip_level = 1.0

F32 = jnp.float32
BF16 = jnp.bfloat16
VMEM_LIMIT = 60 * 1024 * 1024


def mm(left, right):
    return lax.dot_general(left, right, (((1,), (0,)), ((), ())), preferred_element_type=F32)


def mm_nt(left, right):
    return lax.dot_general(left, right, (((1,), (1,)), ((), ())), preferred_element_type=F32)


def mm_tn(left, right):
    return lax.dot_general(left, right, (((0,), (0,)), ((), ())), preferred_element_type=F32)


def halves(values):
    high = values.astype(BF16)
    return high, (values - high.astype(F32)).astype(BF16)


TAIL = (
    0.1795078068971634,
    0.17978088557720184,
    0.14234966039657593,
    0.06379217654466629,
    0.0434231162071228,
    -0.261725515127182,
    0.20454804599285126,
    -0.05167665705084801,
)


def normal_parts(values):
    size = jnp.abs(values)
    t = 1.0 / (1.0 + 0.45 * size)
    poly = TAIL[-1]
    for coeff in TAIL[-2::-1]:
        poly = poly * t + coeff
    bell = jnp.exp(-0.5 * values * values)
    tail = poly * t * bell
    return jnp.where(values >= 0, 1.0 - tail, tail), bell * 0.3989422804014327


def transposed(values):
    row = lax.broadcasted_iota(jnp.int32, (256, 256), 0)
    col = lax.broadcasted_iota(jnp.int32, (256, 256), 1)
    eye = (row == col).astype(F32).astype(BF16)
    return mm_nt(eye, values).astype(BF16)


def head_perm():
    perm = np.zeros((WIDTH, WIDTH), np.float32)
    for head in range(4):
        for half in range(2):
            for i in range(32):
                perm[head * 64 + half * 32 + i, half * 128 + head * 32 + i] = 1.0
    return perm


def make_blocks(lengths, base, first, last):
    def step(s, carry):
        count, begin, begin_row, end = carry
        new_end = end + lengths[0, s]
        full = new_end - begin_row > SPAN

        @pl.when(full)
        def _():
            base[count] = begin_row
            first[count] = begin
            last[count] = s - 1

        row = jnp.minimum((end // 16) * 16, LEN - SPAN)
        return (
            jnp.where(full, count + 1, count),
            jnp.where(full, s, begin),
            jnp.where(full, row, begin_row),
            new_end,
        )

    segments = lengths.shape[1]
    zero = jnp.int32(0)
    count, begin, begin_row, _ = lax.fori_loop(0, segments, step, (zero, zero, zero, zero))
    base[count] = begin_row
    first[count] = begin
    last[count] = segments - 1
    return count + 1


def lane_mask(lo, hi, width, dtype):
    lane = lax.broadcasted_iota(jnp.int32, (1, width), 1)
    return ((lane >= lo) & (lane < hi)).astype(F32).astype(dtype)


def value_rows(v_pair, head):
    keep = lane_mask(64 * head, 64 * head + 64, 128, BF16)
    return jnp.concatenate([v_pair * keep, jnp.broadcast_to(keep, v_pair.shape)], axis=1)


def span_mask(onehot, rows, lo, hi):
    member = onehot[rows, :]
    lane = lax.broadcasted_iota(jnp.int32, (1, 128), 1)
    inside = ((lane >= lo) & (lane <= hi)).astype(F32).astype(BF16)
    return mm_nt(member * inside, member).astype(BF16)


def cost(flops, size):
    return pl.CostEstimate(flops=flops, transcendentals=0, bytes_accessed=size)


def any_spec():
    return pl.BlockSpec(memory_space=pl.ANY)


def in_copies(place, pieces, dst, sems, unit):
    if len(pieces) == 1:
        rows = dst.shape[1] // 3
        here = pl.ds(unit * rows, rows)
        return [pltpu.make_async_copy(pieces[0].at[:, here], dst.at[:, here], sems.at[unit, 0])]
    z, x, core = place[0], place[1], place[3]
    copies = []
    for side in range(2):
        half = core if side == 0 else 1 - core
        for flip in range(2):
            column = x if flip == 0 else 1 - x
            for shift in range(4):
                row = lax.rem(z + 4 - shift, 4) * 2 + column
                start = pl.multiple_of(unit * 96 + half * 48, 16)
                copies.append(
                    pltpu.make_async_copy(
                        pieces[2 * unit + side].at[flip, shift],
                        dst.at[row, pl.ds(start, 48)],
                        sems.at[unit, len(copies)],
                    )
                )
    return copies


def flat_copies(place, pieces, dst, sems):
    if len(pieces) == 1:
        return [pltpu.make_async_copy(pieces[0], dst, sems.at[0])]
    z, x, core = place[0], place[1], place[3]
    span = dst.shape[1] // 2
    copies = []
    for side in range(2):
        half = core if side == 0 else 1 - core
        for flip in range(2):
            column = x if flip == 0 else 1 - x
            for shift in range(4):
                row = lax.rem(z + 4 - shift, 4) * 2 + column
                start = pl.multiple_of(half * span, 16)
                copies.append(
                    pltpu.make_async_copy(
                        pieces[side].at[flip, shift],
                        dst.at[row, pl.ds(start, span)],
                        sems.at[len(copies)],
                    )
                )
    return copies


def attend_kernel(count_in, lengths, place, *refs):
    pieces = refs[:count_in]
    (
        x_ref, norm_ref, bias_ref, perm_ref, proj_ref, cos_ref, sin_ref, onehot_ref,
        attn_ref, mixed_ref, a1t_ref, w_ref, wq_ref, wk_ref, qf_ref, kf_ref, v_ref, rden_ref,
        a1, qb, kb, vb, parts, base, first, last, sems,
    ) = refs[count_in:]
    group = pl.program_id(0)

    @pl.when(group == 0)
    def _():
        for unit in range(GROUPS):
            for copy in in_copies(place, pieces, w_ref, sems, unit):
                copy.start()
        for rows in range(0, LEN, 256):
            here = pl.ds(rows, 256)
            x = x_ref[here, :].astype(F32)
            centre = x - jnp.mean(x, axis=-1, keepdims=True)
            spread = jnp.mean(centre * centre, axis=-1, keepdims=True)
            a1[here, :] = (
                centre * lax.rsqrt(spread + norm_eps) * norm_ref[0:1, :] + norm_ref[1:2, :]
            ).astype(BF16)
        for cols in range(0, D, 256):
            a1t_ref[cols : cols + 256, :] = transposed(a1[:, cols : cols + 256])

    for unit in range(GROUPS):

        @pl.when(group == unit)
        def _():
            for copy in in_copies(place, pieces, w_ref, sems, unit):
                copy.wait()

    count = make_blocks(lengths, base, first, last)
    shard = w_ref.shape[1] // 3
    here = pl.ds(pl.multiple_of(group * shard, 16), shard)
    w = w_ref[:, here, :].reshape(D, D)
    perm = perm_ref[...]
    bias = bias_ref[0]
    proj_high = proj_ref[0]
    proj_low = proj_ref[1]
    square = proj_ref[2]
    for which, (out_w, out_f, low_f) in enumerate(((wq_ref, qf_ref, qb), (wk_ref, kf_ref, kb))):
        weight = mm(w[:, WIDTH * which : WIDTH * (which + 1)], perm).astype(BF16)
        for rows in range(0, LEN, 256):
            here = pl.ds(rows, 256)
            u = (mm(a1[here, :], weight) + bias[which : which + 1, :]) * HD ** (-0.25)
            c = u[:, :128]
            e = u[:, 128:]
            cosine = cos_ref[here, :]
            sine = sin_ref[here, :]
            turned = jnp.concatenate([c * cosine - e * sine, e * cosine + c * sine], axis=1)
            out_w[0, here, :] = turned
            high, low = halves(turned)
            sq_high, sq_low = halves(turned * turned)
            logits = (
                mm(high, proj_high) + mm(high, proj_low) + mm(low, proj_high)
                - (mm(sq_high, square) + mm(sq_low, square))
            )
            phi = jnp.exp(logits) * FEAT ** (-0.5)
            out_f[0, here, :] = phi
            low_f[here, :] = phi.astype(BF16)
    for rows in range(0, LEN, 256):
        here = pl.ds(rows, 256)
        v = mm(a1[here, :], w[:, 2 * WIDTH :]) + bias[2:3, :]
        v_ref[0, here, :] = v
        vb[here, :] = v.astype(BF16)
    parts[...] = jnp.zeros_like(parts)

    def one_span(index, carry):
        rows = pl.ds(pl.multiple_of(base[index], 16), SPAN)
        mask = span_mask(onehot_ref, rows, first[index], last[index])
        q = qb[rows, :]
        k = kb[rows, :]
        for pair in range(2):
            v_pair = vb[rows, 128 * pair : 128 * (pair + 1)]
            total = jnp.zeros((SPAN, WIDTH), F32)
            for side in range(2):
                head = 2 * pair + side
                scores = mm_nt(q * lane_mask(32 * head, 32 * head + 32, 128, BF16), k)
                total = total + mm(scores.astype(BF16) * mask, value_rows(v_pair, side))
            parts[pair, rows, :] += total
        return carry

    lax.fori_loop(0, count, one_span, 0)
    for pair in range(2):
        lanes = slice(128 * pair, 128 * (pair + 1))
        inverse = 1.0 / parts[pair, :, 128:]
        rden_ref[0, :, lanes] = inverse
        mixed = parts[pair, :, :128] * inverse
        mixed_ref[0, :, lanes] = mixed
        attn_ref[:, lanes] = mixed.astype(BF16)


def whole_spec(shape, **options):
    return pl.BlockSpec(shape, lambda *_: (0,) * len(shape), **options)


def group_spec(shape):
    return pl.BlockSpec((1,) + shape, lambda g, *_: (g,) + (0,) * len(shape))


def attend(lengths, place, pieces, wide, tokens, norm, bias, perm, proj, cosine, sine, onehot):
    def out(shape, dtype):
        return jax.ShapeDtypeStruct((GROUPS,) + shape, dtype)

    rows_in = 3 * D // wide
    return pl.pallas_call(
        functools.partial(attend_kernel, len(pieces)),
        grid_spec=pltpu.PrefetchScalarGridSpec(
            num_scalar_prefetch=2,
            grid=(GROUPS,),
            in_specs=[any_spec()] * len(pieces)
            + [
                whole_spec((LEN, D)), whole_spec((2, D)), group_spec((3, WIDTH)),
                whole_spec((WIDTH, WIDTH)), whole_spec((3, WIDTH, 128)), whole_spec((LEN, 128)),
                whole_spec((LEN, 128)), whole_spec((LEN, 128)),
            ],
            out_specs=[
                pl.BlockSpec((LEN, WIDTH), lambda g, *_: (0, g)), group_spec((LEN, WIDTH)),
                whole_spec((D, LEN)), whole_spec((wide, rows_in, D)), group_spec((LEN, WIDTH)),
                group_spec((LEN, WIDTH)), group_spec((LEN, 128)), group_spec((LEN, 128)),
                group_spec((LEN, WIDTH)), group_spec((LEN, WIDTH)),
            ],
            scratch_shapes=[
                pltpu.VMEM((LEN, D), BF16),
                pltpu.VMEM((LEN, 128), BF16), pltpu.VMEM((LEN, 128), BF16),
                pltpu.VMEM((LEN, WIDTH), BF16), pltpu.VMEM((2, LEN, WIDTH), F32),
                pltpu.SMEM((32,), jnp.int32), pltpu.SMEM((32,), jnp.int32),
                pltpu.SMEM((32,), jnp.int32), pltpu.SemaphoreType.DMA((GROUPS, 16)),
            ],
        ),
        out_shape=[
            jax.ShapeDtypeStruct((LEN, D), BF16), out((LEN, WIDTH), F32),
            jax.ShapeDtypeStruct((D, LEN), BF16), jax.ShapeDtypeStruct((wide, rows_in, D), BF16),
            out((LEN, WIDTH), F32), out((LEN, WIDTH), F32), out((LEN, 128), F32),
            out((LEN, 128), F32), out((LEN, WIDTH), F32), out((LEN, WIDTH), F32),
        ],
        compiler_params=pltpu.CompilerParams(
            dimension_semantics=("arbitrary",), vmem_limit_bytes=VMEM_LIMIT
        ),
        cost_estimate=cost(20 * 10**9, 40 * 10**6),
        name="attend",
    )(lengths, place, *pieces, tokens, norm, bias, perm, proj, cosine, sine, onehot)


def attend_back_kernel(
    lengths, place, dmixed_ref, mixed_ref, rden_ref, wq_ref, wk_ref, qf_ref, kf_ref, v_ref,
    a1t_ref, w_ref, perm_ref, proj_ref, cos_ref, sin_ref, onehot_ref, ones_ref, da1_in,
    keep_ref, send_ref, bias_ref, da1_ref,
    qb, kb, dnb, dnh, lift, dqf, dkf, dv, dqkv, base, first, last,
):
    count = make_blocks(lengths, base, first, last)
    qb[...] = qf_ref[0].astype(BF16)
    kb[...] = kf_ref[0].astype(BF16)
    lane = lax.broadcasted_iota(jnp.int32, (1, 128), 1)
    ones = ones_ref[...]
    for pair in range(2):
        lanes = slice(128 * pair, 128 * (pair + 1))
        for rows in range(0, LEN, 256):
            here = pl.ds(rows, 256)
            dnum = dmixed_ref[here, lanes] * rden_ref[0, here, lanes]
            high, low = halves(dnum)
            dnb[here, lanes] = high
            part_high, part_low = halves(dnum * mixed_ref[0, here, lanes])
            dden = -mm(jnp.concatenate([part_high, part_low], axis=1), ones)
            den_high, den_low = halves(dden)
            high, low = high.astype(F32), low.astype(F32)
            den_high = pltpu.roll(den_high.astype(F32), 64, 1)
            den_low = pltpu.roll(den_low.astype(F32), 64, 1)
            low_far = pltpu.roll(low, 64, 1)
            v = v_ref[0, here, lanes]
            v_high, v_low = halves(v)
            v_high, v_low = v_high.astype(F32), v_low.astype(F32)
            v_far = pltpu.roll(v_high, 64, 1)
            for side in range(2):
                own = (lane >= 64 * side) & (lane < 64 * side + 64)
                mark = 64 - 64 * side
                rest = jnp.where(lane == mark, den_high, jnp.where(lane == mark + 1, den_low, 0.0))
                both = ((lane == mark) | (lane == mark + 1)).astype(F32)
                head = 2 * pair + side
                dnh[head, here, :128] = jnp.where(own, high, low_far).astype(BF16)
                dnh[head, here, 128:] = jnp.where(own, high, rest).astype(BF16)
                lift[head, here, :128] = jnp.where(own, v_high, v_far).astype(BF16)
                lift[head, here, 128:] = jnp.where(own, v_low, both).astype(BF16)
    dqf[...] = jnp.zeros_like(dqf)
    dkf[...] = jnp.zeros_like(dkf)
    dv[...] = jnp.zeros_like(dv)

    def one_span(index, carry):
        rows = pl.ds(pl.multiple_of(base[index], 16), SPAN)
        mask = span_mask(onehot_ref, rows, first[index], last[index])
        q = qb[rows, :]
        k = kb[rows, :]
        q_total = jnp.zeros((SPAN, 128), F32)
        k_total = jnp.zeros((SPAN, 128), F32)
        for pair in range(2):
            lanes = slice(128 * pair, 128 * (pair + 1))
            dn_pair = dnb[rows, lanes]
            v_total = jnp.zeros((SPAN, 128), F32)
            for side in range(2):
                head = 2 * pair + side
                feats = lane_mask(32 * head, 32 * head + 32, 128, BF16)
                q_head = q * feats
                k_head = k * feats
                lifted = lift[head, rows, :]
                dn_head = dnh[head, rows, :]
                scores = mm_nt(k, q_head).astype(BF16) * mask
                dscores = mm_nt(dn_head, lifted).astype(BF16) * mask
                dscores_t = mm_nt(lifted, dn_head).astype(BF16) * mask
                q_total = q_total + mm(dscores, k_head)
                k_total = k_total + mm(dscores_t, q_head)
                own = lane_mask(64 * side, 64 * side + 64, 128, BF16)
                v_total = v_total + mm(scores, dn_pair * own)
            dv[rows, lanes] += v_total
        dqf[rows, :] += q_total
        dkf[rows, :] += k_total
        return carry

    lax.fori_loop(0, count, one_span, 0)
    proj_high = proj_ref[0]
    proj_low = proj_ref[1]
    square = proj_ref[2]
    perm = perm_ref[...]
    for which, (w_in, phi_in, dphi) in enumerate(
        ((wq_ref, qf_ref, dqf), (wk_ref, kf_ref, dkf))
    ):
        for rows in range(0, LEN, 256):
            here = pl.ds(rows, 256)
            r = dphi[here, :] * phi_in[0, here, :]
            high, low = halves(r)
            spread = mm_nt(high, square) + mm_nt(low, square)
            dw = mm_nt(high, proj_high) + mm_nt(low, proj_high) + mm_nt(high, proj_low)
            du = (dw - 2.0 * w_in[0, here, :] * spread) * HD ** (-0.25)
            c = du[:, :128]
            e = du[:, 128:]
            cosine = cos_ref[here, :]
            sine = sin_ref[here, :]
            turned = jnp.concatenate([c * cosine + e * sine, e * cosine - c * sine], axis=1)
            dqkv[here, WIDTH * which : WIDTH * (which + 1)] = mm_nt(
                turned.astype(BF16), perm
            ).astype(BF16)
    dqkv[:, 2 * WIDTH :] = dv[...].astype(BF16)
    bias_ref[0] = jnp.sum(dqkv[...].astype(F32), axis=0, keepdims=True)
    grad = mm(a1t_ref[...], dqkv[...]).astype(BF16)
    store_halves(grad, place[3], keep_ref, send_ref)
    w = w_ref[...].reshape(D, D)
    if da1_in is None:
        da1_ref[...] = mm_nt(dqkv[...], w)
    else:
        da1_ref[...] = da1_in[...] + mm_nt(dqkv[...], w)


def store_halves(grad, core, keep_ref, send_ref):
    wide, rows = keep_ref.shape[0], D // keep_ref.shape[0]
    half = rows // 2
    parts = grad.reshape(wide, rows, D)
    for cols in range(3):
        block = parts[:, :, WIDTH * cols : WIDTH * (cols + 1)]
        here = pl.ds(half * cols, half)

        @pl.when(core == 0)
        def _():
            keep_ref[:, here, :] = block[:, :half]
            send_ref[:, here, :] = block[:, half:]

        @pl.when(core == 1)
        def _():
            keep_ref[:, here, :] = block[:, half:]
            send_ref[:, here, :] = block[:, :half]


def attend_back(
    group, lengths, place, wide, dmixed, saved, a1t, w_in, perm, proj, cosine, sine, onehot, ones,
    da1,
):
    mixed, rden, wq, wk, qf, kf, v = saved

    def by_group(shape):
        return pl.BlockSpec((1,) + shape, lambda *_: (group,) + (0,) * len(shape))

    rows_in = D // wide
    kernel = attend_back_kernel
    extra = [da1]
    extra_specs = [whole_spec((LEN, D))]
    if da1 is None:
        extra, extra_specs = [], []

        def kernel(*refs):
            attend_back_kernel(*refs[:18], None, *refs[18:])

    half = jax.ShapeDtypeStruct((wide, 3 * rows_in // 2, WIDTH), BF16)
    return pl.pallas_call(
        kernel,
        grid_spec=pltpu.PrefetchScalarGridSpec(
            num_scalar_prefetch=2,
            grid=(1,),
            in_specs=[
                pl.BlockSpec((LEN, WIDTH), lambda *_: (0, group)),
                by_group((LEN, WIDTH)), by_group((LEN, WIDTH)), by_group((LEN, WIDTH)),
                by_group((LEN, WIDTH)), by_group((LEN, 128)), by_group((LEN, 128)),
                by_group((LEN, WIDTH)), whole_spec((D, LEN)),
                pl.BlockSpec((wide, rows_in, D), lambda *_: (0, group, 0)),
                whole_spec((WIDTH, WIDTH)), whole_spec((3, WIDTH, 128)), whole_spec((LEN, 128)),
                whole_spec((LEN, 128)), whole_spec((LEN, 128)), whole_spec((WIDTH, 128)),
            ] + extra_specs,
            out_specs=[
                whole_spec(half.shape), whole_spec(half.shape), whole_spec((1, 1, D)),
                whole_spec((LEN, D)),
            ],
            scratch_shapes=[
                pltpu.VMEM((LEN, 128), BF16), pltpu.VMEM((LEN, 128), BF16),
                pltpu.VMEM((LEN, WIDTH), BF16), pltpu.VMEM((4, LEN, WIDTH), BF16),
                pltpu.VMEM((4, LEN, WIDTH), BF16), pltpu.VMEM((LEN, 128), F32),
                pltpu.VMEM((LEN, 128), F32), pltpu.VMEM((LEN, WIDTH), F32),
                pltpu.VMEM((LEN, D), BF16),
                pltpu.SMEM((32,), jnp.int32), pltpu.SMEM((32,), jnp.int32),
                pltpu.SMEM((32,), jnp.int32),
            ],
        ),
        out_shape=[
            half, half, jax.ShapeDtypeStruct((1, 1, D), F32), jax.ShapeDtypeStruct((LEN, D), F32),
        ],
        compiler_params=pltpu.CompilerParams(
            dimension_semantics=("arbitrary",), vmem_limit_bytes=VMEM_LIMIT
        ),
        cost_estimate=cost(12 * 10**9, 25 * 10**6),
        name="attend_back",
    )(
        lengths, place, dmixed, mixed, rden, wq, wk, qf, kf, v, a1t, w_in, perm, proj, cosine,
        sine, onehot, ones, *extra,
    )


def chunk_step(
    place, wide, flat, offset, bias_up, dy_ref, a2, a2t, dyt, up, down, act, dhidden, y, back,
    keep_ref, send_ref, dbias_ref, fresh,
):
    rows_up = D // wide
    rows_down = FFC // wide
    for cols in range(4):
        here = pl.ds(offset + rows_up * cols, rows_up)
        up[:, WIDTH * cols : WIDTH * (cols + 1)] = flat[:, here, :].reshape(D, WIDTH)
    for cols in range(3):
        here = pl.ds(offset + 4 * rows_up + rows_down * cols, rows_down)
        down[:, WIDTH * cols : WIDTH * (cols + 1)] = flat[:, here, :].reshape(FFC, WIDTH)
    bias_total = jnp.zeros((1, FFC), F32)
    for rows in range(0, LEN, 256):
        here = pl.ds(rows, 256)
        hidden = mm(a2[here, :], up[...]) + bias_up
        below, density = normal_parts(hidden)
        act_now = (hidden * below).astype(BF16)
        act[here, :] = act_now
        dact = mm_nt(dy_ref[here, :], down[...])
        dhidden_now = (dact * (below + hidden * density)).astype(BF16)
        dhidden[here, :] = dhidden_now
        bias_total = bias_total + jnp.sum(dhidden_now.astype(F32), axis=0, keepdims=True)
        if fresh:
            y[here, :] = mm(act_now, down[...])
            back[here, :] = mm_nt(dhidden_now, up[...])
        else:
            y[here, :] += mm(act_now, down[...])
            back[here, :] += mm_nt(dhidden_now, up[...])
    dbias_ref[...] = bias_total
    grad_up = mm(a2t[...], dhidden[...]).astype(BF16).reshape(wide, rows_up, FFC)
    grad_down = mm(dyt[...], act[...]).astype(BF16)
    core = place[3]

    def store_up(ref):
        for cols in range(4):
            ref[:, rows_up * cols : rows_up * (cols + 1), :] = grad_up[
                :, :, WIDTH * cols : WIDTH * (cols + 1)
            ]

    def store_down(ref):
        if wide == 1:
            for cols in range(4):
                ref[0, D * cols : D * (cols + 1), :] = grad_down[
                    :, WIDTH * cols : WIDTH * (cols + 1)
                ]
            return
        for shard in range(wide):
            block = grad_down[:, rows_down * shard : rows_down * (shard + 1)]
            ref[shard, :, :128] = block[: D // 2]
            ref[shard, :, 128:] = block[D // 2 :]

    @pl.when(core == 0)
    def _():
        store_up(keep_ref)
        store_down(send_ref)

    @pl.when(core == 1)
    def _():
        store_up(send_ref)
        store_down(keep_ref)


def middle_first_kernel(wide, count_in, place, *refs):
    pieces = refs[:count_in]
    (
        x_ref, attn_ref, dy_ref, rows_ref, bias_up_ref,
        x1_ref, a2_ref, a2t_ref, dyt_ref, y_ref, back_ref, out_ref, keep_ref, send_ref, dbias_ref,
        flat, up, down, act, dhidden, sems,
    ) = refs[count_in:]
    copies = flat_copies(place, pieces, flat, sems)
    for copy in copies:
        copy.start()
    for cols in range(0, D, 256):
        dyt_ref[cols : cols + 256, :] = transposed(dy_ref[:, cols : cols + 256])
    for copy in copies:
        copy.wait()
    rows_out = D // wide
    for cols in range(3):
        here = pl.ds(rows_out * cols, rows_out)
        out_ref[:, WIDTH * cols : WIDTH * (cols + 1)] = flat[:, here, :].reshape(D, WIDTH)
    for rows in range(0, LEN, 256):
        here = pl.ds(rows, 256)
        x1 = x_ref[here, :].astype(F32) + (mm(attn_ref[here, :], out_ref[...]) + rows_ref[7:8, :])
        x1_ref[here, :] = x1
        centre = x1 - jnp.mean(x1, axis=-1, keepdims=True)
        spread = jnp.mean(centre * centre, axis=-1, keepdims=True)
        a2_ref[here, :] = (
            centre * lax.rsqrt(spread + norm_eps) * rows_ref[2:3, :] + rows_ref[3:4, :]
        ).astype(BF16)
    for cols in range(0, D, 256):
        a2t_ref[cols : cols + 256, :] = transposed(a2_ref[:, cols : cols + 256])
    chunk_step(
        place, wide, flat, 3 * rows_out, bias_up_ref[...], dy_ref, a2_ref, a2t_ref, dyt_ref, up,
        down, act, dhidden, y_ref, back_ref, keep_ref, send_ref, dbias_ref, True,
    )


def middle_next_kernel(wide, chunk, count_in, place, *refs):
    pieces = refs[:count_in]
    final = chunk == CHUNKS - 1
    refs = refs[count_in:]
    dy_ref, a2_ref, a2t_ref, dyt_ref, bias_up_ref, y_in, back_in = refs[:7]
    refs = refs[7:]
    if final:
        x1_ref, attn_ref, out_ref, rows_ref = refs[:4]
        block_ref, dx1_ref, dmixed_ref, okeep_ref, osend_ref, vec_ref = refs[4:10]
        keep_ref, send_ref, dbias_ref = refs[10:13]
        flat, up, down, act, dhidden, y, back, dbranch, sems = refs[13:]
    else:
        y_ref, back_ref, keep_ref, send_ref, dbias_ref = refs[:5]
        flat, up, down, act, dhidden, y, back, sems = refs[5:]
    if count_in == 2:
        own_here = place[3] == chunk - 1

        @pl.when(own_here)
        def _():
            pltpu.make_async_copy(pieces[0], flat, sems.at[2]).start()

        @pl.when(jnp.logical_not(own_here))
        def _():
            pltpu.make_async_copy(pieces[1], flat, sems.at[2]).start()

    else:
        pltpu.make_async_copy(pieces[0], flat, sems.at[2]).start()
    y_copy = pltpu.make_async_copy(y_in, y, sems.at[0])
    back_copy = pltpu.make_async_copy(back_in, back, sems.at[1])
    y_copy.start()
    back_copy.start()
    pltpu.make_async_copy(pieces[0], flat, sems.at[2]).wait()
    y_copy.wait()
    back_copy.wait()
    chunk_step(
        place, wide, flat, 0, bias_up_ref[...], dy_ref, a2_ref, a2t_ref, dyt_ref, up, down, act,
        dhidden, y, back, keep_ref, send_ref, dbias_ref, False,
    )
    if not final:
        y_ref[...] = y[...]
        back_ref[...] = back[...]
        return
    zero = jnp.zeros((1, D), F32)
    dgain, dshift, dbias_out, dbias_down = zero, zero, zero, zero
    for rows in range(0, LEN, 256):
        here = pl.ds(rows, 256)
        x1 = x1_ref[here, :]
        block_ref[here, :] = x1 + (y[here, :] + rows_ref[8:9, :])
        dn = back[here, :]
        dy = dy_ref[here, :].astype(F32)
        centre = x1 - jnp.mean(x1, axis=-1, keepdims=True)
        spread = jnp.mean(centre * centre, axis=-1, keepdims=True)
        scale = lax.rsqrt(spread + norm_eps)
        zh = centre * scale
        dgain = dgain + jnp.sum(dn * zh, axis=0, keepdims=True)
        dshift = dshift + jnp.sum(dn, axis=0, keepdims=True)
        e = dn * rows_ref[2:3, :]
        dz = (
            e - jnp.mean(e, axis=-1, keepdims=True) - zh * jnp.mean(e * zh, axis=-1, keepdims=True)
        ) * scale
        dx1 = dy + dz
        dx1_ref[here, :] = dx1
        low = dx1.astype(BF16)
        dbranch[here, :] = low
        dbias_out = dbias_out + jnp.sum(low.astype(F32), axis=0, keepdims=True)
        dbias_down = dbias_down + jnp.sum(dy, axis=0, keepdims=True)
        dmixed_ref[here, :] = mm_nt(low, out_ref[...])
    for cols in range(0, D, 256):
        up[cols : cols + 256, :] = transposed(attn_ref[:, cols : cols + 256])
    store_halves(mm(up[...], dbranch[...]).astype(BF16), place[3], okeep_ref, osend_ref)
    vec_ref[0:1, :] = dgain
    vec_ref[1:2, :] = dshift
    vec_ref[2:3, :] = dbias_out
    vec_ref[3:4, :] = dbias_down


def chunk_scratch(wide, rows_flat):
    return [
        pltpu.VMEM((wide, rows_flat, WIDTH), BF16), pltpu.VMEM((D, FFC), BF16),
        pltpu.VMEM((FFC, D), BF16), pltpu.VMEM((LEN, FFC), BF16), pltpu.VMEM((LEN, FFC), BF16),
    ]


def once(shape):
    return whole_spec(shape, pipeline_mode=pl.Buffered(1))


def struct(shape, dtype):
    return jax.ShapeDtypeStruct(shape, dtype)


def middle_first(place, wide, pieces, tokens, attn, cotangent, vectors, bias_up):
    rows_flat = 3 * D // wide + 2 * FFC * D // (WIDTH * wide)
    half = (wide, FFC * D // (WIDTH * wide), WIDTH)
    outs = [
        struct((LEN, D), F32), struct((LEN, D), BF16), struct((D, LEN), BF16),
        struct((D, LEN), BF16), struct((LEN, D), F32), struct((LEN, D), F32),
        struct((D, D), BF16), struct(half, BF16), struct(half, BF16), struct((1, FFC), F32),
    ]
    return pl.pallas_call(
        functools.partial(middle_first_kernel, wide, len(pieces)),
        grid_spec=pltpu.PrefetchScalarGridSpec(
            num_scalar_prefetch=1,
            grid=(1,),
            in_specs=[any_spec()] * len(pieces)
            + [once((LEN, D)), once((LEN, D)), once((LEN, D)), once((13, D)), once((1, FFC))],
            out_specs=[once(out.shape) for out in outs],
            scratch_shapes=chunk_scratch(wide, rows_flat) + [pltpu.SemaphoreType.DMA((16,))],
        ),
        out_shape=outs,
        compiler_params=pltpu.CompilerParams(
            dimension_semantics=("arbitrary",), vmem_limit_bytes=VMEM_LIMIT
        ),
        cost_estimate=cost(14 * 10**9, 30 * 10**6),
        name="middle_first",
    )(place, *pieces, tokens, attn, cotangent, vectors, bias_up)


def middle_next(place, wide, chunk, pieces, cotangent, state, bias_up, y, back, tail):
    a2, a2t, dyt = state
    rows_flat = 2 * FFC * D // (WIDTH * wide)
    half = (wide, FFC * D // (WIDTH * wide), WIDTH)
    out_half = (wide, 3 * D // (2 * wide), WIDTH)
    if tail:
        outs = [
            struct((LEN, D), F32), struct((LEN, D), F32), struct((LEN, D), F32),
            struct(out_half, BF16), struct(out_half, BF16), struct((8, D), F32),
        ]
    else:
        outs = [struct((LEN, D), F32), struct((LEN, D), F32)]
    outs += [struct(half, BF16), struct(half, BF16), struct((1, FFC), F32)]
    scratch = chunk_scratch(wide, rows_flat)
    scratch += [pltpu.VMEM((LEN, D), F32), pltpu.VMEM((LEN, D), F32)]
    if tail:
        scratch += [pltpu.VMEM((LEN, D), BF16)]
    scratch += [pltpu.SemaphoreType.DMA((3,))]
    return pl.pallas_call(
        functools.partial(middle_next_kernel, wide, chunk, len(pieces)),
        grid_spec=pltpu.PrefetchScalarGridSpec(
            num_scalar_prefetch=1,
            grid=(1,),
            in_specs=[any_spec()] * len(pieces)
            + [
                once((LEN, D)), once((LEN, D)), once((D, LEN)), once((D, LEN)), once((1, FFC)),
                any_spec(), any_spec(),
            ]
            + [once(value.shape) for value in tail],
            out_specs=[once(out.shape) for out in outs],
            scratch_shapes=scratch,
        ),
        out_shape=outs,
        compiler_params=pltpu.CompilerParams(
            dimension_semantics=("arbitrary",), vmem_limit_bytes=VMEM_LIMIT
        ),
        cost_estimate=cost(14 * 10**9, 30 * 10**6),
        name="middle_last" if tail else "middle_next",
    )(place, *pieces, cotangent, a2, a2t, dyt, bias_up, y, back, *tail)


def input_kernel(x_ref, dx1_ref, da1_ref, rows_ref, out_ref, vec_ref):
    gain = rows_ref[0:1, :]
    x = x_ref[...].astype(F32)
    dn = da1_ref[...]
    centre = x - jnp.mean(x, axis=-1, keepdims=True)
    spread = jnp.mean(centre * centre, axis=-1, keepdims=True)
    scale = lax.rsqrt(spread + norm_eps)
    zh = centre * scale
    e = dn * gain
    dz = (
        e - jnp.mean(e, axis=-1, keepdims=True) - zh * jnp.mean(e * zh, axis=-1, keepdims=True)
    ) * scale
    out_ref[...] = dx1_ref[...] + dz

    @pl.when(pl.program_id(0) == 0)
    def _():
        vec_ref[...] = jnp.zeros_like(vec_ref)

    vec_ref[0:1, :] += jnp.sum(dn * zh, axis=0, keepdims=True)
    vec_ref[1:2, :] += jnp.sum(dn, axis=0, keepdims=True)


def input_side(tokens, dx1, da1, vectors):
    block = pl.BlockSpec((256, D), lambda i: (i, 0))
    return pl.pallas_call(
        input_kernel,
        grid=(LEN // 256,),
        in_specs=[block, block, block, pl.BlockSpec((13, D), lambda i: (0, 0))],
        out_specs=[block, pl.BlockSpec((8, D), lambda i: (0, 0))],
        out_shape=[
            jax.ShapeDtypeStruct((LEN, D), F32), jax.ShapeDtypeStruct((8, D), F32),
        ],
        compiler_params=pltpu.CompilerParams(dimension_semantics=("arbitrary",)),
        name="input_side",
    )(tokens, dx1, da1, vectors)


def tables(lengths, projection):
    ends = jnp.cumsum(lengths[0])
    starts = ends - lengths[0]
    place = jnp.arange(LEN, dtype=jnp.int32)
    member = (place[:, None] >= starts[None, :]) & (place[:, None] < ends[None, :])
    offset = jnp.sum(jnp.where(member, starts[None, :], 0), axis=1)
    position = (place - offset).astype(F32)
    freq = 10000.0 ** (-jnp.arange(32, dtype=F32) / 32)
    angles = position[:, None] * jnp.tile(freq, 4)[None, :]
    onehot = jnp.pad(member.astype(BF16), ((0, 0), (0, 128 - member.shape[1])))
    eye = jnp.asarray(np.eye(4, dtype=np.float32))
    lifted = jnp.einsum("hif,ab->haibf", projection.reshape(2, 32, FEAT), eye)
    lifted = lifted.reshape(WIDTH, 128)
    rounded = lax.reduce_precision(lifted, 8, 7)
    high, low = rounded.astype(BF16), (lifted - rounded).astype(BF16)
    square = np.zeros((2, 4, 32, 4, 32), np.float32)
    for head in range(4):
        square[:, head, :, head, :] = 0.5
    proj = jnp.stack([high, low, jnp.asarray(square.reshape(WIDTH, 128), BF16)])
    return jnp.cos(angles), jnp.sin(angles), onehot, proj


def wide_perm(shift_z, flip_x):
    pairs = []
    for z in range(4):
        for x in range(2):
            target_x = 1 - x if flip_x else x
            pairs.append((2 * z + x, 2 * ((z + shift_z) % 4) + target_x))
    return pairs


def narrow_perm(flip_y, flip_core):
    pairs = []
    for y in range(2):
        for core in range(2):
            pairs.append(
                (2 * y + core, 2 * (1 - y if flip_y else y) + (1 - core if flip_core else core))
            )
    return pairs


def over_z(values, shift):
    return lax.ppermute(values, "wide", wide_perm(shift, False))


def over_x(values):
    return lax.ppermute(values, "wide", wide_perm(0, True))


def over_y(values):
    return lax.ppermute(values, "narrow", narrow_perm(True, False))


def over_core(values):
    return lax.ppermute(values, "narrow", narrow_perm(False, True))


def tie(*values):
    return lax.optimization_barrier(values)


def special():
    return lax.axis_size("wide") == 8 and lax.axis_size("narrow") == 4


def sum_wide(values):
    if not special():
        return lax.psum(values, "wide")
    for perm in (wide_perm(0, True), [(w, w ^ 2) for w in range(8)], [(w, w ^ 4) for w in range(8)]):
        values = values + lax.ppermute(values, "wide", perm)
    return values


def sum_narrow(values):
    if not special():
        return lax.psum(values, "narrow")
    return_value = values + over_core(values)
    return return_value + over_y(return_value)


def along_z(mine):
    return jnp.stack([mine] + [over_z(mine, shift) for shift in (1, 2, 3)])


def first_sum_kernel(place, *refs):
    count = (len(refs) - 2) // 2
    send_ref, keep_ref = refs[-2:]
    x = place[1]
    at = 0
    for index in range(count):
        own, got = refs[2 * index], refs[2 * index + 1]
        rows = own.shape[2]
        here = pl.ds(at, rows)
        keep_ref[0, here, :] = (own[0, x].astype(F32) + got[0, x].astype(F32)).astype(BF16)
        send_ref[0, here, :] = (
            own[0, 1 - x].astype(F32) + got[0, 1 - x].astype(F32)
        ).astype(BF16)
        at += rows


def first_sum(place, pairs):
    rows = [own.shape[1] for own, _ in pairs]
    total = sum(rows)
    operands, specs = [], []
    for own, got in pairs:
        for value in (own, got):
            operands.append(value.reshape(4, 2, value.shape[1], WIDTH))
            specs.append(pl.BlockSpec((1, 2, value.shape[1], WIDTH), lambda i, *_: (i, 0, 0, 0)))
    block = pl.BlockSpec((1, total, WIDTH), lambda i, *_: (i, 0, 0))
    return pl.pallas_call(
        first_sum_kernel,
        grid_spec=pltpu.PrefetchScalarGridSpec(
            num_scalar_prefetch=1, grid=(4,), in_specs=specs, out_specs=[block, block]
        ),
        out_shape=[struct((4, total, WIDTH), BF16)] * 2,
        compiler_params=pltpu.CompilerParams(dimension_semantics=("arbitrary",)),
        cost_estimate=cost(10**6, 6 * 8 * total * WIDTH),
        name="first_sum",
    )(place, *operands)


def second_sum_kernel(place, own_ref, got_ref, *outs):
    z = place[0]
    for shift, out in enumerate(outs):
        there = lax.rem(z + shift, 4)
        out[...] = (own_ref[there].astype(F32) + got_ref[there].astype(F32)).astype(BF16)


def second_sum(place, own, got):
    shape = own.shape[1:]
    return pl.pallas_call(
        second_sum_kernel,
        grid_spec=pltpu.PrefetchScalarGridSpec(
            num_scalar_prefetch=1,
            grid=(1,),
            in_specs=[once(own.shape), once(own.shape)],
            out_specs=[once(shape)] * 4,
        ),
        out_shape=[struct(shape, BF16)] * 4,
        compiler_params=pltpu.CompilerParams(
            dimension_semantics=("arbitrary",), vmem_limit_bytes=VMEM_LIMIT
        ),
        cost_estimate=cost(10**6, 12 * shape[0] * shape[1] * 4),
        name="second_sum",
    )(place, own, got)


def last_sums(own, others):
    total = own.astype(F32)
    for other in others:
        total = total + other.astype(F32)
    return total.astype(BF16)


def shards(
    tokens, cotangent, lengths, projection, inward, outward, expand, shrink, vectors,
    inward_rows, inward_columns, outward_rows, outward_columns, expand_rows, expand_columns,
    shrink_rows, shrink_columns, vector_state,
):
    full = special()
    rows = outward.shape[0]
    wide = 8 if full else 1
    wide_at = lax.axis_index("wide").astype(jnp.int32)
    narrow_at = lax.axis_index("narrow").astype(jnp.int32)
    core = narrow_at % 2 if full else jnp.int32(0)
    place = jnp.stack([wide_at // 2, wide_at % 2, narrow_at // 2, core])
    in_low = inward.astype(BF16)
    out_low = outward.astype(BF16)
    up_low = expand.astype(BF16)
    down_low = shrink.astype(BF16)
    if not full:
        in_low = lax.all_gather(in_low, "wide", axis=1, tiled=True)
        out_low = lax.all_gather(out_low, "wide", axis=0, tiled=True)
        up_low = lax.all_gather(up_low, "wide", axis=0, tiled=True)
        down_low = lax.all_gather(down_low, "wide", axis=0, tiled=True)
    own_rows = D // wide
    units = jnp.transpose(in_low.reshape(3, own_rows, GROUPS, WIDTH), (2, 1, 0, 3))
    units = units.reshape(GROUPS, own_rows, D)

    def blocks(matrix):
        count = matrix.shape[1] // WIDTH
        return jnp.transpose(matrix.reshape(-1, count, WIDTH), (1, 0, 2)).reshape(-1, WIDTH)

    per = FFC // wide
    ups = up_low.reshape(own_rows, wide, CHUNKS, per)
    chunks = [
        jnp.concatenate(
            [
                blocks(ups[:, :, j].reshape(own_rows, FFC)),
                blocks(down_low[per * j : per * (j + 1)]),
            ]
        )
        for j in range(CHUNKS)
    ]
    flat_first = jnp.concatenate([blocks(out_low), chunks[0]])
    if full:
        own_units = [lax.dynamic_slice_in_dim(units[g], 48 * core, 48, 0) for g in range(GROUPS)]
        half = flat_first.shape[0] // 2
        own_first = lax.dynamic_slice_in_dim(flat_first, half * core, half, 0)
        own_rest = jnp.where(core == 0, chunks[1], chunks[2])
        in_z = [along_z(unit) for unit in own_units]
        first_z = along_z(own_first)
        in_x = [jnp.stack([value, over_x(value)]) for value in in_z]
        pieces_in = []
        for value in in_x:
            pieces_in += [value, over_core(value)]
        rest_own = lax.all_gather(own_rest, "wide", axis=0)
        *pieces_in, first_z = tie(*pieces_in, first_z)
        first_x = jnp.stack([first_z, over_x(first_z)])
    else:
        pieces_in = [units.reshape(1, 3 * D, D)]
    cosine, sine, onehot, proj = tables(lengths, projection)
    perm = jnp.asarray(head_perm(), BF16)
    block_ones = np.kron(np.eye(2, dtype=np.float32), np.ones((64, 64), np.float32))
    ones = jnp.asarray(np.concatenate([block_ones, block_ones]), BF16)
    split = vectors[4:6].reshape(2, GROUPS, 4, 2, 32)
    bias_qk = jnp.transpose(split, (0, 1, 3, 2, 4)).reshape(2, GROUPS, WIDTH)
    bias = jnp.concatenate([bias_qk, vectors[6].reshape(1, GROUPS, WIDTH)])
    bias = jnp.transpose(bias, (1, 0, 2))
    attn, mixed, a1t, w_in, wq, wk, qf, kf, v, rden = attend(
        lengths, place, pieces_in, wide, tokens, vectors[:2], bias, perm, proj, cosine, sine,
        onehot,
    )
    bias_up = vectors[9:].reshape(wide, CHUNKS, per)
    bias_up = jnp.transpose(bias_up, (1, 0, 2)).reshape(CHUNKS, 1, FFC)
    if full:
        pieces_first = [first_x, over_core(first_x)]
        pieces_rest = [[rest_own, over_core(rest_own)]] * 2
    else:
        pieces_first = [flat_first[None]]
        pieces_rest = [[chunks[1][None]], [chunks[2][None]]]
    x1, a2, a2t, dyt, y, back, w_out, keep0, send0, dbias0 = middle_first(
        place, wide, pieces_first, tokens, attn, cotangent, vectors, bias_up[0]
    )
    state = (a2, a2t, dyt)
    y, back, keep1, send1, dbias1 = middle_next(
        place, wide, 1, pieces_rest[0], cotangent, state, bias_up[1], y, back, ()
    )
    block_out, dx1, dmixed, okeep, osend, middle_vec, keep2, send2, dbias2 = middle_next(
        place, wide, 2, pieces_rest[1], cotangent, state, bias_up[2], y, back,
        (x1, attn, w_out, vectors),
    )
    if full:
        send_a, keep_a = first_sum(
            place, [(keep0, over_core(send0)), (keep1, over_core(send1))]
        )
        dmixed, send_a = tie(dmixed, send_a)
    saved = (mixed, rden, wq, wk, qf, kf, v)
    da1 = None
    in_keep, in_send, in_bias = [], [], []
    for g in range(GROUPS):
        keep, send, part, da1 = attend_back(
            g, lengths, place, wide, dmixed, saved, a1t, w_in, perm, proj, cosine, sine, onehot,
            ones, da1,
        )
        in_keep.append(keep)
        in_send.append(send)
        in_bias.append(part)
        if full and g == 0:
            got_a = over_x(send_a)
            send_b, keep_b = first_sum(
                place, [(keep2, over_core(send2)), (okeep, over_core(osend))]
            )
            da1, send_b = tie(da1, send_b)
        if full and g == 1:
            a_parts = second_sum(place, keep_a, got_a)
            da1, *a_parts = tie(da1, *a_parts)
    input_grad, input_vec = input_side(tokens, dx1, da1, vectors)
    dbias_in = jnp.concatenate(in_bias).reshape(GROUPS, 3, WIDTH)
    dbias_in = jnp.transpose(dbias_in, (1, 0, 2)).reshape(3, D)
    dbias_up = jnp.concatenate([dbias0, dbias1, dbias2]).reshape(CHUNKS, wide, per)
    dbias_up = jnp.transpose(dbias_up, (1, 0, 2)).reshape(-1, D)
    vector_local = jnp.concatenate(
        [input_vec[:2], middle_vec[:2], dbias_in, middle_vec[2:4], dbias_up]
    )
    vector_part = sum_narrow(vector_local)
    if full:

        def finish(parts):
            mine = last_sums(
                parts[0], [over_z(parts[shift], shift) for shift in (1, 2, 3)]
            )
            half_sum = mine.astype(F32) + over_y(mine).astype(F32)
            other = over_core(half_sum)
            return (
                jnp.where(core == 0, half_sum, other), jnp.where(core == 0, other, half_sum)
            )

        a_low, a_high = finish(a_parts)
        b_parts = second_sum(place, keep_b, over_x(send_b))
        b_low, b_high = finish(b_parts)
        send_c, keep_c = first_sum(
            place, [(keep, over_core(send)) for keep, send in zip(in_keep, in_send)]
        )
        c_low, c_high = finish(second_sum(place, keep_c, over_x(send_c)))
        ups_grad = [a_low[:384], a_low[384:], b_low[:384]]
        downs_grad = [a_high[:384], a_high[384:], b_high[:384]]
        out_low, out_high = b_low[384:], b_high[384:]
        expand_grad = jnp.stack(ups_grad).reshape(CHUNKS, 4, rows, 2, 128)
        expand_grad = jnp.transpose(expand_grad, (2, 1, 3, 0, 4)).reshape(rows, FF)
        shrink_grad = jnp.stack(downs_grad).reshape(CHUNKS, D // 2, 2, 128)
        shrink_grad = jnp.transpose(shrink_grad, (0, 3, 2, 1)).reshape(CHUNKS * 128, D)

        def joined(low, high):
            low = low.reshape(-1, 3, 48, WIDTH)
            high = high.reshape(-1, 3, 48, WIDTH)
            return jnp.concatenate([low, high], axis=2)

        outward_grad = jnp.transpose(joined(out_low, out_high)[0], (1, 0, 2)).reshape(rows, D)
        inward_grad = jnp.transpose(joined(c_low, c_high), (1, 2, 0, 3)).reshape(3, rows, D)
    else:

        def reduced(values, axis):
            part = lax.psum_scatter(values, "wide", scatter_dimension=axis, tiled=True)
            return lax.psum(part.astype(F32), "narrow")

        up_grads = [
            jnp.transpose(keep.reshape(4, D, WIDTH), (1, 0, 2)).reshape(D, FFC)
            for keep in (keep0, keep1, keep2)
        ]
        down_grads = [
            jnp.transpose(send.reshape(4, D, WIDTH), (0, 2, 1)).reshape(FFC, D)
            for send in (send0, send1, send2)
        ]
        expand_grad = reduced(jnp.concatenate(up_grads, axis=1), 0)
        shrink_grad = reduced(jnp.concatenate(down_grads, axis=0), 0)

        def rebuilt(keep, send):
            both = jnp.concatenate(
                [keep.reshape(3, D // 2, WIDTH), send.reshape(3, D // 2, WIDTH)], axis=1
            )
            return both

        outward_grad = reduced(
            jnp.transpose(rebuilt(okeep, osend), (1, 0, 2)).reshape(D, D), 0
        )
        in_units = jnp.stack([rebuilt(keep, send) for keep, send in zip(in_keep, in_send)])
        inward_grad = reduced(jnp.transpose(in_units, (1, 2, 0, 3)).reshape(3, D, D), 1)
    decay = 1.0 - STEP ** (-0.8)
    wide_count = lax.axis_size("wide")
    grads_list = [inward_grad, outward_grad[None], expand_grad[None], shrink_grad[None]]
    rows_old = [inward_rows, outward_rows[None], expand_rows[None], shrink_rows[None]]
    columns_old = [
        inward_columns,
        outward_columns[None],
        expand_columns[None],
        shrink_columns[None],
    ]
    weights_old = [inward, outward[None], expand[None], shrink[None]]
    rates = [0.3 * D ** (-0.5), 1.2 * D ** (-0.5), 0.3 * D ** (-0.5), 0.3 * FF ** (-0.5)]
    bounds = [0, 3, 4, 5, 6]
    rows_next = []
    column_parts = []
    for member in range(4):
        squares = grads_list[member] * grads_list[member] + square_eps
        rows_next.append(decay * rows_old[member] + (1.0 - decay) * jnp.mean(squares, axis=-1))
        column_parts.append(jnp.sum(squares, axis=-2))
    row_totals = jnp.concatenate([jnp.sum(entry, axis=-1) for entry in rows_next])
    shapes = [part.shape for part in column_parts] + [row_totals.shape, vector_part.shape]
    flat = jnp.concatenate(
        [part.reshape(-1) for part in column_parts + [row_totals, vector_part]]
    )
    flat = jnp.pad(flat, (0, -flat.shape[0] % 1024)).reshape(-1, 128)
    flat = sum_wide(flat).reshape(-1)
    summed = []
    offset = 0
    for shape in shapes:
        size = 1
        for extent in shape:
            size *= extent
        summed.append(flat[offset : offset + size].reshape(shape))
        offset += size
    column_sums = list(summed[0:4])
    totals_sum = summed[4]
    vector_grad = summed[5]
    columns_next = []
    scaled_list = []
    row_means = []
    sizes_full = []
    for member in range(4):
        grad_now = grads_list[member]
        rows_full = grad_now.shape[-2] * wide_count
        sizes_full.append(rows_full * grad_now.shape[-1])
        columns_next.append(
            decay * columns_old[member] + (1.0 - decay) * column_sums[member] / rows_full
        )
        row_mean = totals_sum[bounds[member] : bounds[member + 1]] / rows_full
        row_means.append(row_mean)
        scaled_list.append(
            grad_now
            * lax.rsqrt(rows_next[member] / row_mean[:, None])[..., None]
            * lax.rsqrt(columns_next[member])[:, None, :]
        )
    partial_squares = jnp.concatenate(
        [jnp.sum(entry * entry, axis=(-2, -1)) for entry in scaled_list]
    )
    total_squares = sum_wide(jnp.pad(partial_squares, (0, 122)).reshape(1, 128))[0, :6]
    rms_list = [
        jnp.sqrt(total_squares[bounds[member] : bounds[member + 1]] / sizes_full[member])
        for member in range(4)
    ]
    weights_next = []
    for member in range(4):
        limiter = jnp.maximum(1.0, rms_list[member] / clip_level)
        weights_next.append(
            weights_old[member] - rates[member] * scaled_list[member] / limiter[:, None, None]
        )
    vector_state_next = decay * vector_state + (1.0 - decay) * (
        vector_grad * vector_grad + square_eps
    )
    vector_update = vector_grad * lax.rsqrt(vector_state_next)
    vector_rms = jnp.sqrt(jnp.mean(vector_update * vector_update))
    vectors_next = vectors - 0.25 * vector_update / jnp.maximum(1.0, vector_rms / clip_level)
    return (
        block_out,
        input_grad,
        inward_grad,
        outward_grad,
        expand_grad,
        shrink_grad,
        vector_grad,
        rows_next[0],
        columns_next[0],
        rows_next[1][0],
        columns_next[1][0],
        rows_next[2][0],
        columns_next[2][0],
        rows_next[3][0],
        columns_next[3][0],
        vector_state_next,
        weights_next[0],
        weights_next[1][0],
        weights_next[2][0],
        weights_next[3][0],
        vectors_next,
    )


def solution(mesh):
    placed = (
        P(("narrow", "wide"), None),
        P(("narrow", "wide"), None),
        P(("narrow", "wide"), None),
        P(),
        P(None, "wide", None),
        P("wide", None),
        P("wide", None),
        P("wide", None),
        P(),
        P(None, "wide"),
        P(),
        P("wide"),
        P(),
        P("wide"),
        P(),
        P("wide"),
        P(),
        P(),
    )
    return jax.shard_map(
        shards,
        mesh=mesh,
        in_specs=placed,
        out_specs=(
            P(("narrow", "wide"), None),
            P(("narrow", "wide"), None),
            P(None, "wide", None),
            P("wide", None),
            P("wide", None),
            P("wide", None),
            P(),
            P(None, "wide"),
            P(),
            P("wide"),
            P(),
            P("wide"),
            P(),
            P("wide"),
            P(),
            P(),
            P(None, "wide", None),
            P("wide", None),
            P("wide", None),
            P("wide", None),
            P(),
        ),
        check_vma=False,
    )
```

```python
import functools
import math

import jax
import jax.numpy as jnp
import numpy as np
from jax import lax
from jax.experimental import pallas as pl
from jax.experimental.pallas import tpu as pltpu
from jax.sharding import PartitionSpec as P

D = 768
HEADS = 12
HD = 64
FF = 3072
FEAT = 32
STEP = 10
LEN = 1024
SPAN = 256
CHUNKS = 3
GROUPS = 3
WIDTH = 256
FFC = FF // CHUNKS

norm_eps = 1e-05
square_eps = 1e-30
clip_level = 1.0

F32 = jnp.float32
BF16 = jnp.bfloat16
VMEM_LIMIT = 60 * 1024 * 1024


def mm(left, right):
    return lax.dot_general(left, right, (((1,), (0,)), ((), ())), preferred_element_type=F32)


def mm_nt(left, right):
    return lax.dot_general(left, right, (((1,), (1,)), ((), ())), preferred_element_type=F32)


def mm_tn(left, right):
    return lax.dot_general(left, right, (((0,), (0,)), ((), ())), preferred_element_type=F32)


def halves(values):
    high = values.astype(BF16)
    return high, (values - high.astype(F32)).astype(BF16)


TAIL = (
    0.1795078068971634,
    0.17978088557720184,
    0.14234966039657593,
    0.06379217654466629,
    0.0434231162071228,
    -0.261725515127182,
    0.20454804599285126,
    -0.05167665705084801,
)


def normal_parts(values):
    size = jnp.abs(values)
    t = 1.0 / (1.0 + 0.45 * size)
    poly = TAIL[-1]
    for coeff in TAIL[-2::-1]:
        poly = poly * t + coeff
    bell = jnp.exp(-0.5 * values * values)
    tail = poly * t * bell
    return jnp.where(values >= 0, 1.0 - tail, tail), bell * 0.3989422804014327


def transposed(values):
    row = lax.broadcasted_iota(jnp.int32, (256, 256), 0)
    col = lax.broadcasted_iota(jnp.int32, (256, 256), 1)
    eye = (row == col).astype(F32).astype(BF16)
    return mm_nt(eye, values).astype(BF16)


def head_perm():
    perm = np.zeros((WIDTH, WIDTH), np.float32)
    for head in range(4):
        for half in range(2):
            for i in range(32):
                perm[head * 64 + half * 32 + i, half * 128 + head * 32 + i] = 1.0
    return perm


def make_blocks(lengths, base, first, last):
    def step(s, carry):
        count, begin, begin_row, end = carry
        new_end = end + lengths[0, s]
        full = new_end - begin_row > SPAN

        @pl.when(full)
        def _():
            base[count] = begin_row
            first[count] = begin
            last[count] = s - 1

        row = jnp.minimum((end // 16) * 16, LEN - SPAN)
        return (
            jnp.where(full, count + 1, count),
            jnp.where(full, s, begin),
            jnp.where(full, row, begin_row),
            new_end,
        )

    segments = lengths.shape[1]
    zero = jnp.int32(0)
    count, begin, begin_row, _ = lax.fori_loop(0, segments, step, (zero, zero, zero, zero))
    base[count] = begin_row
    first[count] = begin
    last[count] = segments - 1
    return count + 1


def lane_mask(lo, hi, width, dtype):
    lane = lax.broadcasted_iota(jnp.int32, (1, width), 1)
    return ((lane >= lo) & (lane < hi)).astype(F32).astype(dtype)


def value_rows(v_pair, head):
    keep = lane_mask(64 * head, 64 * head + 64, 128, BF16)
    return jnp.concatenate([v_pair * keep, jnp.broadcast_to(keep, v_pair.shape)], axis=1)


def span_mask(onehot, rows, lo, hi):
    member = onehot[rows, :]
    lane = lax.broadcasted_iota(jnp.int32, (1, 128), 1)
    inside = ((lane >= lo) & (lane <= hi)).astype(F32).astype(BF16)
    return mm_nt(member * inside, member).astype(BF16)


def cost(flops, size):
    return pl.CostEstimate(flops=flops, transcendentals=0, bytes_accessed=size)


def any_spec():
    return pl.BlockSpec(memory_space=pl.ANY)


def in_copies(place, pieces, dst, sems, unit):
    if len(pieces) == 1:
        rows = dst.shape[1] // 3
        here = pl.ds(unit * rows, rows)
        return [pltpu.make_async_copy(pieces[0].at[:, here], dst.at[:, here], sems.at[unit, 0])]
    z, x, core = place[0], place[1], place[3]
    part, index = (0, unit) if unit < 2 else (4, 0)
    copies = []
    for side in range(2):
        half = core if side == 0 else 1 - core
        for flip in range(2):
            column = x if flip == 0 else 1 - x
            for shift in range(4):
                row = lax.rem(z + 4 - shift, 4) * 2 + column
                start = pl.multiple_of(unit * 96 + half * 48, 16)
                copies.append(
                    pltpu.make_async_copy(
                        pieces[part + 2 * side + flip].at[shift, index],
                        dst.at[row, pl.ds(start, 48)],
                        sems.at[unit, len(copies)],
                    )
                )
    return copies


def flat_copies(place, pieces, dst, sems):
    if len(pieces) == 1:
        return [pltpu.make_async_copy(pieces[0], dst, sems.at[0])]
    z, x, core = place[0], place[1], place[3]
    span = dst.shape[1] // 2
    copies = []
    for side in range(2):
        half = core if side == 0 else 1 - core
        for flip in range(2):
            column = x if flip == 0 else 1 - x
            for shift in range(4):
                row = lax.rem(z + 4 - shift, 4) * 2 + column
                start = pl.multiple_of(half * span, 16)
                copies.append(
                    pltpu.make_async_copy(
                        pieces[2 * side + flip].at[shift],
                        dst.at[row, pl.ds(start, span)],
                        sems.at[len(copies)],
                    )
                )
    return copies


def attend_kernel(count_in, lengths, place, *refs):
    pieces = refs[:count_in]
    (
        x_ref, norm_ref, bias_ref, perm_ref, proj_ref, cos_ref, sin_ref, onehot_ref,
        attn_ref, mixed_ref, a1t_ref, w_ref, wq_ref, wk_ref, qf_ref, kf_ref, v_ref, rden_ref,
        a1, qb, kb, vb, parts, base, first, last, sems,
    ) = refs[count_in:]
    group = pl.program_id(0)

    @pl.when(group == 0)
    def _():
        for unit in range(GROUPS):
            for copy in in_copies(place, pieces, w_ref, sems, unit):
                copy.start()
        for rows in range(0, LEN, 256):
            here = pl.ds(rows, 256)
            x = x_ref[here, :].astype(F32)
            centre = x - jnp.mean(x, axis=-1, keepdims=True)
            spread = jnp.mean(centre * centre, axis=-1, keepdims=True)
            a1[here, :] = (
                centre * lax.rsqrt(spread + norm_eps) * norm_ref[0:1, :] + norm_ref[1:2, :]
            ).astype(BF16)
        for cols in range(0, D, 256):
            a1t_ref[cols : cols + 256, :] = transposed(a1[:, cols : cols + 256])

    for unit in range(GROUPS):

        @pl.when(group == unit)
        def _():
            for copy in in_copies(place, pieces, w_ref, sems, unit):
                copy.wait()

    count = make_blocks(lengths, base, first, last)
    shard = w_ref.shape[1] // 3
    here = pl.ds(pl.multiple_of(group * shard, 16), shard)
    w = w_ref[:, here, :].reshape(D, D)
    perm = perm_ref[...]
    bias = bias_ref[0]
    proj_both = proj_ref[0]
    proj_high = proj_ref[1, :, :128]
    square = proj_ref[2, :, :128]
    for which, (out_w, out_f, low_f) in enumerate(((wq_ref, qf_ref, qb), (wk_ref, kf_ref, kb))):
        weight = mm(w[:, WIDTH * which : WIDTH * (which + 1)], perm).astype(BF16)
        for rows in range(0, LEN, 256):
            here = pl.ds(rows, 256)
            u = (mm(a1[here, :], weight) + bias[which : which + 1, :]) * HD ** (-0.25)
            c = u[:, :128]
            e = u[:, 128:]
            cosine = cos_ref[here, :]
            sine = sin_ref[here, :]
            turned = jnp.concatenate([c * cosine - e * sine, e * cosine + c * sine], axis=1)
            out_w[0, here, :] = turned
            high, low = halves(turned)
            sq_high, sq_low = halves(turned * turned)
            both = mm(high, proj_both)
            logits = (
                both[:, :128] + both[:, 128:] + mm(low, proj_high)
                - (mm(sq_high, square) + mm(sq_low, square))
            )
            phi = jnp.exp(logits) * FEAT ** (-0.5)
            out_f[0, here, :] = phi
            low_f[here, :] = phi.astype(BF16)
    for rows in range(0, LEN, 256):
        here = pl.ds(rows, 256)
        v = mm(a1[here, :], w[:, 2 * WIDTH :]) + bias[2:3, :]
        v_ref[0, here, :] = v
        vb[here, :] = v.astype(BF16)
    parts[...] = jnp.zeros_like(parts)

    def one_span(index, carry):
        rows = pl.ds(pl.multiple_of(base[index], 16), SPAN)
        mask = span_mask(onehot_ref, rows, first[index], last[index])
        q = qb[rows, :]
        k = kb[rows, :]
        for pair in range(2):
            v_pair = vb[rows, 128 * pair : 128 * (pair + 1)]
            total = jnp.zeros((SPAN, WIDTH), F32)
            for side in range(2):
                head = 2 * pair + side
                scores = mm_nt(q * lane_mask(32 * head, 32 * head + 32, 128, BF16), k)
                total = total + mm(scores.astype(BF16) * mask, value_rows(v_pair, side))
            parts[pair, rows, :] += total
        return carry

    lax.fori_loop(0, count, one_span, 0)
    for pair in range(2):
        lanes = slice(128 * pair, 128 * (pair + 1))
        inverse = 1.0 / parts[pair, :, 128:]
        rden_ref[0, :, lanes] = inverse
        mixed = parts[pair, :, :128] * inverse
        mixed_ref[0, :, lanes] = mixed
        attn_ref[:, lanes] = mixed.astype(BF16)


def whole_spec(shape, **options):
    return pl.BlockSpec(shape, lambda *_: (0,) * len(shape), **options)


def group_spec(shape):
    return pl.BlockSpec((1,) + shape, lambda g, *_: (g,) + (0,) * len(shape))


def attend(lengths, place, pieces, wide, tokens, norm, bias, perm, proj, cosine, sine, onehot):
    def out(shape, dtype):
        return jax.ShapeDtypeStruct((GROUPS,) + shape, dtype)

    rows_in = 3 * D // wide
    return pl.pallas_call(
        functools.partial(attend_kernel, len(pieces)),
        grid_spec=pltpu.PrefetchScalarGridSpec(
            num_scalar_prefetch=2,
            grid=(GROUPS,),
            in_specs=[any_spec()] * len(pieces)
            + [
                whole_spec((LEN, D)), whole_spec((2, D)), group_spec((3, WIDTH)),
                whole_spec((WIDTH, WIDTH)), whole_spec((3, WIDTH, WIDTH)), whole_spec((LEN, 128)),
                whole_spec((LEN, 128)), whole_spec((LEN, 128)),
            ],
            out_specs=[
                pl.BlockSpec((LEN, WIDTH), lambda g, *_: (0, g)), group_spec((LEN, WIDTH)),
                whole_spec((D, LEN)), whole_spec((wide, rows_in, D)), group_spec((LEN, WIDTH)),
                group_spec((LEN, WIDTH)), group_spec((LEN, 128)), group_spec((LEN, 128)),
                group_spec((LEN, WIDTH)), group_spec((LEN, WIDTH)),
            ],
            scratch_shapes=[
                pltpu.VMEM((LEN, D), BF16),
                pltpu.VMEM((LEN, 128), BF16), pltpu.VMEM((LEN, 128), BF16),
                pltpu.VMEM((LEN, WIDTH), BF16), pltpu.VMEM((2, LEN, WIDTH), F32),
                pltpu.SMEM((32,), jnp.int32), pltpu.SMEM((32,), jnp.int32),
                pltpu.SMEM((32,), jnp.int32), pltpu.SemaphoreType.DMA((GROUPS, 16)),
            ],
        ),
        out_shape=[
            jax.ShapeDtypeStruct((LEN, D), BF16), out((LEN, WIDTH), F32),
            jax.ShapeDtypeStruct((D, LEN), BF16), jax.ShapeDtypeStruct((wide, rows_in, D), BF16),
            out((LEN, WIDTH), F32), out((LEN, WIDTH), F32), out((LEN, 128), F32),
            out((LEN, 128), F32), out((LEN, WIDTH), F32), out((LEN, WIDTH), F32),
        ],
        compiler_params=pltpu.CompilerParams(
            dimension_semantics=("arbitrary",), vmem_limit_bytes=VMEM_LIMIT
        ),
        cost_estimate=cost(20 * 10**9, 40 * 10**6),
        name="attend",
    )(lengths, place, *pieces, tokens, norm, bias, perm, proj, cosine, sine, onehot)


def attend_back_kernel(
    lengths, place, dmixed_ref, mixed_ref, rden_ref, wq_ref, wk_ref, qf_ref, kf_ref, v_ref,
    a1t_ref, w_ref, perm_ref, proj_ref, cos_ref, sin_ref, onehot_ref, ones_ref, da1_in,
    keep_ref, send_ref, bias_ref, da1_ref,
    qb, kb, dnb, dnh, lift, dqf, dkf, dv, dqkv, base, first, last,
):
    count = make_blocks(lengths, base, first, last)
    qb[...] = qf_ref[0].astype(BF16)
    kb[...] = kf_ref[0].astype(BF16)
    lane = lax.broadcasted_iota(jnp.int32, (1, 128), 1)
    ones = ones_ref[...]
    for pair in range(2):
        lanes = slice(128 * pair, 128 * (pair + 1))
        for rows in range(0, LEN, 256):
            here = pl.ds(rows, 256)
            dnum = dmixed_ref[here, lanes] * rden_ref[0, here, lanes]
            high, low = halves(dnum)
            dnb[here, lanes] = high
            part_high, part_low = halves(dnum * mixed_ref[0, here, lanes])
            dden = -mm(jnp.concatenate([part_high, part_low], axis=1), ones)
            den_high, den_low = halves(dden)
            high, low = high.astype(F32), low.astype(F32)
            den_high = pltpu.roll(den_high.astype(F32), 64, 1)
            den_low = pltpu.roll(den_low.astype(F32), 64, 1)
            low_far = pltpu.roll(low, 64, 1)
            v = v_ref[0, here, lanes]
            v_high, v_low = halves(v)
            v_high, v_low = v_high.astype(F32), v_low.astype(F32)
            v_far = pltpu.roll(v_high, 64, 1)
            for side in range(2):
                own = (lane >= 64 * side) & (lane < 64 * side + 64)
                mark = 64 - 64 * side
                rest = jnp.where(lane == mark, den_high, jnp.where(lane == mark + 1, den_low, 0.0))
                both = ((lane == mark) | (lane == mark + 1)).astype(F32)
                head = 2 * pair + side
                dnh[head, here, :128] = jnp.where(own, high, low_far).astype(BF16)
                dnh[head, here, 128:] = jnp.where(own, high, rest).astype(BF16)
                lift[head, here, :128] = jnp.where(own, v_high, v_far).astype(BF16)
                lift[head, here, 128:] = jnp.where(own, v_low, both).astype(BF16)
    dqf[...] = jnp.zeros_like(dqf)
    dkf[...] = jnp.zeros_like(dkf)
    dv[...] = jnp.zeros_like(dv)

    def one_span(index, carry):
        rows = pl.ds(pl.multiple_of(base[index], 16), SPAN)
        mask = span_mask(onehot_ref, rows, first[index], last[index])
        q = qb[rows, :]
        k = kb[rows, :]
        q_total = jnp.zeros((SPAN, 128), F32)
        k_total = jnp.zeros((SPAN, 128), F32)
        for pair in range(2):
            lanes = slice(128 * pair, 128 * (pair + 1))
            dn_pair = dnb[rows, lanes]
            v_total = jnp.zeros((SPAN, 128), F32)
            for side in range(2):
                head = 2 * pair + side
                feats = lane_mask(32 * head, 32 * head + 32, 128, BF16)
                q_head = q * feats
                k_head = k * feats
                lifted = lift[head, rows, :]
                dn_head = dnh[head, rows, :]
                scores = mm_nt(k, q_head).astype(BF16) * mask
                dscores = mm_nt(dn_head, lifted).astype(BF16) * mask
                dscores_t = mm_nt(lifted, dn_head).astype(BF16) * mask
                q_total = q_total + mm(dscores, k_head)
                k_total = k_total + mm(dscores_t, q_head)
                own = lane_mask(64 * side, 64 * side + 64, 128, BF16)
                v_total = v_total + mm(scores, dn_pair * own)
            dv[rows, lanes] += v_total
        dqf[rows, :] += q_total
        dkf[rows, :] += k_total
        return carry

    lax.fori_loop(0, count, one_span, 0)
    proj_low = proj_ref[0, :, 128:]
    proj_high = proj_ref[1]
    square = proj_ref[2]
    perm = perm_ref[...]
    for which, (w_in, phi_in, dphi) in enumerate(
        ((wq_ref, qf_ref, dqf), (wk_ref, kf_ref, dkf))
    ):
        for rows in range(0, LEN, 256):
            here = pl.ds(rows, 256)
            r = dphi[here, :] * phi_in[0, here, :]
            high, low = halves(r)
            both = jnp.concatenate([high, low], axis=1)
            spread = mm_nt(both, square)
            dw = mm_nt(both, proj_high) + mm_nt(high, proj_low)
            du = (dw - 2.0 * w_in[0, here, :] * spread) * HD ** (-0.25)
            c = du[:, :128]
            e = du[:, 128:]
            cosine = cos_ref[here, :]
            sine = sin_ref[here, :]
            turned = jnp.concatenate([c * cosine + e * sine, e * cosine - c * sine], axis=1)
            dqkv[here, WIDTH * which : WIDTH * (which + 1)] = mm_nt(
                turned.astype(BF16), perm
            ).astype(BF16)
    dqkv[:, 2 * WIDTH :] = dv[...].astype(BF16)
    bias_ref[0] = jnp.sum(dqkv[...].astype(F32), axis=0, keepdims=True)
    grad = mm(a1t_ref[...], dqkv[...]).astype(BF16)
    store_halves(grad, place[3], keep_ref.at[0], send_ref.at[0])
    w = w_ref[...].reshape(D, D)
    fresh = pl.program_id(0) == 0

    @pl.when(fresh)
    def _():
        if da1_in is None:
            da1_ref[...] = mm_nt(dqkv[...], w)
        else:
            da1_ref[...] = da1_in[...] + mm_nt(dqkv[...], w)

    @pl.when(jnp.logical_not(fresh))
    def _():
        da1_ref[...] += mm_nt(dqkv[...], w)


def store_halves(grad, core, keep_ref, send_ref):
    wide, rows = keep_ref.shape[0], D // keep_ref.shape[0]
    half = rows // 2
    parts = grad.reshape(wide, rows, D)
    for cols in range(3):
        block = parts[:, :, WIDTH * cols : WIDTH * (cols + 1)]
        here = pl.ds(half * cols, half)

        @pl.when(core == 0)
        def _():
            keep_ref[:, here, :] = block[:, :half]
            send_ref[:, here, :] = block[:, half:]

        @pl.when(core == 1)
        def _():
            keep_ref[:, here, :] = block[:, half:]
            send_ref[:, here, :] = block[:, :half]


def attend_back(
    begin, count, lengths, place, wide, dmixed, saved, a1t, w_in, perm, proj, cosine, sine, onehot, ones,
    da1,
):
    mixed, rden, wq, wk, qf, kf, v = saved

    def by_group(shape):
        return pl.BlockSpec((1,) + shape, lambda g, *_: (begin + g,) + (0,) * len(shape))

    rows_in = D // wide
    kernel = attend_back_kernel
    extra = [da1]
    extra_specs = [once((LEN, D))]
    if da1 is None:
        extra, extra_specs = [], []

        def kernel(*refs):
            attend_back_kernel(*refs[:18], None, *refs[18:])

    half = struct((count, wide, 3 * rows_in // 2, WIDTH), BF16)
    half_spec = group_spec(half.shape[1:])
    return pl.pallas_call(
        kernel,
        grid_spec=pltpu.PrefetchScalarGridSpec(
            num_scalar_prefetch=2,
            grid=(count,),
            in_specs=[
                pl.BlockSpec((LEN, WIDTH), lambda g, *_: (0, begin + g)),
                by_group((LEN, WIDTH)), by_group((LEN, WIDTH)), by_group((LEN, WIDTH)),
                by_group((LEN, WIDTH)), by_group((LEN, 128)), by_group((LEN, 128)),
                by_group((LEN, WIDTH)), once((D, LEN)),
                pl.BlockSpec((wide, rows_in, D), lambda g, *_: (0, begin + g, 0)),
                once((WIDTH, WIDTH)), once((3, WIDTH, WIDTH)), once((LEN, 128)),
                once((LEN, 128)), once((LEN, 128)), once((WIDTH, 128)),
            ] + extra_specs,
            out_specs=[
                half_spec, half_spec, group_spec((1, D)),
                whole_spec((LEN, D)),
            ],
            scratch_shapes=[
                pltpu.VMEM((LEN, 128), BF16), pltpu.VMEM((LEN, 128), BF16),
                pltpu.VMEM((LEN, WIDTH), BF16), pltpu.VMEM((4, LEN, WIDTH), BF16),
                pltpu.VMEM((4, LEN, WIDTH), BF16), pltpu.VMEM((LEN, 128), F32),
                pltpu.VMEM((LEN, 128), F32), pltpu.VMEM((LEN, WIDTH), F32),
                pltpu.VMEM((LEN, D), BF16),
                pltpu.SMEM((32,), jnp.int32), pltpu.SMEM((32,), jnp.int32),
                pltpu.SMEM((32,), jnp.int32),
            ],
        ),
        out_shape=[
            half, half, struct((count, 1, D), F32), struct((LEN, D), F32),
        ],
        compiler_params=pltpu.CompilerParams(
            dimension_semantics=("arbitrary",), vmem_limit_bytes=VMEM_LIMIT
        ),
        cost_estimate=cost(count * 12 * 10**9, count * 20 * 10**6),
        name="attend_back",
    )(
        lengths, place, dmixed, mixed, rden, wq, wk, qf, kf, v, a1t, w_in, perm, proj, cosine,
        sine, onehot, ones, *extra,
    )


def chunk_step(
    place, wide, flat, up_at, down_at, bias_up, dy_ref, a2, a2t, dyt, up, down, act, dhidden, y,
    back, keep_ref, send_ref, dbias_ref, fresh,
):
    rows_up = D // wide
    rows_down = FFC // wide
    for cols in range(4):
        here = pl.ds(up_at + rows_up * cols, rows_up)
        up[:, WIDTH * cols : WIDTH * (cols + 1)] = flat[:, here, :].reshape(D, WIDTH)
    for cols in range(3):
        here = pl.ds(down_at + rows_down * cols, rows_down)
        down[:, WIDTH * cols : WIDTH * (cols + 1)] = flat[:, here, :].reshape(FFC, WIDTH)
    bias_total = jnp.zeros((1, FFC), F32)
    for rows in range(0, LEN, 256):
        here = pl.ds(rows, 256)
        hidden = mm(a2[here, :], up[...]) + bias_up
        below, density = normal_parts(hidden)
        act_now = (hidden * below).astype(BF16)
        act[here, :] = act_now
        dact = mm_nt(dy_ref[here, :], down[...])
        dhidden_now = (dact * (below + hidden * density)).astype(BF16)
        dhidden[here, :] = dhidden_now
        bias_total = bias_total + jnp.sum(dhidden_now.astype(F32), axis=0, keepdims=True)
        if fresh:
            y[here, :] = mm(act_now, down[...])
            back[here, :] = mm_nt(dhidden_now, up[...])
        else:
            y[here, :] += mm(act_now, down[...])
            back[here, :] += mm_nt(dhidden_now, up[...])
    dbias_ref[0] = bias_total
    grad_up = mm(a2t[...], dhidden[...]).astype(BF16).reshape(wide, rows_up, FFC)
    grad_down = mm(dyt[...], act[...]).astype(BF16)
    core = place[3]

    def store_up(ref):
        for cols in range(4):
            ref[0, :, rows_up * cols : rows_up * (cols + 1), :] = grad_up[
                :, :, WIDTH * cols : WIDTH * (cols + 1)
            ]

    def store_down(ref):
        if wide == 1:
            for cols in range(4):
                ref[0, 0, D * cols : D * (cols + 1), :] = grad_down[
                    :, WIDTH * cols : WIDTH * (cols + 1)
                ]
            return
        for shard in range(wide):
            block = grad_down[:, rows_down * shard : rows_down * (shard + 1)]
            ref[0, shard, :, :128] = block[: D // 2]
            ref[0, shard, :, 128:] = block[D // 2 :]

    @pl.when(core == 0)
    def _():
        store_up(keep_ref)
        store_down(send_ref)

    @pl.when(core == 1)
    def _():
        store_up(send_ref)
        store_down(keep_ref)


def middle_first_kernel(wide, count_in, place, *refs):
    pieces = refs[:count_in]
    (
        x_ref, attn_ref, dy_ref, rows_ref, bias_up_ref,
        x1_ref, a2_ref, a2t_ref, dyt_ref, y_ref, back_ref, out_ref, keep_ref, send_ref, dbias_ref,
        flat, up, down, act, dhidden, sems,
    ) = refs[count_in:]
    copies = flat_copies(place, pieces, flat, sems)
    for copy in copies:
        copy.start()
    for cols in range(0, D, 256):
        dyt_ref[cols : cols + 256, :] = transposed(dy_ref[:, cols : cols + 256])
    for copy in copies:
        copy.wait()
    half_out = D // wide // 2
    half_flat = flat.shape[1] // 2
    for cols in range(3):
        upper = flat[:, half_out * cols : half_out * (cols + 1), :]
        lower = flat[:, half_flat + half_out * cols : half_flat + half_out * (cols + 1), :]
        out_ref[:, WIDTH * cols : WIDTH * (cols + 1)] = jnp.concatenate(
            [upper, lower], axis=1
        ).reshape(D, WIDTH)
    for rows in range(0, LEN, 256):
        here = pl.ds(rows, 256)
        x1 = x_ref[here, :].astype(F32) + (mm(attn_ref[here, :], out_ref[...]) + rows_ref[7:8, :])
        x1_ref[here, :] = x1
        centre = x1 - jnp.mean(x1, axis=-1, keepdims=True)
        spread = jnp.mean(centre * centre, axis=-1, keepdims=True)
        a2_ref[here, :] = (
            centre * lax.rsqrt(spread + norm_eps) * rows_ref[2:3, :] + rows_ref[3:4, :]
        ).astype(BF16)
    for cols in range(0, D, 256):
        a2t_ref[cols : cols + 256, :] = transposed(a2_ref[:, cols : cols + 256])
    chunk_step(
        place, wide, flat, 3 * half_out, half_flat + 3 * half_out, bias_up_ref[0], dy_ref, a2_ref,
        a2t_ref, dyt_ref, up, down, act, dhidden, y_ref, back_ref, keep_ref, send_ref, dbias_ref,
        True,
    )


def middle_rest_kernel(wide, count_in, place, *refs):
    pieces = refs[:count_in]
    (
        dy_ref, a2_ref, a2t_ref, dyt_ref, bias_up_ref, attn_ref, out_ref, rows_ref,
        y_in, back_in, x1_in,
        block_ref, dx1_ref, dmixed_ref, okeep_ref, osend_ref, vec_ref,
        keep_ref, send_ref, dbias_ref,
        flat, up, down, act, dhidden, back, dbranch, sems, flat_sems,
    ) = refs[count_in:]
    step = pl.program_id(0)
    y_copy = pltpu.make_async_copy(y_in, block_ref, sems.at[0])
    back_copy = pltpu.make_async_copy(back_in, back, sems.at[1])
    x1_copy = pltpu.make_async_copy(x1_in, dx1_ref, sems.at[2])

    def fetch(chunk, slot):
        if count_in == 2:

            @pl.when(place[3] == chunk)
            def _():
                pltpu.make_async_copy(pieces[0], flat.at[slot], flat_sems.at[slot]).start()

            @pl.when(place[3] != chunk)
            def _():
                pltpu.make_async_copy(pieces[1], flat.at[slot], flat_sems.at[slot]).start()

        else:
            pltpu.make_async_copy(
                pieces[0].at[chunk], flat.at[slot], flat_sems.at[slot]
            ).start()

    def arrived(slot):
        source = pieces[0] if count_in == 2 else pieces[0].at[0]
        pltpu.make_async_copy(source, flat.at[slot], flat_sems.at[slot]).wait()

    @pl.when(step == 0)
    def _():
        fetch(0, 0)
        y_copy.start()
        back_copy.start()
        fetch(1, 1)
        x1_copy.start()
        arrived(0)
        y_copy.wait()
        back_copy.wait()

    @pl.when(step == 1)
    def _():
        arrived(1)

    chunk_step(
        place, wide, flat.at[step], 0, 4 * (D // wide), bias_up_ref[0], dy_ref, a2_ref, a2t_ref,
        dyt_ref, up, down, act, dhidden, block_ref, back, keep_ref, send_ref, dbias_ref, False,
    )

    @pl.when(step == 1)
    def _():
        x1_copy.wait()
        zero = jnp.zeros((1, D), F32)
        dgain, dshift, dbias_out, dbias_down = zero, zero, zero, zero
        for rows in range(0, LEN, 256):
            here = pl.ds(rows, 256)
            x1 = dx1_ref[here, :]
            block_ref[here, :] = x1 + (block_ref[here, :] + rows_ref[8:9, :])
            dn = back[here, :]
            dy = dy_ref[here, :].astype(F32)
            centre = x1 - jnp.mean(x1, axis=-1, keepdims=True)
            spread = jnp.mean(centre * centre, axis=-1, keepdims=True)
            scale = lax.rsqrt(spread + norm_eps)
            zh = centre * scale
            dgain = dgain + jnp.sum(dn * zh, axis=0, keepdims=True)
            dshift = dshift + jnp.sum(dn, axis=0, keepdims=True)
            e = dn * rows_ref[2:3, :]
            dz = (
                e
                - jnp.mean(e, axis=-1, keepdims=True)
                - zh * jnp.mean(e * zh, axis=-1, keepdims=True)
            ) * scale
            dx1 = dy + dz
            dx1_ref[here, :] = dx1
            low = dx1.astype(BF16)
            dbranch[here, :] = low
            dbias_out = dbias_out + jnp.sum(low.astype(F32), axis=0, keepdims=True)
            dbias_down = dbias_down + jnp.sum(dy, axis=0, keepdims=True)
            dmixed_ref[here, :] = mm_nt(low, out_ref[...])
        for cols in range(0, D, 256):
            up[cols : cols + 256, :] = transposed(attn_ref[:, cols : cols + 256])
        store_halves(mm(up[...], dbranch[...]).astype(BF16), place[3], okeep_ref, osend_ref)
        vec_ref[0:1, :] = dgain
        vec_ref[1:2, :] = dshift
        vec_ref[2:3, :] = dbias_out
        vec_ref[3:4, :] = dbias_down


def once(shape):
    return whole_spec(shape, pipeline_mode=pl.Buffered(1))


def struct(shape, dtype):
    return jax.ShapeDtypeStruct(shape, dtype)


def weight_scratch():
    return [
        pltpu.VMEM((D, FFC), BF16), pltpu.VMEM((FFC, D), BF16), pltpu.VMEM((LEN, FFC), BF16),
        pltpu.VMEM((LEN, FFC), BF16),
    ]


def middle_first(place, wide, pieces, tokens, attn, cotangent, vectors, bias_up):
    rows_flat = 3 * D // wide + 2 * FFC * D // (WIDTH * wide)
    half = (1, wide, FFC * D // (WIDTH * wide), WIDTH)
    outs = [
        struct((LEN, D), F32), struct((LEN, D), BF16), struct((D, LEN), BF16),
        struct((D, LEN), BF16), struct((LEN, D), F32), struct((LEN, D), F32),
        struct((D, D), BF16), struct(half, BF16), struct(half, BF16), struct((1, 1, FFC), F32),
    ]
    return pl.pallas_call(
        functools.partial(middle_first_kernel, wide, len(pieces)),
        grid_spec=pltpu.PrefetchScalarGridSpec(
            num_scalar_prefetch=1,
            grid=(1,),
            in_specs=[any_spec()] * len(pieces)
            + [
                once((LEN, D)), once((LEN, D)), once((LEN, D)), once((13, D)),
                pl.BlockSpec((1, 1, FFC), lambda *_: (0, 0, 0)),
            ],
            out_specs=[once(out.shape) for out in outs],
            scratch_shapes=[pltpu.VMEM((wide, rows_flat, WIDTH), BF16)]
            + weight_scratch()
            + [pltpu.SemaphoreType.DMA((16,))],
        ),
        out_shape=outs,
        compiler_params=pltpu.CompilerParams(
            dimension_semantics=("arbitrary",), vmem_limit_bytes=VMEM_LIMIT
        ),
        cost_estimate=cost(14 * 10**9, 30 * 10**6),
        name="middle_first",
    )(place, *pieces, tokens, attn, cotangent, vectors, bias_up)


def middle_rest(place, wide, pieces, cotangent, state, bias_up, attn, w_out, vectors, sums):
    a2, a2t, dyt = state
    rows_flat = 2 * FFC * D // (WIDTH * wide)
    half = (2, wide, FFC * D // (WIDTH * wide), WIDTH)
    out_half = (wide, 3 * D // (2 * wide), WIDTH)
    outs = [
        struct((LEN, D), F32), struct((LEN, D), F32), struct((LEN, D), F32),
        struct(out_half, BF16), struct(out_half, BF16), struct((8, D), F32),
        struct(half, BF16), struct(half, BF16), struct((2, 1, FFC), F32),
    ]
    out_specs = [once(out.shape) for out in outs[:6]]
    out_specs += [group_spec(half[1:]), group_spec(half[1:]), group_spec((1, FFC))]
    return pl.pallas_call(
        functools.partial(middle_rest_kernel, wide, len(pieces)),
        grid_spec=pltpu.PrefetchScalarGridSpec(
            num_scalar_prefetch=1,
            grid=(2,),
            in_specs=[any_spec()] * len(pieces)
            + [
                once((LEN, D)), once((LEN, D)), once((D, LEN)), once((D, LEN)),
                pl.BlockSpec((1, 1, FFC), lambda j, *_: (j + 1, 0, 0)),
                once((LEN, D)), once((D, D)), once((13, D)),
                any_spec(), any_spec(), any_spec(),
            ],
            out_specs=out_specs,
            scratch_shapes=[pltpu.VMEM((2, wide, rows_flat, WIDTH), BF16)]
            + weight_scratch()
            + [
                pltpu.VMEM((LEN, D), F32), pltpu.VMEM((LEN, D), BF16),
                pltpu.SemaphoreType.DMA((3,)), pltpu.SemaphoreType.DMA((2,)),
            ],
        ),
        out_shape=outs,
        compiler_params=pltpu.CompilerParams(
            dimension_semantics=("arbitrary",), vmem_limit_bytes=VMEM_LIMIT
        ),
        cost_estimate=cost(28 * 10**9, 40 * 10**6),
        name="middle_rest",
    )(place, *pieces, cotangent, a2, a2t, dyt, bias_up, attn, w_out, vectors, *sums)


def input_kernel(x_ref, dx1_ref, da1_ref, rows_ref, out_ref, vec_ref):
    gain = rows_ref[0:1, :]
    x = x_ref[...].astype(F32)
    dn = da1_ref[...]
    centre = x - jnp.mean(x, axis=-1, keepdims=True)
    spread = jnp.mean(centre * centre, axis=-1, keepdims=True)
    scale = lax.rsqrt(spread + norm_eps)
    zh = centre * scale
    e = dn * gain
    dz = (
        e - jnp.mean(e, axis=-1, keepdims=True) - zh * jnp.mean(e * zh, axis=-1, keepdims=True)
    ) * scale
    out_ref[...] = dx1_ref[...] + dz

    @pl.when(pl.program_id(0) == 0)
    def _():
        vec_ref[...] = jnp.zeros_like(vec_ref)

    vec_ref[0:1, :] += jnp.sum(dn * zh, axis=0, keepdims=True)
    vec_ref[1:2, :] += jnp.sum(dn, axis=0, keepdims=True)


def input_side(tokens, dx1, da1, vectors):
    block = pl.BlockSpec((256, D), lambda i: (i, 0))
    return pl.pallas_call(
        input_kernel,
        grid=(LEN // 256,),
        in_specs=[block, block, block, pl.BlockSpec((13, D), lambda i: (0, 0))],
        out_specs=[block, pl.BlockSpec((8, D), lambda i: (0, 0))],
        out_shape=[
            jax.ShapeDtypeStruct((LEN, D), F32), jax.ShapeDtypeStruct((8, D), F32),
        ],
        compiler_params=pltpu.CompilerParams(dimension_semantics=("arbitrary",)),
        name="input_side",
    )(tokens, dx1, da1, vectors)


def tables(lengths, projection):
    ends = jnp.cumsum(lengths[0])
    starts = ends - lengths[0]
    place = jnp.arange(LEN, dtype=jnp.int32)
    member = (place[:, None] >= starts[None, :]) & (place[:, None] < ends[None, :])
    offset = jnp.sum(jnp.where(member, starts[None, :], 0), axis=1)
    position = (place - offset).astype(F32)
    freq = 10000.0 ** (-jnp.arange(32, dtype=F32) / 32)
    angles = position[:, None] * jnp.tile(freq, 4)[None, :]
    onehot = jnp.pad(member.astype(BF16), ((0, 0), (0, 128 - member.shape[1])))
    eye = jnp.asarray(np.eye(4, dtype=np.float32))
    lifted = jnp.einsum("hif,ab->haibf", projection.reshape(2, 32, FEAT), eye)
    lifted = lifted.reshape(WIDTH, 128)
    rounded = lax.reduce_precision(lifted, 8, 7)
    high, low = rounded.astype(BF16), (lifted - rounded).astype(BF16)
    square = np.zeros((2, 4, 32, 4, 32), np.float32)
    for head in range(4):
        square[:, head, :, head, :] = 0.5
    square = jnp.asarray(square.reshape(WIDTH, 128), BF16)
    proj = jnp.stack(
        [
            jnp.concatenate([high, low], axis=1),
            jnp.concatenate([high, high], axis=1),
            jnp.concatenate([square, square], axis=1),
        ]
    )
    return jnp.cos(angles), jnp.sin(angles), onehot, proj


def wide_perm(shift_z, flip_x):
    pairs = []
    for z in range(4):
        for x in range(2):
            target_x = 1 - x if flip_x else x
            pairs.append((2 * z + x, 2 * ((z + shift_z) % 4) + target_x))
    return pairs


def narrow_perm(flip_y, flip_core):
    pairs = []
    for y in range(2):
        for core in range(2):
            pairs.append(
                (2 * y + core, 2 * (1 - y if flip_y else y) + (1 - core if flip_core else core))
            )
    return pairs


def over_z(values, shift):
    return lax.ppermute(values, "wide", wide_perm(shift, False))


def over_x(values):
    return lax.ppermute(values, "wide", wide_perm(0, True))


def over_y(values):
    return lax.ppermute(values, "narrow", narrow_perm(True, False))


def over_core(values):
    return lax.ppermute(values, "narrow", narrow_perm(False, True))


def tie(*values):
    return lax.optimization_barrier(values)


def special():
    return lax.axis_size("wide") == 8 and lax.axis_size("narrow") == 4


def sum_wide(values):
    if not special():
        return lax.psum(values, "wide")
    for perm in (wide_perm(0, True), [(w, w ^ 2) for w in range(8)], [(w, w ^ 4) for w in range(8)]):
        values = values + lax.ppermute(values, "wide", perm)
    return values


def sum_narrow(values):
    if not special():
        return lax.psum(values, "narrow")
    pair = values + over_core(values)
    return pair + over_y(pair)


def along_z(mine):
    return jnp.stack([mine] + [over_z(mine, shift) for shift in (1, 2, 3)])


def small_call(kernel, name, place, operands, outs):
    return pl.pallas_call(
        kernel,
        grid_spec=pltpu.PrefetchScalarGridSpec(
            num_scalar_prefetch=1,
            grid=(1,),
            in_specs=[once(value.shape) for value in operands],
            out_specs=[once(out.shape) for out in outs],
        ),
        out_shape=outs,
        compiler_params=pltpu.CompilerParams(
            dimension_semantics=("arbitrary",), vmem_limit_bytes=VMEM_LIMIT
        ),
        cost_estimate=cost(10**6, sum(4 * math.prod(v.shape) for v in operands + outs)),
        name=name,
    )(place, *operands)


def pick_in_kernel(place, in_ref, first_ref, last_ref):
    here = pl.ds(pl.multiple_of(48 * place[3], 16), 48)
    for group in range(GROUPS):
        ref, index = (first_ref, group) if group < 2 else (last_ref, 0)
        for which in range(3):
            ref[index, :, WIDTH * which : WIDTH * (which + 1)] = in_ref[
                which, here, WIDTH * group : WIDTH * (group + 1)
            ].astype(BF16)


def pick_rest_kernel(place, out_ref, up_ref, down_ref, first_ref, rest_ref):
    core = place[3]
    here = pl.ds(pl.multiple_of(48 * core, 16), 48)
    for cols in range(3):
        first_ref[48 * cols : 48 * (cols + 1), :] = out_ref[
            here, WIDTH * cols : WIDTH * (cols + 1)
        ].astype(BF16)

    def put_up(ref, at, chunk):
        for cols in range(4):
            rows = slice(at + 96 * cols, at + 96 * (cols + 1))
            for side in range(2):
                start = 384 * (2 * cols + side) + 128 * chunk
                ref[rows, 128 * side : 128 * (side + 1)] = up_ref[:, start : start + 128].astype(
                    BF16
                )

    def put_down(ref, at, chunk):
        for cols in range(3):
            ref[at + 128 * cols : at + 128 * (cols + 1), :] = down_ref[
                128 * chunk : 128 * (chunk + 1), WIDTH * cols : WIDTH * (cols + 1)
            ].astype(BF16)

    @pl.when(core == 0)
    def _():
        put_up(first_ref, 144, 0)
        put_up(rest_ref, 0, 1)
        put_down(rest_ref, 384, 1)

    @pl.when(core == 1)
    def _():
        put_down(first_ref, 144, 0)
        put_up(rest_ref, 0, 2)
        put_down(rest_ref, 384, 2)


def first_sum_kernel(place, *refs):
    count = (len(refs) - 2) // 2
    send_ref, keep_ref = refs[-2:]
    x = place[1]
    at = 0
    for index in range(count):
        own, got = refs[2 * index], refs[2 * index + 1]
        for part in range(own.shape[0]):
            rows = own.shape[3]
            here = pl.ds(at, rows)
            keep_ref[0, here, :] = (
                own[part, 0, x].astype(F32) + got[part, 0, x].astype(F32)
            ).astype(BF16)
            send_ref[0, here, :] = (
                own[part, 0, 1 - x].astype(F32) + got[part, 0, 1 - x].astype(F32)
            ).astype(BF16)
            at += rows


def first_sum(place, pairs):
    total = 0
    operands, specs = [], []
    for own, got in pairs:
        parts, rows = own.shape[0], own.shape[2]
        total += parts * rows
        for value in (own, got):
            operands.append(value.reshape(parts, 4, 2, rows, WIDTH))
            specs.append(
                pl.BlockSpec((parts, 1, 2, rows, WIDTH), lambda i, *_: (0, i, 0, 0, 0))
            )
    block = pl.BlockSpec((1, total, WIDTH), lambda i, *_: (i, 0, 0))
    return pl.pallas_call(
        first_sum_kernel,
        grid_spec=pltpu.PrefetchScalarGridSpec(
            num_scalar_prefetch=1, grid=(4,), in_specs=specs, out_specs=[block, block]
        ),
        out_shape=[struct((4, total, WIDTH), BF16)] * 2,
        compiler_params=pltpu.CompilerParams(
            dimension_semantics=("arbitrary",), vmem_limit_bytes=VMEM_LIMIT
        ),
        cost_estimate=cost(10**6, 6 * 8 * total * WIDTH),
        name="first_sum",
    )(place, *operands)


def second_sum_kernel(place, own_ref, got_ref, *outs):
    z = place[0]
    for shift, out in enumerate(outs):
        there = lax.rem(z + shift, 4)
        out[...] = (own_ref[there].astype(F32) + got_ref[there].astype(F32)).astype(BF16)


def second_sum(place, own, got):
    outs = [struct(own.shape[1:], BF16)] * 4
    return small_call(second_sum_kernel, "second_sum", place, [own, got], outs)


def z_sum_kernel(place, *refs):
    total = refs[0][...].astype(F32)
    for ref in refs[1:-1]:
        total = total + ref[...].astype(F32)
    refs[-1][...] = total.astype(BF16)


def z_sum(place, parts):
    got = [over_z(parts[shift], shift) for shift in (1, 2, 3)]
    return small_call(
        z_sum_kernel, "z_sum", place, [parts[0]] + got, [struct(parts[0].shape, BF16)]
    )[0]


def to_row(column):
    size = column.shape[0]
    eye = lax.broadcasted_iota(jnp.int32, (size, size), 0) == lax.broadcasted_iota(
        jnp.int32, (size, size), 1
    )
    return jnp.sum(jnp.where(eye, column, 0.0), axis=0, keepdims=True)


def to_column(row):
    size = row.shape[1]
    eye = lax.broadcasted_iota(jnp.int32, (size, size), 0) == lax.broadcasted_iota(
        jnp.int32, (size, size), 1
    )
    return jnp.sum(jnp.where(eye, row, 0.0), axis=1, keepdims=True)


DECAY = 1.0 - STEP ** (-0.8)


def lane_values(values):
    lane = lax.broadcasted_iota(jnp.int32, (1, D), 1)
    row = jnp.zeros((1, D), F32)
    for index, value in enumerate(values):
        row = jnp.where(lane == index, value, row)
    return row


def moments(grad, rows_old):
    squares = grad * grad + square_eps
    mean = jnp.sum(squares, axis=1, keepdims=True) * (1.0 / grad.shape[1])
    rows_new = DECAY * rows_old + (1.0 - DECAY) * to_row(mean)
    total = jnp.sum(rows_new, axis=1, keepdims=True)
    return rows_new, total, jnp.sum(squares, axis=0, keepdims=True)


def scaled_by(grad, rows_new, total, rows_full, columns_new):
    factor = to_column(lax.rsqrt(rows_new / (total * (1.0 / rows_full))))
    return grad * factor * lax.rsqrt(columns_new)


def ffn_moments_kernel(
    place, a_own, a_got, b_own, b_got, up_rows, down_rows, out_rows,
    up_grad, down_grad, out_grad, up_rows_new, down_rows_new, out_rows_new, sums,
):
    core = place[3]

    def collect(low_a, high_a, low_b, high_b):
        for chunk in range(CHUNKS):
            low, high, at = (low_a, high_a, 0) if chunk == 0 else (low_b, high_b, 384 * (chunk - 1))
            for cols in range(4):
                for side in range(2):
                    start = 384 * (2 * cols + side) + 128 * chunk
                    up_grad[:, start : start + 128] = low[
                        at + 96 * cols : at + 96 * (cols + 1), 128 * side : 128 * (side + 1)
                    ]
            for side in range(2):
                down_grad[128 * chunk : 128 * (chunk + 1), 384 * side : 384 * (side + 1)] = (
                    jnp.transpose(high[at : at + 384, 128 * side : 128 * (side + 1)])
                )
        for cols in range(3):
            lanes = slice(WIDTH * cols, WIDTH * (cols + 1))
            out_grad[:48, lanes] = low_b[768 + 48 * cols : 768 + 48 * (cols + 1), :]
            out_grad[48:, lanes] = high_b[768 + 48 * cols : 768 + 48 * (cols + 1), :]

    @pl.when(core == 0)
    def _():
        collect(a_own, a_got, b_own, b_got)

    @pl.when(core == 1)
    def _():
        collect(a_got, a_own, b_got, b_own)

    up_new, up_total, up_sums = moments(up_grad[...], up_rows[...])
    down_new, down_total, down_sums = moments(down_grad[...], down_rows[...])
    out_new, out_total, out_sums = moments(out_grad[...], out_rows[...])
    up_rows_new[...] = up_new
    down_rows_new[...] = down_new
    out_rows_new[...] = out_new
    for part in range(4):
        sums[part : part + 1, :] = up_sums[:, D * part : D * (part + 1)]
    sums[4:5, :] = down_sums
    sums[5:6, :] = out_sums
    sums[6:7, :] = lane_values([up_total, down_total, out_total])
    sums[7:8, :] = jnp.zeros((1, D), F32)


def ffn_scale_kernel(
    place, up_grad, down_grad, out_grad, up_rows, down_rows, out_rows, up_cols, down_cols,
    out_cols, sums, up_cols_new, down_cols_new, out_cols_new, squares,
):
    up_sums = jnp.concatenate([sums[part : part + 1, :] for part in range(4)], axis=1)
    values = []
    for index, (grad, rows, cols, total, out, rows_full) in enumerate((
        (up_grad, up_rows, up_cols, up_sums, up_cols_new, D),
        (down_grad, down_rows, down_cols, sums[4:5, :], down_cols_new, FF),
        (out_grad, out_rows, out_cols, sums[5:6, :], out_cols_new, D),
    )):
        cols_new = DECAY * cols[...] + (1.0 - DECAY) * total * (1.0 / rows_full)
        out[...] = cols_new
        scaled = scaled_by(grad[...], rows[...], sums[6:7, index : index + 1], rows_full, cols_new)
        row = jnp.sum(scaled * scaled, axis=0, keepdims=True)
        values.append(jnp.sum(row, axis=1, keepdims=True))
    squares[...] = jnp.zeros(squares.shape, F32) + lane_values(values)


def weight_step(weight, grad, rows, total, rows_full, cols, square_sum, rate):
    scaled = scaled_by(grad, rows, total, rows_full, cols)
    rms = jnp.sqrt(square_sum * (1.0 / (rows_full * grad.shape[1])))
    return weight - scaled * (rate / jnp.maximum(1.0, rms / clip_level))


def ffn_step_kernel(
    place, up, down, out, up_grad, down_grad, out_grad, up_rows, down_rows, out_rows, up_cols,
    down_cols, out_cols, sums, squares, up_next, down_next, out_next,
):
    for index, (weight, grad, rows, cols, new, rows_full, rate) in enumerate((
        (up, up_grad, up_rows, up_cols, up_next, D, 0.3 * D ** (-0.5)),
        (down, down_grad, down_rows, down_cols, down_next, FF, 0.3 * FF ** (-0.5)),
        (out, out_grad, out_rows, out_cols, out_next, D, 1.2 * D ** (-0.5)),
    )):
        new[...] = weight_step(
            weight[...], grad[...], rows[...], sums[6:7, index : index + 1], rows_full, cols[...],
            squares[3:4, 3 + index : 4 + index], rate,
        )


def in_moments_kernel(
    place, own, got, rows_old, vector, ffn_squares, grad, rows_new, sums,
):
    core = place[3]

    def collect(low, high):
        for group in range(GROUPS):
            for which in range(3):
                at = 144 * group + 48 * which
                lanes = slice(WIDTH * group, WIDTH * (group + 1))
                grad[which, :48, lanes] = low[at : at + 48, :]
                grad[which, 48:, lanes] = high[at : at + 48, :]

    @pl.when(core == 0)
    def _():
        collect(own, got)

    @pl.when(core == 1)
    def _():
        collect(got, own)

    totals = []
    for which in range(3):
        new, total, columns = moments(grad[which], rows_old[which : which + 1, :])
        rows_new[which : which + 1, :] = new
        sums[which : which + 1, :] = columns
        totals.append(total)
    sums[3:4, :] = lane_values(totals + [ffn_squares[0:1, i : i + 1] for i in range(3)])
    sums[4:8, :] = jnp.zeros((4, D), F32)
    sums[8:24, :] = vector[...]


def in_scale_kernel(
    place, grad, rows, cols, sums, vectors, vector_state,
    cols_new, squares, vector_grad, state_next, vectors_next,
):
    values = []
    for which in range(3):
        new = DECAY * cols[which : which + 1, :] + (1.0 - DECAY) * sums[
            which : which + 1, :
        ] * (1.0 / D)
        cols_new[which : which + 1, :] = new
        scaled = scaled_by(
            grad[which], rows[which : which + 1, :], sums[3:4, which : which + 1], D, new
        )
        row = jnp.sum(scaled * scaled, axis=0, keepdims=True)
        values.append(jnp.sum(row, axis=1, keepdims=True))
    squares[...] = jnp.zeros(squares.shape, F32) + lane_values(values)
    g = sums[8:21, :]
    vector_grad[...] = g
    state = DECAY * vector_state[...] + (1.0 - DECAY) * (g * g + square_eps)
    state_next[...] = state
    update = g * lax.rsqrt(state)
    total = jnp.sum(jnp.sum(update * update, axis=0, keepdims=True), axis=1, keepdims=True)
    rms = jnp.sqrt(total * (1.0 / (13 * D)))
    vectors_next[...] = vectors[...] - update * (0.25 / jnp.maximum(1.0, rms / clip_level))


def in_step_kernel(place, weight, grad, rows, cols, sums, squares, weight_next):
    for which in range(3):
        weight_next[which] = weight_step(
            weight[which], grad[which], rows[which : which + 1, :],
            sums[3:4, which : which + 1], D, cols[which : which + 1, :],
            squares[0:1, which : which + 1], 0.3 * D ** (-0.5),
        )


def shards(
    tokens, cotangent, lengths, projection, inward, outward, expand, shrink, vectors,
    inward_rows, inward_columns, outward_rows, outward_columns, expand_rows, expand_columns,
    shrink_rows, shrink_columns, vector_state,
):
    full = special()
    rows = outward.shape[0]
    wide = 8 if full else 1
    wide_at = lax.axis_index("wide").astype(jnp.int32)
    narrow_at = lax.axis_index("narrow").astype(jnp.int32)
    core = narrow_at % 2 if full else jnp.int32(0)
    place = jnp.stack([wide_at // 2, wide_at % 2, narrow_at // 2, core])
    per = FFC // wide
    if full:
        own_in = small_call(
            pick_in_kernel, "pick_in", place, [inward],
            [struct((2, 48, D), BF16), struct((1, 48, D), BF16)],
        )
        *own_in, outward_late = tie(*own_in, outward)
        own_first, own_rest = small_call(
            pick_rest_kernel, "pick_rest", place, [outward_late, expand, shrink],
            [struct((528, WIDTH), BF16), struct((768, WIDTH), BF16)],
        )
        in_z = [along_z(value) for value in own_in]
        rest_own = lax.all_gather(own_rest, "wide", axis=0)
        *in_z, own_first = tie(*in_z, own_first)
        first_z = along_z(own_first)
        in_x = [over_x(value) for value in in_z]
        pieces_in = []
        for near, far in zip(in_z, in_x):
            pieces_in += [near, far, over_core(near), over_core(far)]
        *pieces_in, first_z = tie(*pieces_in, first_z)
        first_x = over_x(first_z)
    else:
        in_low = lax.all_gather(inward.astype(BF16), "wide", axis=1, tiled=True)
        out_low = lax.all_gather(outward.astype(BF16), "wide", axis=0, tiled=True)
        up_low = lax.all_gather(expand.astype(BF16), "wide", axis=0, tiled=True)
        down_low = lax.all_gather(shrink.astype(BF16), "wide", axis=0, tiled=True)
        units = jnp.transpose(in_low.reshape(3, D, GROUPS, WIDTH), (2, 1, 0, 3))
        pieces_in = [units.reshape(1, 3 * D, D)]

        def blocks(matrix):
            count = matrix.shape[1] // WIDTH
            return jnp.transpose(matrix.reshape(-1, count, WIDTH), (1, 0, 2)).reshape(-1, WIDTH)

        ups = [blocks(up_low[:, FFC * j : FFC * (j + 1)]) for j in range(CHUNKS)]
        downs = [blocks(down_low[FFC * j : FFC * (j + 1)]) for j in range(CHUNKS)]
        half = D // 2
        pieces_first = [
            jnp.concatenate([blocks(out_low[:half]), ups[0], blocks(out_low[half:]), downs[0]])[
                None
            ]
        ]
        pieces_rest = [
            jnp.stack(
                [jnp.concatenate([ups[j], downs[j]])[None] for j in range(1, CHUNKS)]
            )
        ]
    cosine, sine, onehot, proj = tables(lengths, projection)
    perm = jnp.asarray(head_perm(), BF16)
    block_ones = np.kron(np.eye(2, dtype=np.float32), np.ones((64, 64), np.float32))
    ones = jnp.asarray(np.concatenate([block_ones, block_ones]), BF16)
    split = vectors[4:6].reshape(2, GROUPS, 4, 2, 32)
    bias_qk = jnp.transpose(split, (0, 1, 3, 2, 4)).reshape(2, GROUPS, WIDTH)
    bias = jnp.concatenate([bias_qk, vectors[6].reshape(1, GROUPS, WIDTH)])
    bias = jnp.transpose(bias, (1, 0, 2))
    bias_up = vectors[9:].reshape(wide, CHUNKS, per)
    bias_up = jnp.transpose(bias_up, (1, 0, 2)).reshape(CHUNKS, 1, FFC)
    attn, mixed, a1t, w_in, wq, wk, qf, kf, v, rden = attend(
        lengths, place, pieces_in, wide, tokens, vectors[:2], bias, perm, proj, cosine, sine,
        onehot,
    )
    if full:
        pieces_first = [first_z, first_x, over_core(first_z), over_core(first_x)]
        pieces_rest = [rest_own, over_core(rest_own)]
    x1, a2, a2t, dyt, y, back, w_out, keep0, send0, dbias0 = middle_first(
        place, wide, pieces_first, tokens, attn, cotangent, vectors, bias_up
    )
    block_out, dx1, dmixed, okeep, osend, middle_vec, keep12, send12, dbias12 = middle_rest(
        place, wide, pieces_rest, cotangent, (a2, a2t, dyt), bias_up, attn, w_out, vectors,
        (y, back, x1),
    )
    if full:
        send_a, keep_a = first_sum(place, [(keep0, over_core(send0))])
        dmixed, send_a, keep_a = tie(dmixed, send_a, keep_a)
        got_a = over_x(send_a)
        got12, got_out = over_core(send12), over_core(osend)
    saved = (mixed, rden, wq, wk, qf, kf, v)
    common = (a1t, w_in, perm, proj, cosine, sine, onehot, ones)
    in_keep1, in_send1, in_bias1, da1 = attend_back(
        0, 1, lengths, place, wide, dmixed, saved, *common, None
    )
    if full:
        a_parts = second_sum(place, keep_a, got_a)
        send_b, keep_b = first_sum(place, [(keep12, got12), (okeep[None], got_out[None])])
        da1, send_b, keep_b, *a_parts = tie(da1, send_b, keep_b, *a_parts)
        got_in1 = over_core(in_send1)
        got_b = over_x(send_b)
    in_keep2, in_send2, in_bias2, da1 = attend_back(
        1, 2, lengths, place, wide, dmixed, saved, *common, da1
    )
    if full:
        send_c, keep_c = first_sum(
            place, [(in_keep1, got_in1), (in_keep2, over_core(in_send2))]
        )
        a_mine = z_sum(place, a_parts)
        b_parts = second_sum(place, keep_b, got_b)
        da1, send_c, keep_c, a_mine, *b_parts = tie(da1, send_c, keep_c, a_mine, *b_parts)
        got_c = over_x(send_c)
    input_grad, input_vec = input_side(tokens, dx1, da1, vectors)
    dbias_in = jnp.concatenate([in_bias1, in_bias2]).reshape(GROUPS, 3, WIDTH)
    dbias_in = jnp.transpose(dbias_in, (1, 0, 2)).reshape(3, D)
    dbias_up = jnp.concatenate([dbias0, dbias12]).reshape(CHUNKS, wide, per)
    dbias_up = jnp.transpose(dbias_up, (1, 0, 2)).reshape(-1, D)
    vector_local = jnp.concatenate(
        [input_vec[:2], middle_vec[:2], dbias_in, middle_vec[2:4], dbias_up]
    )
    if full:
        vector_part = sum_narrow(jnp.pad(vector_local, ((0, 3), (0, 0))))

        def over_pairs(mine):
            half_sum = mine.astype(F32) + over_y(mine).astype(F32)
            return half_sum, over_core(half_sum)

        a_own, a_got = over_pairs(a_mine)
        b_own, b_got = over_pairs(z_sum(place, b_parts))
        expand_grad, shrink_grad, outward_grad, up_rows, down_rows, out_rows, sums = small_call(
            ffn_moments_kernel, "ffn_moments", place,
            [
                a_own, a_got, b_own, b_got, expand_rows[None], shrink_rows[None],
                outward_rows[None],
            ],
            [
                struct(expand.shape, F32), struct(shrink.shape, F32), struct(outward.shape, F32),
                struct((1, 96), F32), struct((1, 384), F32), struct((1, 96), F32),
                struct((8, D), F32),
            ],
        )
        sums = sum_wide(sums)
        grads = [expand_grad, shrink_grad, outward_grad]
        new_rows = [up_rows, down_rows, out_rows]
        up_cols, down_cols, out_cols, squares = small_call(
            ffn_scale_kernel, "ffn_scale", place,
            grads + new_rows
            + [expand_columns[None], shrink_columns[None], outward_columns[None], sums],
            [struct((1, FF), F32), struct((1, D), F32), struct((1, D), F32), struct((8, D), F32)],
        )
        c_parts = second_sum(place, keep_c, got_c)
        c_own, c_got = over_pairs(z_sum(place, c_parts))
        inward_grad, in_rows, in_sums = small_call(
            in_moments_kernel, "in_moments", place,
            [c_own, c_got, inward_rows, vector_part, squares],
            [struct(inward.shape, F32), struct((3, 96), F32), struct((24, D), F32)],
        )
        in_sums = sum_wide(in_sums)
        in_cols, in_squares, vector_grad, vector_state_next, vectors_next = small_call(
            in_scale_kernel, "in_scale", place,
            [inward_grad, in_rows, inward_columns, in_sums, vectors, vector_state],
            [struct((3, D), F32), struct((8, D), F32)] + [struct((13, D), F32)] * 3,
        )
        in_squares = sum_wide(in_squares)
        new_cols = [up_cols, down_cols, out_cols]
        expand_next, shrink_next, outward_next = small_call(
            ffn_step_kernel, "ffn_step", place,
            [expand, shrink, outward] + grads + new_rows + new_cols + [sums, in_sums],
            [struct(expand.shape, F32), struct(shrink.shape, F32), struct(outward.shape, F32)],
        )
        (inward_next,) = small_call(
            in_step_kernel, "in_step", place,
            [inward, inward_grad, in_rows, in_cols, in_sums, in_squares],
            [struct(inward.shape, F32)],
        )
        return (
            block_out, input_grad, inward_grad, outward_grad, expand_grad, shrink_grad,
            vector_grad, in_rows, in_cols, out_rows[0], out_cols[0], up_rows[0], up_cols[0],
            down_rows[0], down_cols[0], vector_state_next, inward_next, outward_next,
            expand_next, shrink_next, vectors_next,
        )
    vector_part = sum_narrow(vector_local)

    def reduced(values, axis):
        part = lax.psum_scatter(values, "wide", scatter_dimension=axis, tiled=True)
        return lax.psum(part.astype(F32), "narrow")

    keeps = [keep0[0], keep12[0], keep12[1]]
    sends = [send0[0], send12[0], send12[1]]
    up_grads = [
        jnp.transpose(keep.reshape(4, D, WIDTH), (1, 0, 2)).reshape(D, FFC) for keep in keeps
    ]
    down_grads = [
        jnp.transpose(send.reshape(4, D, WIDTH), (0, 2, 1)).reshape(FFC, D) for send in sends
    ]
    expand_grad = reduced(jnp.concatenate(up_grads, axis=1), 0)
    shrink_grad = reduced(jnp.concatenate(down_grads, axis=0), 0)

    def rebuilt(keep, send):
        return jnp.concatenate(
            [keep.reshape(-1, 3, D // 2, WIDTH), send.reshape(-1, 3, D // 2, WIDTH)], axis=2
        )

    outward_grad = reduced(jnp.transpose(rebuilt(okeep, osend)[0], (1, 0, 2)).reshape(D, D), 0)
    in_units = rebuilt(
        jnp.concatenate([in_keep1, in_keep2]), jnp.concatenate([in_send1, in_send2])
    )
    inward_grad = reduced(jnp.transpose(in_units, (1, 2, 0, 3)).reshape(3, D, D), 1)
    decay = 1.0 - STEP ** (-0.8)
    wide_count = lax.axis_size("wide")
    grads_list = [inward_grad, outward_grad[None], expand_grad[None], shrink_grad[None]]
    rows_old = [inward_rows, outward_rows[None], expand_rows[None], shrink_rows[None]]
    columns_old = [
        inward_columns,
        outward_columns[None],
        expand_columns[None],
        shrink_columns[None],
    ]
    weights_old = [inward, outward[None], expand[None], shrink[None]]
    rates = [0.3 * D ** (-0.5), 1.2 * D ** (-0.5), 0.3 * D ** (-0.5), 0.3 * FF ** (-0.5)]
    bounds = [0, 3, 4, 5, 6]
    rows_next = []
    column_parts = []
    for member in range(4):
        squares = grads_list[member] * grads_list[member] + square_eps
        rows_next.append(decay * rows_old[member] + (1.0 - decay) * jnp.mean(squares, axis=-1))
        column_parts.append(jnp.sum(squares, axis=-2))
    row_totals = jnp.concatenate([jnp.sum(entry, axis=-1) for entry in rows_next])
    shapes = [part.shape for part in column_parts] + [row_totals.shape, vector_part.shape]
    flat = jnp.concatenate(
        [part.reshape(-1) for part in column_parts + [row_totals, vector_part]]
    )
    flat = jnp.pad(flat, (0, -flat.shape[0] % 1024)).reshape(-1, 128)
    flat = sum_wide(flat).reshape(-1)
    summed = []
    offset = 0
    for shape in shapes:
        size = 1
        for extent in shape:
            size *= extent
        summed.append(flat[offset : offset + size].reshape(shape))
        offset += size
    column_sums = list(summed[0:4])
    totals_sum = summed[4]
    vector_grad = summed[5]
    columns_next = []
    scaled_list = []
    row_means = []
    sizes_full = []
    for member in range(4):
        grad_now = grads_list[member]
        rows_full = grad_now.shape[-2] * wide_count
        sizes_full.append(rows_full * grad_now.shape[-1])
        columns_next.append(
            decay * columns_old[member] + (1.0 - decay) * column_sums[member] / rows_full
        )
        row_mean = totals_sum[bounds[member] : bounds[member + 1]] / rows_full
        row_means.append(row_mean)
        scaled_list.append(
            grad_now
            * lax.rsqrt(rows_next[member] / row_mean[:, None])[..., None]
            * lax.rsqrt(columns_next[member])[:, None, :]
        )
    partial_squares = jnp.concatenate(
        [jnp.sum(entry * entry, axis=(-2, -1)) for entry in scaled_list]
    )
    total_squares = sum_wide(jnp.pad(partial_squares, (0, 122)).reshape(1, 128))[0, :6]
    rms_list = [
        jnp.sqrt(total_squares[bounds[member] : bounds[member + 1]] / sizes_full[member])
        for member in range(4)
    ]
    weights_next = []
    for member in range(4):
        limiter = jnp.maximum(1.0, rms_list[member] / clip_level)
        weights_next.append(
            weights_old[member] - rates[member] * scaled_list[member] / limiter[:, None, None]
        )
    vector_state_next = decay * vector_state + (1.0 - decay) * (
        vector_grad * vector_grad + square_eps
    )
    vector_update = vector_grad * lax.rsqrt(vector_state_next)
    vector_rms = jnp.sqrt(jnp.mean(vector_update * vector_update))
    vectors_next = vectors - 0.25 * vector_update / jnp.maximum(1.0, vector_rms / clip_level)
    return (
        block_out,
        input_grad,
        inward_grad,
        outward_grad,
        expand_grad,
        shrink_grad,
        vector_grad,
        rows_next[0],
        columns_next[0],
        rows_next[1][0],
        columns_next[1][0],
        rows_next[2][0],
        columns_next[2][0],
        rows_next[3][0],
        columns_next[3][0],
        vector_state_next,
        weights_next[0],
        weights_next[1][0],
        weights_next[2][0],
        weights_next[3][0],
        vectors_next,
    )


def solution(mesh):
    placed = (
        P(("narrow", "wide"), None),
        P(("narrow", "wide"), None),
        P(("narrow", "wide"), None),
        P(),
        P(None, "wide", None),
        P("wide", None),
        P("wide", None),
        P("wide", None),
        P(),
        P(None, "wide"),
        P(),
        P("wide"),
        P(),
        P("wide"),
        P(),
        P("wide"),
        P(),
        P(),
    )
    return jax.shard_map(
        shards,
        mesh=mesh,
        in_specs=placed,
        out_specs=(
            P(("narrow", "wide"), None),
            P(("narrow", "wide"), None),
            P(None, "wide", None),
            P("wide", None),
            P("wide", None),
            P("wide", None),
            P(),
            P(None, "wide"),
            P(),
            P("wide"),
            P(),
            P("wide"),
            P(),
            P("wide"),
            P(),
            P(),
            P(None, "wide", None),
            P("wide", None),
            P("wide", None),
            P("wide", None),
            P(),
        ),
        check_vma=False,
    )
```

```python
import functools
import math

import jax
import jax.numpy as jnp
import numpy as np
from jax import lax
from jax.experimental import pallas as pl
from jax.experimental.pallas import tpu as pltpu
from jax.sharding import PartitionSpec as P

D = 768
HEADS = 12
HD = 64
FF = 3072
FEAT = 32
STEP = 10
LEN = 1024
SPAN = 256
CHUNKS = 3
GROUPS = 3
WIDTH = 256
FFC = FF // CHUNKS

norm_eps = 1e-05
square_eps = 1e-30
clip_level = 1.0

F32 = jnp.float32
BF16 = jnp.bfloat16
VMEM_LIMIT = 60 * 1024 * 1024


def mm(left, right):
    return lax.dot_general(left, right, (((1,), (0,)), ((), ())), preferred_element_type=F32)


def mm_nt(left, right):
    return lax.dot_general(left, right, (((1,), (1,)), ((), ())), preferred_element_type=F32)


def mm_tn(left, right):
    return lax.dot_general(left, right, (((0,), (0,)), ((), ())), preferred_element_type=F32)


def halves(values):
    high = values.astype(BF16)
    return high, (values - high.astype(F32)).astype(BF16)


TAIL = (
    0.1795078068971634,
    0.17978088557720184,
    0.14234966039657593,
    0.06379217654466629,
    0.0434231162071228,
    -0.261725515127182,
    0.20454804599285126,
    -0.05167665705084801,
)


def normal_parts(values):
    size = jnp.abs(values)
    t = 1.0 / (1.0 + 0.45 * size)
    poly = TAIL[-1]
    for coeff in TAIL[-2::-1]:
        poly = poly * t + coeff
    bell = jnp.exp(-0.5 * values * values)
    tail = poly * t * bell
    return jnp.where(values >= 0, 1.0 - tail, tail), bell * 0.3989422804014327


def transposed(values):
    row = lax.broadcasted_iota(jnp.int32, (256, 256), 0)
    col = lax.broadcasted_iota(jnp.int32, (256, 256), 1)
    eye = (row == col).astype(F32).astype(BF16)
    return mm_nt(eye, values).astype(BF16)


def head_perm():
    perm = np.zeros((WIDTH, WIDTH), np.float32)
    for head in range(4):
        for half in range(2):
            for i in range(32):
                perm[head * 64 + half * 32 + i, half * 128 + head * 32 + i] = 1.0
    return perm


def make_blocks(lengths, base, first, last):
    def step(s, carry):
        count, begin, begin_row, end = carry
        new_end = end + lengths[0, s]
        full = new_end - begin_row > SPAN

        @pl.when(full)
        def _():
            base[count] = begin_row
            first[count] = begin
            last[count] = s - 1

        row = jnp.minimum((end // 16) * 16, LEN - SPAN)
        return (
            jnp.where(full, count + 1, count),
            jnp.where(full, s, begin),
            jnp.where(full, row, begin_row),
            new_end,
        )

    segments = lengths.shape[1]
    zero = jnp.int32(0)
    count, begin, begin_row, _ = lax.fori_loop(0, segments, step, (zero, zero, zero, zero))
    base[count] = begin_row
    first[count] = begin
    last[count] = segments - 1
    return count + 1


def lane_mask(lo, hi, width, dtype):
    lane = lax.broadcasted_iota(jnp.int32, (1, width), 1)
    return ((lane >= lo) & (lane < hi)).astype(F32).astype(dtype)


def value_rows(v_pair, head):
    keep = lane_mask(64 * head, 64 * head + 64, 128, BF16)
    return jnp.concatenate([v_pair * keep, jnp.broadcast_to(keep, v_pair.shape)], axis=1)


def span_mask(onehot, rows, lo, hi):
    member = onehot[rows, :]
    lane = lax.broadcasted_iota(jnp.int32, (1, 128), 1)
    inside = ((lane >= lo) & (lane <= hi)).astype(F32).astype(BF16)
    return mm_nt(member * inside, member).astype(BF16)


def cost(flops, size):
    return pl.CostEstimate(flops=10**6, transcendentals=0, bytes_accessed=10**5)


def any_spec():
    return pl.BlockSpec(memory_space=pl.ANY)


def in_copies(place, pieces, dst, sems, unit):
    if len(pieces) == 1:
        rows = dst.shape[1] // 3
        here = pl.ds(unit * rows, rows)
        return [pltpu.make_async_copy(pieces[0].at[:, here], dst.at[:, here], sems.at[unit, 0])]
    z, x, core = place[0], place[1], place[3]
    part, index = (0, unit) if unit < 2 else (4, 0)
    copies = []
    for side in range(2):
        half = core if side == 0 else 1 - core
        for flip in range(2):
            column = x if flip == 0 else 1 - x
            for shift in range(4):
                row = lax.rem(z + 4 - shift, 4) * 2 + column
                start = pl.multiple_of(unit * 96 + half * 48, 16)
                copies.append(
                    pltpu.make_async_copy(
                        pieces[part + 2 * side + flip].at[shift, index],
                        dst.at[row, pl.ds(start, 48)],
                        sems.at[unit, len(copies)],
                    )
                )
    return copies


def flat_copies(place, pieces, dst, sems):
    if len(pieces) == 1:
        return [pltpu.make_async_copy(pieces[0], dst, sems.at[0])]
    z, x, core = place[0], place[1], place[3]
    span = dst.shape[1] // 2
    copies = []
    for side in range(2):
        half = core if side == 0 else 1 - core
        for flip in range(2):
            column = x if flip == 0 else 1 - x
            for shift in range(4):
                row = lax.rem(z + 4 - shift, 4) * 2 + column
                start = pl.multiple_of(half * span, 16)
                copies.append(
                    pltpu.make_async_copy(
                        pieces[2 * side + flip].at[shift],
                        dst.at[row, pl.ds(start, span)],
                        sems.at[len(copies)],
                    )
                )
    return copies


def attend_kernel(count_in, lengths, place, *refs):
    pieces = refs[:count_in]
    (
        x_ref, norm_ref, bias_ref, perm_ref, proj_ref, cos_ref, sin_ref, onehot_ref,
        attn_ref, mixed_ref, a1t_ref, w_ref, wq_ref, wk_ref, qf_ref, kf_ref, v_ref, rden_ref,
        a1, qb, kb, vb, parts, base, first, last, sems,
    ) = refs[count_in:]
    group = pl.program_id(0)

    @pl.when(group == 0)
    def _():
        for unit in range(GROUPS):
            for copy in in_copies(place, pieces, w_ref, sems, unit):
                copy.start()
        for rows in range(0, LEN, 256):
            here = pl.ds(rows, 256)
            x = x_ref[here, :].astype(F32)
            centre = x - jnp.mean(x, axis=-1, keepdims=True)
            spread = jnp.mean(centre * centre, axis=-1, keepdims=True)
            a1[here, :] = (
                centre * lax.rsqrt(spread + norm_eps) * norm_ref[0:1, :] + norm_ref[1:2, :]
            ).astype(BF16)
        for cols in range(0, D, 256):
            a1t_ref[cols : cols + 256, :] = transposed(a1[:, cols : cols + 256])

    for unit in range(GROUPS):

        @pl.when(group == unit)
        def _():
            for copy in in_copies(place, pieces, w_ref, sems, unit):
                copy.wait()

    count = make_blocks(lengths, base, first, last)
    shard = w_ref.shape[1] // 3
    here = pl.ds(pl.multiple_of(group * shard, 16), shard)
    w = w_ref[:, here, :].reshape(D, D)
    perm = perm_ref[...]
    bias = bias_ref[0]
    proj_both = proj_ref[0]
    proj_high = proj_ref[1, :, :128]
    square = proj_ref[2, :, :128]
    for which, (out_w, out_f, low_f) in enumerate(((wq_ref, qf_ref, qb), (wk_ref, kf_ref, kb))):
        weight = mm(w[:, WIDTH * which : WIDTH * (which + 1)], perm).astype(BF16)
        for rows in range(0, LEN, 256):
            here = pl.ds(rows, 256)
            u = (mm(a1[here, :], weight) + bias[which : which + 1, :]) * HD ** (-0.25)
            c = u[:, :128]
            e = u[:, 128:]
            cosine = cos_ref[here, :]
            sine = sin_ref[here, :]
            turned = jnp.concatenate([c * cosine - e * sine, e * cosine + c * sine], axis=1)
            out_w[0, here, :] = turned
            high, low = halves(turned)
            sq_high, sq_low = halves(turned * turned)
            both = mm(high, proj_both)
            logits = (
                both[:, :128] + both[:, 128:] + mm(low, proj_high)
                - (mm(sq_high, square) + mm(sq_low, square))
            )
            phi = jnp.exp(logits) * FEAT ** (-0.5)
            out_f[0, here, :] = phi
            low_f[here, :] = phi.astype(BF16)
    for rows in range(0, LEN, 256):
        here = pl.ds(rows, 256)
        v = mm(a1[here, :], w[:, 2 * WIDTH :]) + bias[2:3, :]
        v_ref[0, here, :] = v
        vb[here, :] = v.astype(BF16)
    parts[...] = jnp.zeros_like(parts)

    def one_span(index, carry):
        rows = pl.ds(pl.multiple_of(base[index], 16), SPAN)
        mask = span_mask(onehot_ref, rows, first[index], last[index])
        q = qb[rows, :]
        k = kb[rows, :]
        for pair in range(2):
            v_pair = vb[rows, 128 * pair : 128 * (pair + 1)]
            total = jnp.zeros((SPAN, WIDTH), F32)
            for side in range(2):
                head = 2 * pair + side
                scores = mm_nt(q * lane_mask(32 * head, 32 * head + 32, 128, BF16), k)
                total = total + mm(scores.astype(BF16) * mask, value_rows(v_pair, side))
            parts[pair, rows, :] += total
        return carry

    lax.fori_loop(0, count, one_span, 0)
    for pair in range(2):
        lanes = slice(128 * pair, 128 * (pair + 1))
        inverse = 1.0 / parts[pair, :, 128:]
        rden_ref[0, :, lanes] = inverse
        mixed = parts[pair, :, :128] * inverse
        mixed_ref[0, :, lanes] = mixed
        attn_ref[:, lanes] = mixed.astype(BF16)


def whole_spec(shape, **options):
    return pl.BlockSpec(shape, lambda *_: (0,) * len(shape), **options)


def group_spec(shape):
    return pl.BlockSpec((1,) + shape, lambda g, *_: (g,) + (0,) * len(shape))


def attend(lengths, place, pieces, wide, tokens, norm, bias, perm, proj, cosine, sine, onehot):
    def out(shape, dtype):
        return jax.ShapeDtypeStruct((GROUPS,) + shape, dtype)

    rows_in = 3 * D // wide
    return pl.pallas_call(
        functools.partial(attend_kernel, len(pieces)),
        grid_spec=pltpu.PrefetchScalarGridSpec(
            num_scalar_prefetch=2,
            grid=(GROUPS,),
            in_specs=[any_spec()] * len(pieces)
            + [
                whole_spec((LEN, D)), whole_spec((2, D)), group_spec((3, WIDTH)),
                whole_spec((WIDTH, WIDTH)), whole_spec((3, WIDTH, WIDTH)), whole_spec((LEN, 128)),
                whole_spec((LEN, 128)), whole_spec((LEN, 128)),
            ],
            out_specs=[
                pl.BlockSpec((LEN, WIDTH), lambda g, *_: (0, g)), group_spec((LEN, WIDTH)),
                whole_spec((D, LEN)), whole_spec((wide, rows_in, D)), group_spec((LEN, WIDTH)),
                group_spec((LEN, WIDTH)), group_spec((LEN, 128)), group_spec((LEN, 128)),
                group_spec((LEN, WIDTH)), group_spec((LEN, WIDTH)),
            ],
            scratch_shapes=[
                pltpu.VMEM((LEN, D), BF16),
                pltpu.VMEM((LEN, 128), BF16), pltpu.VMEM((LEN, 128), BF16),
                pltpu.VMEM((LEN, WIDTH), BF16), pltpu.VMEM((2, LEN, WIDTH), F32),
                pltpu.SMEM((32,), jnp.int32), pltpu.SMEM((32,), jnp.int32),
                pltpu.SMEM((32,), jnp.int32), pltpu.SemaphoreType.DMA((GROUPS, 16)),
            ],
        ),
        out_shape=[
            jax.ShapeDtypeStruct((LEN, D), BF16), out((LEN, WIDTH), F32),
            jax.ShapeDtypeStruct((D, LEN), BF16), jax.ShapeDtypeStruct((wide, rows_in, D), BF16),
            out((LEN, WIDTH), F32), out((LEN, WIDTH), F32), out((LEN, 128), F32),
            out((LEN, 128), F32), out((LEN, WIDTH), F32), out((LEN, WIDTH), F32),
        ],
        compiler_params=pltpu.CompilerParams(
            dimension_semantics=("arbitrary",), vmem_limit_bytes=VMEM_LIMIT
        ),
        cost_estimate=cost(20 * 10**9, 40 * 10**6),
        name="attend",
    )(lengths, place, *pieces, tokens, norm, bias, perm, proj, cosine, sine, onehot)


def attend_back_kernel(
    lengths, place, dmixed_ref, mixed_ref, rden_ref, wq_ref, wk_ref, qf_ref, kf_ref, v_ref,
    a1t_ref, w_ref, perm_ref, proj_ref, cos_ref, sin_ref, onehot_ref, ones_ref,
    keep_ref, send_ref, bias_ref, da1_ref,
    qb, kb, dnb, dnh, lift, dqf, dkf, dv, dqkv, base, first, last,
):
    count = make_blocks(lengths, base, first, last)
    qb[...] = qf_ref[0].astype(BF16)
    kb[...] = kf_ref[0].astype(BF16)
    lane = lax.broadcasted_iota(jnp.int32, (1, 128), 1)
    ones = ones_ref[...]
    for pair in range(2):
        lanes = slice(128 * pair, 128 * (pair + 1))
        for rows in range(0, LEN, 256):
            here = pl.ds(rows, 256)
            dnum = dmixed_ref[here, lanes] * rden_ref[0, here, lanes]
            high, low = halves(dnum)
            dnb[here, lanes] = high
            part_high, part_low = halves(dnum * mixed_ref[0, here, lanes])
            dden = -mm(jnp.concatenate([part_high, part_low], axis=1), ones)
            den_high, den_low = halves(dden)
            high, low = high.astype(F32), low.astype(F32)
            den_high = pltpu.roll(den_high.astype(F32), 64, 1)
            den_low = pltpu.roll(den_low.astype(F32), 64, 1)
            low_far = pltpu.roll(low, 64, 1)
            v = v_ref[0, here, lanes]
            v_high, v_low = halves(v)
            v_high, v_low = v_high.astype(F32), v_low.astype(F32)
            v_far = pltpu.roll(v_high, 64, 1)
            for side in range(2):
                own = (lane >= 64 * side) & (lane < 64 * side + 64)
                mark = 64 - 64 * side
                rest = jnp.where(lane == mark, den_high, jnp.where(lane == mark + 1, den_low, 0.0))
                both = ((lane == mark) | (lane == mark + 1)).astype(F32)
                head = 2 * pair + side
                dnh[head, here, :128] = jnp.where(own, high, low_far).astype(BF16)
                dnh[head, here, 128:] = jnp.where(own, high, rest).astype(BF16)
                lift[head, here, :128] = jnp.where(own, v_high, v_far).astype(BF16)
                lift[head, here, 128:] = jnp.where(own, v_low, both).astype(BF16)
    dqf[...] = jnp.zeros_like(dqf)
    dkf[...] = jnp.zeros_like(dkf)
    dv[...] = jnp.zeros_like(dv)

    def one_span(index, carry):
        rows = pl.ds(pl.multiple_of(base[index], 16), SPAN)
        mask = span_mask(onehot_ref, rows, first[index], last[index])
        q = qb[rows, :]
        k = kb[rows, :]
        q_total = jnp.zeros((SPAN, 128), F32)
        k_total = jnp.zeros((SPAN, 128), F32)
        for pair in range(2):
            lanes = slice(128 * pair, 128 * (pair + 1))
            dn_pair = dnb[rows, lanes]
            v_total = jnp.zeros((SPAN, 128), F32)
            for side in range(2):
                head = 2 * pair + side
                feats = lane_mask(32 * head, 32 * head + 32, 128, BF16)
                q_head = q * feats
                k_head = k * feats
                lifted = lift[head, rows, :]
                dn_head = dnh[head, rows, :]
                scores = mm_nt(k, q_head).astype(BF16) * mask
                dscores = mm_nt(dn_head, lifted).astype(BF16) * mask
                dscores_t = mm_nt(lifted, dn_head).astype(BF16) * mask
                q_total = q_total + mm(dscores, k_head)
                k_total = k_total + mm(dscores_t, q_head)
                own = lane_mask(64 * side, 64 * side + 64, 128, BF16)
                v_total = v_total + mm(scores, dn_pair * own)
            dv[rows, lanes] += v_total
        dqf[rows, :] += q_total
        dkf[rows, :] += k_total
        return carry

    lax.fori_loop(0, count, one_span, 0)
    proj_low = proj_ref[0, :, 128:]
    proj_high = proj_ref[1]
    square = proj_ref[2]
    perm = perm_ref[...]
    for which, (w_in, phi_in, dphi) in enumerate(
        ((wq_ref, qf_ref, dqf), (wk_ref, kf_ref, dkf))
    ):
        for rows in range(0, LEN, 256):
            here = pl.ds(rows, 256)
            r = dphi[here, :] * phi_in[0, here, :]
            high, low = halves(r)
            both = jnp.concatenate([high, low], axis=1)
            spread = mm_nt(both, square)
            dw = mm_nt(both, proj_high) + mm_nt(high, proj_low)
            du = (dw - 2.0 * w_in[0, here, :] * spread) * HD ** (-0.25)
            c = du[:, :128]
            e = du[:, 128:]
            cosine = cos_ref[here, :]
            sine = sin_ref[here, :]
            turned = jnp.concatenate([c * cosine + e * sine, e * cosine - c * sine], axis=1)
            dqkv[here, WIDTH * which : WIDTH * (which + 1)] = mm_nt(
                turned.astype(BF16), perm
            ).astype(BF16)
    dqkv[:, 2 * WIDTH :] = dv[...].astype(BF16)
    bias_ref[0] = jnp.sum(dqkv[...].astype(F32), axis=0, keepdims=True)
    grad = mm(a1t_ref[...], dqkv[...]).astype(BF16)
    store_halves(grad, place[3], keep_ref.at[0], send_ref.at[0])
    w = w_ref[...].reshape(D, D)
    fresh = pl.program_id(0) == 0

    @pl.when(fresh)
    def _():
        da1_ref[...] = mm_nt(dqkv[...], w)

    @pl.when(jnp.logical_not(fresh))
    def _():
        da1_ref[...] += mm_nt(dqkv[...], w)


def store_halves(grad, core, keep_ref, send_ref):
    wide, rows = keep_ref.shape[0], D // keep_ref.shape[0]
    half = rows // 2
    parts = grad.reshape(wide, rows, D)
    for cols in range(3):
        block = parts[:, :, WIDTH * cols : WIDTH * (cols + 1)]
        here = pl.ds(half * cols, half)

        @pl.when(core == 0)
        def _():
            keep_ref[:, here, :] = block[:, :half]
            send_ref[:, here, :] = block[:, half:]

        @pl.when(core == 1)
        def _():
            keep_ref[:, here, :] = block[:, half:]
            send_ref[:, here, :] = block[:, :half]


def attend_back(
    lengths, place, wide, dmixed, saved, a1t, w_in, perm, proj, cosine, sine, onehot, ones
):
    mixed, rden, wq, wk, qf, kf, v = saved

    def by_group(shape):
        return pl.BlockSpec((1,) + shape, lambda g, *_: (g,) + (0,) * len(shape))

    rows_in = D // wide
    half = struct((GROUPS, wide, 3 * rows_in // 2, WIDTH), BF16)
    half_spec = group_spec(half.shape[1:])
    return pl.pallas_call(
        attend_back_kernel,
        grid_spec=pltpu.PrefetchScalarGridSpec(
            num_scalar_prefetch=2,
            grid=(GROUPS,),
            in_specs=[
                pl.BlockSpec((LEN, WIDTH), lambda g, *_: (0, g)),
                by_group((LEN, WIDTH)), by_group((LEN, WIDTH)), by_group((LEN, WIDTH)),
                by_group((LEN, WIDTH)), by_group((LEN, 128)), by_group((LEN, 128)),
                by_group((LEN, WIDTH)), once((D, LEN)),
                pl.BlockSpec((wide, rows_in, D), lambda g, *_: (0, g, 0)),
                once((WIDTH, WIDTH)), once((3, WIDTH, WIDTH)), once((LEN, 128)),
                once((LEN, 128)), once((LEN, 128)), once((WIDTH, 128)),
            ],
            out_specs=[
                half_spec, half_spec, group_spec((1, D)),
                whole_spec((LEN, D)),
            ],
            scratch_shapes=[
                pltpu.VMEM((LEN, 128), BF16), pltpu.VMEM((LEN, 128), BF16),
                pltpu.VMEM((LEN, WIDTH), BF16), pltpu.VMEM((4, LEN, WIDTH), BF16),
                pltpu.VMEM((4, LEN, WIDTH), BF16), pltpu.VMEM((LEN, 128), F32),
                pltpu.VMEM((LEN, 128), F32), pltpu.VMEM((LEN, WIDTH), F32),
                pltpu.VMEM((LEN, D), BF16),
                pltpu.SMEM((32,), jnp.int32), pltpu.SMEM((32,), jnp.int32),
                pltpu.SMEM((32,), jnp.int32),
            ],
        ),
        out_shape=[
            half, half, struct((GROUPS, 1, D), F32), struct((LEN, D), F32),
        ],
        compiler_params=pltpu.CompilerParams(
            dimension_semantics=("arbitrary",), vmem_limit_bytes=VMEM_LIMIT
        ),
        cost_estimate=cost(GROUPS * 12 * 10**9, GROUPS * 20 * 10**6),
        name="attend_back",
    )(
        lengths, place, dmixed, mixed, rden, wq, wk, qf, kf, v, a1t, w_in, perm, proj, cosine,
        sine, onehot, ones,
    )


def chunk_step(
    place, wide, bias_up, dy_ref, a2, a2t, dyt, up, down, act, dhidden, y_in, back_in, y, back,
    outs, dbias_ref,
):
    rows_up = D // wide
    rows_down = FFC // wide
    bias_total = jnp.zeros((1, FFC), F32)
    for rows in range(0, LEN, 256):
        here = pl.ds(rows, 256)
        hidden = mm(a2[here, :], up[...]) + bias_up
        below, density = normal_parts(hidden)
        act_now = (hidden * below).astype(BF16)
        act[here, :] = act_now
        dact = mm_nt(dy_ref[here, :], down[...])
        dhidden_now = (dact * (below + hidden * density)).astype(BF16)
        dhidden[here, :] = dhidden_now
        bias_total = bias_total + jnp.sum(dhidden_now.astype(F32), axis=0, keepdims=True)
        if y_in is None:
            y[here, :] = mm(act_now, down[...])
            back[here, :] = mm_nt(dhidden_now, up[...])
        else:
            y[here, :] = y_in[here, :] + mm(act_now, down[...])
            back[here, :] = back_in[here, :] + mm_nt(dhidden_now, up[...])
    dbias_ref[0] = bias_total
    grad_up = mm(a2t[...], dhidden[...]).astype(BF16).reshape(wide, rows_up, FFC)
    grad_down = mm(dyt[...], act[...]).astype(BF16)
    core = place[3]

    def store_up(ref):
        for cols in range(4):
            ref[:, rows_up * cols : rows_up * (cols + 1), :] = grad_up[
                :, :, WIDTH * cols : WIDTH * (cols + 1)
            ]

    def store_down(ref):
        if wide == 1:
            for cols in range(4):
                ref[0, D * cols : D * (cols + 1), :] = grad_down[
                    :, WIDTH * cols : WIDTH * (cols + 1)
                ]
            return
        for shard in range(wide):
            block = grad_down[:, rows_down * shard : rows_down * (shard + 1)]
            ref[shard, :, :128] = block[: D // 2]
            ref[shard, :, 128:] = block[D // 2 :]

    for when, keep_ref, send_ref in outs:

        @pl.when(when & (core == 0))
        def _():
            store_up(keep_ref)
            store_down(send_ref)

        @pl.when(when & (core == 1))
        def _():
            store_up(send_ref)
            store_down(keep_ref)


def load_up(flat, at, up, wide):
    rows = D // wide
    for cols in range(4):
        here = pl.ds(at + rows * cols, rows)
        up[:, WIDTH * cols : WIDTH * (cols + 1)] = flat[:, here, :].reshape(D, WIDTH)


def load_down(flat, at, down, wide):
    rows = FFC // wide
    for cols in range(3):
        here = pl.ds(at + rows * cols, rows)
        down[:, WIDTH * cols : WIDTH * (cols + 1)] = flat[:, here, :].reshape(FFC, WIDTH)


def middle_first_kernel(wide, count_in, place, *refs):
    pieces = refs[:count_in]
    (
        x_ref, attn_ref, dy_ref, rows_ref, bias_up_ref,
        x1_ref, a2_ref, a2t_ref, dyt_ref, y_ref, back_ref, out_ref, keep_ref, send_ref, dbias_ref,
        flat, up, down, act, dhidden, sems,
    ) = refs[count_in:]
    copies = flat_copies(place, pieces, flat, sems)
    for copy in copies:
        copy.start()
    for cols in range(0, D, 256):
        dyt_ref[cols : cols + 256, :] = transposed(dy_ref[:, cols : cols + 256])
    for copy in copies:
        copy.wait()
    half_out = D // wide // 2
    half_flat = flat.shape[1] // 2
    for cols in range(3):
        upper = flat[:, half_out * cols : half_out * (cols + 1), :]
        lower = flat[:, half_flat + half_out * cols : half_flat + half_out * (cols + 1), :]
        out_ref[:, WIDTH * cols : WIDTH * (cols + 1)] = jnp.concatenate(
            [upper, lower], axis=1
        ).reshape(D, WIDTH)
    for rows in range(0, LEN, 256):
        here = pl.ds(rows, 256)
        x1 = x_ref[here, :].astype(F32) + (mm(attn_ref[here, :], out_ref[...]) + rows_ref[7:8, :])
        x1_ref[here, :] = x1
        centre = x1 - jnp.mean(x1, axis=-1, keepdims=True)
        spread = jnp.mean(centre * centre, axis=-1, keepdims=True)
        a2_ref[here, :] = (
            centre * lax.rsqrt(spread + norm_eps) * rows_ref[2:3, :] + rows_ref[3:4, :]
        ).astype(BF16)
    for cols in range(0, D, 256):
        a2t_ref[cols : cols + 256, :] = transposed(a2_ref[:, cols : cols + 256])
    load_up(flat, 3 * half_out, up, wide)
    load_down(flat, half_flat + 3 * half_out, down, wide)
    chunk_step(
        place, wide, bias_up_ref[0], dy_ref, a2_ref, a2t_ref, dyt_ref, up, down, act, dhidden,
        None, None, y_ref, back_ref, [(place[3] >= 0, keep_ref, send_ref)], dbias_ref,
    )


def middle_rest_kernel(wide, count_in, place, *refs):
    pieces = refs[:count_in]
    (
        dy_ref, a2_ref, a2t_ref, dyt_ref, bias_up_ref, attn_ref, out_ref, rows_ref,
        y_in, back_in, x1_in,
        block_ref, dx1_ref, dmixed_ref, okeep_ref, osend_ref, vec_ref,
        keep1_ref, send1_ref, keep2_ref, send2_ref, dbias_ref,
        up, down, act, dhidden, back, dbranch, sems,
    ) = refs[count_in:]
    step = pl.program_id(0)
    x1_copy = pltpu.make_async_copy(x1_in, dx1_ref, sems.at[0])

    @pl.when(step == 0)
    def _():
        x1_copy.start()

    if count_in == 4:
        mine = place[3] == step
        for own in range(2):
            for y_at in range(2):
                near, far = pieces[2 * own], pieces[2 * own + 1]
                which = mine if own == 0 else jnp.logical_not(mine)

                @pl.when(which & (place[2] == y_at))
                def _():
                    load_up(near if y_at == 0 else far, 0, up, wide)
                    load_down(far if y_at == 0 else near, 0, down, wide)

    else:
        load_up(pieces[0].at[0], 0, up, wide)
        load_down(pieces[1].at[0], 0, down, wide)

    def run(y_now, back_now):
        chunk_step(
            place, wide, bias_up_ref[0], dy_ref, a2_ref, a2t_ref, dyt_ref, up, down, act, dhidden,
            y_now, back_now, block_ref, back,
            [(step == 0, keep1_ref, send1_ref), (step == 1, keep2_ref, send2_ref)], dbias_ref,
        )

    @pl.when(step == 0)
    def _():
        block_ref[...] = y_in[...]
        back[...] = back_in[...]

    run(block_ref, back)

    @pl.when(step == 1)
    def _():
        x1_copy.wait()
        zero = jnp.zeros((1, D), F32)
        dgain, dshift, dbias_out, dbias_down = zero, zero, zero, zero
        for rows in range(0, LEN, 256):
            here = pl.ds(rows, 256)
            x1 = dx1_ref[here, :]
            block_ref[here, :] = x1 + (block_ref[here, :] + rows_ref[8:9, :])
            dn = back[here, :]
            dy = dy_ref[here, :].astype(F32)
            centre = x1 - jnp.mean(x1, axis=-1, keepdims=True)
            spread = jnp.mean(centre * centre, axis=-1, keepdims=True)
            scale = lax.rsqrt(spread + norm_eps)
            zh = centre * scale
            dgain = dgain + jnp.sum(dn * zh, axis=0, keepdims=True)
            dshift = dshift + jnp.sum(dn, axis=0, keepdims=True)
            e = dn * rows_ref[2:3, :]
            dz = (
                e
                - jnp.mean(e, axis=-1, keepdims=True)
                - zh * jnp.mean(e * zh, axis=-1, keepdims=True)
            ) * scale
            dx1 = dy + dz
            dx1_ref[here, :] = dx1
            low = dx1.astype(BF16)
            dbranch[here, :] = low
            dbias_out = dbias_out + jnp.sum(low.astype(F32), axis=0, keepdims=True)
            dbias_down = dbias_down + jnp.sum(dy, axis=0, keepdims=True)
            dmixed_ref[here, :] = mm_nt(low, out_ref[...])
        for cols in range(0, D, 256):
            up[cols : cols + 256, :] = transposed(attn_ref[:, cols : cols + 256])
        store_halves(mm(up[...], dbranch[...]).astype(BF16), place[3], okeep_ref, osend_ref)
        vec_ref[0:1, :] = dgain
        vec_ref[1:2, :] = dshift
        vec_ref[2:3, :] = dbias_out
        vec_ref[3:4, :] = dbias_down


def once(shape):
    return whole_spec(shape, pipeline_mode=pl.Buffered(1))


def struct(shape, dtype):
    return jax.ShapeDtypeStruct(shape, dtype)


def weight_scratch():
    return [
        pltpu.VMEM((D, FFC), BF16), pltpu.VMEM((FFC, D), BF16), pltpu.VMEM((LEN, FFC), BF16),
        pltpu.VMEM((LEN, FFC), BF16),
    ]


def middle_first(place, wide, pieces, tokens, attn, cotangent, vectors, bias_up):
    rows_flat = 3 * D // wide + 2 * FFC * D // (WIDTH * wide)
    half = (wide, FFC * D // (WIDTH * wide), WIDTH)
    outs = [
        struct((LEN, D), F32), struct((LEN, D), BF16), struct((D, LEN), BF16),
        struct((D, LEN), BF16), struct((LEN, D), F32), struct((LEN, D), F32),
        struct((D, D), BF16), struct(half, BF16), struct(half, BF16), struct((1, 1, FFC), F32),
    ]
    return pl.pallas_call(
        functools.partial(middle_first_kernel, wide, len(pieces)),
        grid_spec=pltpu.PrefetchScalarGridSpec(
            num_scalar_prefetch=1,
            grid=(1,),
            in_specs=[any_spec()] * len(pieces)
            + [
                once((LEN, D)), once((LEN, D)), once((LEN, D)), once((13, D)),
                pl.BlockSpec((1, 1, FFC), lambda *_: (0, 0, 0)),
            ],
            out_specs=[once(out.shape) for out in outs],
            scratch_shapes=[pltpu.VMEM((wide, rows_flat, WIDTH), BF16)]
            + weight_scratch()
            + [pltpu.SemaphoreType.DMA((16,))],
        ),
        out_shape=outs,
        compiler_params=pltpu.CompilerParams(
            dimension_semantics=("arbitrary",), vmem_limit_bytes=VMEM_LIMIT
        ),
        cost_estimate=cost(14 * 10**9, 30 * 10**6),
        name="middle_first",
    )(place, *pieces, tokens, attn, cotangent, vectors, bias_up)


def middle_rest(place, wide, pieces, cotangent, state, bias_up, attn, w_out, vectors, sums):
    a2, a2t, dyt = state
    half = (wide, FFC * D // (WIDTH * wide), WIDTH)
    out_half = (wide, 3 * D // (2 * wide), WIDTH)
    outs = [
        struct((LEN, D), F32), struct((LEN, D), F32), struct((LEN, D), F32),
        struct(out_half, BF16), struct(out_half, BF16), struct((8, D), F32),
        struct(half, BF16), struct(half, BF16), struct(half, BF16), struct(half, BF16),
        struct((2, 1, FFC), F32),
    ]
    out_specs = [once(out.shape) for out in outs[:-1]] + [group_spec((1, FFC))]
    if wide == 1:
        piece_specs = [group_spec(piece.shape[1:]) for piece in pieces]
    else:
        piece_specs = [once(piece.shape) for piece in pieces]
    return pl.pallas_call(
        functools.partial(middle_rest_kernel, wide, len(pieces)),
        grid_spec=pltpu.PrefetchScalarGridSpec(
            num_scalar_prefetch=1,
            grid=(2,),
            in_specs=piece_specs
            + [
                once((LEN, D)), once((LEN, D)), once((D, LEN)), once((D, LEN)),
                pl.BlockSpec((1, 1, FFC), lambda j, *_: (j + 1, 0, 0)),
                once((LEN, D)), once((D, D)), once((13, D)),
                once((LEN, D)), once((LEN, D)), any_spec(),
            ],
            out_specs=out_specs,
            scratch_shapes=weight_scratch()
            + [
                pltpu.VMEM((LEN, D), F32), pltpu.VMEM((LEN, D), BF16),
                pltpu.SemaphoreType.DMA((1,)),
            ],
        ),
        out_shape=outs,
        compiler_params=pltpu.CompilerParams(
            dimension_semantics=("arbitrary",), vmem_limit_bytes=VMEM_LIMIT
        ),
        cost_estimate=cost(28 * 10**9, 40 * 10**6),
        name="middle_rest",
    )(place, *pieces, cotangent, a2, a2t, dyt, bias_up, attn, w_out, vectors, *sums)


def input_kernel(
    wide, x_ref, dx1_ref, da1_ref, rows_ref, middle_ref, bias_in_ref, bias_first_ref, bias_rest_ref,
    out_ref, vec_ref,
):
    gain = rows_ref[0:1, :]
    x = x_ref[...].astype(F32)
    dn = da1_ref[...]
    centre = x - jnp.mean(x, axis=-1, keepdims=True)
    spread = jnp.mean(centre * centre, axis=-1, keepdims=True)
    scale = lax.rsqrt(spread + norm_eps)
    zh = centre * scale
    e = dn * gain
    dz = (
        e - jnp.mean(e, axis=-1, keepdims=True) - zh * jnp.mean(e * zh, axis=-1, keepdims=True)
    ) * scale
    out_ref[...] = dx1_ref[...] + dz

    @pl.when(pl.program_id(0) == 0)
    def _():
        vec_ref[...] = jnp.zeros_like(vec_ref)
        vec_ref[2:4, :] = middle_ref[0:2, :]
        vec_ref[7:9, :] = middle_ref[2:4, :]
        for group in range(GROUPS):
            lanes = slice(WIDTH * group, WIDTH * (group + 1))
            for which in range(3):
                vec_ref[4 + which : 5 + which, lanes] = bias_in_ref[
                    group, :, WIDTH * which : WIDTH * (which + 1)
                ]
        for chunk in range(CHUNKS):
            for part in range(8):
                value = (
                    bias_first_ref[0] if chunk == 0 else bias_rest_ref[chunk - 1]
                )[:, 128 * part : 128 * (part + 1)]
                start = FFC * chunk + 128 * part if wide == 1 else 384 * part + 128 * chunk
                row, lane = 9 + start // D, start % D
                vec_ref[row : row + 1, lane : lane + 128] = value

    vec_ref[0:1, :] += jnp.sum(dn * zh, axis=0, keepdims=True)
    vec_ref[1:2, :] += jnp.sum(dn, axis=0, keepdims=True)


def input_side(wide, tokens, dx1, da1, vectors, middle_vec, bias_in, bias_first, bias_rest):
    block = pl.BlockSpec((256, D), lambda i: (i, 0))
    return pl.pallas_call(
        functools.partial(input_kernel, wide),
        grid=(LEN // 256,),
        in_specs=[
            block, block, block, whole_spec((13, D)), whole_spec((8, D)),
            whole_spec((GROUPS, 1, D)), whole_spec((1, 1, FFC)), whole_spec((2, 1, FFC)),
        ],
        out_specs=[block, whole_spec((16, D))],
        out_shape=[struct((LEN, D), F32), struct((16, D), F32)],
        compiler_params=pltpu.CompilerParams(dimension_semantics=("arbitrary",)),
        cost_estimate=cost(10**6, 12 * 10**6),
        name="input_side",
    )(tokens, dx1, da1, vectors, middle_vec, bias_in, bias_first, bias_rest)


def tables(lengths, projection):
    ends = jnp.cumsum(lengths[0])
    starts = ends - lengths[0]
    place = jnp.arange(LEN, dtype=jnp.int32)
    member = (place[:, None] >= starts[None, :]) & (place[:, None] < ends[None, :])
    offset = jnp.sum(jnp.where(member, starts[None, :], 0), axis=1)
    position = (place - offset).astype(F32)
    freq = 10000.0 ** (-jnp.arange(32, dtype=F32) / 32)
    angles = position[:, None] * jnp.tile(freq, 4)[None, :]
    onehot = jnp.pad(member.astype(BF16), ((0, 0), (0, 128 - member.shape[1])))
    eye = jnp.asarray(np.eye(4, dtype=np.float32))
    lifted = jnp.einsum("hif,ab->haibf", projection.reshape(2, 32, FEAT), eye)
    lifted = lifted.reshape(WIDTH, 128)
    rounded = lax.reduce_precision(lifted, 8, 7)
    high, low = rounded.astype(BF16), (lifted - rounded).astype(BF16)
    square = np.zeros((2, 4, 32, 4, 32), np.float32)
    for head in range(4):
        square[:, head, :, head, :] = 0.5
    square = jnp.asarray(square.reshape(WIDTH, 128), BF16)
    proj = jnp.stack(
        [
            jnp.concatenate([high, low], axis=1),
            jnp.concatenate([high, high], axis=1),
            jnp.concatenate([square, square], axis=1),
        ]
    )
    return jnp.cos(angles), jnp.sin(angles), onehot, proj


def wide_perm(shift_z, flip_x):
    pairs = []
    for z in range(4):
        for x in range(2):
            target_x = 1 - x if flip_x else x
            pairs.append((2 * z + x, 2 * ((z + shift_z) % 4) + target_x))
    return pairs


def narrow_perm(flip_y, flip_core):
    pairs = []
    for y in range(2):
        for core in range(2):
            pairs.append(
                (2 * y + core, 2 * (1 - y if flip_y else y) + (1 - core if flip_core else core))
            )
    return pairs


def over_z(values, shift):
    return lax.ppermute(values, "wide", wide_perm(shift, False))


def over_x(values):
    return lax.ppermute(values, "wide", wide_perm(0, True))


def over_far(values, bit):
    return lax.ppermute(values, "wide", [(w, w ^ bit) for w in range(8)])


def over_y(values):
    return lax.ppermute(values, "narrow", narrow_perm(True, False))


def over_core(values):
    return lax.ppermute(values, "narrow", narrow_perm(False, True))


def tie(*values):
    return lax.optimization_barrier(values)


def special():
    return lax.axis_size("wide") == 8 and lax.axis_size("narrow") == 4


def sum_wide(values):
    if not special():
        return lax.psum(values, "wide")
    for perm in (wide_perm(0, True), [(w, w ^ 2) for w in range(8)], [(w, w ^ 4) for w in range(8)]):
        values = values + lax.ppermute(values, "wide", perm)
    return values


def sum_narrow(values):
    if not special():
        return lax.psum(values, "narrow")
    pair = values + over_core(values)
    return pair + over_y(pair)


def along_z(mine):
    return jnp.stack([mine] + [over_z(mine, shift) for shift in (1, 2, 3)])


def small_call(kernel, name, place, operands, outs):
    return pl.pallas_call(
        kernel,
        grid_spec=pltpu.PrefetchScalarGridSpec(
            num_scalar_prefetch=1,
            grid=(1,),
            in_specs=[once(value.shape) for value in operands],
            out_specs=[once(out.shape) for out in outs],
        ),
        out_shape=outs,
        compiler_params=pltpu.CompilerParams(
            dimension_semantics=("arbitrary",), vmem_limit_bytes=VMEM_LIMIT
        ),
        cost_estimate=cost(10**6, sum(4 * math.prod(v.shape) for v in operands + outs)),
        name=name,
    )(place, *operands)


def pick_kernel(
    place, in_ref, out_ref, up_ref, down_ref, near_ref, last_ref, first_ref, rest_ref
):
    core = place[3]
    here = pl.ds(pl.multiple_of(48 * core, 16), 48)
    for group in range(GROUPS):
        ref, index = (near_ref, group) if group < 2 else (last_ref, 0)
        for which in range(3):
            ref[index, :, WIDTH * which : WIDTH * (which + 1)] = in_ref[
                which, here, WIDTH * group : WIDTH * (group + 1)
            ].astype(BF16)
    for cols in range(3):
        first_ref[48 * cols : 48 * (cols + 1), :] = out_ref[
            here, WIDTH * cols : WIDTH * (cols + 1)
        ].astype(BF16)

    def put_up(ref, at, chunk):
        for cols in range(4):
            rows = slice(at + 96 * cols, at + 96 * (cols + 1))
            for side in range(2):
                start = 384 * (2 * cols + side) + 128 * chunk
                ref[rows, 128 * side : 128 * (side + 1)] = up_ref[:, start : start + 128].astype(
                    BF16
                )

    def put_down(ref, at, chunk):
        for cols in range(3):
            ref[at + 128 * cols : at + 128 * (cols + 1), :] = down_ref[
                128 * chunk : 128 * (chunk + 1), WIDTH * cols : WIDTH * (cols + 1)
            ].astype(BF16)

    for side in range(2):

        @pl.when(core == side)
        def _():
            if side == 0:
                put_up(first_ref, 144, 0)
            else:
                put_down(first_ref, 144, 0)

        @pl.when((core == side) & (place[2] == 0))
        def _():
            put_up(rest_ref, 0, 1 + side)

        @pl.when((core == side) & (place[2] == 1))
        def _():
            put_down(rest_ref, 0, 1 + side)


def core_sum(own, got):
    return (own.astype(F32) + got.astype(F32)).astype(BF16)


def first_sum_kernel(place, *refs):
    count = (len(refs) - 2) // 2
    send_ref, keep_ref = refs[-2:]
    x = place[1]
    at = 0
    for index in range(count):
        own, got = refs[2 * index], refs[2 * index + 1]
        for part in range(own.shape[0]):
            rows = own.shape[3]
            here = pl.ds(at, rows)
            keep_ref[0, here, :] = (
                own[part, 0, x].astype(F32) + got[part, 0, x].astype(F32)
            ).astype(BF16)
            send_ref[0, here, :] = (
                own[part, 0, 1 - x].astype(F32) + got[part, 0, 1 - x].astype(F32)
            ).astype(BF16)
            at += rows


def first_sum(place, pairs):
    total = 0
    operands, specs = [], []
    for own, got in pairs:
        parts, rows = own.shape[0], own.shape[2]
        total += parts * rows
        for value in (own, got):
            operands.append(value.reshape(parts, 4, 2, rows, WIDTH))
            specs.append(
                pl.BlockSpec((parts, 1, 2, rows, WIDTH), lambda i, *_: (0, i, 0, 0, 0))
            )
    block = pl.BlockSpec((1, total, WIDTH), lambda i, *_: (i, 0, 0))
    return pl.pallas_call(
        first_sum_kernel,
        grid_spec=pltpu.PrefetchScalarGridSpec(
            num_scalar_prefetch=1, grid=(4,), in_specs=specs, out_specs=[block, block]
        ),
        out_shape=[struct((4, total, WIDTH), BF16)] * 2,
        compiler_params=pltpu.CompilerParams(
            dimension_semantics=("arbitrary",), vmem_limit_bytes=VMEM_LIMIT
        ),
        cost_estimate=cost(10**6, 6 * 8 * total * WIDTH),
        name="first_sum",
    )(place, *operands)


def second_sum_kernel(place, own_ref, got_ref, *outs):
    z = place[0]
    for shift, out in enumerate(outs):
        there = lax.rem(z + shift, 4)
        out[...] = (own_ref[there].astype(F32) + got_ref[there].astype(F32)).astype(BF16)


def second_sum(place, own, got):
    outs = [struct(own.shape[1:], BF16)] * 4
    return small_call(second_sum_kernel, "second_sum", place, [own, got], outs)


def z_sum_kernel(place, *refs):
    total = refs[0][...].astype(F32)
    for ref in refs[1:4]:
        total = total + ref[...].astype(F32)
    at = 0
    for ref in refs[4:-1]:
        refs[-1][at : at + ref.shape[0], :] = ref[...]
        at += ref.shape[0]
    refs[-1][at:, :] = total.astype(BF16)


def z_sum(place, parts, ahead=(), got=None):
    if got is None:
        got = [over_z(parts[shift], shift) for shift in (1, 2, 3)]
    rows = parts[0].shape[0] + sum(value.shape[0] for value in ahead)
    return small_call(
        z_sum_kernel, "z_sum", place, [parts[0]] + got + list(ahead),
        [struct((rows, WIDTH), BF16)],
    )[0]


def to_row(column):
    size = column.shape[0]
    eye = lax.broadcasted_iota(jnp.int32, (size, size), 0) == lax.broadcasted_iota(
        jnp.int32, (size, size), 1
    )
    return jnp.sum(jnp.where(eye, column, 0.0), axis=0, keepdims=True)


def to_column(row):
    size = row.shape[1]
    eye = lax.broadcasted_iota(jnp.int32, (size, size), 0) == lax.broadcasted_iota(
        jnp.int32, (size, size), 1
    )
    return jnp.sum(jnp.where(eye, row, 0.0), axis=1, keepdims=True)


DECAY = 1.0 - STEP ** (-0.8)


def lane_values(values):
    lane = lax.broadcasted_iota(jnp.int32, (1, D), 1)
    row = jnp.zeros((1, D), F32)
    for index, value in enumerate(values):
        row = jnp.where(lane == index, value, row)
    return row


def moments(grad, rows_old):
    plain = grad * grad
    squares = plain + square_eps
    mean = jnp.sum(squares, axis=1, keepdims=True) * (1.0 / grad.shape[1])
    rows_new = DECAY * rows_old + (1.0 - DECAY) * to_row(mean)
    total = jnp.sum(rows_new, axis=1, keepdims=True)
    divided = jnp.sum(plain * to_column(1.0 / rows_new), axis=0, keepdims=True)
    return rows_new, total, jnp.sum(squares, axis=0, keepdims=True), divided


def ffn_moments_kernel(
    place, own, got, up_rows, down_rows, out_rows,
    up_grad, down_grad, out_grad, up_rows_new, down_rows_new, out_rows_new, sums,
):
    core = place[3]

    def collect(low, high):
        for chunk in range(CHUNKS):
            at = 384 * chunk
            for cols in range(4):
                for side in range(2):
                    start = 384 * (2 * cols + side) + 128 * chunk
                    up_grad[:, start : start + 128] = low[
                        at + 96 * cols : at + 96 * (cols + 1), 128 * side : 128 * (side + 1)
                    ]
            for side in range(2):
                down_grad[128 * chunk : 128 * (chunk + 1), 384 * side : 384 * (side + 1)] = (
                    jnp.transpose(high[at : at + 384, 128 * side : 128 * (side + 1)])
                )
        for cols in range(3):
            lanes = slice(WIDTH * cols, WIDTH * (cols + 1))
            at = 1152 + 48 * cols
            out_grad[:48, lanes] = low[at : at + 48, :]
            out_grad[48:, lanes] = high[at : at + 48, :]

    @pl.when(core == 0)
    def _():
        collect(own, got)

    @pl.when(core == 1)
    def _():
        collect(got, own)

    up_new, up_total, up_sums, up_divided = moments(up_grad[...], up_rows[...])
    down_new, down_total, down_sums, down_divided = moments(down_grad[...], down_rows[...])
    out_new, out_total, out_sums, out_divided = moments(out_grad[...], out_rows[...])
    up_rows_new[...] = up_new
    down_rows_new[...] = down_new
    out_rows_new[...] = out_new
    for part in range(4):
        lanes = slice(D * part, D * (part + 1))
        sums[part : part + 1, :] = up_sums[:, lanes]
        sums[4 + part : 5 + part, :] = up_divided[:, lanes]
    sums[8:9, :] = down_sums
    sums[9:10, :] = down_divided
    sums[10:11, :] = out_sums
    sums[11:12, :] = out_divided
    sums[12:13, :] = lane_values([up_total, down_total, out_total])
    sums[13:16, :] = jnp.zeros((3, D), F32)


def in_moments_kernel(
    place, own, got, rows_old, vector, ffn_sums, grad, rows_new, sums,
):
    core = place[3]

    def collect(low, high):
        for group in range(GROUPS):
            for which in range(3):
                at = 144 * group + 48 * which
                lanes = slice(WIDTH * group, WIDTH * (group + 1))
                grad[which, :48, lanes] = low[at : at + 48, :]
                grad[which, 48:, lanes] = high[at : at + 48, :]

    @pl.when(core == 0)
    def _():
        collect(own, got)

    @pl.when(core == 1)
    def _():
        collect(got, own)

    totals = []
    for which in range(3):
        new, total, columns, divided = moments(grad[which], rows_old[which : which + 1, :])
        rows_new[which : which + 1, :] = new
        sums[which : which + 1, :] = columns
        sums[3 + which : 4 + which, :] = divided
        totals.append(total)
    sums[6:7, :] = lane_values(totals)
    sums[7:8, :] = jnp.zeros((1, D), F32)
    sums[8:24, :] = vector[...]
    sums[24:40, :] = ffn_sums[...]


def matrix_step(weight, grad, rows, cols, total, col_sums, divided, rows_full, rate):
    cols_new = DECAY * cols + (1.0 - DECAY) * col_sums * (1.0 / rows_full)
    mean = total * (1.0 / rows_full)
    square_sum = mean * jnp.sum(divided / cols_new, axis=1, keepdims=True)
    rms = jnp.sqrt(square_sum * (1.0 / (rows_full * grad.shape[1])))
    factor = to_column(lax.rsqrt(rows / mean)) * (rate / jnp.maximum(1.0, rms / clip_level))
    return cols_new, weight - grad * factor * lax.rsqrt(cols_new)


def finish_kernel(
    place, inward, up, down, out, in_grad, up_grad, down_grad, out_grad, in_rows, up_rows,
    down_rows, out_rows, in_cols, up_cols, down_cols, out_cols, sums, vectors, vector_state,
    in_cols_new, up_cols_new, down_cols_new, out_cols_new, in_next, up_next, down_next, out_next,
    vector_grad, state_next, vectors_next,
):
    base_rate = 0.3 * D ** (-0.5)
    for which in range(3):
        here = slice(which, which + 1)
        in_cols_new[here, :], in_next[which] = matrix_step(
            inward[which], in_grad[which], in_rows[here, :], in_cols[here, :],
            sums[6:7, which : which + 1], sums[here, :], sums[3 + which : 4 + which, :], D,
            base_rate,
        )

    def wide_row(first):
        return jnp.concatenate([sums[first + i : first + i + 1, :] for i in range(4)], axis=1)

    up_cols_new[...], up_next[...] = matrix_step(
        up[...], up_grad[...], up_rows[...], up_cols[...], sums[36:37, 0:1], wide_row(24),
        wide_row(28), D, base_rate,
    )
    down_cols_new[...], down_next[...] = matrix_step(
        down[...], down_grad[...], down_rows[...], down_cols[...], sums[36:37, 1:2],
        sums[32:33, :], sums[33:34, :], FF, 0.3 * FF ** (-0.5),
    )
    out_cols_new[...], out_next[...] = matrix_step(
        out[...], out_grad[...], out_rows[...], out_cols[...], sums[36:37, 2:3],
        sums[34:35, :], sums[35:36, :], D, 1.2 * D ** (-0.5),
    )
    g = sums[8:21, :]
    vector_grad[...] = g
    state = DECAY * vector_state[...] + (1.0 - DECAY) * (g * g + square_eps)
    state_next[...] = state
    update = g * lax.rsqrt(state)
    total = jnp.sum(jnp.sum(update * update, axis=0, keepdims=True), axis=1, keepdims=True)
    rms = jnp.sqrt(total * (1.0 / (13 * D)))
    vectors_next[...] = vectors[...] - update * (0.25 / jnp.maximum(1.0, rms / clip_level))


def shards(
    tokens, cotangent, lengths, projection, inward, outward, expand, shrink, vectors,
    inward_rows, inward_columns, outward_rows, outward_columns, expand_rows, expand_columns,
    shrink_rows, shrink_columns, vector_state,
):
    full = special()
    rows = outward.shape[0]
    wide = 8 if full else 1
    wide_at = lax.axis_index("wide").astype(jnp.int32)
    narrow_at = lax.axis_index("narrow").astype(jnp.int32)
    core = narrow_at % 2 if full else jnp.int32(0)
    place = jnp.stack([wide_at // 2, wide_at % 2, narrow_at // 2, core])
    per = FFC // wide
    if full:
        *own_in, own_first, own_rest = small_call(
            pick_kernel, "pick", place, [inward, outward, expand, shrink],
            [
                struct((2, 48, D), BF16), struct((1, 48, D), BF16), struct((528, WIDTH), BF16),
                struct((384, WIDTH), BF16),
            ],
        )
        in_z = [along_z(value) for value in own_in]
        rest_own = lax.all_gather(own_rest, "wide", axis=0)
        *in_z, own_first = tie(*in_z, own_first)
        first_z = along_z(own_first)
        in_x = [over_x(value) for value in in_z]
        pieces_in = []
        for near, far in zip(in_z, in_x):
            pieces_in += [near, far, over_core(near), over_core(far)]
        *pieces_in, first_z, rest_own = tie(*pieces_in, first_z, rest_own)
        first_x = over_x(first_z)
        rest_y = over_y(rest_own)
    else:
        in_low = lax.all_gather(inward.astype(BF16), "wide", axis=1, tiled=True)
        out_low = lax.all_gather(outward.astype(BF16), "wide", axis=0, tiled=True)
        up_low = lax.all_gather(expand.astype(BF16), "wide", axis=0, tiled=True)
        down_low = lax.all_gather(shrink.astype(BF16), "wide", axis=0, tiled=True)
        units = jnp.transpose(in_low.reshape(3, D, GROUPS, WIDTH), (2, 1, 0, 3))
        pieces_in = [units.reshape(1, 3 * D, D)]

        def blocks(matrix):
            count = matrix.shape[1] // WIDTH
            return jnp.transpose(matrix.reshape(-1, count, WIDTH), (1, 0, 2)).reshape(-1, WIDTH)

        ups = [blocks(up_low[:, FFC * j : FFC * (j + 1)]) for j in range(CHUNKS)]
        downs = [blocks(down_low[FFC * j : FFC * (j + 1)]) for j in range(CHUNKS)]
        half = D // 2
        pieces_first = [
            jnp.concatenate([blocks(out_low[:half]), ups[0], blocks(out_low[half:]), downs[0]])[
                None
            ]
        ]
        pieces_rest = [jnp.stack(ups[1:])[:, None], jnp.stack(downs[1:])[:, None]]
    cosine, sine, onehot, proj = tables(lengths, projection)
    perm = jnp.asarray(head_perm(), BF16)
    block_ones = np.kron(np.eye(2, dtype=np.float32), np.ones((64, 64), np.float32))
    ones = jnp.asarray(np.concatenate([block_ones, block_ones]), BF16)
    split = vectors[4:6].reshape(2, GROUPS, 4, 2, 32)
    bias_qk = jnp.transpose(split, (0, 1, 3, 2, 4)).reshape(2, GROUPS, WIDTH)
    bias = jnp.concatenate([bias_qk, vectors[6].reshape(1, GROUPS, WIDTH)])
    bias = jnp.transpose(bias, (1, 0, 2))
    bias_up = vectors[9:].reshape(wide, CHUNKS, per)
    bias_up = jnp.transpose(bias_up, (1, 0, 2)).reshape(CHUNKS, 1, FFC)
    attn, mixed, a1t, w_in, wq, wk, qf, kf, v, rden = attend(
        lengths, place, pieces_in, wide, tokens, vectors[:2], bias, perm, proj, cosine, sine,
        onehot,
    )
    if full:
        attn, first_x, rest_own, rest_y = tie(attn, first_x, rest_own, rest_y)
        pieces_first = [first_z, first_x, over_core(first_z), over_core(first_x)]
        pieces_rest = [rest_own, rest_y, over_core(rest_own), over_core(rest_y)]
    x1, a2, a2t, dyt, y, back, w_out, keep0, send0, dbias0 = middle_first(
        place, wide, pieces_first, tokens, attn, cotangent, vectors, bias_up
    )
    if full:
        send0, *pieces_rest = tie(send0, *pieces_rest)
        send_a, keep_a = first_sum(place, [(keep0[None], over_core(send0)[None])])
        y, send_a = tie(y, send_a)
        got_a = over_x(send_a)
    (
        block_out, dx1, dmixed, okeep, osend, middle_vec, keep1, send1, keep2, send2, dbias12,
    ) = middle_rest(
        place, wide, pieces_rest, cotangent, (a2, a2t, dyt), bias_up, attn, w_out, vectors,
        (y, back, x1),
    )
    if full:
        a_parts = second_sum(place, keep_a, got_a)
        send1, send2, osend, *a_parts = tie(send1, send2, osend, *a_parts)
        send_b, keep_b = first_sum(
            place,
            [
                (keep1[None], over_core(send1)[None]), (keep2[None], over_core(send2)[None]),
                (okeep[None], over_core(osend)[None]),
            ],
        )
        dmixed, send_b, keep_b, *a_parts = tie(dmixed, send_b, keep_b, *a_parts)
        got_b = over_x(send_b)
    saved = (mixed, rden, wq, wk, qf, kf, v)
    in_keep, in_send, in_bias, da1 = attend_back(
        lengths, place, wide, dmixed, saved, a1t, w_in, perm, proj, cosine, sine, onehot, ones
    )
    if full:
        a_mine = z_sum(place, a_parts)
        a_mine, in_send, keep_b, got_b, da1 = tie(a_mine, in_send, keep_b, got_b, da1)
        b_parts = second_sum(place, keep_b, got_b)
        got_in = over_core(in_send)
        got_in, *b_parts = tie(got_in, *b_parts)
        send_c, keep_c = first_sum(place, [(in_keep, got_in)])
        da1, send_c = tie(da1, send_c)
        got_c = over_x(send_c)
    input_grad, vector_local = input_side(
        wide, tokens, dx1, da1, vectors, middle_vec, in_bias, dbias0, dbias12
    )
    if full:
        vector_part = sum_narrow(vector_local)

        def pair_sum(mine, got):
            half_sum = mine.astype(F32) + got.astype(F32)
            return half_sum, over_core(half_sum)

        got_c, input_grad, vector_part = tie(got_c, input_grad, vector_part)
        c_parts = second_sum(place, keep_c, got_c)
        b_parts[0], *c_parts = tie(b_parts[0], *c_parts)
        ffn_mine = z_sum(place, b_parts, [a_mine])
        ffn_mine, *c_parts = tie(ffn_mine, *c_parts)
        ffn_y = over_y(ffn_mine)
        c_got = [over_z(c_parts[shift], shift) for shift in (1, 2, 3)]
        ffn_y, *c_got = tie(ffn_y, *c_got)
        c_mine = z_sum(place, c_parts, (), c_got)
        c_mine, ffn_y = tie(c_mine, ffn_y)
        c_y = over_y(c_mine)
        ffn_own, ffn_got = pair_sum(ffn_mine, ffn_y)
        expand_grad, shrink_grad, outward_grad, up_rows, down_rows, out_rows, sums = small_call(
            ffn_moments_kernel, "ffn_moments", place,
            [
                ffn_own, ffn_got, expand_rows[None], shrink_rows[None], outward_rows[None],
            ],
            [
                struct(expand.shape, F32), struct(shrink.shape, F32), struct(outward.shape, F32),
                struct((1, 96), F32), struct((1, 384), F32), struct((1, 96), F32),
                struct((16, D), F32),
            ],
        )
        c_y, sums = tie(c_y, sums)
        c_own, c_got = pair_sum(c_mine, c_y)
        inward_grad, in_rows, sums = small_call(
            in_moments_kernel, "in_moments", place,
            [c_own, c_got, inward_rows, vector_part, sums],
            [struct(inward.shape, F32), struct((3, 96), F32), struct((40, D), F32)],
        )
        sums = sum_wide(sums)
        (
            in_cols, up_cols, down_cols, out_cols, inward_next, expand_next, shrink_next,
            outward_next, vector_grad, vector_state_next, vectors_next,
        ) = small_call(
            finish_kernel, "finish", place,
            [
                inward, expand, shrink, outward, inward_grad, expand_grad, shrink_grad,
                outward_grad, in_rows, up_rows, down_rows, out_rows, inward_columns,
                expand_columns[None], shrink_columns[None], outward_columns[None], sums, vectors,
                vector_state,
            ],
            [
                struct((3, D), F32), struct((1, FF), F32), struct((1, D), F32),
                struct((1, D), F32), struct(inward.shape, F32), struct(expand.shape, F32),
                struct(shrink.shape, F32), struct(outward.shape, F32), struct((13, D), F32),
                struct((13, D), F32), struct((13, D), F32),
            ],
        )
        return (
            block_out, input_grad, inward_grad, outward_grad, expand_grad, shrink_grad,
            vector_grad, in_rows, in_cols, out_rows[0], out_cols[0], up_rows[0], up_cols[0],
            down_rows[0], down_cols[0], vector_state_next, inward_next, outward_next,
            expand_next, shrink_next, vectors_next,
        )
    vector_part = sum_narrow(vector_local[:13])

    def reduced(values, axis):
        part = lax.psum_scatter(values, "wide", scatter_dimension=axis, tiled=True)
        return lax.psum(part.astype(F32), "narrow")

    keeps = [keep0, keep1, keep2]
    sends = [send0, send1, send2]
    up_grads = [
        jnp.transpose(keep.reshape(4, D, WIDTH), (1, 0, 2)).reshape(D, FFC) for keep in keeps
    ]
    down_grads = [
        jnp.transpose(send.reshape(4, D, WIDTH), (0, 2, 1)).reshape(FFC, D) for send in sends
    ]
    expand_grad = reduced(jnp.concatenate(up_grads, axis=1), 0)
    shrink_grad = reduced(jnp.concatenate(down_grads, axis=0), 0)

    def rebuilt(keep, send):
        return jnp.concatenate(
            [keep.reshape(-1, 3, D // 2, WIDTH), send.reshape(-1, 3, D // 2, WIDTH)], axis=2
        )

    outward_grad = reduced(jnp.transpose(rebuilt(okeep, osend)[0], (1, 0, 2)).reshape(D, D), 0)
    in_units = rebuilt(in_keep, in_send)
    inward_grad = reduced(jnp.transpose(in_units, (1, 2, 0, 3)).reshape(3, D, D), 1)
    decay = 1.0 - STEP ** (-0.8)
    wide_count = lax.axis_size("wide")
    grads_list = [inward_grad, outward_grad[None], expand_grad[None], shrink_grad[None]]
    rows_old = [inward_rows, outward_rows[None], expand_rows[None], shrink_rows[None]]
    columns_old = [
        inward_columns,
        outward_columns[None],
        expand_columns[None],
        shrink_columns[None],
    ]
    weights_old = [inward, outward[None], expand[None], shrink[None]]
    rates = [0.3 * D ** (-0.5), 1.2 * D ** (-0.5), 0.3 * D ** (-0.5), 0.3 * FF ** (-0.5)]
    bounds = [0, 3, 4, 5, 6]
    rows_next = []
    column_parts = []
    for member in range(4):
        squares = grads_list[member] * grads_list[member] + square_eps
        rows_next.append(decay * rows_old[member] + (1.0 - decay) * jnp.mean(squares, axis=-1))
        column_parts.append(jnp.sum(squares, axis=-2))
    row_totals = jnp.concatenate([jnp.sum(entry, axis=-1) for entry in rows_next])
    shapes = [part.shape for part in column_parts] + [row_totals.shape, vector_part.shape]
    flat = jnp.concatenate(
        [part.reshape(-1) for part in column_parts + [row_totals, vector_part]]
    )
    flat = jnp.pad(flat, (0, -flat.shape[0] % 1024)).reshape(-1, 128)
    flat = sum_wide(flat).reshape(-1)
    summed = []
    offset = 0
    for shape in shapes:
        size = 1
        for extent in shape:
            size *= extent
        summed.append(flat[offset : offset + size].reshape(shape))
        offset += size
    column_sums = list(summed[0:4])
    totals_sum = summed[4]
    vector_grad = summed[5]
    columns_next = []
    scaled_list = []
    row_means = []
    sizes_full = []
    for member in range(4):
        grad_now = grads_list[member]
        rows_full = grad_now.shape[-2] * wide_count
        sizes_full.append(rows_full * grad_now.shape[-1])
        columns_next.append(
            decay * columns_old[member] + (1.0 - decay) * column_sums[member] / rows_full
        )
        row_mean = totals_sum[bounds[member] : bounds[member + 1]] / rows_full
        row_means.append(row_mean)
        scaled_list.append(
            grad_now
            * lax.rsqrt(rows_next[member] / row_mean[:, None])[..., None]
            * lax.rsqrt(columns_next[member])[:, None, :]
        )
    partial_squares = jnp.concatenate(
        [jnp.sum(entry * entry, axis=(-2, -1)) for entry in scaled_list]
    )
    total_squares = sum_wide(jnp.pad(partial_squares, (0, 122)).reshape(1, 128))[0, :6]
    rms_list = [
        jnp.sqrt(total_squares[bounds[member] : bounds[member + 1]] / sizes_full[member])
        for member in range(4)
    ]
    weights_next = []
    for member in range(4):
        limiter = jnp.maximum(1.0, rms_list[member] / clip_level)
        weights_next.append(
            weights_old[member] - rates[member] * scaled_list[member] / limiter[:, None, None]
        )
    vector_state_next = decay * vector_state + (1.0 - decay) * (
        vector_grad * vector_grad + square_eps
    )
    vector_update = vector_grad * lax.rsqrt(vector_state_next)
    vector_rms = jnp.sqrt(jnp.mean(vector_update * vector_update))
    vectors_next = vectors - 0.25 * vector_update / jnp.maximum(1.0, vector_rms / clip_level)
    return (
        block_out,
        input_grad,
        inward_grad,
        outward_grad,
        expand_grad,
        shrink_grad,
        vector_grad,
        rows_next[0],
        columns_next[0],
        rows_next[1][0],
        columns_next[1][0],
        rows_next[2][0],
        columns_next[2][0],
        rows_next[3][0],
        columns_next[3][0],
        vector_state_next,
        weights_next[0],
        weights_next[1][0],
        weights_next[2][0],
        weights_next[3][0],
        vectors_next,
    )


def solution(mesh):
    placed = (
        P(("narrow", "wide"), None),
        P(("narrow", "wide"), None),
        P(("narrow", "wide"), None),
        P(),
        P(None, "wide", None),
        P("wide", None),
        P("wide", None),
        P("wide", None),
        P(),
        P(None, "wide"),
        P(),
        P("wide"),
        P(),
        P("wide"),
        P(),
        P("wide"),
        P(),
        P(),
    )
    return jax.shard_map(
        shards,
        mesh=mesh,
        in_specs=placed,
        out_specs=(
            P(("narrow", "wide"), None),
            P(("narrow", "wide"), None),
            P(None, "wide", None),
            P("wide", None),
            P("wide", None),
            P("wide", None),
            P(),
            P(None, "wide"),
            P(),
            P("wide"),
            P(),
            P("wide"),
            P(),
            P("wide"),
            P(),
            P(),
            P(None, "wide", None),
            P("wide", None),
            P("wide", None),
            P("wide", None),
            P(),
        ),
        check_vma=False,
    )
```

```python
import functools
import math

import jax
import jax.numpy as jnp
import numpy as np
from jax import lax
from jax.experimental import pallas as pl
from jax.experimental.pallas import tpu as pltpu
from jax.sharding import PartitionSpec as P

D = 768
HEADS = 12
HD = 64
FF = 3072
FEAT = 32
STEP = 10
LEN = 1024
SPAN = 256
CHUNKS = 3
GROUPS = 3
WIDTH = 256
FFC = FF // CHUNKS

norm_eps = 1e-05
square_eps = 1e-30
clip_level = 1.0

F32 = jnp.float32
BF16 = jnp.bfloat16
VMEM_LIMIT = 60 * 1024 * 1024


def mm(left, right):
    return lax.dot_general(left, right, (((1,), (0,)), ((), ())), preferred_element_type=F32)


def mm_nt(left, right):
    return lax.dot_general(left, right, (((1,), (1,)), ((), ())), preferred_element_type=F32)


def mm_tn(left, right):
    return lax.dot_general(left, right, (((0,), (0,)), ((), ())), preferred_element_type=F32)


def halves(values):
    high = values.astype(BF16)
    return high, (values - high.astype(F32)).astype(BF16)


TAIL = (
    0.1795078068971634,
    0.17978088557720184,
    0.14234966039657593,
    0.06379217654466629,
    0.0434231162071228,
    -0.261725515127182,
    0.20454804599285126,
    -0.05167665705084801,
)


def normal_parts(values):
    size = jnp.abs(values)
    t = 1.0 / (1.0 + 0.45 * size)
    poly = TAIL[-1]
    for coeff in TAIL[-2::-1]:
        poly = poly * t + coeff
    bell = jnp.exp(-0.5 * values * values)
    tail = poly * t * bell
    return jnp.where(values >= 0, 1.0 - tail, tail), bell * 0.3989422804014327


def transposed(values):
    row = lax.broadcasted_iota(jnp.int32, (256, 256), 0)
    col = lax.broadcasted_iota(jnp.int32, (256, 256), 1)
    eye = (row == col).astype(F32).astype(BF16)
    return mm_nt(eye, values).astype(BF16)


def head_perm():
    perm = np.zeros((WIDTH, WIDTH), np.float32)
    for head in range(4):
        for half in range(2):
            for i in range(32):
                perm[head * 64 + half * 32 + i, half * 128 + head * 32 + i] = 1.0
    return perm


def make_blocks(lengths, base, first, last):
    def step(s, carry):
        count, begin, begin_row, end = carry
        new_end = end + lengths[0, s]
        full = new_end - begin_row > SPAN

        @pl.when(full)
        def _():
            base[count] = begin_row
            first[count] = begin
            last[count] = s - 1

        row = jnp.minimum((end // 16) * 16, LEN - SPAN)
        return (
            jnp.where(full, count + 1, count),
            jnp.where(full, s, begin),
            jnp.where(full, row, begin_row),
            new_end,
        )

    segments = lengths.shape[1]
    zero = jnp.int32(0)
    count, begin, begin_row, _ = lax.fori_loop(0, segments, step, (zero, zero, zero, zero))
    base[count] = begin_row
    first[count] = begin
    last[count] = segments - 1
    return count + 1


def lane_mask(lo, hi, width, dtype):
    lane = lax.broadcasted_iota(jnp.int32, (1, width), 1)
    return ((lane >= lo) & (lane < hi)).astype(F32).astype(dtype)


def value_rows(v_pair, head):
    keep = lane_mask(64 * head, 64 * head + 64, 128, BF16)
    return jnp.concatenate([v_pair * keep, jnp.broadcast_to(keep, v_pair.shape)], axis=1)


def span_mask(onehot, rows, lo, hi):
    member = onehot[rows, :]
    lane = lax.broadcasted_iota(jnp.int32, (1, 128), 1)
    inside = ((lane >= lo) & (lane <= hi)).astype(F32).astype(BF16)
    return mm_nt(member * inside, member).astype(BF16)


def cost(flops, size):
    return pl.CostEstimate(flops=10**6, transcendentals=0, bytes_accessed=10**5)


def any_spec():
    return pl.BlockSpec(memory_space=pl.ANY)


def in_copies(place, pieces, dst, sems, unit):
    if len(pieces) == 1:
        rows = dst.shape[1] // 3
        here = pl.ds(unit * rows, rows)
        return [pltpu.make_async_copy(pieces[0].at[:, here], dst.at[:, here], sems.at[unit, 0])]
    z, x, core = place[0], place[1], place[3]
    part, index = (0, unit) if unit < 2 else (4, 0)
    copies = []
    for side in range(2):
        half = core if side == 0 else 1 - core
        for flip in range(2):
            column = x if flip == 0 else 1 - x
            for shift in range(4):
                row = lax.rem(z + 4 - shift, 4) * 2 + column
                start = pl.multiple_of(unit * 96 + half * 48, 16)
                copies.append(
                    pltpu.make_async_copy(
                        pieces[part + 2 * side + flip].at[shift, index],
                        dst.at[row, pl.ds(start, 48)],
                        sems.at[unit, len(copies)],
                    )
                )
    return copies


def flat_copies(place, pieces, dst, sems):
    if len(pieces) == 1:
        return [pltpu.make_async_copy(pieces[0], dst, sems.at[0])]
    z, x, core = place[0], place[1], place[3]
    span = dst.shape[1] // 2
    copies = []
    for side in range(2):
        half = core if side == 0 else 1 - core
        for flip in range(2):
            column = x if flip == 0 else 1 - x
            for shift in range(4):
                row = lax.rem(z + 4 - shift, 4) * 2 + column
                start = pl.multiple_of(half * span, 16)
                copies.append(
                    pltpu.make_async_copy(
                        pieces[2 * side + flip].at[shift],
                        dst.at[row, pl.ds(start, span)],
                        sems.at[len(copies)],
                    )
                )
    return copies


def attend_kernel(count_in, lengths, place, *refs):
    pieces = refs[:count_in]
    (
        x_ref, norm_ref, bias_ref, perm_ref, proj_ref, cos_ref, sin_ref, onehot_ref,
        attn_ref, mixed_ref, a1t_ref, w_ref, wq_ref, wk_ref, qf_ref, kf_ref, v_ref, rden_ref,
        a1, qb, kb, vb, parts, base, first, last, sems,
    ) = refs[count_in:]
    group = pl.program_id(0)

    @pl.when(group == 0)
    def _():
        for unit in range(GROUPS):
            for copy in in_copies(place, pieces, w_ref, sems, unit):
                copy.start()
        for rows in range(0, LEN, 256):
            here = pl.ds(rows, 256)
            x = x_ref[here, :].astype(F32)
            centre = x - jnp.mean(x, axis=-1, keepdims=True)
            spread = jnp.mean(centre * centre, axis=-1, keepdims=True)
            a1[here, :] = (
                centre * lax.rsqrt(spread + norm_eps) * norm_ref[0:1, :] + norm_ref[1:2, :]
            ).astype(BF16)
        for cols in range(0, D, 256):
            a1t_ref[cols : cols + 256, :] = transposed(a1[:, cols : cols + 256])

    for unit in range(GROUPS):

        @pl.when(group == unit)
        def _():
            for copy in in_copies(place, pieces, w_ref, sems, unit):
                copy.wait()

    count = make_blocks(lengths, base, first, last)
    shard = w_ref.shape[1] // 3
    here = pl.ds(pl.multiple_of(group * shard, 16), shard)
    w = w_ref[:, here, :].reshape(D, D)
    perm = perm_ref[...]
    bias = bias_ref[0]
    proj_both = proj_ref[0]
    proj_high = proj_ref[1, :, :128]
    square = proj_ref[2, :, :128]
    for which, (out_w, out_f, low_f) in enumerate(((wq_ref, qf_ref, qb), (wk_ref, kf_ref, kb))):
        weight = mm(w[:, WIDTH * which : WIDTH * (which + 1)], perm).astype(BF16)
        for rows in range(0, LEN, 256):
            here = pl.ds(rows, 256)
            u = (mm(a1[here, :], weight) + bias[which : which + 1, :]) * HD ** (-0.25)
            c = u[:, :128]
            e = u[:, 128:]
            cosine = cos_ref[here, :]
            sine = sin_ref[here, :]
            turned = jnp.concatenate([c * cosine - e * sine, e * cosine + c * sine], axis=1)
            out_w[0, here, :] = turned
            high, low = halves(turned)
            sq_high, sq_low = halves(turned * turned)
            both = mm(high, proj_both)
            logits = (
                both[:, :128] + both[:, 128:] + mm(low, proj_high)
                - (mm(sq_high, square) + mm(sq_low, square))
            )
            phi = jnp.exp(logits) * FEAT ** (-0.5)
            out_f[0, here, :] = phi
            low_f[here, :] = phi.astype(BF16)
    for rows in range(0, LEN, 256):
        here = pl.ds(rows, 256)
        v = mm(a1[here, :], w[:, 2 * WIDTH :]) + bias[2:3, :]
        v_ref[0, here, :] = v
        vb[here, :] = v.astype(BF16)
    parts[...] = jnp.zeros_like(parts)

    def one_span(index, carry):
        rows = pl.ds(pl.multiple_of(base[index], 16), SPAN)
        mask = span_mask(onehot_ref, rows, first[index], last[index])
        q = qb[rows, :]
        k = kb[rows, :]
        for pair in range(2):
            v_pair = vb[rows, 128 * pair : 128 * (pair + 1)]
            total = jnp.zeros((SPAN, WIDTH), F32)
            for side in range(2):
                head = 2 * pair + side
                scores = mm_nt(q * lane_mask(32 * head, 32 * head + 32, 128, BF16), k)
                total = total + mm(scores.astype(BF16) * mask, value_rows(v_pair, side))
            parts[pair, rows, :] += total
        return carry

    lax.fori_loop(0, count, one_span, 0)
    for pair in range(2):
        lanes = slice(128 * pair, 128 * (pair + 1))
        inverse = 1.0 / parts[pair, :, 128:]
        rden_ref[0, :, lanes] = inverse
        mixed = parts[pair, :, :128] * inverse
        mixed_ref[0, :, lanes] = mixed
        attn_ref[:, lanes] = mixed.astype(BF16)


def whole_spec(shape, **options):
    return pl.BlockSpec(shape, lambda *_: (0,) * len(shape), **options)


def group_spec(shape):
    return pl.BlockSpec((1,) + shape, lambda g, *_: (g,) + (0,) * len(shape))


def attend(lengths, place, pieces, wide, tokens, norm, bias, perm, proj, cosine, sine, onehot):
    def out(shape, dtype):
        return jax.ShapeDtypeStruct((GROUPS,) + shape, dtype)

    rows_in = 3 * D // wide
    return pl.pallas_call(
        functools.partial(attend_kernel, len(pieces)),
        grid_spec=pltpu.PrefetchScalarGridSpec(
            num_scalar_prefetch=2,
            grid=(GROUPS,),
            in_specs=[any_spec()] * len(pieces)
            + [
                whole_spec((LEN, D)), whole_spec((2, D)), group_spec((3, WIDTH)),
                whole_spec((WIDTH, WIDTH)), whole_spec((3, WIDTH, WIDTH)), whole_spec((LEN, 128)),
                whole_spec((LEN, 128)), whole_spec((LEN, 128)),
            ],
            out_specs=[
                pl.BlockSpec((LEN, WIDTH), lambda g, *_: (0, g)), group_spec((LEN, WIDTH)),
                whole_spec((D, LEN)), whole_spec((wide, rows_in, D)), group_spec((LEN, WIDTH)),
                group_spec((LEN, WIDTH)), group_spec((LEN, 128)), group_spec((LEN, 128)),
                group_spec((LEN, WIDTH)), group_spec((LEN, WIDTH)),
            ],
            scratch_shapes=[
                pltpu.VMEM((LEN, D), BF16),
                pltpu.VMEM((LEN, 128), BF16), pltpu.VMEM((LEN, 128), BF16),
                pltpu.VMEM((LEN, WIDTH), BF16), pltpu.VMEM((2, LEN, WIDTH), F32),
                pltpu.SMEM((32,), jnp.int32), pltpu.SMEM((32,), jnp.int32),
                pltpu.SMEM((32,), jnp.int32), pltpu.SemaphoreType.DMA((GROUPS, 16)),
            ],
        ),
        out_shape=[
            jax.ShapeDtypeStruct((LEN, D), BF16), out((LEN, WIDTH), F32),
            jax.ShapeDtypeStruct((D, LEN), BF16), jax.ShapeDtypeStruct((wide, rows_in, D), BF16),
            out((LEN, WIDTH), F32), out((LEN, WIDTH), F32), out((LEN, 128), F32),
            out((LEN, 128), F32), out((LEN, WIDTH), F32), out((LEN, WIDTH), F32),
        ],
        compiler_params=pltpu.CompilerParams(
            dimension_semantics=("arbitrary",), vmem_limit_bytes=VMEM_LIMIT
        ),
        cost_estimate=cost(20 * 10**9, 40 * 10**6),
        name="attend",
    )(lengths, place, *pieces, tokens, norm, bias, perm, proj, cosine, sine, onehot)


def attend_back_kernel(
    lengths, place, dmixed_ref, mixed_ref, rden_ref, wq_ref, wk_ref, qf_ref, kf_ref, v_ref,
    a1t_ref, w_ref, perm_ref, proj_ref, cos_ref, sin_ref, onehot_ref, ones_ref,
    keep_ref, send_ref, bias_ref, da1_ref,
    qb, kb, dnb, dnh, lift, dqf, dkf, dv, dqkv, base, first, last,
):
    count = make_blocks(lengths, base, first, last)
    qb[...] = qf_ref[0].astype(BF16)
    kb[...] = kf_ref[0].astype(BF16)
    lane = lax.broadcasted_iota(jnp.int32, (1, 128), 1)
    ones = ones_ref[...]
    for pair in range(2):
        lanes = slice(128 * pair, 128 * (pair + 1))
        for rows in range(0, LEN, 256):
            here = pl.ds(rows, 256)
            dnum = dmixed_ref[here, lanes] * rden_ref[0, here, lanes]
            high, low = halves(dnum)
            dnb[here, lanes] = high
            part_high, part_low = halves(dnum * mixed_ref[0, here, lanes])
            dden = -mm(jnp.concatenate([part_high, part_low], axis=1), ones)
            den_high, den_low = halves(dden)
            high, low = high.astype(F32), low.astype(F32)
            den_high = pltpu.roll(den_high.astype(F32), 64, 1)
            den_low = pltpu.roll(den_low.astype(F32), 64, 1)
            low_far = pltpu.roll(low, 64, 1)
            v = v_ref[0, here, lanes]
            v_high, v_low = halves(v)
            v_high, v_low = v_high.astype(F32), v_low.astype(F32)
            v_far = pltpu.roll(v_high, 64, 1)
            for side in range(2):
                own = (lane >= 64 * side) & (lane < 64 * side + 64)
                mark = 64 - 64 * side
                rest = jnp.where(lane == mark, den_high, jnp.where(lane == mark + 1, den_low, 0.0))
                both = ((lane == mark) | (lane == mark + 1)).astype(F32)
                head = 2 * pair + side
                dnh[head, here, :128] = jnp.where(own, high, low_far).astype(BF16)
                dnh[head, here, 128:] = jnp.where(own, high, rest).astype(BF16)
                lift[head, here, :128] = jnp.where(own, v_high, v_far).astype(BF16)
                lift[head, here, 128:] = jnp.where(own, v_low, both).astype(BF16)
    dqf[...] = jnp.zeros_like(dqf)
    dkf[...] = jnp.zeros_like(dkf)
    dv[...] = jnp.zeros_like(dv)

    def one_span(index, carry):
        rows = pl.ds(pl.multiple_of(base[index], 16), SPAN)
        mask = span_mask(onehot_ref, rows, first[index], last[index])
        q = qb[rows, :]
        k = kb[rows, :]
        q_total = jnp.zeros((SPAN, 128), F32)
        k_total = jnp.zeros((SPAN, 128), F32)
        for pair in range(2):
            lanes = slice(128 * pair, 128 * (pair + 1))
            dn_pair = dnb[rows, lanes]
            v_total = jnp.zeros((SPAN, 128), F32)
            for side in range(2):
                head = 2 * pair + side
                feats = lane_mask(32 * head, 32 * head + 32, 128, BF16)
                q_head = q * feats
                k_head = k * feats
                lifted = lift[head, rows, :]
                dn_head = dnh[head, rows, :]
                scores = mm_nt(k, q_head).astype(BF16) * mask
                dscores = mm_nt(dn_head, lifted).astype(BF16) * mask
                dscores_t = mm_nt(lifted, dn_head).astype(BF16) * mask
                q_total = q_total + mm(dscores, k_head)
                k_total = k_total + mm(dscores_t, q_head)
                own = lane_mask(64 * side, 64 * side + 64, 128, BF16)
                v_total = v_total + mm(scores, dn_pair * own)
            dv[rows, lanes] += v_total
        dqf[rows, :] += q_total
        dkf[rows, :] += k_total
        return carry

    lax.fori_loop(0, count, one_span, 0)
    proj_low = proj_ref[0, :, 128:]
    proj_high = proj_ref[1]
    square = proj_ref[2]
    perm = perm_ref[...]
    for which, (w_in, phi_in, dphi) in enumerate(
        ((wq_ref, qf_ref, dqf), (wk_ref, kf_ref, dkf))
    ):
        for rows in range(0, LEN, 256):
            here = pl.ds(rows, 256)
            r = dphi[here, :] * phi_in[0, here, :]
            high, low = halves(r)
            both = jnp.concatenate([high, low], axis=1)
            spread = mm_nt(both, square)
            dw = mm_nt(both, proj_high) + mm_nt(high, proj_low)
            du = (dw - 2.0 * w_in[0, here, :] * spread) * HD ** (-0.25)
            c = du[:, :128]
            e = du[:, 128:]
            cosine = cos_ref[here, :]
            sine = sin_ref[here, :]
            turned = jnp.concatenate([c * cosine + e * sine, e * cosine - c * sine], axis=1)
            dqkv[here, WIDTH * which : WIDTH * (which + 1)] = mm_nt(
                turned.astype(BF16), perm
            ).astype(BF16)
    dqkv[:, 2 * WIDTH :] = dv[...].astype(BF16)
    bias_ref[0] = jnp.sum(dqkv[...].astype(F32), axis=0, keepdims=True)
    grad = mm(a1t_ref[...], dqkv[...]).astype(BF16)
    store_halves(grad, place[3], keep_ref.at[0], send_ref.at[0])
    w = w_ref[...].reshape(D, D)
    fresh = pl.program_id(0) == 0

    @pl.when(fresh)
    def _():
        da1_ref[...] = mm_nt(dqkv[...], w)

    @pl.when(jnp.logical_not(fresh))
    def _():
        da1_ref[...] += mm_nt(dqkv[...], w)


def store_halves(grad, core, keep_ref, send_ref):
    wide, rows = keep_ref.shape[0], D // keep_ref.shape[0]
    half = rows // 2
    parts = grad.reshape(wide, rows, D)
    for cols in range(3):
        block = parts[:, :, WIDTH * cols : WIDTH * (cols + 1)]
        here = pl.ds(half * cols, half)

        @pl.when(core == 0)
        def _():
            keep_ref[:, here, :] = block[:, :half]
            send_ref[:, here, :] = block[:, half:]

        @pl.when(core == 1)
        def _():
            keep_ref[:, here, :] = block[:, half:]
            send_ref[:, here, :] = block[:, :half]


def attend_back(
    lengths, place, wide, dmixed, saved, a1t, w_in, perm, proj, cosine, sine, onehot, ones
):
    mixed, rden, wq, wk, qf, kf, v = saved

    def by_group(shape):
        return pl.BlockSpec((1,) + shape, lambda g, *_: (g,) + (0,) * len(shape))

    rows_in = D // wide
    half = struct((GROUPS, wide, 3 * rows_in // 2, WIDTH), BF16)
    half_spec = group_spec(half.shape[1:])
    return pl.pallas_call(
        attend_back_kernel,
        grid_spec=pltpu.PrefetchScalarGridSpec(
            num_scalar_prefetch=2,
            grid=(GROUPS,),
            in_specs=[
                pl.BlockSpec((LEN, WIDTH), lambda g, *_: (0, g)),
                by_group((LEN, WIDTH)), by_group((LEN, WIDTH)), by_group((LEN, WIDTH)),
                by_group((LEN, WIDTH)), by_group((LEN, 128)), by_group((LEN, 128)),
                by_group((LEN, WIDTH)), once((D, LEN)),
                pl.BlockSpec((wide, rows_in, D), lambda g, *_: (0, g, 0)),
                once((WIDTH, WIDTH)), once((3, WIDTH, WIDTH)), once((LEN, 128)),
                once((LEN, 128)), once((LEN, 128)), once((WIDTH, 128)),
            ],
            out_specs=[
                half_spec, half_spec, group_spec((1, D)),
                whole_spec((LEN, D)),
            ],
            scratch_shapes=[
                pltpu.VMEM((LEN, 128), BF16), pltpu.VMEM((LEN, 128), BF16),
                pltpu.VMEM((LEN, WIDTH), BF16), pltpu.VMEM((4, LEN, WIDTH), BF16),
                pltpu.VMEM((4, LEN, WIDTH), BF16), pltpu.VMEM((LEN, 128), F32),
                pltpu.VMEM((LEN, 128), F32), pltpu.VMEM((LEN, WIDTH), F32),
                pltpu.VMEM((LEN, D), BF16),
                pltpu.SMEM((32,), jnp.int32), pltpu.SMEM((32,), jnp.int32),
                pltpu.SMEM((32,), jnp.int32),
            ],
        ),
        out_shape=[
            half, half, struct((GROUPS, 1, D), F32), struct((LEN, D), F32),
        ],
        compiler_params=pltpu.CompilerParams(
            dimension_semantics=("arbitrary",), vmem_limit_bytes=VMEM_LIMIT
        ),
        cost_estimate=cost(GROUPS * 12 * 10**9, GROUPS * 20 * 10**6),
        name="attend_back",
    )(
        lengths, place, dmixed, mixed, rden, wq, wk, qf, kf, v, a1t, w_in, perm, proj, cosine,
        sine, onehot, ones,
    )


def chunk_step(
    place, wide, bias_up, dy_ref, a2, a2t, dyt, up, down, act, dhidden, y_in, back_in, y, back,
    outs, dbias_ref,
):
    rows_up = D // wide
    rows_down = FFC // wide
    bias_total = jnp.zeros((1, FFC), F32)
    for rows in range(0, LEN, 256):
        here = pl.ds(rows, 256)
        hidden = mm(a2[here, :], up[...]) + bias_up
        below, density = normal_parts(hidden)
        act_now = (hidden * below).astype(BF16)
        act[here, :] = act_now
        dact = mm_nt(dy_ref[here, :], down[...])
        dhidden_now = (dact * (below + hidden * density)).astype(BF16)
        dhidden[here, :] = dhidden_now
        bias_total = bias_total + jnp.sum(dhidden_now.astype(F32), axis=0, keepdims=True)
        if y_in is None:
            y[here, :] = mm(act_now, down[...])
            back[here, :] = mm_nt(dhidden_now, up[...])
        else:
            y[here, :] = y_in[here, :] + mm(act_now, down[...])
            back[here, :] = back_in[here, :] + mm_nt(dhidden_now, up[...])
    dbias_ref[0] = bias_total
    grad_up = mm(a2t[...], dhidden[...]).astype(BF16).reshape(wide, rows_up, FFC)
    grad_down = mm(dyt[...], act[...]).astype(BF16)
    core = place[3]

    def store_up(ref):
        for cols in range(4):
            ref[:, rows_up * cols : rows_up * (cols + 1), :] = grad_up[
                :, :, WIDTH * cols : WIDTH * (cols + 1)
            ]

    def store_down(ref):
        if wide == 1:
            for cols in range(4):
                ref[0, D * cols : D * (cols + 1), :] = grad_down[
                    :, WIDTH * cols : WIDTH * (cols + 1)
                ]
            return
        for shard in range(wide):
            block = grad_down[:, rows_down * shard : rows_down * (shard + 1)]
            ref[shard, :, :128] = block[: D // 2]
            ref[shard, :, 128:] = block[D // 2 :]

    for when, keep_ref, send_ref in outs:

        @pl.when(when & (core == 0))
        def _():
            store_up(keep_ref)
            store_down(send_ref)

        @pl.when(when & (core == 1))
        def _():
            store_up(send_ref)
            store_down(keep_ref)


def load_up(flat, at, up, wide):
    rows = D // wide
    for cols in range(4):
        here = pl.ds(at + rows * cols, rows)
        up[:, WIDTH * cols : WIDTH * (cols + 1)] = flat[:, here, :].reshape(D, WIDTH)


def load_down(flat, at, down, wide):
    rows = FFC // wide
    for cols in range(3):
        here = pl.ds(at + rows * cols, rows)
        down[:, WIDTH * cols : WIDTH * (cols + 1)] = flat[:, here, :].reshape(FFC, WIDTH)


def middle_first_kernel(wide, count_in, place, *refs):
    pieces = refs[:count_in]
    (
        x_ref, attn_ref, dy_ref, rows_ref, bias_up_ref,
        x1_ref, a2_ref, a2t_ref, dyt_ref, y_ref, back_ref, out_ref, keep_ref, send_ref, dbias_ref,
        flat, up, down, act, dhidden, sems,
    ) = refs[count_in:]
    copies = flat_copies(place, pieces, flat, sems)
    for copy in copies:
        copy.start()
    for cols in range(0, D, 256):
        dyt_ref[cols : cols + 256, :] = transposed(dy_ref[:, cols : cols + 256])
    for copy in copies:
        copy.wait()
    half_out = D // wide // 2
    half_flat = flat.shape[1] // 2
    for cols in range(3):
        upper = flat[:, half_out * cols : half_out * (cols + 1), :]
        lower = flat[:, half_flat + half_out * cols : half_flat + half_out * (cols + 1), :]
        out_ref[:, WIDTH * cols : WIDTH * (cols + 1)] = jnp.concatenate(
            [upper, lower], axis=1
        ).reshape(D, WIDTH)
    for rows in range(0, LEN, 256):
        here = pl.ds(rows, 256)
        x1 = x_ref[here, :].astype(F32) + (mm(attn_ref[here, :], out_ref[...]) + rows_ref[7:8, :])
        x1_ref[here, :] = x1
        centre = x1 - jnp.mean(x1, axis=-1, keepdims=True)
        spread = jnp.mean(centre * centre, axis=-1, keepdims=True)
        a2_ref[here, :] = (
            centre * lax.rsqrt(spread + norm_eps) * rows_ref[2:3, :] + rows_ref[3:4, :]
        ).astype(BF16)
    for cols in range(0, D, 256):
        a2t_ref[cols : cols + 256, :] = transposed(a2_ref[:, cols : cols + 256])
    load_up(flat, 3 * half_out, up, wide)
    load_down(flat, half_flat + 3 * half_out, down, wide)
    chunk_step(
        place, wide, bias_up_ref[0], dy_ref, a2_ref, a2t_ref, dyt_ref, up, down, act, dhidden,
        None, None, y_ref, back_ref, [(place[3] >= 0, keep_ref, send_ref)], dbias_ref,
    )


def middle_rest_kernel(wide, count_in, place, *refs):
    pieces = refs[:count_in]
    (
        dy_ref, a2_ref, a2t_ref, dyt_ref, bias_up_ref, attn_ref, out_ref, rows_ref,
        y_in, back_in, x1_in,
        block_ref, dx1_ref, dmixed_ref, okeep_ref, osend_ref, vec_ref,
        keep1_ref, send1_ref, keep2_ref, send2_ref, dbias_ref,
        up, down, act, dhidden, back, dbranch, sems,
    ) = refs[count_in:]
    step = pl.program_id(0)
    x1_copy = pltpu.make_async_copy(x1_in, dx1_ref, sems.at[0])

    @pl.when(step == 0)
    def _():
        x1_copy.start()

    if count_in == 4:
        mine = place[3] == step
        for own in range(2):
            which = mine if own == 0 else jnp.logical_not(mine)

            @pl.when(which)
            def _():
                for flip in range(2):
                    column = place[1] if flip == 0 else 1 - place[1]
                    for shift in range(4):
                        shard = lax.rem(place[0] + 4 - shift, 4) * 2 + column
                        piece = pieces[2 * own + flip].at[shift]
                        here = pl.ds(pl.multiple_of(shard * 96, 16), 96)
                        for cols in range(4):
                            up[here, WIDTH * cols : WIDTH * (cols + 1)] = piece[
                                96 * cols : 96 * (cols + 1), :
                            ]
                        here = pl.ds(pl.multiple_of(shard * 128, 16), 128)
                        for cols in range(3):
                            down[here, WIDTH * cols : WIDTH * (cols + 1)] = piece[
                                384 + 128 * cols : 512 + 128 * cols, :
                            ]

    else:
        load_up(pieces[0].at[0], 0, up, wide)
        load_down(pieces[1].at[0], 0, down, wide)

    def run(y_now, back_now):
        chunk_step(
            place, wide, bias_up_ref[0], dy_ref, a2_ref, a2t_ref, dyt_ref, up, down, act, dhidden,
            y_now, back_now, block_ref, back,
            [(step == 0, keep1_ref, send1_ref), (step == 1, keep2_ref, send2_ref)], dbias_ref,
        )

    @pl.when(step == 0)
    def _():
        block_ref[...] = y_in[...]
        back[...] = back_in[...]

    run(block_ref, back)

    @pl.when(step == 1)
    def _():
        x1_copy.wait()
        zero = jnp.zeros((1, D), F32)
        dgain, dshift, dbias_out, dbias_down = zero, zero, zero, zero
        for rows in range(0, LEN, 256):
            here = pl.ds(rows, 256)
            x1 = dx1_ref[here, :]
            block_ref[here, :] = x1 + (block_ref[here, :] + rows_ref[8:9, :])
            dn = back[here, :]
            dy = dy_ref[here, :].astype(F32)
            centre = x1 - jnp.mean(x1, axis=-1, keepdims=True)
            spread = jnp.mean(centre * centre, axis=-1, keepdims=True)
            scale = lax.rsqrt(spread + norm_eps)
            zh = centre * scale
            dgain = dgain + jnp.sum(dn * zh, axis=0, keepdims=True)
            dshift = dshift + jnp.sum(dn, axis=0, keepdims=True)
            e = dn * rows_ref[2:3, :]
            dz = (
                e
                - jnp.mean(e, axis=-1, keepdims=True)
                - zh * jnp.mean(e * zh, axis=-1, keepdims=True)
            ) * scale
            dx1 = dy + dz
            dx1_ref[here, :] = dx1
            low = dx1.astype(BF16)
            dbranch[here, :] = low
            dbias_out = dbias_out + jnp.sum(low.astype(F32), axis=0, keepdims=True)
            dbias_down = dbias_down + jnp.sum(dy, axis=0, keepdims=True)
            dmixed_ref[here, :] = mm_nt(low, out_ref[...])
        for cols in range(0, D, 256):
            up[cols : cols + 256, :] = transposed(attn_ref[:, cols : cols + 256])
        store_halves(mm(up[...], dbranch[...]).astype(BF16), place[3], okeep_ref, osend_ref)
        vec_ref[0:1, :] = dgain
        vec_ref[1:2, :] = dshift
        vec_ref[2:3, :] = dbias_out
        vec_ref[3:4, :] = dbias_down


def once(shape):
    return whole_spec(shape, pipeline_mode=pl.Buffered(1))


def struct(shape, dtype):
    return jax.ShapeDtypeStruct(shape, dtype)


def weight_scratch():
    return [
        pltpu.VMEM((D, FFC), BF16), pltpu.VMEM((FFC, D), BF16), pltpu.VMEM((LEN, FFC), BF16),
        pltpu.VMEM((LEN, FFC), BF16),
    ]


def middle_first(place, wide, pieces, tokens, attn, cotangent, vectors, bias_up):
    rows_flat = 3 * D // wide + 2 * FFC * D // (WIDTH * wide)
    half = (wide, FFC * D // (WIDTH * wide), WIDTH)
    outs = [
        struct((LEN, D), F32), struct((LEN, D), BF16), struct((D, LEN), BF16),
        struct((D, LEN), BF16), struct((LEN, D), F32), struct((LEN, D), F32),
        struct((D, D), BF16), struct(half, BF16), struct(half, BF16), struct((1, 1, FFC), F32),
    ]
    return pl.pallas_call(
        functools.partial(middle_first_kernel, wide, len(pieces)),
        grid_spec=pltpu.PrefetchScalarGridSpec(
            num_scalar_prefetch=1,
            grid=(1,),
            in_specs=[any_spec()] * len(pieces)
            + [
                once((LEN, D)), once((LEN, D)), once((LEN, D)), once((13, D)),
                pl.BlockSpec((1, 1, FFC), lambda *_: (0, 0, 0)),
            ],
            out_specs=[once(out.shape) for out in outs],
            scratch_shapes=[pltpu.VMEM((wide, rows_flat, WIDTH), BF16)]
            + weight_scratch()
            + [pltpu.SemaphoreType.DMA((16,))],
        ),
        out_shape=outs,
        compiler_params=pltpu.CompilerParams(
            dimension_semantics=("arbitrary",), vmem_limit_bytes=VMEM_LIMIT
        ),
        cost_estimate=cost(14 * 10**9, 30 * 10**6),
        name="middle_first",
    )(place, *pieces, tokens, attn, cotangent, vectors, bias_up)


def middle_rest(place, wide, pieces, cotangent, state, bias_up, attn, w_out, vectors, sums):
    a2, a2t, dyt = state
    half = (wide, FFC * D // (WIDTH * wide), WIDTH)
    out_half = (wide, 3 * D // (2 * wide), WIDTH)
    outs = [
        struct((LEN, D), F32), struct((LEN, D), F32), struct((LEN, D), F32),
        struct(out_half, BF16), struct(out_half, BF16), struct((8, D), F32),
        struct(half, BF16), struct(half, BF16), struct(half, BF16), struct(half, BF16),
        struct((2, 1, FFC), F32),
    ]
    out_specs = [once(out.shape) for out in outs[:-1]] + [group_spec((1, FFC))]
    if wide == 1:
        piece_specs = [group_spec(piece.shape[1:]) for piece in pieces]
    else:
        piece_specs = [once(piece.shape) for piece in pieces]
    return pl.pallas_call(
        functools.partial(middle_rest_kernel, wide, len(pieces)),
        grid_spec=pltpu.PrefetchScalarGridSpec(
            num_scalar_prefetch=1,
            grid=(2,),
            in_specs=piece_specs
            + [
                once((LEN, D)), once((LEN, D)), once((D, LEN)), once((D, LEN)),
                pl.BlockSpec((1, 1, FFC), lambda j, *_: (j + 1, 0, 0)),
                once((LEN, D)), once((D, D)), once((13, D)),
                once((LEN, D)), once((LEN, D)), any_spec(),
            ],
            out_specs=out_specs,
            scratch_shapes=weight_scratch()
            + [
                pltpu.VMEM((LEN, D), F32), pltpu.VMEM((LEN, D), BF16),
                pltpu.SemaphoreType.DMA((1,)),
            ],
        ),
        out_shape=outs,
        compiler_params=pltpu.CompilerParams(
            dimension_semantics=("arbitrary",), vmem_limit_bytes=VMEM_LIMIT
        ),
        cost_estimate=cost(28 * 10**9, 40 * 10**6),
        name="middle_rest",
    )(place, *pieces, cotangent, a2, a2t, dyt, bias_up, attn, w_out, vectors, *sums)


def input_kernel(
    wide, x_ref, dx1_ref, da1_ref, rows_ref, middle_ref, bias_in_ref, bias_first_ref, bias_rest_ref,
    out_ref, vec_ref,
):
    gain = rows_ref[0:1, :]
    x = x_ref[...].astype(F32)
    dn = da1_ref[...]
    centre = x - jnp.mean(x, axis=-1, keepdims=True)
    spread = jnp.mean(centre * centre, axis=-1, keepdims=True)
    scale = lax.rsqrt(spread + norm_eps)
    zh = centre * scale
    e = dn * gain
    dz = (
        e - jnp.mean(e, axis=-1, keepdims=True) - zh * jnp.mean(e * zh, axis=-1, keepdims=True)
    ) * scale
    out_ref[...] = dx1_ref[...] + dz

    @pl.when(pl.program_id(0) == 0)
    def _():
        vec_ref[...] = jnp.zeros_like(vec_ref)
        vec_ref[2:4, :] = middle_ref[0:2, :]
        vec_ref[7:9, :] = middle_ref[2:4, :]
        for group in range(GROUPS):
            lanes = slice(WIDTH * group, WIDTH * (group + 1))
            for which in range(3):
                vec_ref[4 + which : 5 + which, lanes] = bias_in_ref[
                    group, :, WIDTH * which : WIDTH * (which + 1)
                ]
        for chunk in range(CHUNKS):
            for part in range(8):
                value = (
                    bias_first_ref[0] if chunk == 0 else bias_rest_ref[chunk - 1]
                )[:, 128 * part : 128 * (part + 1)]
                start = FFC * chunk + 128 * part if wide == 1 else 384 * part + 128 * chunk
                row, lane = 9 + start // D, start % D
                vec_ref[row : row + 1, lane : lane + 128] = value

    vec_ref[0:1, :] += jnp.sum(dn * zh, axis=0, keepdims=True)
    vec_ref[1:2, :] += jnp.sum(dn, axis=0, keepdims=True)


def input_side(wide, tokens, dx1, da1, vectors, middle_vec, bias_in, bias_first, bias_rest):
    block = pl.BlockSpec((256, D), lambda i: (i, 0))
    return pl.pallas_call(
        functools.partial(input_kernel, wide),
        grid=(LEN // 256,),
        in_specs=[
            block, block, block, whole_spec((13, D)), whole_spec((8, D)),
            whole_spec((GROUPS, 1, D)), whole_spec((1, 1, FFC)), whole_spec((2, 1, FFC)),
        ],
        out_specs=[block, whole_spec((16, D))],
        out_shape=[struct((LEN, D), F32), struct((16, D), F32)],
        compiler_params=pltpu.CompilerParams(dimension_semantics=("arbitrary",)),
        cost_estimate=cost(10**6, 12 * 10**6),
        name="input_side",
    )(tokens, dx1, da1, vectors, middle_vec, bias_in, bias_first, bias_rest)


def tables(lengths, projection):
    ends = jnp.cumsum(lengths[0])
    starts = ends - lengths[0]
    place = jnp.arange(LEN, dtype=jnp.int32)
    member = (place[:, None] >= starts[None, :]) & (place[:, None] < ends[None, :])
    offset = jnp.sum(jnp.where(member, starts[None, :], 0), axis=1)
    position = (place - offset).astype(F32)
    freq = 10000.0 ** (-jnp.arange(32, dtype=F32) / 32)
    angles = position[:, None] * jnp.tile(freq, 4)[None, :]
    onehot = jnp.pad(member.astype(BF16), ((0, 0), (0, 128 - member.shape[1])))
    eye = jnp.asarray(np.eye(4, dtype=np.float32))
    lifted = jnp.einsum("hif,ab->haibf", projection.reshape(2, 32, FEAT), eye)
    lifted = lifted.reshape(WIDTH, 128)
    rounded = lax.reduce_precision(lifted, 8, 7)
    high, low = rounded.astype(BF16), (lifted - rounded).astype(BF16)
    square = np.zeros((2, 4, 32, 4, 32), np.float32)
    for head in range(4):
        square[:, head, :, head, :] = 0.5
    square = jnp.asarray(square.reshape(WIDTH, 128), BF16)
    proj = jnp.stack(
        [
            jnp.concatenate([high, low], axis=1),
            jnp.concatenate([high, high], axis=1),
            jnp.concatenate([square, square], axis=1),
        ]
    )
    return jnp.cos(angles), jnp.sin(angles), onehot, proj


def wide_perm(shift_z, flip_x):
    pairs = []
    for z in range(4):
        for x in range(2):
            target_x = 1 - x if flip_x else x
            pairs.append((2 * z + x, 2 * ((z + shift_z) % 4) + target_x))
    return pairs


def narrow_perm(flip_y, flip_core):
    pairs = []
    for y in range(2):
        for core in range(2):
            pairs.append(
                (2 * y + core, 2 * (1 - y if flip_y else y) + (1 - core if flip_core else core))
            )
    return pairs


def over_z(values, shift):
    return lax.ppermute(values, "wide", wide_perm(shift, False))


def over_x(values):
    return lax.ppermute(values, "wide", wide_perm(0, True))


def over_far(values, bit):
    return lax.ppermute(values, "wide", [(w, w ^ bit) for w in range(8)])


def over_y(values):
    return lax.ppermute(values, "narrow", narrow_perm(True, False))


def over_core(values):
    return lax.ppermute(values, "narrow", narrow_perm(False, True))


def tie(*values):
    return lax.optimization_barrier(values)


def special():
    return lax.axis_size("wide") == 8 and lax.axis_size("narrow") == 4


def sum_wide(values):
    if not special():
        return lax.psum(values, "wide")
    for perm in (wide_perm(0, True), [(w, w ^ 2) for w in range(8)], [(w, w ^ 4) for w in range(8)]):
        values = values + lax.ppermute(values, "wide", perm)
    return values


def sum_narrow(values):
    if not special():
        return lax.psum(values, "narrow")
    pair = values + over_core(values)
    return pair + over_y(pair)


def along_z(mine):
    return jnp.stack([mine] + [over_z(mine, shift) for shift in (1, 2, 3)])


def small_call(kernel, name, place, operands, outs):
    return pl.pallas_call(
        kernel,
        grid_spec=pltpu.PrefetchScalarGridSpec(
            num_scalar_prefetch=1,
            grid=(1,),
            in_specs=[once(value.shape) for value in operands],
            out_specs=[once(out.shape) for out in outs],
        ),
        out_shape=outs,
        compiler_params=pltpu.CompilerParams(
            dimension_semantics=("arbitrary",), vmem_limit_bytes=VMEM_LIMIT
        ),
        cost_estimate=cost(10**6, sum(4 * math.prod(v.shape) for v in operands + outs)),
        name=name,
    )(place, *operands)


def pick_kernel(
    place, in_ref, out_ref, up_ref, down_ref, near_ref, last_ref, first_ref, rest_ref
):
    core = place[3]
    here = pl.ds(pl.multiple_of(48 * core, 16), 48)
    for group in range(GROUPS):
        ref, index = (near_ref, group) if group < 2 else (last_ref, 0)
        for which in range(3):
            ref[index, :, WIDTH * which : WIDTH * (which + 1)] = in_ref[
                which, here, WIDTH * group : WIDTH * (group + 1)
            ].astype(BF16)
    for cols in range(3):
        first_ref[48 * cols : 48 * (cols + 1), :] = out_ref[
            here, WIDTH * cols : WIDTH * (cols + 1)
        ].astype(BF16)

    def put_up(ref, at, chunk):
        for cols in range(4):
            rows = slice(at + 96 * cols, at + 96 * (cols + 1))
            for side in range(2):
                start = 384 * (2 * cols + side) + 128 * chunk
                ref[rows, 128 * side : 128 * (side + 1)] = up_ref[:, start : start + 128].astype(
                    BF16
                )

    def put_down(ref, at, chunk):
        for cols in range(3):
            ref[at + 128 * cols : at + 128 * (cols + 1), :] = down_ref[
                128 * chunk : 128 * (chunk + 1), WIDTH * cols : WIDTH * (cols + 1)
            ].astype(BF16)

    for side in range(2):

        @pl.when(core == side)
        def _():
            if side == 0:
                put_up(first_ref, 144, 0)
            else:
                put_down(first_ref, 144, 0)

        @pl.when(core == side)
        def _():
            put_up(rest_ref, 0, 1 + side)
            put_down(rest_ref, 384, 1 + side)


def first_sum_kernel(place, *refs):
    count = (len(refs) - 2) // 2
    send_ref, keep_ref = refs[-2:]
    x = place[1]
    at = 0
    for index in range(count):
        own, got = refs[2 * index], refs[2 * index + 1]
        for part in range(own.shape[0]):
            rows = own.shape[3]
            here = pl.ds(at, rows)
            keep_ref[0, here, :] = (
                own[part, 0, x].astype(F32) + got[part, 0, x].astype(F32)
            ).astype(BF16)
            send_ref[0, here, :] = (
                own[part, 0, 1 - x].astype(F32) + got[part, 0, 1 - x].astype(F32)
            ).astype(BF16)
            at += rows


def first_sum(place, pairs):
    total = 0
    operands, specs = [], []
    for own, got in pairs:
        parts, rows = own.shape[0], own.shape[2]
        total += parts * rows
        for value in (own, got):
            operands.append(value.reshape(parts, 4, 2, rows, WIDTH))
            specs.append(
                pl.BlockSpec((parts, 1, 2, rows, WIDTH), lambda i, *_: (0, i, 0, 0, 0))
            )
    block = pl.BlockSpec((1, total, WIDTH), lambda i, *_: (i, 0, 0))
    return pl.pallas_call(
        first_sum_kernel,
        grid_spec=pltpu.PrefetchScalarGridSpec(
            num_scalar_prefetch=1, grid=(4,), in_specs=specs, out_specs=[block, block]
        ),
        out_shape=[struct((4, total, WIDTH), BF16)] * 2,
        compiler_params=pltpu.CompilerParams(
            dimension_semantics=("arbitrary",), vmem_limit_bytes=VMEM_LIMIT
        ),
        cost_estimate=cost(10**6, 6 * 8 * total * WIDTH),
        name="first_sum",
    )(place, *operands)


def second_sum_kernel(place, own_ref, got_ref, *outs):
    z = place[0]
    for shift, out in enumerate(outs):
        there = lax.rem(z + shift, 4)
        out[...] = (own_ref[there].astype(F32) + got_ref[there].astype(F32)).astype(BF16)


def second_sum(place, own, got):
    outs = [struct(own.shape[1:], BF16)] * 4
    return small_call(second_sum_kernel, "second_sum", place, [own, got], outs)


def z_sum_kernel(place, *refs):
    total = refs[0][...].astype(F32)
    for ref in refs[1:4]:
        total = total + ref[...].astype(F32)
    rows = refs[0].shape[0]
    refs[-1][:rows, :] = total.astype(BF16)
    if len(refs) == 7:
        refs[-1][rows:, :] = (refs[4][...].astype(F32) + refs[5][...].astype(F32)).astype(BF16)


def z_sum(place, parts, below=(), got=None):
    if got is None:
        got = [over_z(parts[shift], shift) for shift in (1, 2, 3)]
    rows = parts[0].shape[0] + (below[0].shape[0] if below else 0)
    return small_call(
        z_sum_kernel, "z_sum", place, [parts[0]] + got + list(below),
        [struct((rows, WIDTH), BF16)],
    )[0]


def first_sum_z_kernel(place, *refs):
    z = place[0]
    outs = refs[-4:]
    for shift, out in enumerate(outs):
        there = lax.rem(z + shift, 4) * 2
        at = 0
        for index in range(0, len(refs) - 4, 2):
            own, got = refs[index], refs[index + 1]
            rows = own.shape[1]
            for x in range(2):
                out[x, at : at + rows, :] = (
                    own[there + x].astype(F32) + got[there + x].astype(F32)
                ).astype(BF16)
            at += rows


def first_sum_z(place, pairs):
    rows = sum(own.shape[1] for own, _ in pairs)
    return small_call(
        first_sum_z_kernel, "first_sum_z", place, [value for pair in pairs for value in pair],
        [struct((2, rows, WIDTH), BF16)] * 4,
    )


def split_sum_kernel(place, *refs):
    keep, send = refs[-2:]
    x = place[1]
    for out, at in ((keep, x), (send, 1 - x)):
        total = refs[0][at].astype(F32)
        for ref in refs[1:4]:
            total = total + ref[at].astype(F32)
        out[...] = total.astype(BF16)


def split_sum(place, parts):
    return small_call(
        split_sum_kernel, "split_sum", place, parts, [struct(parts[0].shape[1:], BF16)] * 2
    )


def to_row(column):
    size = column.shape[0]
    eye = lax.broadcasted_iota(jnp.int32, (size, size), 0) == lax.broadcasted_iota(
        jnp.int32, (size, size), 1
    )
    return jnp.sum(jnp.where(eye, column, 0.0), axis=0, keepdims=True)


def to_column(row):
    size = row.shape[1]
    eye = lax.broadcasted_iota(jnp.int32, (size, size), 0) == lax.broadcasted_iota(
        jnp.int32, (size, size), 1
    )
    return jnp.sum(jnp.where(eye, row, 0.0), axis=1, keepdims=True)


DECAY = 1.0 - STEP ** (-0.8)


def lane_values(values):
    lane = lax.broadcasted_iota(jnp.int32, (1, D), 1)
    row = jnp.zeros((1, D), F32)
    for index, value in enumerate(values):
        row = jnp.where(lane == index, value, row)
    return row


def moments(grad, rows_old):
    plain = grad * grad
    squares = plain + square_eps
    mean = jnp.sum(squares, axis=1, keepdims=True) * (1.0 / grad.shape[1])
    rows_new = DECAY * rows_old + (1.0 - DECAY) * to_row(mean)
    total = jnp.sum(rows_new, axis=1, keepdims=True)
    divided = jnp.sum(plain * to_column(1.0 / rows_new), axis=0, keepdims=True)
    return rows_new, total, jnp.sum(squares, axis=0, keepdims=True), divided


def ffn_moments_kernel(
    place, own, got, up_rows, down_rows, out_rows,
    up_grad, down_grad, out_grad, up_rows_new, down_rows_new, out_rows_new, sums,
):
    core = place[3]

    def collect(low, high):
        for chunk in range(CHUNKS):
            at = 384 * chunk
            for cols in range(4):
                for side in range(2):
                    start = 384 * (2 * cols + side) + 128 * chunk
                    up_grad[:, start : start + 128] = low[
                        at + 96 * cols : at + 96 * (cols + 1), 128 * side : 128 * (side + 1)
                    ]
            for side in range(2):
                down_grad[128 * chunk : 128 * (chunk + 1), 384 * side : 384 * (side + 1)] = (
                    jnp.transpose(high[at : at + 384, 128 * side : 128 * (side + 1)])
                )
        for cols in range(3):
            lanes = slice(WIDTH * cols, WIDTH * (cols + 1))
            at = 1152 + 48 * cols
            out_grad[:48, lanes] = low[at : at + 48, :]
            out_grad[48:, lanes] = high[at : at + 48, :]

    @pl.when(core == 0)
    def _():
        collect(own, got)

    @pl.when(core == 1)
    def _():
        collect(got, own)

    up_new, up_total, up_sums, up_divided = moments(up_grad[...], up_rows[...])
    down_new, down_total, down_sums, down_divided = moments(down_grad[...], down_rows[...])
    out_new, out_total, out_sums, out_divided = moments(out_grad[...], out_rows[...])
    up_rows_new[...] = up_new
    down_rows_new[...] = down_new
    out_rows_new[...] = out_new
    for part in range(4):
        lanes = slice(D * part, D * (part + 1))
        sums[part : part + 1, :] = up_sums[:, lanes]
        sums[4 + part : 5 + part, :] = up_divided[:, lanes]
    sums[8:9, :] = down_sums
    sums[9:10, :] = down_divided
    sums[10:11, :] = out_sums
    sums[11:12, :] = out_divided
    sums[12:13, :] = lane_values([up_total, down_total, out_total])
    sums[13:16, :] = jnp.zeros((3, D), F32)


def in_moments_kernel(
    place, own, got, rows_old, vector, ffn_sums, grad, rows_new, sums,
):
    core = place[3]

    def collect(low, high):
        for group in range(GROUPS):
            for which in range(3):
                at = 144 * group + 48 * which
                lanes = slice(WIDTH * group, WIDTH * (group + 1))
                grad[which, :48, lanes] = low[at : at + 48, :]
                grad[which, 48:, lanes] = high[at : at + 48, :]

    @pl.when(core == 0)
    def _():
        collect(own, got)

    @pl.when(core == 1)
    def _():
        collect(got, own)

    totals = []
    for which in range(3):
        new, total, columns, divided = moments(grad[which], rows_old[which : which + 1, :])
        rows_new[which : which + 1, :] = new
        sums[which : which + 1, :] = columns
        sums[3 + which : 4 + which, :] = divided
        totals.append(total)
    sums[6:7, :] = lane_values(totals)
    sums[7:8, :] = jnp.zeros((1, D), F32)
    sums[8:24, :] = vector[...]
    sums[24:40, :] = ffn_sums[...]


def matrix_step(weight, grad, rows, cols, total, col_sums, divided, rows_full, rate):
    cols_new = DECAY * cols + (1.0 - DECAY) * col_sums * (1.0 / rows_full)
    mean = total * (1.0 / rows_full)
    square_sum = mean * jnp.sum(divided / cols_new, axis=1, keepdims=True)
    rms = jnp.sqrt(square_sum * (1.0 / (rows_full * grad.shape[1])))
    factor = to_column(lax.rsqrt(rows / mean)) * (rate / jnp.maximum(1.0, rms / clip_level))
    return cols_new, weight - grad * factor * lax.rsqrt(cols_new)


def finish_kernel(
    place, inward, up, down, out, in_grad, up_grad, down_grad, out_grad, in_rows, up_rows,
    down_rows, out_rows, in_cols, up_cols, down_cols, out_cols, sums, vectors, vector_state,
    in_cols_new, up_cols_new, down_cols_new, out_cols_new, in_next, up_next, down_next, out_next,
    vector_grad, state_next, vectors_next,
):
    base_rate = 0.3 * D ** (-0.5)
    for which in range(3):
        here = slice(which, which + 1)
        in_cols_new[here, :], in_next[which] = matrix_step(
            inward[which], in_grad[which], in_rows[here, :], in_cols[here, :],
            sums[6:7, which : which + 1], sums[here, :], sums[3 + which : 4 + which, :], D,
            base_rate,
        )

    def wide_row(first):
        return jnp.concatenate([sums[first + i : first + i + 1, :] for i in range(4)], axis=1)

    up_cols_new[...], up_next[...] = matrix_step(
        up[...], up_grad[...], up_rows[...], up_cols[...], sums[36:37, 0:1], wide_row(24),
        wide_row(28), D, base_rate,
    )
    down_cols_new[...], down_next[...] = matrix_step(
        down[...], down_grad[...], down_rows[...], down_cols[...], sums[36:37, 1:2],
        sums[32:33, :], sums[33:34, :], FF, 0.3 * FF ** (-0.5),
    )
    out_cols_new[...], out_next[...] = matrix_step(
        out[...], out_grad[...], out_rows[...], out_cols[...], sums[36:37, 2:3],
        sums[34:35, :], sums[35:36, :], D, 1.2 * D ** (-0.5),
    )
    g = sums[8:21, :]
    vector_grad[...] = g
    state = DECAY * vector_state[...] + (1.0 - DECAY) * (g * g + square_eps)
    state_next[...] = state
    update = g * lax.rsqrt(state)
    total = jnp.sum(jnp.sum(update * update, axis=0, keepdims=True), axis=1, keepdims=True)
    rms = jnp.sqrt(total * (1.0 / (13 * D)))
    vectors_next[...] = vectors[...] - update * (0.25 / jnp.maximum(1.0, rms / clip_level))


def shards(
    tokens, cotangent, lengths, projection, inward, outward, expand, shrink, vectors,
    inward_rows, inward_columns, outward_rows, outward_columns, expand_rows, expand_columns,
    shrink_rows, shrink_columns, vector_state,
):
    full = special()
    rows = outward.shape[0]
    wide = 8 if full else 1
    wide_at = lax.axis_index("wide").astype(jnp.int32)
    narrow_at = lax.axis_index("narrow").astype(jnp.int32)
    core = narrow_at % 2 if full else jnp.int32(0)
    place = jnp.stack([wide_at // 2, wide_at % 2, narrow_at // 2, core])
    per = FFC // wide
    cosine, sine, onehot, proj = tables(lengths, projection)
    if full:
        *own_in, own_first, own_rest = small_call(
            pick_kernel, "pick", place, [inward, outward, expand, shrink],
            [
                struct((2, 48, D), BF16), struct((1, 48, D), BF16), struct((528, WIDTH), BF16),
                struct((768, WIDTH), BF16),
            ],
        )
        in_z = [along_z(value) for value in own_in]
        *in_z, own_first, cosine, sine, onehot, proj = tie(
            *in_z, own_first, cosine, sine, onehot, proj
        )
        first_z = along_z(own_first)
        in_x = [over_x(value) for value in in_z]
        pieces_in = []
        *in_z, first_z = tie(*in_z, *in_x, first_z)
        for near, far in zip(in_z[:2], in_z[2:]):
            pieces_in += [near, far, over_core(near), over_core(far)]
        *pieces_in, first_z, own_rest = tie(*pieces_in, first_z, own_rest)
        first_x = over_x(first_z)
        rest_got = [over_z(own_rest, shift) for shift in (1, 2, 3)]
    else:
        in_low = lax.all_gather(inward.astype(BF16), "wide", axis=1, tiled=True)
        out_low = lax.all_gather(outward.astype(BF16), "wide", axis=0, tiled=True)
        up_low = lax.all_gather(expand.astype(BF16), "wide", axis=0, tiled=True)
        down_low = lax.all_gather(shrink.astype(BF16), "wide", axis=0, tiled=True)
        units = jnp.transpose(in_low.reshape(3, D, GROUPS, WIDTH), (2, 1, 0, 3))
        pieces_in = [units.reshape(1, 3 * D, D)]

        def blocks(matrix):
            count = matrix.shape[1] // WIDTH
            return jnp.transpose(matrix.reshape(-1, count, WIDTH), (1, 0, 2)).reshape(-1, WIDTH)

        ups = [blocks(up_low[:, FFC * j : FFC * (j + 1)]) for j in range(CHUNKS)]
        downs = [blocks(down_low[FFC * j : FFC * (j + 1)]) for j in range(CHUNKS)]
        half = D // 2
        pieces_first = [
            jnp.concatenate([blocks(out_low[:half]), ups[0], blocks(out_low[half:]), downs[0]])[
                None
            ]
        ]
        pieces_rest = [jnp.stack(ups[1:])[:, None], jnp.stack(downs[1:])[:, None]]
    perm = jnp.asarray(head_perm(), BF16)
    block_ones = np.kron(np.eye(2, dtype=np.float32), np.ones((64, 64), np.float32))
    ones = jnp.asarray(np.concatenate([block_ones, block_ones]), BF16)
    split = vectors[4:6].reshape(2, GROUPS, 4, 2, 32)
    bias_qk = jnp.transpose(split, (0, 1, 3, 2, 4)).reshape(2, GROUPS, WIDTH)
    bias = jnp.concatenate([bias_qk, vectors[6].reshape(1, GROUPS, WIDTH)])
    bias = jnp.transpose(bias, (1, 0, 2))
    bias_up = vectors[9:].reshape(wide, CHUNKS, per)
    bias_up = jnp.transpose(bias_up, (1, 0, 2)).reshape(CHUNKS, 1, FFC)
    attn, mixed, a1t, w_in, wq, wk, qf, kf, v, rden = attend(
        lengths, place, pieces_in, wide, tokens, vectors[:2], bias, perm, proj, cosine, sine,
        onehot,
    )
    if full:
        attn, first_x, *rest_got = tie(attn, first_x, *rest_got)
        rest_z = jnp.stack([own_rest] + rest_got)
        first_cores = [over_core(first_z), over_core(first_x)]
        *first_cores, rest_z = tie(*first_cores, rest_z)
        pieces_first = [first_z, first_x] + first_cores
        rest_x = over_x(rest_z)
    x1, a2, a2t, dyt, y, back, w_out, keep0, send0, dbias0 = middle_first(
        place, wide, pieces_first, tokens, attn, cotangent, vectors, bias_up
    )
    if full:
        rest_core = over_core(rest_z)
        rest_x, rest_core, send0, y = tie(rest_x, rest_core, send0, y)
        pieces_rest = [rest_z, rest_x, rest_core, over_core(rest_x)]
        got0 = over_core(send0)
    (
        block_out, dx1, dmixed, okeep, osend, middle_vec, keep1, send1, keep2, send2, dbias12,
    ) = middle_rest(
        place, wide, pieces_rest, cotangent, (a2, a2t, dyt), bias_up, attn, w_out, vectors,
        (y, back, x1),
    )
    if full:
        send_b, keep_b = first_sum(
            place, [(keep0[None], got0[None]), (keep1[None], over_core(send1)[None])]
        )
        e_parts = first_sum_z(place, [(keep2, over_core(send2)), (okeep, over_core(osend))])
        dmixed, send_b, keep_b, *e_parts = tie(dmixed, send_b, keep_b, *e_parts)
        got_b = over_x(send_b)
        e_got = [over_z(e_parts[shift], shift) for shift in (1, 2, 3)]
    saved = (mixed, rden, wq, wk, qf, kf, v)
    in_keep, in_send, in_bias, da1 = attend_back(
        lengths, place, wide, dmixed, saved, a1t, w_in, perm, proj, cosine, sine, onehot, ones
    )
    if full:
        keep_e, send_e = split_sum(place, [e_parts[0]] + e_got)
        send_e, in_send, keep_b, got_b, da1 = tie(send_e, in_send, keep_b, got_b, da1)
        got_e = over_x(send_e)
        b_parts = second_sum(place, keep_b, got_b)
        got_in = over_core(in_send)
        got_in, *b_parts = tie(got_in, *b_parts)
        send_c, keep_c = first_sum(place, [(in_keep, got_in)])
        da1, send_c, got_e = tie(da1, send_c, got_e)
        got_c = over_x(send_c)
    input_grad, vector_local = input_side(
        wide, tokens, dx1, da1, vectors, middle_vec, in_bias, dbias0, dbias12
    )
    if full:
        vector_part = sum_narrow(vector_local)

        def pair_sum(mine, got):
            half_sum = mine.astype(F32) + got.astype(F32)
            return half_sum, over_core(half_sum)

        got_c, input_grad, vector_part = tie(got_c, input_grad, vector_part)
        c_parts = second_sum(place, keep_c, got_c)
        b_parts[0], *c_parts = tie(b_parts[0], *c_parts)
        ffn_mine = z_sum(place, b_parts, (keep_e, got_e))
        ffn_mine, *c_parts = tie(ffn_mine, *c_parts)
        ffn_y = over_y(ffn_mine)
        c_got = [over_z(c_parts[shift], shift) for shift in (1, 2, 3)]
        ffn_y, *c_got = tie(ffn_y, *c_got)
        c_mine = z_sum(place, c_parts, (), c_got)
        c_mine, ffn_y = tie(c_mine, ffn_y)
        c_y = over_y(c_mine)
        ffn_own, ffn_got = pair_sum(ffn_mine, ffn_y)
        expand_grad, shrink_grad, outward_grad, up_rows, down_rows, out_rows, sums = small_call(
            ffn_moments_kernel, "ffn_moments", place,
            [
                ffn_own, ffn_got, expand_rows[None], shrink_rows[None], outward_rows[None],
            ],
            [
                struct(expand.shape, F32), struct(shrink.shape, F32), struct(outward.shape, F32),
                struct((1, 96), F32), struct((1, 384), F32), struct((1, 96), F32),
                struct((16, D), F32),
            ],
        )
        c_y, sums = tie(c_y, sums)
        c_own, c_got = pair_sum(c_mine, c_y)
        inward_grad, in_rows, sums = small_call(
            in_moments_kernel, "in_moments", place,
            [c_own, c_got, inward_rows, vector_part, sums],
            [struct(inward.shape, F32), struct((3, 96), F32), struct((40, D), F32)],
        )
        sums = sum_wide(sums)
        (
            in_cols, up_cols, down_cols, out_cols, inward_next, expand_next, shrink_next,
            outward_next, vector_grad, vector_state_next, vectors_next,
        ) = small_call(
            finish_kernel, "finish", place,
            [
                inward, expand, shrink, outward, inward_grad, expand_grad, shrink_grad,
                outward_grad, in_rows, up_rows, down_rows, out_rows, inward_columns,
                expand_columns[None], shrink_columns[None], outward_columns[None], sums, vectors,
                vector_state,
            ],
            [
                struct((3, D), F32), struct((1, FF), F32), struct((1, D), F32),
                struct((1, D), F32), struct(inward.shape, F32), struct(expand.shape, F32),
                struct(shrink.shape, F32), struct(outward.shape, F32), struct((13, D), F32),
                struct((13, D), F32), struct((13, D), F32),
            ],
        )
        return (
            block_out, input_grad, inward_grad, outward_grad, expand_grad, shrink_grad,
            vector_grad, in_rows, in_cols, out_rows[0], out_cols[0], up_rows[0], up_cols[0],
            down_rows[0], down_cols[0], vector_state_next, inward_next, outward_next,
            expand_next, shrink_next, vectors_next,
        )
    vector_part = sum_narrow(vector_local[:13])

    def reduced(values, axis):
        part = lax.psum_scatter(values, "wide", scatter_dimension=axis, tiled=True)
        return lax.psum(part.astype(F32), "narrow")

    keeps = [keep0, keep1, keep2]
    sends = [send0, send1, send2]
    up_grads = [
        jnp.transpose(keep.reshape(4, D, WIDTH), (1, 0, 2)).reshape(D, FFC) for keep in keeps
    ]
    down_grads = [
        jnp.transpose(send.reshape(4, D, WIDTH), (0, 2, 1)).reshape(FFC, D) for send in sends
    ]
    expand_grad = reduced(jnp.concatenate(up_grads, axis=1), 0)
    shrink_grad = reduced(jnp.concatenate(down_grads, axis=0), 0)

    def rebuilt(keep, send):
        return jnp.concatenate(
            [keep.reshape(-1, 3, D // 2, WIDTH), send.reshape(-1, 3, D // 2, WIDTH)], axis=2
        )

    outward_grad = reduced(jnp.transpose(rebuilt(okeep, osend)[0], (1, 0, 2)).reshape(D, D), 0)
    in_units = rebuilt(in_keep, in_send)
    inward_grad = reduced(jnp.transpose(in_units, (1, 2, 0, 3)).reshape(3, D, D), 1)
    decay = 1.0 - STEP ** (-0.8)
    wide_count = lax.axis_size("wide")
    grads_list = [inward_grad, outward_grad[None], expand_grad[None], shrink_grad[None]]
    rows_old = [inward_rows, outward_rows[None], expand_rows[None], shrink_rows[None]]
    columns_old = [
        inward_columns,
        outward_columns[None],
        expand_columns[None],
        shrink_columns[None],
    ]
    weights_old = [inward, outward[None], expand[None], shrink[None]]
    rates = [0.3 * D ** (-0.5), 1.2 * D ** (-0.5), 0.3 * D ** (-0.5), 0.3 * FF ** (-0.5)]
    bounds = [0, 3, 4, 5, 6]
    rows_next = []
    column_parts = []
    for member in range(4):
        squares = grads_list[member] * grads_list[member] + square_eps
        rows_next.append(decay * rows_old[member] + (1.0 - decay) * jnp.mean(squares, axis=-1))
        column_parts.append(jnp.sum(squares, axis=-2))
    row_totals = jnp.concatenate([jnp.sum(entry, axis=-1) for entry in rows_next])
    shapes = [part.shape for part in column_parts] + [row_totals.shape, vector_part.shape]
    flat = jnp.concatenate(
        [part.reshape(-1) for part in column_parts + [row_totals, vector_part]]
    )
    flat = jnp.pad(flat, (0, -flat.shape[0] % 1024)).reshape(-1, 128)
    flat = sum_wide(flat).reshape(-1)
    summed = []
    offset = 0
    for shape in shapes:
        size = 1
        for extent in shape:
            size *= extent
        summed.append(flat[offset : offset + size].reshape(shape))
        offset += size
    column_sums = list(summed[0:4])
    totals_sum = summed[4]
    vector_grad = summed[5]
    columns_next = []
    scaled_list = []
    row_means = []
    sizes_full = []
    for member in range(4):
        grad_now = grads_list[member]
        rows_full = grad_now.shape[-2] * wide_count
        sizes_full.append(rows_full * grad_now.shape[-1])
        columns_next.append(
            decay * columns_old[member] + (1.0 - decay) * column_sums[member] / rows_full
        )
        row_mean = totals_sum[bounds[member] : bounds[member + 1]] / rows_full
        row_means.append(row_mean)
        scaled_list.append(
            grad_now
            * lax.rsqrt(rows_next[member] / row_mean[:, None])[..., None]
            * lax.rsqrt(columns_next[member])[:, None, :]
        )
    partial_squares = jnp.concatenate(
        [jnp.sum(entry * entry, axis=(-2, -1)) for entry in scaled_list]
    )
    total_squares = sum_wide(jnp.pad(partial_squares, (0, 122)).reshape(1, 128))[0, :6]
    rms_list = [
        jnp.sqrt(total_squares[bounds[member] : bounds[member + 1]] / sizes_full[member])
        for member in range(4)
    ]
    weights_next = []
    for member in range(4):
        limiter = jnp.maximum(1.0, rms_list[member] / clip_level)
        weights_next.append(
            weights_old[member] - rates[member] * scaled_list[member] / limiter[:, None, None]
        )
    vector_state_next = decay * vector_state + (1.0 - decay) * (
        vector_grad * vector_grad + square_eps
    )
    vector_update = vector_grad * lax.rsqrt(vector_state_next)
    vector_rms = jnp.sqrt(jnp.mean(vector_update * vector_update))
    vectors_next = vectors - 0.25 * vector_update / jnp.maximum(1.0, vector_rms / clip_level)
    return (
        block_out,
        input_grad,
        inward_grad,
        outward_grad,
        expand_grad,
        shrink_grad,
        vector_grad,
        rows_next[0],
        columns_next[0],
        rows_next[1][0],
        columns_next[1][0],
        rows_next[2][0],
        columns_next[2][0],
        rows_next[3][0],
        columns_next[3][0],
        vector_state_next,
        weights_next[0],
        weights_next[1][0],
        weights_next[2][0],
        weights_next[3][0],
        vectors_next,
    )


def solution(mesh):
    placed = (
        P(("narrow", "wide"), None),
        P(("narrow", "wide"), None),
        P(("narrow", "wide"), None),
        P(),
        P(None, "wide", None),
        P("wide", None),
        P("wide", None),
        P("wide", None),
        P(),
        P(None, "wide"),
        P(),
        P("wide"),
        P(),
        P("wide"),
        P(),
        P("wide"),
        P(),
        P(),
    )
    return jax.shard_map(
        shards,
        mesh=mesh,
        in_specs=placed,
        out_specs=(
            P(("narrow", "wide"), None),
            P(("narrow", "wide"), None),
            P(None, "wide", None),
            P("wide", None),
            P("wide", None),
            P("wide", None),
            P(),
            P(None, "wide"),
            P(),
            P("wide"),
            P(),
            P("wide"),
            P(),
            P("wide"),
            P(),
            P(),
            P(None, "wide", None),
            P("wide", None),
            P("wide", None),
            P("wide", None),
            P(),
        ),
        check_vma=False,
    )
```

```python
import functools
import math

import jax
import jax.numpy as jnp
import numpy as np
from jax import lax
from jax.experimental import pallas as pl
from jax.experimental.pallas import tpu as pltpu
from jax.sharding import PartitionSpec as P

D = 768
HEADS = 12
HD = 64
FF = 3072
FEAT = 32
STEP = 10
LEN = 1024
SPAN = 256
CHUNKS = 3
GROUPS = 3
WIDTH = 256
FFC = FF // CHUNKS

norm_eps = 1e-05
square_eps = 1e-30
clip_level = 1.0

F32 = jnp.float32
BF16 = jnp.bfloat16
VMEM_LIMIT = 60 * 1024 * 1024


def mm(left, right):
    return lax.dot_general(left, right, (((1,), (0,)), ((), ())), preferred_element_type=F32)


def mm_nt(left, right):
    return lax.dot_general(left, right, (((1,), (1,)), ((), ())), preferred_element_type=F32)


def mm_tn(left, right):
    return lax.dot_general(left, right, (((0,), (0,)), ((), ())), preferred_element_type=F32)


def halves(values):
    high = values.astype(BF16)
    return high, (values - high.astype(F32)).astype(BF16)


TAIL = (
    0.1795078068971634,
    0.17978088557720184,
    0.14234966039657593,
    0.06379217654466629,
    0.0434231162071228,
    -0.261725515127182,
    0.20454804599285126,
    -0.05167665705084801,
)


def normal_parts(values):
    size = jnp.abs(values)
    t = 1.0 / (1.0 + 0.45 * size)
    poly = TAIL[-1]
    for coeff in TAIL[-2::-1]:
        poly = poly * t + coeff
    bell = jnp.exp(-0.5 * values * values)
    tail = poly * t * bell
    return jnp.where(values >= 0, 1.0 - tail, tail), bell * 0.3989422804014327


def transposed(values):
    row = lax.broadcasted_iota(jnp.int32, (256, 256), 0)
    col = lax.broadcasted_iota(jnp.int32, (256, 256), 1)
    eye = (row == col).astype(F32).astype(BF16)
    return mm_nt(eye, values).astype(BF16)


def head_perm():
    perm = np.zeros((WIDTH, WIDTH), np.float32)
    for head in range(4):
        for half in range(2):
            for i in range(32):
                perm[head * 64 + half * 32 + i, half * 128 + head * 32 + i] = 1.0
    return perm


def make_blocks(lengths, base, first, last):
    def step(s, carry):
        count, begin, begin_row, end = carry
        new_end = end + lengths[0, s]
        full = new_end - begin_row > SPAN

        @pl.when(full)
        def _():
            base[count] = begin_row
            first[count] = begin
            last[count] = s - 1

        row = jnp.minimum((end // 16) * 16, LEN - SPAN)
        return (
            jnp.where(full, count + 1, count),
            jnp.where(full, s, begin),
            jnp.where(full, row, begin_row),
            new_end,
        )

    segments = lengths.shape[1]
    zero = jnp.int32(0)
    count, begin, begin_row, _ = lax.fori_loop(0, segments, step, (zero, zero, zero, zero))
    base[count] = begin_row
    first[count] = begin
    last[count] = segments - 1
    return count + 1


def lane_mask(lo, hi, width, dtype):
    lane = lax.broadcasted_iota(jnp.int32, (1, width), 1)
    return ((lane >= lo) & (lane < hi)).astype(F32).astype(dtype)


def value_rows(v_pair, head):
    keep = lane_mask(64 * head, 64 * head + 64, 128, BF16)
    return jnp.concatenate([v_pair * keep, jnp.broadcast_to(keep, v_pair.shape)], axis=1)


def span_mask(onehot, rows, lo, hi):
    member = onehot[rows, :]
    lane = lax.broadcasted_iota(jnp.int32, (1, 128), 1)
    inside = ((lane >= lo) & (lane <= hi)).astype(F32).astype(BF16)
    return mm_nt(member * inside, member).astype(BF16)


def cost(flops, size):
    return pl.CostEstimate(flops=10**6, transcendentals=0, bytes_accessed=10**5)


def row_blocks(body):
    def step(index, carry):
        body(pl.ds(pl.multiple_of(index * 256, 256), 256))
        return carry

    lax.fori_loop(0, LEN // 256, step, 0)


def any_spec():
    return pl.BlockSpec(memory_space=pl.ANY)


def in_copies(place, pieces, dst, sems, unit):
    if len(pieces) == 1:
        rows = dst.shape[1] // 3
        here = pl.ds(unit * rows, rows)
        return [pltpu.make_async_copy(pieces[0].at[:, here], dst.at[:, here], sems.at[unit, 0])]
    z, x, core = place[0], place[1], place[3]
    part, index = (0, unit) if unit < 2 else (4, 0)
    copies = []
    for side in range(2):
        half = core if side == 0 else 1 - core
        for flip in range(2):
            column = x if flip == 0 else 1 - x
            for shift in range(4):
                row = lax.rem(z + 4 - shift, 4) * 2 + column
                start = pl.multiple_of(unit * 96 + half * 48, 16)
                copies.append(
                    pltpu.make_async_copy(
                        pieces[part + 2 * side + flip].at[shift, index],
                        dst.at[row, pl.ds(start, 48)],
                        sems.at[unit, len(copies)],
                    )
                )
    return copies


def flat_copies(place, pieces, dst, sems):
    if len(pieces) == 1:
        return [pltpu.make_async_copy(pieces[0], dst, sems.at[0])]
    z, x, core = place[0], place[1], place[3]
    span = dst.shape[1] // 2
    copies = []
    for side in range(2):
        half = core if side == 0 else 1 - core
        for flip in range(2):
            column = x if flip == 0 else 1 - x
            for shift in range(4):
                row = lax.rem(z + 4 - shift, 4) * 2 + column
                start = pl.multiple_of(half * span, 16)
                copies.append(
                    pltpu.make_async_copy(
                        pieces[2 * side + flip].at[shift],
                        dst.at[row, pl.ds(start, span)],
                        sems.at[len(copies)],
                    )
                )
    return copies


def attend_kernel(count_in, lengths, place, *refs):
    pieces = refs[:count_in]
    (
        x_ref, norm_ref, bias_ref, perm_ref, proj_ref, cos_ref, sin_ref, onehot_ref,
        attn_ref, mixed_ref, a1t_ref, w_ref, wq_ref, wk_ref, qf_ref, kf_ref, v_ref, rden_ref,
        a1, qb, kb, vb, parts, base, first, last, sems,
    ) = refs[count_in:]
    group = pl.program_id(0)

    @pl.when(group == 0)
    def _():
        for unit in range(GROUPS):
            for copy in in_copies(place, pieces, w_ref, sems, unit):
                copy.start()
        def norm_rows(here):
            x = x_ref[here, :].astype(F32)
            centre = x - jnp.mean(x, axis=-1, keepdims=True)
            spread = jnp.mean(centre * centre, axis=-1, keepdims=True)
            a1[here, :] = (
                centre * lax.rsqrt(spread + norm_eps) * norm_ref[0:1, :] + norm_ref[1:2, :]
            ).astype(BF16)

        row_blocks(norm_rows)
        for cols in range(0, D, 256):
            a1t_ref[cols : cols + 256, :] = transposed(a1[:, cols : cols + 256])

    for unit in range(GROUPS):

        @pl.when(group == unit)
        def _():
            for copy in in_copies(place, pieces, w_ref, sems, unit):
                copy.wait()

    count = make_blocks(lengths, base, first, last)
    shard = w_ref.shape[1] // 3
    here = pl.ds(pl.multiple_of(group * shard, 16), shard)
    w = w_ref[:, here, :].reshape(D, D)
    perm = perm_ref[...]
    bias = bias_ref[0]
    proj_both = proj_ref[0]
    proj_high = proj_ref[1, :, :128]
    square = proj_ref[2, :, :128]
    weights = [mm(w[:, WIDTH * i : WIDTH * (i + 1)], perm).astype(BF16) for i in range(2)]

    def feature_rows(here):
        for which, (out_w, out_f, low_f) in enumerate(
            ((wq_ref, qf_ref, qb), (wk_ref, kf_ref, kb))
        ):
            u = (mm(a1[here, :], weights[which]) + bias[which : which + 1, :]) * HD ** (-0.25)
            c = u[:, :128]
            e = u[:, 128:]
            cosine = cos_ref[here, :]
            sine = sin_ref[here, :]
            turned = jnp.concatenate([c * cosine - e * sine, e * cosine + c * sine], axis=1)
            out_w[0, here, :] = turned
            high, low = halves(turned)
            sq_high, sq_low = halves(turned * turned)
            both = mm(high, proj_both)
            logits = (
                both[:, :128] + both[:, 128:] + mm(low, proj_high)
                - (mm(sq_high, square) + mm(sq_low, square))
            )
            phi = jnp.exp(logits) * FEAT ** (-0.5)
            out_f[0, here, :] = phi
            low_f[here, :] = phi.astype(BF16)
        v = mm(a1[here, :], w[:, 2 * WIDTH :]) + bias[2:3, :]
        v_ref[0, here, :] = v
        vb[here, :] = v.astype(BF16)

    row_blocks(feature_rows)
    parts[...] = jnp.zeros_like(parts)

    def one_span(index, carry):
        rows = pl.ds(pl.multiple_of(base[index], 16), SPAN)
        mask = span_mask(onehot_ref, rows, first[index], last[index])
        q = qb[rows, :]
        k = kb[rows, :]
        for pair in range(2):
            v_pair = vb[rows, 128 * pair : 128 * (pair + 1)]
            total = jnp.zeros((SPAN, WIDTH), F32)
            for side in range(2):
                head = 2 * pair + side
                scores = mm_nt(q * lane_mask(32 * head, 32 * head + 32, 128, BF16), k)
                total = total + mm(scores.astype(BF16) * mask, value_rows(v_pair, side))
            parts[pair, rows, :] += total
        return carry

    lax.fori_loop(0, count, one_span, 0)
    for pair in range(2):
        lanes = slice(128 * pair, 128 * (pair + 1))
        inverse = 1.0 / parts[pair, :, 128:]
        rden_ref[0, :, lanes] = inverse
        mixed = parts[pair, :, :128] * inverse
        mixed_ref[0, :, lanes] = mixed
        attn_ref[:, lanes] = mixed.astype(BF16)


def whole_spec(shape, **options):
    return pl.BlockSpec(shape, lambda *_: (0,) * len(shape), **options)


def group_spec(shape):
    return pl.BlockSpec((1,) + shape, lambda g, *_: (g,) + (0,) * len(shape))


def attend(lengths, place, pieces, wide, tokens, norm, bias, perm, proj, cosine, sine, onehot):
    def out(shape, dtype):
        return jax.ShapeDtypeStruct((GROUPS,) + shape, dtype)

    rows_in = 3 * D // wide
    return pl.pallas_call(
        functools.partial(attend_kernel, len(pieces)),
        grid_spec=pltpu.PrefetchScalarGridSpec(
            num_scalar_prefetch=2,
            grid=(GROUPS,),
            in_specs=[any_spec()] * len(pieces)
            + [
                whole_spec((LEN, D)), whole_spec((2, D)), group_spec((3, WIDTH)),
                whole_spec((WIDTH, WIDTH)), whole_spec((3, WIDTH, WIDTH)), whole_spec((LEN, 128)),
                whole_spec((LEN, 128)), whole_spec((LEN, 128)),
            ],
            out_specs=[
                pl.BlockSpec((LEN, WIDTH), lambda g, *_: (0, g)), group_spec((LEN, WIDTH)),
                whole_spec((D, LEN)), whole_spec((wide, rows_in, D)), group_spec((LEN, WIDTH)),
                group_spec((LEN, WIDTH)), group_spec((LEN, 128)), group_spec((LEN, 128)),
                group_spec((LEN, WIDTH)), group_spec((LEN, WIDTH)),
            ],
            scratch_shapes=[
                pltpu.VMEM((LEN, D), BF16),
                pltpu.VMEM((LEN, 128), BF16), pltpu.VMEM((LEN, 128), BF16),
                pltpu.VMEM((LEN, WIDTH), BF16), pltpu.VMEM((2, LEN, WIDTH), F32),
                pltpu.SMEM((32,), jnp.int32), pltpu.SMEM((32,), jnp.int32),
                pltpu.SMEM((32,), jnp.int32), pltpu.SemaphoreType.DMA((GROUPS, 16)),
            ],
        ),
        out_shape=[
            jax.ShapeDtypeStruct((LEN, D), BF16), out((LEN, WIDTH), F32),
            jax.ShapeDtypeStruct((D, LEN), BF16), jax.ShapeDtypeStruct((wide, rows_in, D), BF16),
            out((LEN, WIDTH), F32), out((LEN, WIDTH), F32), out((LEN, 128), F32),
            out((LEN, 128), F32), out((LEN, WIDTH), F32), out((LEN, WIDTH), F32),
        ],
        compiler_params=pltpu.CompilerParams(
            dimension_semantics=("arbitrary",), vmem_limit_bytes=VMEM_LIMIT
        ),
        cost_estimate=cost(20 * 10**9, 40 * 10**6),
        name="attend",
    )(lengths, place, *pieces, tokens, norm, bias, perm, proj, cosine, sine, onehot)


def attend_back_kernel(
    lengths, place, dmixed_ref, mixed_ref, rden_ref, wq_ref, wk_ref, qf_ref, kf_ref, v_ref,
    a1t_ref, w_ref, perm_ref, proj_ref, cos_ref, sin_ref, onehot_ref, ones_ref,
    keep_ref, send_ref, bias_ref, da1_ref,
    qb, kb, dnb, dnh, lift, dqf, dkf, dv, dqkv, base, first, last,
):
    count = make_blocks(lengths, base, first, last)
    qb[...] = qf_ref[0].astype(BF16)
    kb[...] = kf_ref[0].astype(BF16)
    lane = lax.broadcasted_iota(jnp.int32, (1, 128), 1)
    ones = ones_ref[...]
    def lift_rows(here):
        for pair in range(2):
            lanes = slice(128 * pair, 128 * (pair + 1))
            dnum = dmixed_ref[here, lanes] * rden_ref[0, here, lanes]
            high, low = halves(dnum)
            dnb[here, lanes] = high
            part_high, part_low = halves(dnum * mixed_ref[0, here, lanes])
            dden = -mm(jnp.concatenate([part_high, part_low], axis=1), ones)
            den_high, den_low = halves(dden)
            high, low = high.astype(F32), low.astype(F32)
            den_high = pltpu.roll(den_high.astype(F32), 64, 1)
            den_low = pltpu.roll(den_low.astype(F32), 64, 1)
            low_far = pltpu.roll(low, 64, 1)
            v = v_ref[0, here, lanes]
            v_high, v_low = halves(v)
            v_high, v_low = v_high.astype(F32), v_low.astype(F32)
            v_far = pltpu.roll(v_high, 64, 1)
            for side in range(2):
                own = (lane >= 64 * side) & (lane < 64 * side + 64)
                mark = 64 - 64 * side
                rest = jnp.where(lane == mark, den_high, jnp.where(lane == mark + 1, den_low, 0.0))
                both = ((lane == mark) | (lane == mark + 1)).astype(F32)
                head = 2 * pair + side
                dnh[head, here, :128] = jnp.where(own, high, low_far).astype(BF16)
                dnh[head, here, 128:] = jnp.where(own, high, rest).astype(BF16)
                lift[head, here, :128] = jnp.where(own, v_high, v_far).astype(BF16)
                lift[head, here, 128:] = jnp.where(own, v_low, both).astype(BF16)
    row_blocks(lift_rows)
    dqf[...] = jnp.zeros_like(dqf)
    dkf[...] = jnp.zeros_like(dkf)
    dv[...] = jnp.zeros_like(dv)

    def one_span(index, carry):
        rows = pl.ds(pl.multiple_of(base[index], 16), SPAN)
        mask = span_mask(onehot_ref, rows, first[index], last[index])
        q = qb[rows, :]
        k = kb[rows, :]
        q_total = jnp.zeros((SPAN, 128), F32)
        k_total = jnp.zeros((SPAN, 128), F32)
        for pair in range(2):
            lanes = slice(128 * pair, 128 * (pair + 1))
            dn_pair = dnb[rows, lanes]
            v_total = jnp.zeros((SPAN, 128), F32)
            for side in range(2):
                head = 2 * pair + side
                feats = lane_mask(32 * head, 32 * head + 32, 128, BF16)
                q_head = q * feats
                k_head = k * feats
                lifted = lift[head, rows, :]
                dn_head = dnh[head, rows, :]
                scores = mm_nt(k, q_head).astype(BF16) * mask
                dscores = mm_nt(dn_head, lifted).astype(BF16) * mask
                dscores_t = mm_nt(lifted, dn_head).astype(BF16) * mask
                q_total = q_total + mm(dscores, k_head)
                k_total = k_total + mm(dscores_t, q_head)
                own = lane_mask(64 * side, 64 * side + 64, 128, BF16)
                v_total = v_total + mm(scores, dn_pair * own)
            dv[rows, lanes] += v_total
        dqf[rows, :] += q_total
        dkf[rows, :] += k_total
        return carry

    lax.fori_loop(0, count, one_span, 0)
    proj_low = proj_ref[0, :, 128:]
    proj_high = proj_ref[1]
    square = proj_ref[2]
    perm = perm_ref[...]
    def feature_rows(here):
        for which, (w_in, phi_in, dphi) in enumerate(
            ((wq_ref, qf_ref, dqf), (wk_ref, kf_ref, dkf))
        ):
            r = dphi[here, :] * phi_in[0, here, :]
            high, low = halves(r)
            both = jnp.concatenate([high, low], axis=1)
            spread = mm_nt(both, square)
            dw = mm_nt(both, proj_high) + mm_nt(high, proj_low)
            du = (dw - 2.0 * w_in[0, here, :] * spread) * HD ** (-0.25)
            c = du[:, :128]
            e = du[:, 128:]
            cosine = cos_ref[here, :]
            sine = sin_ref[here, :]
            turned = jnp.concatenate([c * cosine + e * sine, e * cosine - c * sine], axis=1)
            dqkv[here, WIDTH * which : WIDTH * (which + 1)] = mm_nt(
                turned.astype(BF16), perm
            ).astype(BF16)

    row_blocks(feature_rows)
    dqkv[:, 2 * WIDTH :] = dv[...].astype(BF16)
    bias_ref[0] = jnp.sum(dqkv[...].astype(F32), axis=0, keepdims=True)
    grad = mm(a1t_ref[...], dqkv[...]).astype(BF16)
    store_halves(grad, place[3], keep_ref.at[0], send_ref.at[0])
    w = w_ref[...].reshape(D, D)
    fresh = pl.program_id(0) == 0

    @pl.when(fresh)
    def _():
        da1_ref[...] = mm_nt(dqkv[...], w)

    @pl.when(jnp.logical_not(fresh))
    def _():
        da1_ref[...] += mm_nt(dqkv[...], w)


def store_halves(grad, core, keep_ref, send_ref):
    wide, rows = keep_ref.shape[0], D // keep_ref.shape[0]
    half = rows // 2
    parts = grad.reshape(wide, rows, D)
    for cols in range(3):
        block = parts[:, :, WIDTH * cols : WIDTH * (cols + 1)]
        here = pl.ds(half * cols, half)

        @pl.when(core == 0)
        def _():
            keep_ref[:, here, :] = block[:, :half]
            send_ref[:, here, :] = block[:, half:]

        @pl.when(core == 1)
        def _():
            keep_ref[:, here, :] = block[:, half:]
            send_ref[:, here, :] = block[:, :half]


def attend_back(
    lengths, place, wide, dmixed, saved, a1t, w_in, perm, proj, cosine, sine, onehot, ones
):
    mixed, rden, wq, wk, qf, kf, v = saved

    def by_group(shape):
        return pl.BlockSpec((1,) + shape, lambda g, *_: (g,) + (0,) * len(shape))

    rows_in = D // wide
    half = struct((GROUPS, wide, 3 * rows_in // 2, WIDTH), BF16)
    half_spec = group_spec(half.shape[1:])
    return pl.pallas_call(
        attend_back_kernel,
        grid_spec=pltpu.PrefetchScalarGridSpec(
            num_scalar_prefetch=2,
            grid=(GROUPS,),
            in_specs=[
                pl.BlockSpec((LEN, WIDTH), lambda g, *_: (0, g)),
                by_group((LEN, WIDTH)), by_group((LEN, WIDTH)), by_group((LEN, WIDTH)),
                by_group((LEN, WIDTH)), by_group((LEN, 128)), by_group((LEN, 128)),
                by_group((LEN, WIDTH)), once((D, LEN)),
                pl.BlockSpec((wide, rows_in, D), lambda g, *_: (0, g, 0)),
                once((WIDTH, WIDTH)), once((3, WIDTH, WIDTH)), once((LEN, 128)),
                once((LEN, 128)), once((LEN, 128)), once((WIDTH, 128)),
            ],
            out_specs=[
                half_spec, half_spec, group_spec((1, D)),
                whole_spec((LEN, D)),
            ],
            scratch_shapes=[
                pltpu.VMEM((LEN, 128), BF16), pltpu.VMEM((LEN, 128), BF16),
                pltpu.VMEM((LEN, WIDTH), BF16), pltpu.VMEM((4, LEN, WIDTH), BF16),
                pltpu.VMEM((4, LEN, WIDTH), BF16), pltpu.VMEM((LEN, 128), F32),
                pltpu.VMEM((LEN, 128), F32), pltpu.VMEM((LEN, WIDTH), F32),
                pltpu.VMEM((LEN, D), BF16),
                pltpu.SMEM((32,), jnp.int32), pltpu.SMEM((32,), jnp.int32),
                pltpu.SMEM((32,), jnp.int32),
            ],
        ),
        out_shape=[
            half, half, struct((GROUPS, 1, D), F32), struct((LEN, D), F32),
        ],
        compiler_params=pltpu.CompilerParams(
            dimension_semantics=("arbitrary",), vmem_limit_bytes=VMEM_LIMIT
        ),
        cost_estimate=cost(GROUPS * 12 * 10**9, GROUPS * 20 * 10**6),
        name="attend_back",
    )(
        lengths, place, dmixed, mixed, rden, wq, wk, qf, kf, v, a1t, w_in, perm, proj, cosine,
        sine, onehot, ones,
    )


def chunk_step(
    place, wide, bias_up, dy_ref, a2, a2t, dyt, up, down, act, dhidden, y, back, outs, dbias_ref,
    fresh,
):
    rows_up = D // wide
    rows_down = FFC // wide
    dbias_ref[0] = jnp.zeros((1, FFC), F32)

    def chunk_rows(here):
        hidden = mm(a2[here, :], up[...]) + bias_up
        below, density = normal_parts(hidden)
        act_now = (hidden * below).astype(BF16)
        act[here, :] = act_now
        dact = mm_nt(dy_ref[here, :], down[...])
        dhidden_now = (dact * (below + hidden * density)).astype(BF16)
        dhidden[here, :] = dhidden_now
        dbias_ref[0] += jnp.sum(dhidden_now.astype(F32), axis=0, keepdims=True)
        if fresh:
            y[here, :] = mm(act_now, down[...])
            back[here, :] = mm_nt(dhidden_now, up[...])
        else:
            y[here, :] += mm(act_now, down[...])
            back[here, :] += mm_nt(dhidden_now, up[...])

    row_blocks(chunk_rows)
    grad_up = mm(a2t[...], dhidden[...]).astype(BF16).reshape(wide, rows_up, FFC)
    grad_down = mm(dyt[...], act[...]).astype(BF16)
    core = place[3]

    def store_up(ref):
        for cols in range(4):
            ref[:, rows_up * cols : rows_up * (cols + 1), :] = grad_up[
                :, :, WIDTH * cols : WIDTH * (cols + 1)
            ]

    def store_down(ref):
        if wide == 1:
            for cols in range(4):
                ref[0, D * cols : D * (cols + 1), :] = grad_down[
                    :, WIDTH * cols : WIDTH * (cols + 1)
                ]
            return
        for shard in range(wide):
            block = grad_down[:, rows_down * shard : rows_down * (shard + 1)]
            ref[shard, :, :128] = block[: D // 2]
            ref[shard, :, 128:] = block[D // 2 :]

    for when, keep_ref, send_ref in outs:
        for side in range(2):
            now = core == side

            @pl.when(now if when is None else now & when)
            def _():
                store_up(keep_ref if side == 0 else send_ref)
                store_down(send_ref if side == 0 else keep_ref)


def load_up(flat, at, up, wide):
    rows = D // wide
    for cols in range(4):
        here = pl.ds(at + rows * cols, rows)
        up[:, WIDTH * cols : WIDTH * (cols + 1)] = flat[:, here, :].reshape(D, WIDTH)


def load_down(flat, at, down, wide):
    rows = FFC // wide
    for cols in range(3):
        here = pl.ds(at + rows * cols, rows)
        down[:, WIDTH * cols : WIDTH * (cols + 1)] = flat[:, here, :].reshape(FFC, WIDTH)


def middle_first_kernel(wide, count_in, place, *refs):
    pieces = refs[:count_in]
    (
        x_ref, attn_ref, dy_ref, rows_ref, bias_up_ref,
        x1_ref, a2_ref, a2t_ref, dyt_ref, y_ref, back_ref, out_ref, keep_ref, send_ref, dbias_ref,
        flat, up, down, act, dhidden, sems,
    ) = refs[count_in:]
    copies = flat_copies(place, pieces, flat, sems)
    for copy in copies:
        copy.start()
    for cols in range(0, D, 256):
        dyt_ref[cols : cols + 256, :] = transposed(dy_ref[:, cols : cols + 256])
    for copy in copies:
        copy.wait()
    half_out = D // wide // 2
    half_flat = flat.shape[1] // 2
    for cols in range(3):
        upper = flat[:, half_out * cols : half_out * (cols + 1), :]
        lower = flat[:, half_flat + half_out * cols : half_flat + half_out * (cols + 1), :]
        out_ref[:, WIDTH * cols : WIDTH * (cols + 1)] = jnp.concatenate(
            [upper, lower], axis=1
        ).reshape(D, WIDTH)
    def norm_rows(here):
        x1 = x_ref[here, :].astype(F32) + (mm(attn_ref[here, :], out_ref[...]) + rows_ref[7:8, :])
        x1_ref[here, :] = x1
        centre = x1 - jnp.mean(x1, axis=-1, keepdims=True)
        spread = jnp.mean(centre * centre, axis=-1, keepdims=True)
        a2_ref[here, :] = (
            centre * lax.rsqrt(spread + norm_eps) * rows_ref[2:3, :] + rows_ref[3:4, :]
        ).astype(BF16)

    row_blocks(norm_rows)
    for cols in range(0, D, 256):
        a2t_ref[cols : cols + 256, :] = transposed(a2_ref[:, cols : cols + 256])
    load_up(flat, 3 * half_out, up, wide)
    load_down(flat, half_flat + 3 * half_out, down, wide)
    chunk_step(
        place, wide, bias_up_ref[0], dy_ref, a2_ref, a2t_ref, dyt_ref, up, down, act, dhidden,
        y_ref, back_ref, [(None, keep_ref, send_ref)], dbias_ref, True,
    )


def middle_rest_kernel(wide, count_in, place, *refs):
    pieces = refs[:count_in]
    (
        dy_ref, a2_ref, a2t_ref, dyt_ref, bias_up_ref, attn_ref, out_ref, rows_ref,
        y_in, back_in, x1_in,
        block_ref, dx1_ref, dmixed_ref, okeep_ref, osend_ref, vec_ref,
        keep_ref, send_ref, dbias_ref,
        flat, up, down, act, dhidden, back, dbranch, sems, flat_sems,
    ) = refs[count_in:]
    step = pl.program_id(0)
    y_copy = pltpu.make_async_copy(y_in, block_ref, sems.at[0])
    back_copy = pltpu.make_async_copy(back_in, back, sems.at[1])
    x1_copy = pltpu.make_async_copy(x1_in, dx1_ref, sems.at[2])

    def chunk_copies(chunk, side):
        if count_in == 1:
            return [
                pltpu.make_async_copy(
                    pieces[0].at[chunk], flat.at[chunk], flat_sems.at[chunk, 0]
                )
            ]
        copies = []
        for flip in range(2):
            column = place[1] if flip == 0 else 1 - place[1]
            for shift in range(4):
                shard = lax.rem(place[0] + 4 - shift, 4) * 2 + column
                copies.append(
                    pltpu.make_async_copy(
                        pieces[2 * side + flip].at[shift], flat.at[chunk, shard],
                        flat_sems.at[chunk, len(copies)],
                    )
                )
        return copies

    def fetch(chunk):
        for side in range(2):

            @pl.when((place[3] == chunk) if side == 0 else (place[3] != chunk))
            def _():
                if side == 0 or count_in > 1:
                    for copy in chunk_copies(chunk, side):
                        copy.start()

    def arrived(chunk):
        for copy in chunk_copies(chunk, 0):
            copy.wait()

    @pl.when(step == 0)
    def _():
        if count_in == 1:
            for chunk in range(2):
                for copy in chunk_copies(chunk, 0):
                    copy.start()
        else:
            fetch(0)
        y_copy.start()
        back_copy.start()
        if count_in > 1:
            fetch(1)
        x1_copy.start()
        arrived(0)
        y_copy.wait()
        back_copy.wait()

    @pl.when(step == 1)
    def _():
        arrived(1)

    load_up(flat.at[step], 0, up, wide)
    load_down(flat.at[step], 4 * (D // wide), down, wide)
    chunk_step(
        place, wide, bias_up_ref[0], dy_ref, a2_ref, a2t_ref, dyt_ref, up, down, act, dhidden,
        block_ref, back, [(None, keep_ref.at[0], send_ref.at[0])], dbias_ref, False,
    )

    @pl.when(step == 1)
    def _():
        x1_copy.wait()
        vec_ref[...] = jnp.zeros_like(vec_ref)

        def last_rows(here):
            x1 = dx1_ref[here, :]
            block_ref[here, :] = x1 + (block_ref[here, :] + rows_ref[8:9, :])
            dn = back[here, :]
            dy = dy_ref[here, :].astype(F32)
            centre = x1 - jnp.mean(x1, axis=-1, keepdims=True)
            spread = jnp.mean(centre * centre, axis=-1, keepdims=True)
            scale = lax.rsqrt(spread + norm_eps)
            zh = centre * scale
            vec_ref[0:1, :] += jnp.sum(dn * zh, axis=0, keepdims=True)
            vec_ref[1:2, :] += jnp.sum(dn, axis=0, keepdims=True)
            e = dn * rows_ref[2:3, :]
            dz = (
                e
                - jnp.mean(e, axis=-1, keepdims=True)
                - zh * jnp.mean(e * zh, axis=-1, keepdims=True)
            ) * scale
            dx1 = dy + dz
            dx1_ref[here, :] = dx1
            low = dx1.astype(BF16)
            dbranch[here, :] = low
            vec_ref[2:3, :] += jnp.sum(low.astype(F32), axis=0, keepdims=True)
            vec_ref[3:4, :] += jnp.sum(dy, axis=0, keepdims=True)
            dmixed_ref[here, :] = mm_nt(low, out_ref[...])

        row_blocks(last_rows)
        for cols in range(0, D, 256):
            up[cols : cols + 256, :] = transposed(attn_ref[:, cols : cols + 256])
        store_halves(mm(up[...], dbranch[...]).astype(BF16), place[3], okeep_ref, osend_ref)


def once(shape):
    return whole_spec(shape, pipeline_mode=pl.Buffered(1))


def struct(shape, dtype):
    return jax.ShapeDtypeStruct(shape, dtype)


def weight_scratch():
    return [
        pltpu.VMEM((D, FFC), BF16), pltpu.VMEM((FFC, D), BF16), pltpu.VMEM((LEN, FFC), BF16),
        pltpu.VMEM((LEN, FFC), BF16),
    ]


def middle_first(place, wide, pieces, tokens, attn, cotangent, vectors, bias_up):
    rows_flat = 3 * D // wide + 2 * FFC * D // (WIDTH * wide)
    half = (wide, FFC * D // (WIDTH * wide), WIDTH)
    outs = [
        struct((LEN, D), F32), struct((LEN, D), BF16), struct((D, LEN), BF16),
        struct((D, LEN), BF16), struct((LEN, D), F32), struct((LEN, D), F32),
        struct((D, D), BF16), struct(half, BF16), struct(half, BF16), struct((1, 1, FFC), F32),
    ]
    return pl.pallas_call(
        functools.partial(middle_first_kernel, wide, len(pieces)),
        grid_spec=pltpu.PrefetchScalarGridSpec(
            num_scalar_prefetch=1,
            grid=(1,),
            in_specs=[any_spec()] * len(pieces)
            + [
                once((LEN, D)), once((LEN, D)), once((LEN, D)), once((13, D)),
                pl.BlockSpec((1, 1, FFC), lambda *_: (0, 0, 0)),
            ],
            out_specs=[once(out.shape) for out in outs],
            scratch_shapes=[pltpu.VMEM((wide, rows_flat, WIDTH), BF16)]
            + weight_scratch()
            + [pltpu.SemaphoreType.DMA((16,))],
        ),
        out_shape=outs,
        compiler_params=pltpu.CompilerParams(
            dimension_semantics=("arbitrary",), vmem_limit_bytes=VMEM_LIMIT
        ),
        cost_estimate=cost(14 * 10**9, 30 * 10**6),
        name="middle_first",
    )(place, *pieces, tokens, attn, cotangent, vectors, bias_up)


def middle_rest(place, wide, pieces, cotangent, state, bias_up, attn, w_out, vectors, sums):
    a2, a2t, dyt = state
    half = (wide, FFC * D // (WIDTH * wide), WIDTH)
    out_half = (wide, 3 * D // (2 * wide), WIDTH)
    outs = [
        struct((LEN, D), F32), struct((LEN, D), F32), struct((LEN, D), F32),
        struct(out_half, BF16), struct(out_half, BF16), struct((8, D), F32),
        struct((2,) + half, BF16), struct((2,) + half, BF16), struct((2, 1, FFC), F32),
    ]
    out_specs = [once(out.shape) for out in outs[:6]]
    out_specs += [group_spec(half), group_spec(half), group_spec((1, FFC))]
    rows_flat = 2 * FFC * D // (WIDTH * wide)
    return pl.pallas_call(
        functools.partial(middle_rest_kernel, wide, len(pieces)),
        grid_spec=pltpu.PrefetchScalarGridSpec(
            num_scalar_prefetch=1,
            grid=(2,),
            in_specs=[any_spec()] * len(pieces)
            + [
                once((LEN, D)), once((LEN, D)), once((D, LEN)), once((D, LEN)),
                pl.BlockSpec((1, 1, FFC), lambda j, *_: (j + 1, 0, 0)),
                once((LEN, D)), once((D, D)), once((13, D)),
                any_spec(), any_spec(), any_spec(),
            ],
            out_specs=out_specs,
            scratch_shapes=[pltpu.VMEM((2, wide, rows_flat, WIDTH), BF16)]
            + weight_scratch()
            + [
                pltpu.VMEM((LEN, D), F32), pltpu.VMEM((LEN, D), BF16),
                pltpu.SemaphoreType.DMA((3,)), pltpu.SemaphoreType.DMA((2, 8)),
            ],
        ),
        out_shape=outs,
        compiler_params=pltpu.CompilerParams(
            dimension_semantics=("arbitrary",), vmem_limit_bytes=VMEM_LIMIT
        ),
        cost_estimate=cost(28 * 10**9, 40 * 10**6),
        name="middle_rest",
    )(place, *pieces, cotangent, a2, a2t, dyt, bias_up, attn, w_out, vectors, *sums)


def input_kernel(
    wide, x_ref, dx1_ref, da1_ref, rows_ref, middle_ref, bias_in_ref, bias_first_ref, bias_rest_ref,
    out_ref, vec_ref,
):
    gain = rows_ref[0:1, :]
    x = x_ref[...].astype(F32)
    dn = da1_ref[...]
    centre = x - jnp.mean(x, axis=-1, keepdims=True)
    spread = jnp.mean(centre * centre, axis=-1, keepdims=True)
    scale = lax.rsqrt(spread + norm_eps)
    zh = centre * scale
    e = dn * gain
    dz = (
        e - jnp.mean(e, axis=-1, keepdims=True) - zh * jnp.mean(e * zh, axis=-1, keepdims=True)
    ) * scale
    out_ref[...] = dx1_ref[...] + dz

    @pl.when(pl.program_id(0) == 0)
    def _():
        vec_ref[...] = jnp.zeros_like(vec_ref)
        vec_ref[2:4, :] = middle_ref[0:2, :]
        vec_ref[7:9, :] = middle_ref[2:4, :]
        for group in range(GROUPS):
            lanes = slice(WIDTH * group, WIDTH * (group + 1))
            for which in range(3):
                vec_ref[4 + which : 5 + which, lanes] = bias_in_ref[
                    group, :, WIDTH * which : WIDTH * (which + 1)
                ]
        for chunk in range(CHUNKS):
            for part in range(8):
                value = (
                    bias_first_ref[0] if chunk == 0 else bias_rest_ref[chunk - 1]
                )[:, 128 * part : 128 * (part + 1)]
                start = FFC * chunk + 128 * part if wide == 1 else 384 * part + 128 * chunk
                row, lane = 9 + start // D, start % D
                vec_ref[row : row + 1, lane : lane + 128] = value

    vec_ref[0:1, :] += jnp.sum(dn * zh, axis=0, keepdims=True)
    vec_ref[1:2, :] += jnp.sum(dn, axis=0, keepdims=True)


def input_side(wide, tokens, dx1, da1, vectors, middle_vec, bias_in, bias_first, bias_rest):
    block = pl.BlockSpec((256, D), lambda i: (i, 0))
    return pl.pallas_call(
        functools.partial(input_kernel, wide),
        grid=(LEN // 256,),
        in_specs=[
            block, block, block, whole_spec((13, D)), whole_spec((8, D)),
            whole_spec((GROUPS, 1, D)), whole_spec((1, 1, FFC)), whole_spec((2, 1, FFC)),
        ],
        out_specs=[block, whole_spec((16, D))],
        out_shape=[struct((LEN, D), F32), struct((16, D), F32)],
        compiler_params=pltpu.CompilerParams(dimension_semantics=("arbitrary",)),
        cost_estimate=cost(10**6, 12 * 10**6),
        name="input_side",
    )(tokens, dx1, da1, vectors, middle_vec, bias_in, bias_first, bias_rest)


def tables(lengths, projection):
    ends = jnp.cumsum(lengths[0])
    starts = ends - lengths[0]
    place = jnp.arange(LEN, dtype=jnp.int32)
    member = (place[:, None] >= starts[None, :]) & (place[:, None] < ends[None, :])
    offset = jnp.sum(jnp.where(member, starts[None, :], 0), axis=1)
    position = (place - offset).astype(F32)
    freq = 10000.0 ** (-jnp.arange(32, dtype=F32) / 32)
    angles = position[:, None] * jnp.tile(freq, 4)[None, :]
    onehot = jnp.pad(member.astype(BF16), ((0, 0), (0, 128 - member.shape[1])))
    eye = jnp.asarray(np.eye(4, dtype=np.float32))
    lifted = jnp.einsum("hif,ab->haibf", projection.reshape(2, 32, FEAT), eye)
    lifted = lifted.reshape(WIDTH, 128)
    rounded = lax.reduce_precision(lifted, 8, 7)
    high, low = rounded.astype(BF16), (lifted - rounded).astype(BF16)
    square = np.zeros((2, 4, 32, 4, 32), np.float32)
    for head in range(4):
        square[:, head, :, head, :] = 0.5
    square = jnp.asarray(square.reshape(WIDTH, 128), BF16)
    proj = jnp.stack(
        [
            jnp.concatenate([high, low], axis=1),
            jnp.concatenate([high, high], axis=1),
            jnp.concatenate([square, square], axis=1),
        ]
    )
    return jnp.cos(angles), jnp.sin(angles), onehot, proj


def wide_perm(shift_z, flip_x):
    pairs = []
    for z in range(4):
        for x in range(2):
            target_x = 1 - x if flip_x else x
            pairs.append((2 * z + x, 2 * ((z + shift_z) % 4) + target_x))
    return pairs


def narrow_perm(flip_y, flip_core):
    pairs = []
    for y in range(2):
        for core in range(2):
            pairs.append(
                (2 * y + core, 2 * (1 - y if flip_y else y) + (1 - core if flip_core else core))
            )
    return pairs


def over_z(values, shift):
    return lax.ppermute(values, "wide", wide_perm(shift, False))


def over_x(values):
    return lax.ppermute(values, "wide", wide_perm(0, True))


def over_far(values, bit):
    return lax.ppermute(values, "wide", [(w, w ^ bit) for w in range(8)])


def over_y(values):
    return lax.ppermute(values, "narrow", narrow_perm(True, False))


def over_core(values):
    return lax.ppermute(values, "narrow", narrow_perm(False, True))


def tie(*values):
    return lax.optimization_barrier(values)


def special():
    return lax.axis_size("wide") == 8 and lax.axis_size("narrow") == 4


def sum_wide(values):
    if not special():
        return lax.psum(values, "wide")
    for perm in (wide_perm(0, True), [(w, w ^ 2) for w in range(8)], [(w, w ^ 4) for w in range(8)]):
        values = values + lax.ppermute(values, "wide", perm)
    return values


def sum_narrow(values):
    if not special():
        return lax.psum(values, "narrow")
    pair = values + over_core(values)
    return pair + over_y(pair)


def along_z(mine):
    return jnp.stack([mine] + [over_z(mine, shift) for shift in (1, 2, 3)])


def small_call(kernel, name, place, operands, outs):
    return pl.pallas_call(
        kernel,
        grid_spec=pltpu.PrefetchScalarGridSpec(
            num_scalar_prefetch=1,
            grid=(1,),
            in_specs=[once(value.shape) for value in operands],
            out_specs=[once(out.shape) for out in outs],
        ),
        out_shape=outs,
        compiler_params=pltpu.CompilerParams(
            dimension_semantics=("arbitrary",), vmem_limit_bytes=VMEM_LIMIT
        ),
        cost_estimate=cost(10**6, sum(4 * math.prod(v.shape) for v in operands + outs)),
        name=name,
    )(place, *operands)


def held_call(kernel, name, place, operands, outs, held=None):
    here = pl.BlockSpec(memory_space=pltpu.VMEM)
    held = len(outs) if held is None else held
    return pl.pallas_call(
        kernel,
        in_specs=[pl.BlockSpec(memory_space=pltpu.SMEM)] + [here] * len(operands),
        out_specs=[here] * len(outs),
        out_shape=[
            pltpu.VMEM(out.shape, out.dtype) if index < held else out
            for index, out in enumerate(outs)
        ],
        compiler_params=pltpu.CompilerParams(vmem_limit_bytes=24 * 1024 * 1024),
        cost_estimate=cost(10**6, 10**6),
        name=name,
    )(place, *[pltpu.with_memory_space_constraint(value, pltpu.VMEM) for value in operands])


def pick_kernel(
    place, in_ref, out_ref, up_ref, down_ref, near_ref, last_ref, first_ref, rest_ref
):
    core = place[3]
    here = pl.ds(pl.multiple_of(48 * core, 16), 48)
    for group in range(GROUPS):
        ref, index = (near_ref, group) if group < 2 else (last_ref, 0)
        for which in range(3):
            ref[index, :, WIDTH * which : WIDTH * (which + 1)] = in_ref[
                which, here, WIDTH * group : WIDTH * (group + 1)
            ].astype(BF16)
    for cols in range(3):
        first_ref[48 * cols : 48 * (cols + 1), :] = out_ref[
            here, WIDTH * cols : WIDTH * (cols + 1)
        ].astype(BF16)

    def put_up(ref, at, chunk):
        for cols in range(4):
            rows = slice(at + 96 * cols, at + 96 * (cols + 1))
            for side in range(2):
                start = 384 * (2 * cols + side) + 128 * chunk
                ref[rows, 128 * side : 128 * (side + 1)] = up_ref[:, start : start + 128].astype(
                    BF16
                )

    def put_down(ref, at, chunk):
        for cols in range(3):
            ref[at + 128 * cols : at + 128 * (cols + 1), :] = down_ref[
                128 * chunk : 128 * (chunk + 1), WIDTH * cols : WIDTH * (cols + 1)
            ].astype(BF16)

    for side in range(2):

        @pl.when(core == side)
        def _():
            if side == 0:
                put_up(first_ref, 144, 0)
            else:
                put_down(first_ref, 144, 0)

        @pl.when(core == side)
        def _():
            put_up(rest_ref, 0, 1 + side)
            put_down(rest_ref, 384, 1 + side)


def chunk_of(ref, chunk, shard):
    return ref[chunk, shard] if len(ref.shape) == 4 else ref[shard]


def first_sum_kernel(place, *refs):
    send_ref, keep_ref = refs[-2:]
    x = place[1]
    at = 0
    for index in range(0, len(refs) - 2, 2):
        own, got = refs[index], refs[index + 1]
        for part in range(own.shape[0] if len(own.shape) == 4 and own.shape[0] == 3 else 1):
            rows = own.shape[-2]
            here = pl.ds(at, rows)
            for z in range(4):
                for out, side in ((keep_ref, x), (send_ref, 1 - x)):
                    out[z, here, :] = (
                        chunk_of(own, part, 2 * z + side).astype(F32)
                        + chunk_of(got, part, 2 * z + side).astype(F32)
                    ).astype(BF16)
            at += rows


def first_sum(place, pairs):
    rows = sum(
        own.shape[-2] * (own.shape[0] if own.ndim == 4 and own.shape[0] == 3 else 1)
        for own, _ in pairs
    )
    return held_call(
        first_sum_kernel, "first_sum", place, [value for pair in pairs for value in pair],
        [struct((4, rows, WIDTH), BF16)] * 2,
    )


def second_sum_kernel(place, own_ref, got_ref, *outs):
    z = place[0]
    for shift, out in enumerate(outs):
        there = lax.rem(z + shift, 4)
        out[...] = (own_ref[there].astype(F32) + got_ref[there].astype(F32)).astype(BF16)


def second_sum(place, own, got):
    outs = [struct(own.shape[1:], BF16)] * 4
    return held_call(second_sum_kernel, "second_sum", place, [own, got], outs)


def z_sum_kernel(place, *refs):
    total = refs[0][...].astype(F32)
    for ref in refs[1:4]:
        total = total + ref[...].astype(F32)
    rows = refs[0].shape[0]
    refs[-1][:rows, :] = total.astype(BF16)
    if len(refs) == 7:
        refs[-1][rows:, :] = (refs[4][...].astype(F32) + refs[5][...].astype(F32)).astype(BF16)


def z_sum(place, parts, below=(), got=None):
    if got is None:
        got = [over_z(parts[shift], shift) for shift in (1, 2, 3)]
    rows = parts[0].shape[0] + (below[0].shape[0] if below else 0)
    return held_call(
        z_sum_kernel, "z_sum", place, [parts[0]] + got + list(below),
        [struct((rows, WIDTH), BF16)],
    )[0]


def first_sum_z_kernel(place, *refs):
    z = place[0]
    outs = refs[-4:]
    for shift, out in enumerate(outs):
        there = lax.rem(z + shift, 4) * 2
        at = 0
        for index in range(0, len(refs) - 4, 2):
            own, got = refs[index], refs[index + 1]
            rows = own.shape[-2]
            for x in range(2):
                out[x, at : at + rows, :] = (
                    chunk_of(own, 1, there + x).astype(F32)
                    + chunk_of(got, 1, there + x).astype(F32)
                ).astype(BF16)
            at += rows


def first_sum_z(place, pairs):
    rows = sum(own.shape[-2] for own, _ in pairs)
    return held_call(
        first_sum_z_kernel, "first_sum_z", place, [value for pair in pairs for value in pair],
        [struct((2, rows, WIDTH), BF16)] * 4,
    )


def split_sum_kernel(place, *refs):
    keep, send = refs[-2:]
    x = place[1]
    for out, at in ((keep, x), (send, 1 - x)):
        total = refs[0][at].astype(F32)
        for ref in refs[1:4]:
            total = total + ref[at].astype(F32)
        out[...] = total.astype(BF16)


def split_sum(place, parts):
    return held_call(
        split_sum_kernel, "split_sum", place, parts, [struct(parts[0].shape[1:], BF16)] * 2
    )


def to_row(column):
    size = column.shape[0]
    eye = lax.broadcasted_iota(jnp.int32, (size, size), 0) == lax.broadcasted_iota(
        jnp.int32, (size, size), 1
    )
    return jnp.sum(jnp.where(eye, column, 0.0), axis=0, keepdims=True)


def to_column(row):
    size = row.shape[1]
    eye = lax.broadcasted_iota(jnp.int32, (size, size), 0) == lax.broadcasted_iota(
        jnp.int32, (size, size), 1
    )
    return jnp.sum(jnp.where(eye, row, 0.0), axis=1, keepdims=True)


DECAY = 1.0 - STEP ** (-0.8)


def lane_values(values):
    lane = lax.broadcasted_iota(jnp.int32, (1, D), 1)
    row = jnp.zeros((1, D), F32)
    for index, value in enumerate(values):
        row = jnp.where(lane == index, value, row)
    return row


def moments(grad, rows_old):
    plain = grad * grad
    squares = plain + square_eps
    mean = jnp.sum(squares, axis=1, keepdims=True) * (1.0 / grad.shape[1])
    rows_new = DECAY * rows_old + (1.0 - DECAY) * to_row(mean)
    total = jnp.sum(rows_new, axis=1, keepdims=True)
    divided = jnp.sum(plain * to_column(1.0 / rows_new), axis=0, keepdims=True)
    return rows_new, total, jnp.sum(squares, axis=0, keepdims=True), divided


def ffn_moments_kernel(
    place, own, got, up_rows, down_rows, out_rows,
    up_grad, down_grad, out_grad, up_rows_new, down_rows_new, out_rows_new, sums,
):
    core = place[3]

    def collect(low, high):
        for chunk in range(CHUNKS):
            at = 384 * chunk
            for cols in range(4):
                for side in range(2):
                    start = 384 * (2 * cols + side) + 128 * chunk
                    up_grad[:, start : start + 128] = low[
                        at + 96 * cols : at + 96 * (cols + 1), 128 * side : 128 * (side + 1)
                    ]
            for side in range(2):
                down_grad[128 * chunk : 128 * (chunk + 1), 384 * side : 384 * (side + 1)] = (
                    jnp.transpose(high[at : at + 384, 128 * side : 128 * (side + 1)])
                )
        for cols in range(3):
            lanes = slice(WIDTH * cols, WIDTH * (cols + 1))
            at = 1152 + 48 * cols
            out_grad[:48, lanes] = low[at : at + 48, :]
            out_grad[48:, lanes] = high[at : at + 48, :]

    @pl.when(core == 0)
    def _():
        collect(own, got)

    @pl.when(core == 1)
    def _():
        collect(got, own)

    up_new, up_total, up_sums, up_divided = moments(up_grad[...], up_rows[...])
    down_new, down_total, down_sums, down_divided = moments(down_grad[...], down_rows[...])
    out_new, out_total, out_sums, out_divided = moments(out_grad[...], out_rows[...])
    up_rows_new[...] = up_new
    down_rows_new[...] = down_new
    out_rows_new[...] = out_new
    for part in range(4):
        lanes = slice(D * part, D * (part + 1))
        sums[part : part + 1, :] = up_sums[:, lanes]
        sums[4 + part : 5 + part, :] = up_divided[:, lanes]
    sums[8:9, :] = down_sums
    sums[9:10, :] = down_divided
    sums[10:11, :] = out_sums
    sums[11:12, :] = out_divided
    sums[12:13, :] = lane_values([up_total, down_total, out_total])
    sums[13:16, :] = jnp.zeros((3, D), F32)


def in_moments_kernel(
    place, own, got, rows_old, vector, ffn_sums, grad, rows_new, sums,
):
    core = place[3]

    def collect(low, high):
        for group in range(GROUPS):
            for which in range(3):
                at = 144 * group + 48 * which
                lanes = slice(WIDTH * group, WIDTH * (group + 1))
                grad[which, :48, lanes] = low[at : at + 48, :]
                grad[which, 48:, lanes] = high[at : at + 48, :]

    @pl.when(core == 0)
    def _():
        collect(own, got)

    @pl.when(core == 1)
    def _():
        collect(got, own)

    totals = []
    for which in range(3):
        new, total, columns, divided = moments(grad[which], rows_old[which : which + 1, :])
        rows_new[which : which + 1, :] = new
        sums[which : which + 1, :] = columns
        sums[3 + which : 4 + which, :] = divided
        totals.append(total)
    sums[6:7, :] = lane_values(totals)
    sums[7:8, :] = jnp.zeros((1, D), F32)
    sums[8:24, :] = vector[...]
    sums[24:40, :] = ffn_sums[...]


def matrix_step(weight, grad, rows, cols, total, col_sums, divided, rows_full, rate):
    cols_new = DECAY * cols + (1.0 - DECAY) * col_sums * (1.0 / rows_full)
    mean = total * (1.0 / rows_full)
    square_sum = mean * jnp.sum(divided / cols_new, axis=1, keepdims=True)
    rms = jnp.sqrt(square_sum * (1.0 / (rows_full * grad.shape[1])))
    factor = to_column(lax.rsqrt(rows / mean)) * (rate / jnp.maximum(1.0, rms / clip_level))
    return cols_new, weight - grad * factor * lax.rsqrt(cols_new)


def finish_kernel(
    place, inward, up, down, out, in_grad, up_grad, down_grad, out_grad, in_rows, up_rows,
    down_rows, out_rows, in_cols, up_cols, down_cols, out_cols, sums, vectors, vector_state,
    in_cols_new, up_cols_new, down_cols_new, out_cols_new, in_next, up_next, down_next, out_next,
    vector_grad, state_next, vectors_next,
):
    base_rate = 0.3 * D ** (-0.5)
    for which in range(3):
        here = slice(which, which + 1)
        in_cols_new[here, :], in_next[which] = matrix_step(
            inward[which], in_grad[which], in_rows[here, :], in_cols[here, :],
            sums[6:7, which : which + 1], sums[here, :], sums[3 + which : 4 + which, :], D,
            base_rate,
        )

    def wide_row(first):
        return jnp.concatenate([sums[first + i : first + i + 1, :] for i in range(4)], axis=1)

    up_cols_new[...], up_next[...] = matrix_step(
        up[...], up_grad[...], up_rows[...], up_cols[...], sums[36:37, 0:1], wide_row(24),
        wide_row(28), D, base_rate,
    )
    down_cols_new[...], down_next[...] = matrix_step(
        down[...], down_grad[...], down_rows[...], down_cols[...], sums[36:37, 1:2],
        sums[32:33, :], sums[33:34, :], FF, 0.3 * FF ** (-0.5),
    )
    out_cols_new[...], out_next[...] = matrix_step(
        out[...], out_grad[...], out_rows[...], out_cols[...], sums[36:37, 2:3],
        sums[34:35, :], sums[35:36, :], D, 1.2 * D ** (-0.5),
    )
    g = sums[8:21, :]
    vector_grad[...] = g
    state = DECAY * vector_state[...] + (1.0 - DECAY) * (g * g + square_eps)
    state_next[...] = state
    update = g * lax.rsqrt(state)
    total = jnp.sum(jnp.sum(update * update, axis=0, keepdims=True), axis=1, keepdims=True)
    rms = jnp.sqrt(total * (1.0 / (13 * D)))
    vectors_next[...] = vectors[...] - update * (0.25 / jnp.maximum(1.0, rms / clip_level))


def shards(
    tokens, cotangent, lengths, projection, inward, outward, expand, shrink, vectors,
    inward_rows, inward_columns, outward_rows, outward_columns, expand_rows, expand_columns,
    shrink_rows, shrink_columns, vector_state,
):
    full = special()
    rows = outward.shape[0]
    wide = 8 if full else 1
    wide_at = lax.axis_index("wide").astype(jnp.int32)
    narrow_at = lax.axis_index("narrow").astype(jnp.int32)
    core = narrow_at % 2 if full else jnp.int32(0)
    place = jnp.stack([wide_at // 2, wide_at % 2, narrow_at // 2, core])
    per = FFC // wide
    cosine, sine, onehot, proj = tables(lengths, projection)
    if full:
        *own_in, own_first, own_rest = small_call(
            pick_kernel, "pick", place, [inward, outward, expand, shrink],
            [
                struct((2, 48, D), BF16), struct((1, 48, D), BF16), struct((528, WIDTH), BF16),
                struct((768, WIDTH), BF16),
            ],
        )
        in_z = [along_z(value) for value in own_in]
        *in_z, own_first, cosine, sine, onehot, proj = tie(
            *in_z, own_first, cosine, sine, onehot, proj
        )
        first_z = along_z(own_first)
        in_x = [over_x(value) for value in in_z]
        pieces_in = []
        *in_z, first_z = tie(*in_z, *in_x, first_z)
        for near, far in zip(in_z[:2], in_z[2:]):
            pieces_in += [near, far, over_core(near), over_core(far)]
        *pieces_in, first_z, own_rest = tie(*pieces_in, first_z, own_rest)
        first_x = over_x(first_z)
        rest_got = [over_z(own_rest, shift) for shift in (1, 2, 3)]
    else:
        in_low = lax.all_gather(inward.astype(BF16), "wide", axis=1, tiled=True)
        out_low = lax.all_gather(outward.astype(BF16), "wide", axis=0, tiled=True)
        up_low = lax.all_gather(expand.astype(BF16), "wide", axis=0, tiled=True)
        down_low = lax.all_gather(shrink.astype(BF16), "wide", axis=0, tiled=True)
        units = jnp.transpose(in_low.reshape(3, D, GROUPS, WIDTH), (2, 1, 0, 3))
        pieces_in = [units.reshape(1, 3 * D, D)]

        def blocks(matrix):
            count = matrix.shape[1] // WIDTH
            return jnp.transpose(matrix.reshape(-1, count, WIDTH), (1, 0, 2)).reshape(-1, WIDTH)

        ups = [blocks(up_low[:, FFC * j : FFC * (j + 1)]) for j in range(CHUNKS)]
        downs = [blocks(down_low[FFC * j : FFC * (j + 1)]) for j in range(CHUNKS)]
        half = D // 2
        pieces_first = [
            jnp.concatenate([blocks(out_low[:half]), ups[0], blocks(out_low[half:]), downs[0]])[
                None
            ]
        ]
        pieces_rest = [
            jnp.stack([jnp.concatenate([ups[j], downs[j]])[None] for j in range(1, CHUNKS)])
        ]
    perm = jnp.asarray(head_perm(), BF16)
    block_ones = np.kron(np.eye(2, dtype=np.float32), np.ones((64, 64), np.float32))
    ones = jnp.asarray(np.concatenate([block_ones, block_ones]), BF16)
    split = vectors[4:6].reshape(2, GROUPS, 4, 2, 32)
    bias_qk = jnp.transpose(split, (0, 1, 3, 2, 4)).reshape(2, GROUPS, WIDTH)
    bias = jnp.concatenate([bias_qk, vectors[6].reshape(1, GROUPS, WIDTH)])
    bias = jnp.transpose(bias, (1, 0, 2))
    bias_up = vectors[9:].reshape(wide, CHUNKS, per)
    bias_up = jnp.transpose(bias_up, (1, 0, 2)).reshape(CHUNKS, 1, FFC)
    attn, mixed, a1t, w_in, wq, wk, qf, kf, v, rden = attend(
        lengths, place, pieces_in, wide, tokens, vectors[:2], bias, perm, proj, cosine, sine,
        onehot,
    )
    if full:
        attn, first_x, *rest_got = tie(attn, first_x, *rest_got)
        rest_z = jnp.stack([own_rest] + rest_got)
        first_cores = [over_core(first_z), over_core(first_x)]
        *first_cores, rest_z = tie(*first_cores, rest_z)
        pieces_first = [first_z, first_x] + first_cores
        rest_x = over_x(rest_z)
    x1, a2, a2t, dyt, y, back, w_out, keep0, send0, dbias0 = middle_first(
        place, wide, pieces_first, tokens, attn, cotangent, vectors, bias_up
    )
    if full:
        rest_core = over_core(rest_z)
        rest_x, rest_core, send0, y = tie(rest_x, rest_core, send0, y)
        pieces_rest = [rest_z, rest_x, rest_core, over_core(rest_x)]
        got0 = over_core(send0)
    (
        block_out, dx1, dmixed, okeep, osend, middle_vec, keep12, send12, dbias12,
    ) = middle_rest(
        place, wide, pieces_rest, cotangent, (a2, a2t, dyt), bias_up, attn, w_out, vectors,
        (y, back, x1),
    )
    if full:
        got12 = over_core(send12)
        send_b, keep_b = first_sum(place, [(keep0, got0), (keep12, got12)])
        e_parts = first_sum_z(place, [(keep12, got12), (okeep, over_core(osend))])
        dmixed, send_b, keep_b, *e_parts = tie(dmixed, send_b, keep_b, *e_parts)
        got_b = over_x(send_b)
        e_got = [over_z(e_parts[shift], shift) for shift in (1, 2, 3)]
    saved = (mixed, rden, wq, wk, qf, kf, v)
    in_keep, in_send, in_bias, da1 = attend_back(
        lengths, place, wide, dmixed, saved, a1t, w_in, perm, proj, cosine, sine, onehot, ones
    )
    if full:
        keep_e, send_e = split_sum(place, [e_parts[0]] + e_got)
        send_e, in_send, keep_b, got_b, da1 = tie(send_e, in_send, keep_b, got_b, da1)
        got_e = over_x(send_e)
        b_parts = second_sum(place, keep_b, got_b)
        got_in = over_core(in_send)
        got_in, *b_parts = tie(got_in, *b_parts)
        send_c, keep_c = first_sum(place, [(in_keep, got_in)])
        da1, send_c, got_e = tie(da1, send_c, got_e)
        got_c = over_x(send_c)
    input_grad, vector_local = input_side(
        wide, tokens, dx1, da1, vectors, middle_vec, in_bias, dbias0, dbias12
    )
    if full:
        vector_part = sum_narrow(vector_local)

        def pair_sum(mine, got):
            half_sum = mine.astype(F32) + got.astype(F32)
            return half_sum, over_core(half_sum)

        got_c, input_grad, vector_part = tie(got_c, input_grad, vector_part)
        c_parts = second_sum(place, keep_c, got_c)
        b_parts[0], *c_parts = tie(b_parts[0], *c_parts)
        ffn_mine = z_sum(place, b_parts, (keep_e, got_e))
        ffn_mine, *c_parts = tie(ffn_mine, *c_parts)
        ffn_y = over_y(ffn_mine)
        c_got = [over_z(c_parts[shift], shift) for shift in (1, 2, 3)]
        ffn_y, *c_got = tie(ffn_y, *c_got)
        c_mine = z_sum(place, c_parts, (), c_got)
        c_mine, ffn_y = tie(c_mine, ffn_y)
        c_y = over_y(c_mine)
        ffn_own, ffn_got = pair_sum(ffn_mine, ffn_y)
        expand_grad, shrink_grad, outward_grad, up_rows, down_rows, out_rows, sums = held_call(
            ffn_moments_kernel, "ffn_moments", place,
            [
                ffn_own, ffn_got, expand_rows[None], shrink_rows[None], outward_rows[None],
            ],
            [
                struct(expand.shape, F32), struct(shrink.shape, F32), struct(outward.shape, F32),
                struct((1, 96), F32), struct((1, 384), F32), struct((1, 96), F32),
                struct((16, D), F32),
            ],
        )
        c_y, sums = tie(c_y, sums)
        c_own, c_got = pair_sum(c_mine, c_y)
        inward_grad, in_rows, sums = held_call(
            in_moments_kernel, "in_moments", place,
            [c_own, c_got, inward_rows, vector_part, sums],
            [struct(inward.shape, F32), struct((3, 96), F32), struct((40, D), F32)],
        )
        sums = sum_wide(sums)
        (
            in_cols, up_cols, down_cols, out_cols, inward_next, expand_next, shrink_next,
            outward_next, vector_grad, vector_state_next, vectors_next,
        ) = held_call(
            finish_kernel, "finish", place,
            [
                inward, expand, shrink, outward, inward_grad, expand_grad, shrink_grad,
                outward_grad, in_rows, up_rows, down_rows, out_rows, inward_columns,
                expand_columns[None], shrink_columns[None], outward_columns[None], sums, vectors,
                vector_state,
            ],
            [
                struct((3, D), F32), struct((1, FF), F32), struct((1, D), F32),
                struct((1, D), F32), struct(inward.shape, F32), struct(expand.shape, F32),
                struct(shrink.shape, F32), struct(outward.shape, F32), struct((13, D), F32),
                struct((13, D), F32), struct((13, D), F32),
            ],
            0,
        )
        return (
            block_out, input_grad, inward_grad, outward_grad, expand_grad, shrink_grad,
            vector_grad, in_rows, in_cols, out_rows[0], out_cols[0], up_rows[0], up_cols[0],
            down_rows[0], down_cols[0], vector_state_next, inward_next, outward_next,
            expand_next, shrink_next, vectors_next,
        )
    vector_part = sum_narrow(vector_local[:13])

    def reduced(values, axis):
        part = lax.psum_scatter(values, "wide", scatter_dimension=axis, tiled=True)
        return lax.psum(part.astype(F32), "narrow")

    keeps = [keep0, keep12[0], keep12[1]]
    sends = [send0, send12[0], send12[1]]
    up_grads = [
        jnp.transpose(keep.reshape(4, D, WIDTH), (1, 0, 2)).reshape(D, FFC) for keep in keeps
    ]
    down_grads = [
        jnp.transpose(send.reshape(4, D, WIDTH), (0, 2, 1)).reshape(FFC, D) for send in sends
    ]
    expand_grad = reduced(jnp.concatenate(up_grads, axis=1), 0)
    shrink_grad = reduced(jnp.concatenate(down_grads, axis=0), 0)

    def rebuilt(keep, send):
        return jnp.concatenate(
            [keep.reshape(-1, 3, D // 2, WIDTH), send.reshape(-1, 3, D // 2, WIDTH)], axis=2
        )

    outward_grad = reduced(jnp.transpose(rebuilt(okeep, osend)[0], (1, 0, 2)).reshape(D, D), 0)
    in_units = rebuilt(in_keep, in_send)
    inward_grad = reduced(jnp.transpose(in_units, (1, 2, 0, 3)).reshape(3, D, D), 1)
    decay = 1.0 - STEP ** (-0.8)
    wide_count = lax.axis_size("wide")
    grads_list = [inward_grad, outward_grad[None], expand_grad[None], shrink_grad[None]]
    rows_old = [inward_rows, outward_rows[None], expand_rows[None], shrink_rows[None]]
    columns_old = [
        inward_columns,
        outward_columns[None],
        expand_columns[None],
        shrink_columns[None],
    ]
    weights_old = [inward, outward[None], expand[None], shrink[None]]
    rates = [0.3 * D ** (-0.5), 1.2 * D ** (-0.5), 0.3 * D ** (-0.5), 0.3 * FF ** (-0.5)]
    bounds = [0, 3, 4, 5, 6]
    rows_next = []
    column_parts = []
    for member in range(4):
        squares = grads_list[member] * grads_list[member] + square_eps
        rows_next.append(decay * rows_old[member] + (1.0 - decay) * jnp.mean(squares, axis=-1))
        column_parts.append(jnp.sum(squares, axis=-2))
    row_totals = jnp.concatenate([jnp.sum(entry, axis=-1) for entry in rows_next])
    shapes = [part.shape for part in column_parts] + [row_totals.shape, vector_part.shape]
    flat = jnp.concatenate(
        [part.reshape(-1) for part in column_parts + [row_totals, vector_part]]
    )
    flat = jnp.pad(flat, (0, -flat.shape[0] % 1024)).reshape(-1, 128)
    flat = sum_wide(flat).reshape(-1)
    summed = []
    offset = 0
    for shape in shapes:
        size = 1
        for extent in shape:
            size *= extent
        summed.append(flat[offset : offset + size].reshape(shape))
        offset += size
    column_sums = list(summed[0:4])
    totals_sum = summed[4]
    vector_grad = summed[5]
    columns_next = []
    scaled_list = []
    row_means = []
    sizes_full = []
    for member in range(4):
        grad_now = grads_list[member]
        rows_full = grad_now.shape[-2] * wide_count
        sizes_full.append(rows_full * grad_now.shape[-1])
        columns_next.append(
            decay * columns_old[member] + (1.0 - decay) * column_sums[member] / rows_full
        )
        row_mean = totals_sum[bounds[member] : bounds[member + 1]] / rows_full
        row_means.append(row_mean)
        scaled_list.append(
            grad_now
            * lax.rsqrt(rows_next[member] / row_mean[:, None])[..., None]
            * lax.rsqrt(columns_next[member])[:, None, :]
        )
    partial_squares = jnp.concatenate(
        [jnp.sum(entry * entry, axis=(-2, -1)) for entry in scaled_list]
    )
    total_squares = sum_wide(jnp.pad(partial_squares, (0, 122)).reshape(1, 128))[0, :6]
    rms_list = [
        jnp.sqrt(total_squares[bounds[member] : bounds[member + 1]] / sizes_full[member])
        for member in range(4)
    ]
    weights_next = []
    for member in range(4):
        limiter = jnp.maximum(1.0, rms_list[member] / clip_level)
        weights_next.append(
            weights_old[member] - rates[member] * scaled_list[member] / limiter[:, None, None]
        )
    vector_state_next = decay * vector_state + (1.0 - decay) * (
        vector_grad * vector_grad + square_eps
    )
    vector_update = vector_grad * lax.rsqrt(vector_state_next)
    vector_rms = jnp.sqrt(jnp.mean(vector_update * vector_update))
    vectors_next = vectors - 0.25 * vector_update / jnp.maximum(1.0, vector_rms / clip_level)
    return (
        block_out,
        input_grad,
        inward_grad,
        outward_grad,
        expand_grad,
        shrink_grad,
        vector_grad,
        rows_next[0],
        columns_next[0],
        rows_next[1][0],
        columns_next[1][0],
        rows_next[2][0],
        columns_next[2][0],
        rows_next[3][0],
        columns_next[3][0],
        vector_state_next,
        weights_next[0],
        weights_next[1][0],
        weights_next[2][0],
        weights_next[3][0],
        vectors_next,
    )


def solution(mesh):
    placed = (
        P(("narrow", "wide"), None),
        P(("narrow", "wide"), None),
        P(("narrow", "wide"), None),
        P(),
        P(None, "wide", None),
        P("wide", None),
        P("wide", None),
        P("wide", None),
        P(),
        P(None, "wide"),
        P(),
        P("wide"),
        P(),
        P("wide"),
        P(),
        P("wide"),
        P(),
        P(),
    )
    return jax.shard_map(
        shards,
        mesh=mesh,
        in_specs=placed,
        out_specs=(
            P(("narrow", "wide"), None),
            P(("narrow", "wide"), None),
            P(None, "wide", None),
            P("wide", None),
            P("wide", None),
            P("wide", None),
            P(),
            P(None, "wide"),
            P(),
            P("wide"),
            P(),
            P("wide"),
            P(),
            P("wide"),
            P(),
            P(),
            P(None, "wide", None),
            P("wide", None),
            P("wide", None),
            P("wide", None),
            P(),
        ),
        check_vma=False,
    )
```

```python
import functools
import math

import jax
import jax.numpy as jnp
import numpy as np
from jax import lax
from jax.experimental import pallas as pl
from jax.experimental.pallas import tpu as pltpu
from jax.sharding import PartitionSpec as P

D = 768
HEADS = 12
HD = 64
FF = 3072
FEAT = 32
STEP = 10
LEN = 1024
SPAN = 256
CHUNKS = 3
GROUPS = 3
WIDTH = 256
FFC = FF // CHUNKS

norm_eps = 1e-05
square_eps = 1e-30
clip_level = 1.0

F32 = jnp.float32
BF16 = jnp.bfloat16
VMEM_LIMIT = 60 * 1024 * 1024


def mm(left, right):
    return lax.dot_general(left, right, (((1,), (0,)), ((), ())), preferred_element_type=F32)


def mm_nt(left, right):
    return lax.dot_general(left, right, (((1,), (1,)), ((), ())), preferred_element_type=F32)


def mm_tn(left, right):
    return lax.dot_general(left, right, (((0,), (0,)), ((), ())), preferred_element_type=F32)


def halves(values):
    high = values.astype(BF16)
    return high, (values - high.astype(F32)).astype(BF16)


TAIL = (
    0.1795078068971634,
    0.17978088557720184,
    0.14234966039657593,
    0.06379217654466629,
    0.0434231162071228,
    -0.261725515127182,
    0.20454804599285126,
    -0.05167665705084801,
)


def normal_parts(values):
    size = jnp.abs(values)
    t = 1.0 / (1.0 + 0.45 * size)
    poly = TAIL[-1]
    for coeff in TAIL[-2::-1]:
        poly = poly * t + coeff
    bell = jnp.exp(-0.5 * values * values)
    tail = poly * t * bell
    return jnp.where(values >= 0, 1.0 - tail, tail), bell * 0.3989422804014327


def transposed(values):
    row = lax.broadcasted_iota(jnp.int32, (256, 256), 0)
    col = lax.broadcasted_iota(jnp.int32, (256, 256), 1)
    eye = (row == col).astype(F32).astype(BF16)
    return mm_nt(eye, values).astype(BF16)


def head_perm():
    perm = np.zeros((WIDTH, WIDTH), np.float32)
    for head in range(4):
        for half in range(2):
            for i in range(32):
                perm[head * 64 + half * 32 + i, half * 128 + head * 32 + i] = 1.0
    return perm


def make_blocks(lengths, base, first, last):
    def step(s, carry):
        count, begin, begin_row, end = carry
        new_end = end + lengths[0, s]
        full = new_end - begin_row > SPAN

        @pl.when(full)
        def _():
            base[count] = begin_row
            first[count] = begin
            last[count] = s - 1

        row = jnp.minimum((end // 16) * 16, LEN - SPAN)
        return (
            jnp.where(full, count + 1, count),
            jnp.where(full, s, begin),
            jnp.where(full, row, begin_row),
            new_end,
        )

    segments = lengths.shape[1]
    zero = jnp.int32(0)
    count, begin, begin_row, _ = lax.fori_loop(0, segments, step, (zero, zero, zero, zero))
    base[count] = begin_row
    first[count] = begin
    last[count] = segments - 1
    return count + 1


def lane_mask(lo, hi, width, dtype):
    lane = lax.broadcasted_iota(jnp.int32, (1, width), 1)
    return ((lane >= lo) & (lane < hi)).astype(F32).astype(dtype)


def value_rows(v_pair, head):
    keep = lane_mask(64 * head, 64 * head + 64, 128, BF16)
    return jnp.concatenate([v_pair * keep, jnp.broadcast_to(keep, v_pair.shape)], axis=1)


def span_mask(onehot, rows, lo, hi):
    member = onehot[rows, :]
    lane = lax.broadcasted_iota(jnp.int32, (1, 128), 1)
    inside = ((lane >= lo) & (lane <= hi)).astype(F32).astype(BF16)
    return mm_nt(member * inside, member).astype(BF16)


def cost(flops, size):
    return pl.CostEstimate(flops=10**6, transcendentals=0, bytes_accessed=10**5)


def row_blocks(body):
    for rows in range(0, LEN, 256):
        body(pl.ds(rows, 256))


def any_spec():
    return pl.BlockSpec(memory_space=pl.ANY)


def in_copies(place, pieces, dst, sems, unit):
    if len(pieces) == 1:
        rows = dst.shape[1] // 3
        here = pl.ds(unit * rows, rows)
        return [pltpu.make_async_copy(pieces[0].at[:, here], dst.at[:, here], sems.at[unit, 0])]
    z, x, core = place[0], place[1], place[3]
    part, index = (0, unit) if unit < 2 else (4, 0)
    copies = []
    for side in range(2):
        half = core if side == 0 else 1 - core
        for flip in range(2):
            column = x if flip == 0 else 1 - x
            for shift in range(4):
                row = lax.rem(z + 4 - shift, 4) * 2 + column
                start = pl.multiple_of(unit * 96 + half * 48, 16)
                copies.append(
                    pltpu.make_async_copy(
                        pieces[part + 2 * side + flip].at[shift, index],
                        dst.at[row, pl.ds(start, 48)],
                        sems.at[unit, len(copies)],
                    )
                )
    return copies


def flat_copies(place, pieces, dst, sems):
    if len(pieces) == 1:
        return [pltpu.make_async_copy(pieces[0], dst, sems.at[0])]
    z, x, core = place[0], place[1], place[3]
    span = dst.shape[1] // 2
    copies = []
    for side in range(2):
        half = core if side == 0 else 1 - core
        for flip in range(2):
            column = x if flip == 0 else 1 - x
            for shift in range(4):
                row = lax.rem(z + 4 - shift, 4) * 2 + column
                start = pl.multiple_of(half * span, 16)
                copies.append(
                    pltpu.make_async_copy(
                        pieces[2 * side + flip].at[shift],
                        dst.at[row, pl.ds(start, span)],
                        sems.at[len(copies)],
                    )
                )
    return copies


def attend_kernel(count_in, lengths, place, *refs):
    pieces = refs[:count_in]
    (
        x_ref, norm_ref, bias_ref, perm_ref, proj_ref, cos_ref, sin_ref, onehot_ref,
        attn_ref, mixed_ref, a1t_ref, w_ref, wq_ref, wk_ref, qf_ref, kf_ref, v_ref, rden_ref,
        a1, qb, kb, vb, parts, base, first, last, sems,
    ) = refs[count_in:]
    group = pl.program_id(0)

    @pl.when(group == 0)
    def _():
        for unit in range(GROUPS):
            for copy in in_copies(place, pieces, w_ref, sems, unit):
                copy.start()
        def norm_rows(here):
            x = x_ref[here, :].astype(F32)
            centre = x - jnp.mean(x, axis=-1, keepdims=True)
            spread = jnp.mean(centre * centre, axis=-1, keepdims=True)
            a1[here, :] = (
                centre * lax.rsqrt(spread + norm_eps) * norm_ref[0:1, :] + norm_ref[1:2, :]
            ).astype(BF16)

        row_blocks(norm_rows)
        for cols in range(0, D, 256):
            a1t_ref[cols : cols + 256, :] = transposed(a1[:, cols : cols + 256])

    for unit in range(GROUPS):

        @pl.when(group == unit)
        def _():
            for copy in in_copies(place, pieces, w_ref, sems, unit):
                copy.wait()

    count = make_blocks(lengths, base, first, last)
    shard = w_ref.shape[1] // 3
    here = pl.ds(pl.multiple_of(group * shard, 16), shard)
    w = w_ref[:, here, :].reshape(D, D)
    perm = perm_ref[...]
    bias = bias_ref[0]
    proj_both = proj_ref[0]
    proj_high = proj_ref[1, :, :128]
    square = proj_ref[2, :, :128]
    weights = [mm(w[:, WIDTH * i : WIDTH * (i + 1)], perm).astype(BF16) for i in range(2)]

    def feature_rows(here):
        for which, (out_w, out_f, low_f) in enumerate(
            ((wq_ref, qf_ref, qb), (wk_ref, kf_ref, kb))
        ):
            u = (mm(a1[here, :], weights[which]) + bias[which : which + 1, :]) * HD ** (-0.25)
            c = u[:, :128]
            e = u[:, 128:]
            cosine = cos_ref[here, :]
            sine = sin_ref[here, :]
            turned = jnp.concatenate([c * cosine - e * sine, e * cosine + c * sine], axis=1)
            out_w[0, here, :] = turned
            high, low = halves(turned)
            sq_high, sq_low = halves(turned * turned)
            both = mm(high, proj_both)
            logits = (
                both[:, :128] + both[:, 128:] + mm(low, proj_high)
                - (mm(sq_high, square) + mm(sq_low, square))
            )
            phi = jnp.exp(logits) * FEAT ** (-0.5)
            out_f[0, here, :] = phi
            low_f[here, :] = phi.astype(BF16)
        v = mm(a1[here, :], w[:, 2 * WIDTH :]) + bias[2:3, :]
        v_ref[0, here, :] = v
        vb[here, :] = v.astype(BF16)

    row_blocks(feature_rows)
    parts[...] = jnp.zeros_like(parts)

    def one_span(index, carry):
        rows = pl.ds(pl.multiple_of(base[index], 16), SPAN)
        mask = span_mask(onehot_ref, rows, first[index], last[index])
        q = qb[rows, :]
        k = kb[rows, :]
        for pair in range(2):
            v_pair = vb[rows, 128 * pair : 128 * (pair + 1)]
            total = jnp.zeros((SPAN, WIDTH), F32)
            for side in range(2):
                head = 2 * pair + side
                scores = mm_nt(q * lane_mask(32 * head, 32 * head + 32, 128, BF16), k)
                total = total + mm(scores.astype(BF16) * mask, value_rows(v_pair, side))
            parts[pair, rows, :] += total
        return carry

    lax.fori_loop(0, count, one_span, 0)
    for pair in range(2):
        lanes = slice(128 * pair, 128 * (pair + 1))
        inverse = 1.0 / parts[pair, :, 128:]
        rden_ref[0, :, lanes] = inverse
        mixed = parts[pair, :, :128] * inverse
        mixed_ref[0, :, lanes] = mixed
        attn_ref[:, lanes] = mixed.astype(BF16)


def whole_spec(shape, **options):
    return pl.BlockSpec(shape, lambda *_: (0,) * len(shape), **options)


def group_spec(shape):
    return pl.BlockSpec((1,) + shape, lambda g, *_: (g,) + (0,) * len(shape))


def attend(lengths, place, pieces, wide, tokens, norm, bias, perm, proj, cosine, sine, onehot):
    def out(shape, dtype):
        return jax.ShapeDtypeStruct((GROUPS,) + shape, dtype)

    rows_in = 3 * D // wide
    return pl.pallas_call(
        functools.partial(attend_kernel, len(pieces)),
        grid_spec=pltpu.PrefetchScalarGridSpec(
            num_scalar_prefetch=2,
            grid=(GROUPS,),
            in_specs=[any_spec()] * len(pieces)
            + [
                whole_spec((LEN, D)), whole_spec((2, D)), group_spec((3, WIDTH)),
                whole_spec((WIDTH, WIDTH)), whole_spec((3, WIDTH, WIDTH)), whole_spec((LEN, 128)),
                whole_spec((LEN, 128)), whole_spec((LEN, 128)),
            ],
            out_specs=[
                pl.BlockSpec((LEN, WIDTH), lambda g, *_: (0, g)), group_spec((LEN, WIDTH)),
                whole_spec((D, LEN)), whole_spec((wide, rows_in, D)), group_spec((LEN, WIDTH)),
                group_spec((LEN, WIDTH)), group_spec((LEN, 128)), group_spec((LEN, 128)),
                group_spec((LEN, WIDTH)), group_spec((LEN, WIDTH)),
            ],
            scratch_shapes=[
                pltpu.VMEM((LEN, D), BF16),
                pltpu.VMEM((LEN, 128), BF16), pltpu.VMEM((LEN, 128), BF16),
                pltpu.VMEM((LEN, WIDTH), BF16), pltpu.VMEM((2, LEN, WIDTH), F32),
                pltpu.SMEM((32,), jnp.int32), pltpu.SMEM((32,), jnp.int32),
                pltpu.SMEM((32,), jnp.int32), pltpu.SemaphoreType.DMA((GROUPS, 16)),
            ],
        ),
        out_shape=[
            jax.ShapeDtypeStruct((LEN, D), BF16), out((LEN, WIDTH), F32),
            jax.ShapeDtypeStruct((D, LEN), BF16), jax.ShapeDtypeStruct((wide, rows_in, D), BF16),
            out((LEN, WIDTH), F32), out((LEN, WIDTH), F32), out((LEN, 128), F32),
            out((LEN, 128), F32), out((LEN, WIDTH), F32), out((LEN, WIDTH), F32),
        ],
        compiler_params=pltpu.CompilerParams(
            dimension_semantics=("arbitrary",), vmem_limit_bytes=VMEM_LIMIT
        ),
        cost_estimate=cost(20 * 10**9, 40 * 10**6),
        name="attend",
    )(lengths, place, *pieces, tokens, norm, bias, perm, proj, cosine, sine, onehot)


def attend_back_kernel(
    lengths, place, dmixed_ref, mixed_ref, rden_ref, wq_ref, wk_ref, qf_ref, kf_ref, v_ref,
    a1t_ref, w_ref, perm_ref, proj_ref, cos_ref, sin_ref, onehot_ref, ones_ref,
    keep_ref, send_ref, bias_ref, da1_ref,
    qb, kb, dnb, dnh, lift, dqf, dkf, dv, dqkv, base, first, last,
):
    count = make_blocks(lengths, base, first, last)
    qb[...] = qf_ref[0].astype(BF16)
    kb[...] = kf_ref[0].astype(BF16)
    lane = lax.broadcasted_iota(jnp.int32, (1, 128), 1)
    ones = ones_ref[...]
    def lift_rows(here):
        for pair in range(2):
            lanes = slice(128 * pair, 128 * (pair + 1))
            dnum = dmixed_ref[here, lanes] * rden_ref[0, here, lanes]
            high, low = halves(dnum)
            dnb[here, lanes] = high
            part_high, part_low = halves(dnum * mixed_ref[0, here, lanes])
            dden = -mm(jnp.concatenate([part_high, part_low], axis=1), ones)
            den_high, den_low = halves(dden)
            high, low = high.astype(F32), low.astype(F32)
            den_high = pltpu.roll(den_high.astype(F32), 64, 1)
            den_low = pltpu.roll(den_low.astype(F32), 64, 1)
            low_far = pltpu.roll(low, 64, 1)
            v = v_ref[0, here, lanes]
            v_high, v_low = halves(v)
            v_high, v_low = v_high.astype(F32), v_low.astype(F32)
            v_far = pltpu.roll(v_high, 64, 1)
            for side in range(2):
                own = (lane >= 64 * side) & (lane < 64 * side + 64)
                mark = 64 - 64 * side
                rest = jnp.where(lane == mark, den_high, jnp.where(lane == mark + 1, den_low, 0.0))
                both = ((lane == mark) | (lane == mark + 1)).astype(F32)
                head = 2 * pair + side
                dnh[head, here, :128] = jnp.where(own, high, low_far).astype(BF16)
                dnh[head, here, 128:] = jnp.where(own, high, rest).astype(BF16)
                lift[head, here, :128] = jnp.where(own, v_high, v_far).astype(BF16)
                lift[head, here, 128:] = jnp.where(own, v_low, both).astype(BF16)
    row_blocks(lift_rows)
    dqf[...] = jnp.zeros_like(dqf)
    dkf[...] = jnp.zeros_like(dkf)
    dv[...] = jnp.zeros_like(dv)

    def one_span(index, carry):
        rows = pl.ds(pl.multiple_of(base[index], 16), SPAN)
        mask = span_mask(onehot_ref, rows, first[index], last[index])
        q = qb[rows, :]
        k = kb[rows, :]
        q_total = jnp.zeros((SPAN, 128), F32)
        k_total = jnp.zeros((SPAN, 128), F32)
        for pair in range(2):
            lanes = slice(128 * pair, 128 * (pair + 1))
            dn_pair = dnb[rows, lanes]
            v_total = jnp.zeros((SPAN, 128), F32)
            for side in range(2):
                head = 2 * pair + side
                feats = lane_mask(32 * head, 32 * head + 32, 128, BF16)
                q_head = q * feats
                k_head = k * feats
                lifted = lift[head, rows, :]
                dn_head = dnh[head, rows, :]
                scores = mm_nt(k, q_head).astype(BF16) * mask
                dscores = mm_nt(dn_head, lifted).astype(BF16) * mask
                dscores_t = mm_nt(lifted, dn_head).astype(BF16) * mask
                q_total = q_total + mm(dscores, k_head)
                k_total = k_total + mm(dscores_t, q_head)
                own = lane_mask(64 * side, 64 * side + 64, 128, BF16)
                v_total = v_total + mm(scores, dn_pair * own)
            dv[rows, lanes] += v_total
        dqf[rows, :] += q_total
        dkf[rows, :] += k_total
        return carry

    lax.fori_loop(0, count, one_span, 0)
    proj_low = proj_ref[0, :, 128:]
    proj_high = proj_ref[1]
    square = proj_ref[2]
    perm = perm_ref[...]
    def feature_rows(here):
        for which, (w_in, phi_in, dphi) in enumerate(
            ((wq_ref, qf_ref, dqf), (wk_ref, kf_ref, dkf))
        ):
            r = dphi[here, :] * phi_in[0, here, :]
            high, low = halves(r)
            both = jnp.concatenate([high, low], axis=1)
            spread = mm_nt(both, square)
            dw = mm_nt(both, proj_high) + mm_nt(high, proj_low)
            du = (dw - 2.0 * w_in[0, here, :] * spread) * HD ** (-0.25)
            c = du[:, :128]
            e = du[:, 128:]
            cosine = cos_ref[here, :]
            sine = sin_ref[here, :]
            turned = jnp.concatenate([c * cosine + e * sine, e * cosine - c * sine], axis=1)
            dqkv[here, WIDTH * which : WIDTH * (which + 1)] = mm_nt(
                turned.astype(BF16), perm
            ).astype(BF16)

    row_blocks(feature_rows)
    dqkv[:, 2 * WIDTH :] = dv[...].astype(BF16)
    bias_ref[0] = jnp.sum(dqkv[...].astype(F32), axis=0, keepdims=True)
    grad = mm(a1t_ref[...], dqkv[...]).astype(BF16)
    store_halves(grad, place[3], keep_ref.at[0], send_ref.at[0])
    w = w_ref[...].reshape(D, D)
    fresh = pl.program_id(0) == 0

    @pl.when(fresh)
    def _():
        da1_ref[...] = mm_nt(dqkv[...], w)

    @pl.when(jnp.logical_not(fresh))
    def _():
        da1_ref[...] += mm_nt(dqkv[...], w)


def store_halves(grad, core, keep_ref, send_ref):
    wide, rows = keep_ref.shape[0], D // keep_ref.shape[0]
    half = rows // 2
    parts = grad.reshape(wide, rows, D)
    for cols in range(3):
        block = parts[:, :, WIDTH * cols : WIDTH * (cols + 1)]
        here = pl.ds(half * cols, half)

        @pl.when(core == 0)
        def _():
            keep_ref[:, here, :] = block[:, :half]
            send_ref[:, here, :] = block[:, half:]

        @pl.when(core == 1)
        def _():
            keep_ref[:, here, :] = block[:, half:]
            send_ref[:, here, :] = block[:, :half]


def attend_back(
    lengths, place, wide, dmixed, saved, a1t, w_in, perm, proj, cosine, sine, onehot, ones
):
    mixed, rden, wq, wk, qf, kf, v = saved

    def by_group(shape):
        return pl.BlockSpec((1,) + shape, lambda g, *_: (g,) + (0,) * len(shape))

    rows_in = D // wide
    half = struct((GROUPS, wide, 3 * rows_in // 2, WIDTH), BF16)
    half_spec = group_spec(half.shape[1:])
    return pl.pallas_call(
        attend_back_kernel,
        grid_spec=pltpu.PrefetchScalarGridSpec(
            num_scalar_prefetch=2,
            grid=(GROUPS,),
            in_specs=[
                pl.BlockSpec((LEN, WIDTH), lambda g, *_: (0, g)),
                by_group((LEN, WIDTH)), by_group((LEN, WIDTH)), by_group((LEN, WIDTH)),
                by_group((LEN, WIDTH)), by_group((LEN, 128)), by_group((LEN, 128)),
                by_group((LEN, WIDTH)), once((D, LEN)),
                pl.BlockSpec((wide, rows_in, D), lambda g, *_: (0, g, 0)),
                once((WIDTH, WIDTH)), once((3, WIDTH, WIDTH)), once((LEN, 128)),
                once((LEN, 128)), once((LEN, 128)), once((WIDTH, 128)),
            ],
            out_specs=[
                half_spec, half_spec, group_spec((1, D)),
                whole_spec((LEN, D)),
            ],
            scratch_shapes=[
                pltpu.VMEM((LEN, 128), BF16), pltpu.VMEM((LEN, 128), BF16),
                pltpu.VMEM((LEN, WIDTH), BF16), pltpu.VMEM((4, LEN, WIDTH), BF16),
                pltpu.VMEM((4, LEN, WIDTH), BF16), pltpu.VMEM((LEN, 128), F32),
                pltpu.VMEM((LEN, 128), F32), pltpu.VMEM((LEN, WIDTH), F32),
                pltpu.VMEM((LEN, D), BF16),
                pltpu.SMEM((32,), jnp.int32), pltpu.SMEM((32,), jnp.int32),
                pltpu.SMEM((32,), jnp.int32),
            ],
        ),
        out_shape=[
            half, half, struct((GROUPS, 1, D), F32), struct((LEN, D), F32),
        ],
        compiler_params=pltpu.CompilerParams(
            dimension_semantics=("arbitrary",), vmem_limit_bytes=VMEM_LIMIT
        ),
        cost_estimate=cost(GROUPS * 12 * 10**9, GROUPS * 20 * 10**6),
        name="attend_back",
    )(
        lengths, place, dmixed, mixed, rden, wq, wk, qf, kf, v, a1t, w_in, perm, proj, cosine,
        sine, onehot, ones,
    )


def chunk_step(
    place, wide, bias_up, dy_ref, a2, a2t, dyt, up, down, act, dhidden, y, back, outs, dbias_ref,
    fresh,
):
    rows_up = D // wide
    rows_down = FFC // wide
    dbias_ref[0] = jnp.zeros((1, FFC), F32)

    def chunk_rows(here):
        hidden = mm(a2[here, :], up[...]) + bias_up
        below, density = normal_parts(hidden)
        act_now = (hidden * below).astype(BF16)
        act[here, :] = act_now
        dact = mm_nt(dy_ref[here, :], down[...])
        dhidden_now = (dact * (below + hidden * density)).astype(BF16)
        dhidden[here, :] = dhidden_now
        dbias_ref[0] += jnp.sum(dhidden_now.astype(F32), axis=0, keepdims=True)
        if fresh:
            y[here, :] = mm(act_now, down[...])
            back[here, :] = mm_nt(dhidden_now, up[...])
        else:
            y[here, :] += mm(act_now, down[...])
            back[here, :] += mm_nt(dhidden_now, up[...])

    row_blocks(chunk_rows)
    grad_up = mm(a2t[...], dhidden[...]).astype(BF16).reshape(wide, rows_up, FFC)
    grad_down = mm(dyt[...], act[...]).astype(BF16)
    core = place[3]

    def store_up(ref):
        for cols in range(4):
            ref[:, rows_up * cols : rows_up * (cols + 1), :] = grad_up[
                :, :, WIDTH * cols : WIDTH * (cols + 1)
            ]

    def store_down(ref):
        if wide == 1:
            for cols in range(4):
                ref[0, D * cols : D * (cols + 1), :] = grad_down[
                    :, WIDTH * cols : WIDTH * (cols + 1)
                ]
            return
        for shard in range(wide):
            block = grad_down[:, rows_down * shard : rows_down * (shard + 1)]
            ref[shard, :, :128] = block[: D // 2]
            ref[shard, :, 128:] = block[D // 2 :]

    for when, keep_ref, send_ref in outs:
        for side in range(2):
            now = core == side

            @pl.when(now if when is None else now & when)
            def _():
                store_up(keep_ref if side == 0 else send_ref)
                store_down(send_ref if side == 0 else keep_ref)


def load_up(flat, at, up, wide):
    rows = D // wide
    for cols in range(4):
        here = pl.ds(at + rows * cols, rows)
        up[:, WIDTH * cols : WIDTH * (cols + 1)] = flat[:, here, :].reshape(D, WIDTH)


def load_down(flat, at, down, wide):
    rows = FFC // wide
    for cols in range(3):
        here = pl.ds(at + rows * cols, rows)
        down[:, WIDTH * cols : WIDTH * (cols + 1)] = flat[:, here, :].reshape(FFC, WIDTH)


def middle_first_kernel(wide, count_in, place, *refs):
    pieces = refs[:count_in]
    (
        x_ref, attn_ref, dy_ref, rows_ref, bias_up_ref,
        x1_ref, a2_ref, a2t_ref, dyt_ref, y_ref, back_ref, out_ref, keep_ref, send_ref, dbias_ref,
        flat, up, down, act, dhidden, sems,
    ) = refs[count_in:]
    copies = flat_copies(place, pieces, flat, sems)
    for copy in copies:
        copy.start()
    for cols in range(0, D, 256):
        dyt_ref[cols : cols + 256, :] = transposed(dy_ref[:, cols : cols + 256])
    for copy in copies:
        copy.wait()
    half_out = D // wide // 2
    half_flat = flat.shape[1] // 2
    for cols in range(3):
        upper = flat[:, half_out * cols : half_out * (cols + 1), :]
        lower = flat[:, half_flat + half_out * cols : half_flat + half_out * (cols + 1), :]
        out_ref[:, WIDTH * cols : WIDTH * (cols + 1)] = jnp.concatenate(
            [upper, lower], axis=1
        ).reshape(D, WIDTH)
    def norm_rows(here):
        x1 = x_ref[here, :].astype(F32) + (mm(attn_ref[here, :], out_ref[...]) + rows_ref[7:8, :])
        x1_ref[here, :] = x1
        centre = x1 - jnp.mean(x1, axis=-1, keepdims=True)
        spread = jnp.mean(centre * centre, axis=-1, keepdims=True)
        a2_ref[here, :] = (
            centre * lax.rsqrt(spread + norm_eps) * rows_ref[2:3, :] + rows_ref[3:4, :]
        ).astype(BF16)

    row_blocks(norm_rows)
    for cols in range(0, D, 256):
        a2t_ref[cols : cols + 256, :] = transposed(a2_ref[:, cols : cols + 256])
    load_up(flat, 3 * half_out, up, wide)
    load_down(flat, half_flat + 3 * half_out, down, wide)
    chunk_step(
        place, wide, bias_up_ref[0], dy_ref, a2_ref, a2t_ref, dyt_ref, up, down, act, dhidden,
        y_ref, back_ref, [(None, keep_ref, send_ref)], dbias_ref, True,
    )


def middle_rest_kernel(wide, count_in, place, *refs):
    pieces = refs[:count_in]
    (
        dy_ref, a2_ref, a2t_ref, dyt_ref, bias_up_ref, attn_ref, out_ref, rows_ref,
        y_in, back_in, x1_in,
        block_ref, dx1_ref, dmixed_ref, okeep_ref, osend_ref, vec_ref,
        keep_ref, send_ref, dbias_ref,
        flat, up, down, act, dhidden, back, dbranch, sems, flat_sems,
    ) = refs[count_in:]
    step = pl.program_id(0)
    y_copy = pltpu.make_async_copy(y_in, block_ref, sems.at[0])
    back_copy = pltpu.make_async_copy(back_in, back, sems.at[1])
    x1_copy = pltpu.make_async_copy(x1_in, dx1_ref, sems.at[2])

    def chunk_copies(chunk, side):
        if count_in == 1:
            return [
                pltpu.make_async_copy(
                    pieces[0].at[chunk], flat.at[chunk], flat_sems.at[chunk, 0]
                )
            ]
        copies = []
        for flip in range(2):
            column = place[1] if flip == 0 else 1 - place[1]
            for shift in range(4):
                shard = lax.rem(place[0] + 4 - shift, 4) * 2 + column
                copies.append(
                    pltpu.make_async_copy(
                        pieces[2 * side + flip].at[shift], flat.at[chunk, shard],
                        flat_sems.at[chunk, len(copies)],
                    )
                )
        return copies

    def fetch(chunk):
        for side in range(2):

            @pl.when((place[3] == chunk) if side == 0 else (place[3] != chunk))
            def _():
                if side == 0 or count_in > 1:
                    for copy in chunk_copies(chunk, side):
                        copy.start()

    def arrived(chunk):
        for copy in chunk_copies(chunk, 0):
            copy.wait()

    @pl.when(step == 0)
    def _():
        if count_in == 1:
            for chunk in range(2):
                for copy in chunk_copies(chunk, 0):
                    copy.start()
        else:
            fetch(0)
        y_copy.start()
        back_copy.start()
        if count_in > 1:
            fetch(1)
        x1_copy.start()
        arrived(0)
        y_copy.wait()
        back_copy.wait()

    @pl.when(step == 1)
    def _():
        arrived(1)

    load_up(flat.at[step], 0, up, wide)
    load_down(flat.at[step], 4 * (D // wide), down, wide)
    chunk_step(
        place, wide, bias_up_ref[0], dy_ref, a2_ref, a2t_ref, dyt_ref, up, down, act, dhidden,
        block_ref, back, [(None, keep_ref.at[0], send_ref.at[0])], dbias_ref, False,
    )

    @pl.when(step == 1)
    def _():
        x1_copy.wait()
        vec_ref[...] = jnp.zeros_like(vec_ref)

        def last_rows(here):
            x1 = dx1_ref[here, :]
            block_ref[here, :] = x1 + (block_ref[here, :] + rows_ref[8:9, :])
            dn = back[here, :]
            dy = dy_ref[here, :].astype(F32)
            centre = x1 - jnp.mean(x1, axis=-1, keepdims=True)
            spread = jnp.mean(centre * centre, axis=-1, keepdims=True)
            scale = lax.rsqrt(spread + norm_eps)
            zh = centre * scale
            vec_ref[0:1, :] += jnp.sum(dn * zh, axis=0, keepdims=True)
            vec_ref[1:2, :] += jnp.sum(dn, axis=0, keepdims=True)
            e = dn * rows_ref[2:3, :]
            dz = (
                e
                - jnp.mean(e, axis=-1, keepdims=True)
                - zh * jnp.mean(e * zh, axis=-1, keepdims=True)
            ) * scale
            dx1 = dy + dz
            dx1_ref[here, :] = dx1
            low = dx1.astype(BF16)
            dbranch[here, :] = low
            vec_ref[2:3, :] += jnp.sum(low.astype(F32), axis=0, keepdims=True)
            vec_ref[3:4, :] += jnp.sum(dy, axis=0, keepdims=True)
            dmixed_ref[here, :] = mm_nt(low, out_ref[...])

        row_blocks(last_rows)
        for cols in range(0, D, 256):
            up[cols : cols + 256, :] = transposed(attn_ref[:, cols : cols + 256])
        store_halves(mm(up[...], dbranch[...]).astype(BF16), place[3], okeep_ref, osend_ref)


def once(shape):
    return whole_spec(shape, pipeline_mode=pl.Buffered(1))


def struct(shape, dtype):
    return jax.ShapeDtypeStruct(shape, dtype)


def weight_scratch():
    return [
        pltpu.VMEM((D, FFC), BF16), pltpu.VMEM((FFC, D), BF16), pltpu.VMEM((LEN, FFC), BF16),
        pltpu.VMEM((LEN, FFC), BF16),
    ]


def middle_first(place, wide, pieces, tokens, attn, cotangent, vectors, bias_up):
    rows_flat = 3 * D // wide + 2 * FFC * D // (WIDTH * wide)
    half = (wide, FFC * D // (WIDTH * wide), WIDTH)
    outs = [
        struct((LEN, D), F32), struct((LEN, D), BF16), struct((D, LEN), BF16),
        struct((D, LEN), BF16), struct((LEN, D), F32), struct((LEN, D), F32),
        struct((D, D), BF16), struct(half, BF16), struct(half, BF16), struct((1, 1, FFC), F32),
    ]
    return pl.pallas_call(
        functools.partial(middle_first_kernel, wide, len(pieces)),
        grid_spec=pltpu.PrefetchScalarGridSpec(
            num_scalar_prefetch=1,
            grid=(1,),
            in_specs=[any_spec()] * len(pieces)
            + [
                once((LEN, D)), once((LEN, D)), once((LEN, D)), once((13, D)),
                pl.BlockSpec((1, 1, FFC), lambda *_: (0, 0, 0)),
            ],
            out_specs=[once(out.shape) for out in outs],
            scratch_shapes=[pltpu.VMEM((wide, rows_flat, WIDTH), BF16)]
            + weight_scratch()
            + [pltpu.SemaphoreType.DMA((16,))],
        ),
        out_shape=outs,
        compiler_params=pltpu.CompilerParams(
            dimension_semantics=("arbitrary",), vmem_limit_bytes=VMEM_LIMIT
        ),
        cost_estimate=cost(14 * 10**9, 30 * 10**6),
        name="middle_first",
    )(place, *pieces, tokens, attn, cotangent, vectors, bias_up)


def middle_rest(place, wide, pieces, cotangent, state, bias_up, attn, w_out, vectors, sums):
    a2, a2t, dyt = state
    half = (wide, FFC * D // (WIDTH * wide), WIDTH)
    out_half = (wide, 3 * D // (2 * wide), WIDTH)
    outs = [
        struct((LEN, D), F32), struct((LEN, D), F32), struct((LEN, D), F32),
        struct(out_half, BF16), struct(out_half, BF16), struct((8, D), F32),
        struct((2,) + half, BF16), struct((2,) + half, BF16), struct((2, 1, FFC), F32),
    ]
    out_specs = [once(out.shape) for out in outs[:6]]
    out_specs += [group_spec(half), group_spec(half), group_spec((1, FFC))]
    rows_flat = 2 * FFC * D // (WIDTH * wide)
    return pl.pallas_call(
        functools.partial(middle_rest_kernel, wide, len(pieces)),
        grid_spec=pltpu.PrefetchScalarGridSpec(
            num_scalar_prefetch=1,
            grid=(2,),
            in_specs=[any_spec()] * len(pieces)
            + [
                once((LEN, D)), once((LEN, D)), once((D, LEN)), once((D, LEN)),
                pl.BlockSpec((1, 1, FFC), lambda j, *_: (j + 1, 0, 0)),
                once((LEN, D)), once((D, D)), once((13, D)),
                any_spec(), any_spec(), any_spec(),
            ],
            out_specs=out_specs,
            scratch_shapes=[pltpu.VMEM((2, wide, rows_flat, WIDTH), BF16)]
            + weight_scratch()
            + [
                pltpu.VMEM((LEN, D), F32), pltpu.VMEM((LEN, D), BF16),
                pltpu.SemaphoreType.DMA((3,)), pltpu.SemaphoreType.DMA((2, 8)),
            ],
        ),
        out_shape=outs,
        compiler_params=pltpu.CompilerParams(
            dimension_semantics=("arbitrary",), vmem_limit_bytes=VMEM_LIMIT
        ),
        cost_estimate=cost(28 * 10**9, 40 * 10**6),
        name="middle_rest",
    )(place, *pieces, cotangent, a2, a2t, dyt, bias_up, attn, w_out, vectors, *sums)


def input_kernel(
    wide, x_ref, dx1_ref, da1_ref, rows_ref, middle_ref, bias_in_ref, bias_first_ref, bias_rest_ref,
    out_ref, vec_ref,
):
    gain = rows_ref[0:1, :]
    x = x_ref[...].astype(F32)
    dn = da1_ref[...]
    centre = x - jnp.mean(x, axis=-1, keepdims=True)
    spread = jnp.mean(centre * centre, axis=-1, keepdims=True)
    scale = lax.rsqrt(spread + norm_eps)
    zh = centre * scale
    e = dn * gain
    dz = (
        e - jnp.mean(e, axis=-1, keepdims=True) - zh * jnp.mean(e * zh, axis=-1, keepdims=True)
    ) * scale
    out_ref[...] = dx1_ref[...] + dz

    @pl.when(pl.program_id(0) == 0)
    def _():
        vec_ref[...] = jnp.zeros_like(vec_ref)
        vec_ref[2:4, :] = middle_ref[0:2, :]
        vec_ref[7:9, :] = middle_ref[2:4, :]
        for group in range(GROUPS):
            lanes = slice(WIDTH * group, WIDTH * (group + 1))
            for which in range(3):
                vec_ref[4 + which : 5 + which, lanes] = bias_in_ref[
                    group, :, WIDTH * which : WIDTH * (which + 1)
                ]
        for chunk in range(CHUNKS):
            for part in range(8):
                value = (
                    bias_first_ref[0] if chunk == 0 else bias_rest_ref[chunk - 1]
                )[:, 128 * part : 128 * (part + 1)]
                start = FFC * chunk + 128 * part if wide == 1 else 384 * part + 128 * chunk
                row, lane = 9 + start // D, start % D
                vec_ref[row : row + 1, lane : lane + 128] = value

    vec_ref[0:1, :] += jnp.sum(dn * zh, axis=0, keepdims=True)
    vec_ref[1:2, :] += jnp.sum(dn, axis=0, keepdims=True)


def input_side(wide, tokens, dx1, da1, vectors, middle_vec, bias_in, bias_first, bias_rest):
    block = pl.BlockSpec((256, D), lambda i: (i, 0))
    return pl.pallas_call(
        functools.partial(input_kernel, wide),
        grid=(LEN // 256,),
        in_specs=[
            block, block, block, whole_spec((13, D)), whole_spec((8, D)),
            whole_spec((GROUPS, 1, D)), whole_spec((1, 1, FFC)), whole_spec((2, 1, FFC)),
        ],
        out_specs=[block, whole_spec((16, D))],
        out_shape=[struct((LEN, D), F32), struct((16, D), F32)],
        compiler_params=pltpu.CompilerParams(dimension_semantics=("arbitrary",)),
        cost_estimate=cost(10**6, 12 * 10**6),
        name="input_side",
    )(tokens, dx1, da1, vectors, middle_vec, bias_in, bias_first, bias_rest)


def tables(lengths, projection):
    ends = jnp.cumsum(lengths[0])
    starts = ends - lengths[0]
    place = jnp.arange(LEN, dtype=jnp.int32)
    member = (place[:, None] >= starts[None, :]) & (place[:, None] < ends[None, :])
    offset = jnp.sum(jnp.where(member, starts[None, :], 0), axis=1)
    position = (place - offset).astype(F32)
    freq = 10000.0 ** (-jnp.arange(32, dtype=F32) / 32)
    angles = position[:, None] * jnp.tile(freq, 4)[None, :]
    onehot = jnp.pad(member.astype(BF16), ((0, 0), (0, 128 - member.shape[1])))
    eye = jnp.asarray(np.eye(4, dtype=np.float32))
    lifted = jnp.einsum("hif,ab->haibf", projection.reshape(2, 32, FEAT), eye)
    lifted = lifted.reshape(WIDTH, 128)
    rounded = lax.reduce_precision(lifted, 8, 7)
    high, low = rounded.astype(BF16), (lifted - rounded).astype(BF16)
    square = np.zeros((2, 4, 32, 4, 32), np.float32)
    for head in range(4):
        square[:, head, :, head, :] = 0.5
    square = jnp.asarray(square.reshape(WIDTH, 128), BF16)
    proj = jnp.stack(
        [
            jnp.concatenate([high, low], axis=1),
            jnp.concatenate([high, high], axis=1),
            jnp.concatenate([square, square], axis=1),
        ]
    )
    return jnp.cos(angles), jnp.sin(angles), onehot, proj


def wide_perm(shift_z, flip_x):
    pairs = []
    for z in range(4):
        for x in range(2):
            target_x = 1 - x if flip_x else x
            pairs.append((2 * z + x, 2 * ((z + shift_z) % 4) + target_x))
    return pairs


def narrow_perm(flip_y, flip_core):
    pairs = []
    for y in range(2):
        for core in range(2):
            pairs.append(
                (2 * y + core, 2 * (1 - y if flip_y else y) + (1 - core if flip_core else core))
            )
    return pairs


def over_z(values, shift):
    return lax.ppermute(values, "wide", wide_perm(shift, False))


def over_x(values):
    return lax.ppermute(values, "wide", wide_perm(0, True))


def over_far(values, bit):
    return lax.ppermute(values, "wide", [(w, w ^ bit) for w in range(8)])


def over_y(values):
    return lax.ppermute(values, "narrow", narrow_perm(True, False))


def over_core(values):
    return lax.ppermute(values, "narrow", narrow_perm(False, True))


def tie(*values):
    return lax.optimization_barrier(values)


def special():
    return lax.axis_size("wide") == 8 and lax.axis_size("narrow") == 4


def sum_wide(values):
    if not special():
        return lax.psum(values, "wide")
    for perm in (wide_perm(0, True), [(w, w ^ 2) for w in range(8)], [(w, w ^ 4) for w in range(8)]):
        values = values + lax.ppermute(values, "wide", perm)
    return values


def sum_narrow(values):
    if not special():
        return lax.psum(values, "narrow")
    pair = values + over_core(values)
    return pair + over_y(pair)


def along_z(mine):
    return jnp.stack([mine] + [over_z(mine, shift) for shift in (1, 2, 3)])


def small_call(kernel, name, place, operands, outs):
    return pl.pallas_call(
        kernel,
        grid_spec=pltpu.PrefetchScalarGridSpec(
            num_scalar_prefetch=1,
            grid=(1,),
            in_specs=[once(value.shape) for value in operands],
            out_specs=[once(out.shape) for out in outs],
        ),
        out_shape=outs,
        compiler_params=pltpu.CompilerParams(
            dimension_semantics=("arbitrary",), vmem_limit_bytes=VMEM_LIMIT
        ),
        cost_estimate=cost(10**6, sum(4 * math.prod(v.shape) for v in operands + outs)),
        name=name,
    )(place, *operands)


def held_call(kernel, name, place, operands, outs, held=None, flops=10**6):
    here = pl.BlockSpec(memory_space=pltpu.VMEM)
    held = len(outs) if held is None else held
    return pl.pallas_call(
        kernel,
        in_specs=[pl.BlockSpec(memory_space=pltpu.SMEM)] + [here] * len(operands),
        out_specs=[here] * len(outs),
        out_shape=[
            pltpu.VMEM(out.shape, out.dtype) if index < held else out
            for index, out in enumerate(outs)
        ],
        compiler_params=pltpu.CompilerParams(vmem_limit_bytes=24 * 1024 * 1024),
        cost_estimate=pl.CostEstimate(flops=flops, transcendentals=0, bytes_accessed=10**5),
        name=name,
    )(place, *[pltpu.with_memory_space_constraint(value, pltpu.VMEM) for value in operands])


def pick_kernel(
    place, in_ref, out_ref, up_ref, down_ref, near_ref, last_ref, first_ref, rest_ref
):
    core = place[3]
    here = pl.ds(pl.multiple_of(48 * core, 16), 48)
    for group in range(GROUPS):
        ref, index = (near_ref, group) if group < 2 else (last_ref, 0)
        for which in range(3):
            ref[index, :, WIDTH * which : WIDTH * (which + 1)] = in_ref[
                which, here, WIDTH * group : WIDTH * (group + 1)
            ].astype(BF16)
    for cols in range(3):
        first_ref[48 * cols : 48 * (cols + 1), :] = out_ref[
            here, WIDTH * cols : WIDTH * (cols + 1)
        ].astype(BF16)

    def put_up(ref, at, chunk):
        for cols in range(4):
            rows = slice(at + 96 * cols, at + 96 * (cols + 1))
            for side in range(2):
                start = 384 * (2 * cols + side) + 128 * chunk
                ref[rows, 128 * side : 128 * (side + 1)] = up_ref[:, start : start + 128].astype(
                    BF16
                )

    def put_down(ref, at, chunk):
        for cols in range(3):
            ref[at + 128 * cols : at + 128 * (cols + 1), :] = down_ref[
                128 * chunk : 128 * (chunk + 1), WIDTH * cols : WIDTH * (cols + 1)
            ].astype(BF16)

    for side in range(2):

        @pl.when(core == side)
        def _():
            if side == 0:
                put_up(first_ref, 144, 0)
            else:
                put_down(first_ref, 144, 0)

        @pl.when(core == side)
        def _():
            put_up(rest_ref, 0, 1 + side)
            put_down(rest_ref, 384, 1 + side)


def chunk_of(ref, chunk, shard):
    return ref[chunk, shard] if len(ref.shape) == 4 else ref[shard]


def first_sum_kernel(place, *refs):
    send_ref, keep_ref = refs[-2:]
    x = place[1]
    at = 0
    for index in range(0, len(refs) - 2, 2):
        own, got = refs[index], refs[index + 1]
        for part in range(own.shape[0] if len(own.shape) == 4 and own.shape[0] == 3 else 1):
            rows = own.shape[-2]
            here = pl.ds(at, rows)
            for z in range(4):
                for out, side in ((keep_ref, x), (send_ref, 1 - x)):
                    out[z, here, :] = (
                        chunk_of(own, part, 2 * z + side).astype(F32)
                        + chunk_of(got, part, 2 * z + side).astype(F32)
                    ).astype(BF16)
            at += rows


def first_sum(place, pairs):
    rows = sum(
        own.shape[-2] * (own.shape[0] if own.ndim == 4 and own.shape[0] == 3 else 1)
        for own, _ in pairs
    )
    return held_call(
        first_sum_kernel, "first_sum", place, [value for pair in pairs for value in pair],
        [struct((4, rows, WIDTH), BF16)] * 2,
    )


def first_sum_y_kernel(place, own, got, send, keep):
    y = place[2]
    for group in range(GROUPS):
        here = pl.ds(144 * group, 144)
        for shard in range(8):
            total = own[group, shard].astype(F32) + got[group, shard].astype(F32)
            left, right = total[:, :128].astype(BF16), total[:, 128:].astype(BF16)
            keep[shard, here, :] = jnp.where(y == 0, left, right)
            send[shard, here, :] = jnp.where(y == 0, right, left)


def split_x_kernel(place, own, got, send, keep):
    x = place[1]
    for z in range(4):
        for out, side in ((keep, x), (send, 1 - x)):
            out[z] = (own[2 * z + side].astype(F32) + got[2 * z + side].astype(F32)).astype(BF16)


def second_sum_kernel(place, own_ref, got_ref, *outs):
    z = place[0]
    for shift, out in enumerate(outs):
        there = lax.rem(z + shift, 4)
        out[...] = (own_ref[there].astype(F32) + got_ref[there].astype(F32)).astype(BF16)


def second_sum(place, own, got):
    outs = [struct(own.shape[1:], BF16)] * 4
    return held_call(second_sum_kernel, "second_sum", place, [own, got], outs)


def z_sum_kernel(place, *refs):
    total = refs[0][...].astype(F32)
    for ref in refs[1:4]:
        total = total + ref[...].astype(F32)
    rows = refs[0].shape[0]
    refs[-1][:rows, :] = total.astype(refs[-1].dtype)
    if len(refs) == 7:
        refs[-1][rows:, :] = (refs[4][...].astype(F32) + refs[5][...].astype(F32)).astype(BF16)


def z_sum(place, parts, below=(), got=None):
    if got is None:
        got = [over_z(parts[shift], shift) for shift in (1, 2, 3)]
    rows = parts[0].shape[0] + (below[0].shape[0] if below else 0)
    return held_call(
        z_sum_kernel, "z_sum", place, [parts[0]] + got + list(below),
        [struct((rows, parts[0].shape[1]), BF16 if below else F32)],
        flops=3 * 10**10 if below else 10**6,
    )[0]


def first_sum_z_kernel(place, *refs):
    z = place[0]
    outs = refs[-4:]
    for shift, out in enumerate(outs):
        there = lax.rem(z + shift, 4) * 2
        at = 0
        for index in range(0, len(refs) - 4, 2):
            own, got = refs[index], refs[index + 1]
            rows = own.shape[-2]
            for x in range(2):
                out[x, at : at + rows, :] = (
                    chunk_of(own, 1, there + x).astype(F32)
                    + chunk_of(got, 1, there + x).astype(F32)
                ).astype(BF16)
            at += rows


def first_sum_z(place, pairs):
    rows = sum(own.shape[-2] for own, _ in pairs)
    return held_call(
        first_sum_z_kernel, "first_sum_z", place, [value for pair in pairs for value in pair],
        [struct((2, rows, WIDTH), BF16)] * 4,
    )


def split_sum_kernel(place, *refs):
    keep, send = refs[-2:]
    x = place[1]
    for out, at in ((keep, x), (send, 1 - x)):
        total = refs[0][at].astype(F32)
        for ref in refs[1:4]:
            total = total + ref[at].astype(F32)
        out[...] = total.astype(BF16)


def split_sum(place, parts):
    return held_call(
        split_sum_kernel, "split_sum", place, parts, [struct(parts[0].shape[1:], BF16)] * 2
    )


def to_row(column):
    size = column.shape[0]
    eye = lax.broadcasted_iota(jnp.int32, (size, size), 0) == lax.broadcasted_iota(
        jnp.int32, (size, size), 1
    )
    return jnp.sum(jnp.where(eye, column, 0.0), axis=0, keepdims=True)


def to_column(row):
    size = row.shape[1]
    eye = lax.broadcasted_iota(jnp.int32, (size, size), 0) == lax.broadcasted_iota(
        jnp.int32, (size, size), 1
    )
    return jnp.sum(jnp.where(eye, row, 0.0), axis=1, keepdims=True)


DECAY = 1.0 - STEP ** (-0.8)


def lane_values(values):
    lane = lax.broadcasted_iota(jnp.int32, (1, D), 1)
    row = jnp.zeros((1, D), F32)
    for index, value in enumerate(values):
        row = jnp.where(lane == index, value, row)
    return row


def moments(grad, rows_old):
    plain = grad * grad
    squares = plain + square_eps
    mean = jnp.sum(squares, axis=1, keepdims=True) * (1.0 / grad.shape[1])
    rows_new = DECAY * rows_old + (1.0 - DECAY) * to_row(mean)
    total = jnp.sum(rows_new, axis=1, keepdims=True)
    divided = jnp.sum(plain * to_column(1.0 / rows_new), axis=0, keepdims=True)
    return rows_new, total, jnp.sum(squares, axis=0, keepdims=True), divided


def ffn_moments_kernel(
    place, own, got, up_rows, down_rows, out_rows,
    up_grad, down_grad, out_grad, up_rows_new, down_rows_new, out_rows_new, sums,
):
    core = place[3]

    def collect(low, high):
        for chunk in range(CHUNKS):
            at = 384 * chunk
            for cols in range(4):
                for side in range(2):
                    start = 384 * (2 * cols + side) + 128 * chunk
                    up_grad[:, start : start + 128] = low[
                        at + 96 * cols : at + 96 * (cols + 1), 128 * side : 128 * (side + 1)
                    ]
            for side in range(2):
                down_grad[128 * chunk : 128 * (chunk + 1), 384 * side : 384 * (side + 1)] = (
                    jnp.transpose(high[at : at + 384, 128 * side : 128 * (side + 1)])
                )
        for cols in range(3):
            lanes = slice(WIDTH * cols, WIDTH * (cols + 1))
            at = 1152 + 48 * cols
            out_grad[:48, lanes] = low[at : at + 48, :]
            out_grad[48:, lanes] = high[at : at + 48, :]

    @pl.when(core == 0)
    def _():
        collect(own, got)

    @pl.when(core == 1)
    def _():
        collect(got, own)

    up_new, up_total, up_sums, up_divided = moments(up_grad[...], up_rows[...])
    down_new, down_total, down_sums, down_divided = moments(down_grad[...], down_rows[...])
    out_new, out_total, out_sums, out_divided = moments(out_grad[...], out_rows[...])
    up_rows_new[...] = up_new
    down_rows_new[...] = down_new
    out_rows_new[...] = out_new
    for part in range(4):
        lanes = slice(D * part, D * (part + 1))
        sums[part : part + 1, :] = up_sums[:, lanes]
        sums[4 + part : 5 + part, :] = up_divided[:, lanes]
    sums[8:9, :] = down_sums
    sums[9:10, :] = down_divided
    sums[10:11, :] = out_sums
    sums[11:12, :] = out_divided
    sums[12:13, :] = lane_values([up_total, down_total, out_total])
    sums[13:16, :] = jnp.zeros((3, D), F32)


def in_moments_kernel(
    place, own, own_y, other, other_y, rows_old, vector, ffn_sums, grad, rows_new, sums,
):
    def collect(low, high):
        for group in range(GROUPS):
            for which in range(3):
                rows = slice(144 * group + 48 * which, 144 * group + 48 * (which + 1))
                for side in range(2):
                    start = WIDTH * group + 128 * side
                    grad[which, :48, start : start + 128] = low[side][rows, :]
                    grad[which, 48:, start : start + 128] = high[side][rows, :]

    for core in range(2):
        for y in range(2):

            @pl.when((place[3] == core) & (place[2] == y))
            def _():
                mine = (own, own_y) if y == 0 else (own_y, own)
                far = (other, other_y) if y == 0 else (other_y, other)
                collect(mine if core == 0 else far, far if core == 0 else mine)

    totals = []
    for which in range(3):
        new, total, columns, divided = moments(grad[which], rows_old[which : which + 1, :])
        rows_new[which : which + 1, :] = new
        sums[which : which + 1, :] = columns
        sums[3 + which : 4 + which, :] = divided
        totals.append(total)
    sums[6:7, :] = lane_values(totals)
    sums[7:8, :] = jnp.zeros((1, D), F32)
    sums[8:24, :] = vector[...]
    sums[24:40, :] = ffn_sums[...]


def matrix_step(weight, grad, rows, cols, total, col_sums, divided, rows_full, rate):
    cols_new = DECAY * cols + (1.0 - DECAY) * col_sums * (1.0 / rows_full)
    mean = total * (1.0 / rows_full)
    square_sum = mean * jnp.sum(divided / cols_new, axis=1, keepdims=True)
    rms = jnp.sqrt(square_sum * (1.0 / (rows_full * grad.shape[1])))
    factor = to_column(lax.rsqrt(rows / mean)) * (rate / jnp.maximum(1.0, rms / clip_level))
    return cols_new, weight - grad * factor * lax.rsqrt(cols_new)


def finish_kernel(
    place, inward, up, down, out, in_grad, up_grad, down_grad, out_grad, in_rows, up_rows,
    down_rows, out_rows, in_cols, up_cols, down_cols, out_cols, sums, vectors, vector_state,
    in_cols_new, up_cols_new, down_cols_new, out_cols_new, in_next, up_next, down_next, out_next,
    vector_grad, state_next, vectors_next,
):
    base_rate = 0.3 * D ** (-0.5)
    for which in range(3):
        here = slice(which, which + 1)
        in_cols_new[here, :], in_next[which] = matrix_step(
            inward[which], in_grad[which], in_rows[here, :], in_cols[here, :],
            sums[6:7, which : which + 1], sums[here, :], sums[3 + which : 4 + which, :], D,
            base_rate,
        )

    def wide_row(first):
        return jnp.concatenate([sums[first + i : first + i + 1, :] for i in range(4)], axis=1)

    up_cols_new[...], up_next[...] = matrix_step(
        up[...], up_grad[...], up_rows[...], up_cols[...], sums[36:37, 0:1], wide_row(24),
        wide_row(28), D, base_rate,
    )
    down_cols_new[...], down_next[...] = matrix_step(
        down[...], down_grad[...], down_rows[...], down_cols[...], sums[36:37, 1:2],
        sums[32:33, :], sums[33:34, :], FF, 0.3 * FF ** (-0.5),
    )
    out_cols_new[...], out_next[...] = matrix_step(
        out[...], out_grad[...], out_rows[...], out_cols[...], sums[36:37, 2:3],
        sums[34:35, :], sums[35:36, :], D, 1.2 * D ** (-0.5),
    )
    g = sums[8:21, :]
    vector_grad[...] = g
    state = DECAY * vector_state[...] + (1.0 - DECAY) * (g * g + square_eps)
    state_next[...] = state
    update = g * lax.rsqrt(state)
    total = jnp.sum(jnp.sum(update * update, axis=0, keepdims=True), axis=1, keepdims=True)
    rms = jnp.sqrt(total * (1.0 / (13 * D)))
    vectors_next[...] = vectors[...] - update * (0.25 / jnp.maximum(1.0, rms / clip_level))


def shards(
    tokens, cotangent, lengths, projection, inward, outward, expand, shrink, vectors,
    inward_rows, inward_columns, outward_rows, outward_columns, expand_rows, expand_columns,
    shrink_rows, shrink_columns, vector_state,
):
    full = special()
    rows = outward.shape[0]
    wide = 8 if full else 1
    wide_at = lax.axis_index("wide").astype(jnp.int32)
    narrow_at = lax.axis_index("narrow").astype(jnp.int32)
    core = narrow_at % 2 if full else jnp.int32(0)
    place = jnp.stack([wide_at // 2, wide_at % 2, narrow_at // 2, core])
    per = FFC // wide
    cosine, sine, onehot, proj = tables(lengths, projection)
    if full:
        *own_in, own_first, own_rest = small_call(
            pick_kernel, "pick", place, [inward, outward, expand, shrink],
            [
                struct((2, 48, D), BF16), struct((1, 48, D), BF16), struct((528, WIDTH), BF16),
                struct((768, WIDTH), BF16),
            ],
        )
        in_z = [along_z(value) for value in own_in]
        *in_z, own_first, cosine, sine, onehot, proj = tie(
            *in_z, own_first, cosine, sine, onehot, proj
        )
        first_z = along_z(own_first)
        in_x = [over_x(value) for value in in_z]
        pieces_in = []
        *in_z, first_z = tie(*in_z, *in_x, first_z)
        for near, far in zip(in_z[:2], in_z[2:]):
            pieces_in += [near, far, over_core(near), over_core(far)]
        *pieces_in, first_z, own_rest = tie(*pieces_in, first_z, own_rest)
        first_x = over_x(first_z)
        rest_got = [over_z(own_rest, shift) for shift in (1, 2, 3)]
    else:
        in_low = lax.all_gather(inward.astype(BF16), "wide", axis=1, tiled=True)
        out_low = lax.all_gather(outward.astype(BF16), "wide", axis=0, tiled=True)
        up_low = lax.all_gather(expand.astype(BF16), "wide", axis=0, tiled=True)
        down_low = lax.all_gather(shrink.astype(BF16), "wide", axis=0, tiled=True)
        units = jnp.transpose(in_low.reshape(3, D, GROUPS, WIDTH), (2, 1, 0, 3))
        pieces_in = [units.reshape(1, 3 * D, D)]

        def blocks(matrix):
            count = matrix.shape[1] // WIDTH
            return jnp.transpose(matrix.reshape(-1, count, WIDTH), (1, 0, 2)).reshape(-1, WIDTH)

        ups = [blocks(up_low[:, FFC * j : FFC * (j + 1)]) for j in range(CHUNKS)]
        downs = [blocks(down_low[FFC * j : FFC * (j + 1)]) for j in range(CHUNKS)]
        half = D // 2
        pieces_first = [
            jnp.concatenate([blocks(out_low[:half]), ups[0], blocks(out_low[half:]), downs[0]])[
                None
            ]
        ]
        pieces_rest = [
            jnp.stack([jnp.concatenate([ups[j], downs[j]])[None] for j in range(1, CHUNKS)])
        ]
    perm = jnp.asarray(head_perm(), BF16)
    block_ones = np.kron(np.eye(2, dtype=np.float32), np.ones((64, 64), np.float32))
    ones = jnp.asarray(np.concatenate([block_ones, block_ones]), BF16)
    split = vectors[4:6].reshape(2, GROUPS, 4, 2, 32)
    bias_qk = jnp.transpose(split, (0, 1, 3, 2, 4)).reshape(2, GROUPS, WIDTH)
    bias = jnp.concatenate([bias_qk, vectors[6].reshape(1, GROUPS, WIDTH)])
    bias = jnp.transpose(bias, (1, 0, 2))
    bias_up = vectors[9:].reshape(wide, CHUNKS, per)
    bias_up = jnp.transpose(bias_up, (1, 0, 2)).reshape(CHUNKS, 1, FFC)
    attn, mixed, a1t, w_in, wq, wk, qf, kf, v, rden = attend(
        lengths, place, pieces_in, wide, tokens, vectors[:2], bias, perm, proj, cosine, sine,
        onehot,
    )
    if full:
        attn, first_x, *rest_got = tie(attn, first_x, *rest_got)
        rest_z = jnp.stack([own_rest] + rest_got)
        first_cores = [over_core(first_z), over_core(first_x)]
        *first_cores, rest_z = tie(*first_cores, rest_z)
        pieces_first = [first_z, first_x] + first_cores
        rest_x = over_x(rest_z)
    x1, a2, a2t, dyt, y, back, w_out, keep0, send0, dbias0 = middle_first(
        place, wide, pieces_first, tokens, attn, cotangent, vectors, bias_up
    )
    if full:
        rest_core = over_core(rest_z)
        rest_x, rest_core, send0, y = tie(rest_x, rest_core, send0, y)
        pieces_rest = [rest_z, rest_x, rest_core, over_core(rest_x)]
        got0 = over_core(send0)
    (
        block_out, dx1, dmixed, okeep, osend, middle_vec, keep12, send12, dbias12,
    ) = middle_rest(
        place, wide, pieces_rest, cotangent, (a2, a2t, dyt), bias_up, attn, w_out, vectors,
        (y, back, x1),
    )
    if full:
        got0, send12, osend = tie(got0, send12, osend)
        got12 = over_core(send12)
        send_b, keep_b = first_sum(place, [(keep0, got0), (keep12, got12)])
        e_parts = first_sum_z(place, [(keep12, got12), (okeep, over_core(osend))])
        dmixed, send_b, keep_b, *e_parts = tie(dmixed, send_b, keep_b, *e_parts)
        got_b = over_x(send_b)
        e_got = [over_z(e_parts[shift], shift) for shift in (1, 2, 3)]
    saved = (mixed, rden, wq, wk, qf, kf, v)
    in_keep, in_send, in_bias, da1 = attend_back(
        lengths, place, wide, dmixed, saved, a1t, w_in, perm, proj, cosine, sine, onehot, ones
    )
    if full:
        keep_e, send_e = split_sum(place, [e_parts[0]] + e_got)
        send_e, in_send, keep_b, got_b, da1 = tie(send_e, in_send, keep_b, got_b, da1)
        got_e = over_x(send_e)
        b_parts = second_sum(place, keep_b, got_b)
        got_in = over_core(in_send)
        got_in, *b_parts = tie(got_in, *b_parts)
        send_c, keep_c = held_call(
            first_sum_y_kernel, "first_sum_y", place, [in_keep, got_in],
            [struct((8, 432, 128), BF16)] * 2,
        )
        da1, send_c, got_e = tie(da1, send_c, got_e)
        got_c = over_y(send_c)
    input_grad, vector_local = input_side(
        wide, tokens, dx1, da1, vectors, middle_vec, in_bias, dbias0, dbias12
    )
    if full:
        vector_part = sum_narrow(vector_local)

        def pair_sum(mine, got):
            half_sum = mine.astype(F32) + got.astype(F32)
            return half_sum, over_core(half_sum)

        got_c, input_grad, vector_part = tie(got_c, input_grad, vector_part)
        send_c, keep_c = held_call(
            split_x_kernel, "split_x", place, [keep_c, got_c], [struct((4, 432, 128), BF16)] * 2
        )
        got_c = over_x(send_c)
        ffn_mine = z_sum(place, b_parts, (keep_e, got_e))
        ffn_mine, got_c = tie(ffn_mine, got_c)
        c_parts = second_sum(place, keep_c, got_c)
        ffn_mine, *c_parts = tie(ffn_mine, *c_parts)
        ffn_y = over_y(ffn_mine)
        c_got = [over_z(c_parts[shift], shift) for shift in (1, 2, 3)]
        ffn_y, *c_got = tie(ffn_y, *c_got)
        c_mine = z_sum(place, c_parts, (), c_got)
        c_mine, ffn_y = tie(c_mine, ffn_y)
        c_y = over_y(c_mine)
        c_core = over_core(c_mine)
        ffn_own, ffn_got = pair_sum(ffn_mine, ffn_y)
        expand_grad, shrink_grad, outward_grad, up_rows, down_rows, out_rows, sums = held_call(
            ffn_moments_kernel, "ffn_moments", place,
            [
                ffn_own, ffn_got, expand_rows[None], shrink_rows[None], outward_rows[None],
            ],
            [
                struct(expand.shape, F32), struct(shrink.shape, F32), struct(outward.shape, F32),
                struct((1, 96), F32), struct((1, 384), F32), struct((1, 96), F32),
                struct((16, D), F32),
            ],
            0,
        )
        c_y, sums = tie(c_y, sums)
        inward_grad, in_rows, sums = held_call(
            in_moments_kernel, "in_moments", place,
            [c_mine, c_y, c_core, over_core(c_y), inward_rows, vector_part, sums],
            [struct(inward.shape, F32), struct((3, 96), F32), struct((40, D), F32)],
            0,
        )
        sums = sum_wide(sums)
        (
            in_cols, up_cols, down_cols, out_cols, inward_next, expand_next, shrink_next,
            outward_next, vector_grad, vector_state_next, vectors_next,
        ) = small_call(
            finish_kernel, "finish", place,
            [
                inward, expand, shrink, outward, inward_grad, expand_grad, shrink_grad,
                outward_grad, in_rows, up_rows, down_rows, out_rows, inward_columns,
                expand_columns[None], shrink_columns[None], outward_columns[None], sums, vectors,
                vector_state,
            ],
            [
                struct((3, D), F32), struct((1, FF), F32), struct((1, D), F32),
                struct((1, D), F32), struct(inward.shape, F32), struct(expand.shape, F32),
                struct(shrink.shape, F32), struct(outward.shape, F32), struct((13, D), F32),
                struct((13, D), F32), struct((13, D), F32),
            ],
        )
        return (
            block_out, input_grad, inward_grad, outward_grad, expand_grad, shrink_grad,
            vector_grad, in_rows, in_cols, out_rows[0], out_cols[0], up_rows[0], up_cols[0],
            down_rows[0], down_cols[0], vector_state_next, inward_next, outward_next,
            expand_next, shrink_next, vectors_next,
        )
    vector_part = sum_narrow(vector_local[:13])

    def reduced(values, axis):
        part = lax.psum_scatter(values, "wide", scatter_dimension=axis, tiled=True)
        return lax.psum(part.astype(F32), "narrow")

    keeps = [keep0, keep12[0], keep12[1]]
    sends = [send0, send12[0], send12[1]]
    up_grads = [
        jnp.transpose(keep.reshape(4, D, WIDTH), (1, 0, 2)).reshape(D, FFC) for keep in keeps
    ]
    down_grads = [
        jnp.transpose(send.reshape(4, D, WIDTH), (0, 2, 1)).reshape(FFC, D) for send in sends
    ]
    expand_grad = reduced(jnp.concatenate(up_grads, axis=1), 0)
    shrink_grad = reduced(jnp.concatenate(down_grads, axis=0), 0)

    def rebuilt(keep, send):
        return jnp.concatenate(
            [keep.reshape(-1, 3, D // 2, WIDTH), send.reshape(-1, 3, D // 2, WIDTH)], axis=2
        )

    outward_grad = reduced(jnp.transpose(rebuilt(okeep, osend)[0], (1, 0, 2)).reshape(D, D), 0)
    in_units = rebuilt(in_keep, in_send)
    inward_grad = reduced(jnp.transpose(in_units, (1, 2, 0, 3)).reshape(3, D, D), 1)
    decay = 1.0 - STEP ** (-0.8)
    wide_count = lax.axis_size("wide")
    grads_list = [inward_grad, outward_grad[None], expand_grad[None], shrink_grad[None]]
    rows_old = [inward_rows, outward_rows[None], expand_rows[None], shrink_rows[None]]
    columns_old = [
        inward_columns,
        outward_columns[None],
        expand_columns[None],
        shrink_columns[None],
    ]
    weights_old = [inward, outward[None], expand[None], shrink[None]]
    rates = [0.3 * D ** (-0.5), 1.2 * D ** (-0.5), 0.3 * D ** (-0.5), 0.3 * FF ** (-0.5)]
    bounds = [0, 3, 4, 5, 6]
    rows_next = []
    column_parts = []
    for member in range(4):
        squares = grads_list[member] * grads_list[member] + square_eps
        rows_next.append(decay * rows_old[member] + (1.0 - decay) * jnp.mean(squares, axis=-1))
        column_parts.append(jnp.sum(squares, axis=-2))
    row_totals = jnp.concatenate([jnp.sum(entry, axis=-1) for entry in rows_next])
    shapes = [part.shape for part in column_parts] + [row_totals.shape, vector_part.shape]
    flat = jnp.concatenate(
        [part.reshape(-1) for part in column_parts + [row_totals, vector_part]]
    )
    flat = jnp.pad(flat, (0, -flat.shape[0] % 1024)).reshape(-1, 128)
    flat = sum_wide(flat).reshape(-1)
    summed = []
    offset = 0
    for shape in shapes:
        size = 1
        for extent in shape:
            size *= extent
        summed.append(flat[offset : offset + size].reshape(shape))
        offset += size
    column_sums = list(summed[0:4])
    totals_sum = summed[4]
    vector_grad = summed[5]
    columns_next = []
    scaled_list = []
    row_means = []
    sizes_full = []
    for member in range(4):
        grad_now = grads_list[member]
        rows_full = grad_now.shape[-2] * wide_count
        sizes_full.append(rows_full * grad_now.shape[-1])
        columns_next.append(
            decay * columns_old[member] + (1.0 - decay) * column_sums[member] / rows_full
        )
        row_mean = totals_sum[bounds[member] : bounds[member + 1]] / rows_full
        row_means.append(row_mean)
        scaled_list.append(
            grad_now
            * lax.rsqrt(rows_next[member] / row_mean[:, None])[..., None]
            * lax.rsqrt(columns_next[member])[:, None, :]
        )
    partial_squares = jnp.concatenate(
        [jnp.sum(entry * entry, axis=(-2, -1)) for entry in scaled_list]
    )
    total_squares = sum_wide(jnp.pad(partial_squares, (0, 122)).reshape(1, 128))[0, :6]
    rms_list = [
        jnp.sqrt(total_squares[bounds[member] : bounds[member + 1]] / sizes_full[member])
        for member in range(4)
    ]
    weights_next = []
    for member in range(4):
        limiter = jnp.maximum(1.0, rms_list[member] / clip_level)
        weights_next.append(
            weights_old[member] - rates[member] * scaled_list[member] / limiter[:, None, None]
        )
    vector_state_next = decay * vector_state + (1.0 - decay) * (
        vector_grad * vector_grad + square_eps
    )
    vector_update = vector_grad * lax.rsqrt(vector_state_next)
    vector_rms = jnp.sqrt(jnp.mean(vector_update * vector_update))
    vectors_next = vectors - 0.25 * vector_update / jnp.maximum(1.0, vector_rms / clip_level)
    return (
        block_out,
        input_grad,
        inward_grad,
        outward_grad,
        expand_grad,
        shrink_grad,
        vector_grad,
        rows_next[0],
        columns_next[0],
        rows_next[1][0],
        columns_next[1][0],
        rows_next[2][0],
        columns_next[2][0],
        rows_next[3][0],
        columns_next[3][0],
        vector_state_next,
        weights_next[0],
        weights_next[1][0],
        weights_next[2][0],
        weights_next[3][0],
        vectors_next,
    )


def solution(mesh):
    placed = (
        P(("narrow", "wide"), None),
        P(("narrow", "wide"), None),
        P(("narrow", "wide"), None),
        P(),
        P(None, "wide", None),
        P("wide", None),
        P("wide", None),
        P("wide", None),
        P(),
        P(None, "wide"),
        P(),
        P("wide"),
        P(),
        P("wide"),
        P(),
        P("wide"),
        P(),
        P(),
    )
    return jax.shard_map(
        shards,
        mesh=mesh,
        in_specs=placed,
        out_specs=(
            P(("narrow", "wide"), None),
            P(("narrow", "wide"), None),
            P(None, "wide", None),
            P("wide", None),
            P("wide", None),
            P("wide", None),
            P(),
            P(None, "wide"),
            P(),
            P("wide"),
            P(),
            P("wide"),
            P(),
            P("wide"),
            P(),
            P(),
            P(None, "wide", None),
            P("wide", None),
            P("wide", None),
            P("wide", None),
            P(),
        ),
        check_vma=False,
    )
```

```python
import functools
import math

import jax
import jax.numpy as jnp
import numpy as np
from jax import lax
from jax.experimental import pallas as pl
from jax.experimental.pallas import tpu as pltpu
from jax.sharding import PartitionSpec as P

D = 768
HEADS = 12
HD = 64
FF = 3072
FEAT = 32
STEP = 10
LEN = 1024
SPAN = 256
CHUNKS = 3
GROUPS = 3
WIDTH = 256
FFC = FF // CHUNKS

norm_eps = 1e-05
square_eps = 1e-30
clip_level = 1.0

F32 = jnp.float32
BF16 = jnp.bfloat16
VMEM_LIMIT = 60 * 1024 * 1024
REST_LIMIT = 54 * 1024 * 1024
BACK_LIMIT = 46 * 1024 * 1024


def mm(left, right):
    return lax.dot_general(left, right, (((1,), (0,)), ((), ())), preferred_element_type=F32)


def mm_nt(left, right):
    return lax.dot_general(left, right, (((1,), (1,)), ((), ())), preferred_element_type=F32)


def mm_tn(left, right):
    return lax.dot_general(left, right, (((0,), (0,)), ((), ())), preferred_element_type=F32)


def halves(values):
    high = values.astype(BF16)
    return high, (values - high.astype(F32)).astype(BF16)


TAIL = (
    0.1795078068971634,
    0.17978088557720184,
    0.14234966039657593,
    0.06379217654466629,
    0.0434231162071228,
    -0.261725515127182,
    0.20454804599285126,
    -0.05167665705084801,
)


def normal_parts(values):
    size = jnp.abs(values)
    t = 1.0 / (1.0 + 0.45 * size)
    poly = TAIL[-1]
    for coeff in TAIL[-2::-1]:
        poly = poly * t + coeff
    bell = jnp.exp(-0.5 * values * values)
    tail = poly * t * bell
    return jnp.where(values >= 0, 1.0 - tail, tail), bell * 0.3989422804014327


def transposed(values):
    row = lax.broadcasted_iota(jnp.int32, (256, 256), 0)
    col = lax.broadcasted_iota(jnp.int32, (256, 256), 1)
    eye = (row == col).astype(F32).astype(BF16)
    return mm_nt(eye, values).astype(BF16)


def head_perm():
    perm = np.zeros((WIDTH, WIDTH), np.float32)
    for head in range(4):
        for half in range(2):
            for i in range(32):
                perm[head * 64 + half * 32 + i, half * 128 + head * 32 + i] = 1.0
    return perm


def make_blocks(lengths, base, first, last):
    def step(s, carry):
        count, begin, begin_row, end = carry
        new_end = end + lengths[0, s]
        full = new_end - begin_row > SPAN

        @pl.when(full)
        def _():
            base[count] = begin_row
            first[count] = begin
            last[count] = s - 1

        row = jnp.minimum((end // 16) * 16, LEN - SPAN)
        return (
            jnp.where(full, count + 1, count),
            jnp.where(full, s, begin),
            jnp.where(full, row, begin_row),
            new_end,
        )

    segments = lengths.shape[1]
    zero = jnp.int32(0)
    count, begin, begin_row, _ = lax.fori_loop(0, segments, step, (zero, zero, zero, zero))
    base[count] = begin_row
    first[count] = begin
    last[count] = segments - 1
    return count + 1


def lane_mask(lo, hi, width, dtype):
    lane = lax.broadcasted_iota(jnp.int32, (1, width), 1)
    return ((lane >= lo) & (lane < hi)).astype(F32).astype(dtype)


def value_rows(v_pair, head):
    keep = lane_mask(64 * head, 64 * head + 64, 128, BF16)
    return jnp.concatenate([v_pair * keep, jnp.broadcast_to(keep, v_pair.shape)], axis=1)


def span_mask(onehot, rows, lo, hi):
    member = onehot[rows, :]
    lane = lax.broadcasted_iota(jnp.int32, (1, 128), 1)
    inside = ((lane >= lo) & (lane <= hi)).astype(F32).astype(BF16)
    return mm_nt(member * inside, member).astype(BF16)


def cost(flops, size):
    return pl.CostEstimate(flops=10**6, transcendentals=0, bytes_accessed=10**5)


def row_blocks(body, loop=False):
    if not loop:
        for rows in range(0, LEN, 256):
            body(pl.ds(rows, 256))
        return

    def step(index, carry):
        body(pl.ds(pl.multiple_of(index * 256, 256), 256))
        return carry

    lax.fori_loop(0, LEN // 256, step, 0)


def any_spec():
    return pl.BlockSpec(memory_space=pl.ANY)


def in_copies(place, pieces, dst, sems, unit):
    if len(pieces) == 1:
        rows = dst.shape[1] // 3
        here = pl.ds(unit * rows, rows)
        return [pltpu.make_async_copy(pieces[0].at[:, here], dst.at[:, here], sems.at[unit, 0])]
    z, x, core = place[0], place[1], place[3]
    part, index = (0, unit) if unit < 2 else (4, 0)
    copies = []
    for side in range(2):
        half = core if side == 0 else 1 - core
        for flip in range(2):
            column = x if flip == 0 else 1 - x
            for shift in range(4):
                row = lax.rem(z + 4 - shift, 4) * 2 + column
                start = pl.multiple_of(unit * 96 + half * 48, 16)
                copies.append(
                    pltpu.make_async_copy(
                        pieces[part + 2 * side + flip].at[shift, index],
                        dst.at[row, pl.ds(start, 48)],
                        sems.at[unit, len(copies)],
                    )
                )
    return copies


def flat_copies(place, pieces, dst, sems):
    if len(pieces) == 1:
        return [pltpu.make_async_copy(pieces[0], dst, sems.at[0])]
    z, x, core = place[0], place[1], place[3]
    span = dst.shape[1] // 2
    copies = []
    for side in range(2):
        half = core if side == 0 else 1 - core
        for flip in range(2):
            column = x if flip == 0 else 1 - x
            for shift in range(4):
                row = lax.rem(z + 4 - shift, 4) * 2 + column
                start = pl.multiple_of(half * span, 16)
                copies.append(
                    pltpu.make_async_copy(
                        pieces[2 * side + flip].at[shift],
                        dst.at[row, pl.ds(start, span)],
                        sems.at[len(copies)],
                    )
                )
    return copies


def attend_kernel(count_in, lengths, place, *refs):
    pieces = refs[:count_in]
    (
        x_ref, norm_ref, bias_ref, perm_ref, proj_ref, cos_ref, sin_ref, onehot_ref,
        attn_ref, mixed_ref, a1t_ref, w_ref, wq_ref, wk_ref, qf_ref, kf_ref, v_ref, rden_ref,
        a1, qb, kb, vb, parts, base, first, last, sems,
    ) = refs[count_in:]
    group = pl.program_id(0)

    @pl.when(group == 0)
    def _():
        for unit in range(GROUPS):
            for copy in in_copies(place, pieces, w_ref, sems, unit):
                copy.start()
        def norm_rows(here):
            x = x_ref[here, :].astype(F32)
            centre = x - jnp.mean(x, axis=-1, keepdims=True)
            spread = jnp.mean(centre * centre, axis=-1, keepdims=True)
            a1[here, :] = (
                centre * lax.rsqrt(spread + norm_eps) * norm_ref[0:1, :] + norm_ref[1:2, :]
            ).astype(BF16)

        row_blocks(norm_rows)
        for cols in range(0, D, 256):
            a1t_ref[cols : cols + 256, :] = transposed(a1[:, cols : cols + 256])

    for unit in range(GROUPS):

        @pl.when(group == unit)
        def _():
            for copy in in_copies(place, pieces, w_ref, sems, unit):
                copy.wait()

    count = make_blocks(lengths, base, first, last)
    shard = w_ref.shape[1] // 3
    here = pl.ds(pl.multiple_of(group * shard, 16), shard)
    w = w_ref[:, here, :].reshape(D, D)
    perm = perm_ref[...]
    bias = bias_ref[0]
    proj_both = proj_ref[0]
    proj_high = proj_ref[1, :, :128]
    square = proj_ref[2, :, :128]
    weights = [mm(w[:, WIDTH * i : WIDTH * (i + 1)], perm).astype(BF16) for i in range(2)]

    def feature_rows(here):
        for which, (out_w, out_f, low_f) in enumerate(
            ((wq_ref, qf_ref, qb), (wk_ref, kf_ref, kb))
        ):
            u = (mm(a1[here, :], weights[which]) + bias[which : which + 1, :]) * HD ** (-0.25)
            c = u[:, :128]
            e = u[:, 128:]
            cosine = cos_ref[here, :]
            sine = sin_ref[here, :]
            turned = jnp.concatenate([c * cosine - e * sine, e * cosine + c * sine], axis=1)
            out_w[0, here, :] = turned
            high, low = halves(turned)
            sq_high, sq_low = halves(turned * turned)
            both = mm(high, proj_both)
            logits = (
                both[:, :128] + both[:, 128:] + mm(low, proj_high)
                - (mm(sq_high, square) + mm(sq_low, square))
            )
            phi = jnp.exp(logits) * FEAT ** (-0.5)
            out_f[0, here, :] = phi
            low_f[here, :] = phi.astype(BF16)
        v = mm(a1[here, :], w[:, 2 * WIDTH :]) + bias[2:3, :]
        v_ref[0, here, :] = v
        vb[here, :] = v.astype(BF16)

    row_blocks(feature_rows)
    parts[...] = jnp.zeros_like(parts)

    def one_span(index, carry):
        rows = pl.ds(pl.multiple_of(base[index], 16), SPAN)
        mask = span_mask(onehot_ref, rows, first[index], last[index])
        q = qb[rows, :]
        k = kb[rows, :]
        for pair in range(2):
            v_pair = vb[rows, 128 * pair : 128 * (pair + 1)]
            total = jnp.zeros((SPAN, WIDTH), F32)
            for side in range(2):
                head = 2 * pair + side
                scores = mm_nt(q * lane_mask(32 * head, 32 * head + 32, 128, BF16), k)
                total = total + mm(scores.astype(BF16) * mask, value_rows(v_pair, side))
            parts[pair, rows, :] += total
        return carry

    lax.fori_loop(0, count, one_span, 0)
    for pair in range(2):
        lanes = slice(128 * pair, 128 * (pair + 1))
        inverse = 1.0 / parts[pair, :, 128:]
        rden_ref[0, :, lanes] = inverse
        mixed = parts[pair, :, :128] * inverse
        mixed_ref[0, :, lanes] = mixed
        attn_ref[:, lanes] = mixed.astype(BF16)


def whole_spec(shape, **options):
    return pl.BlockSpec(shape, lambda *_: (0,) * len(shape), **options)


def group_spec(shape):
    return pl.BlockSpec((1,) + shape, lambda g, *_: (g,) + (0,) * len(shape))


def attend(lengths, place, pieces, wide, tokens, norm, bias, perm, proj, cosine, sine, onehot):
    def out(shape, dtype):
        return jax.ShapeDtypeStruct((GROUPS,) + shape, dtype)

    rows_in = 3 * D // wide
    return pl.pallas_call(
        functools.partial(attend_kernel, len(pieces)),
        grid_spec=pltpu.PrefetchScalarGridSpec(
            num_scalar_prefetch=2,
            grid=(GROUPS,),
            in_specs=[any_spec()] * len(pieces)
            + [
                whole_spec((LEN, D)), whole_spec((2, D)), group_spec((3, WIDTH)),
                whole_spec((WIDTH, WIDTH)), whole_spec((3, WIDTH, WIDTH)), whole_spec((LEN, 128)),
                whole_spec((LEN, 128)), whole_spec((LEN, 128)),
            ],
            out_specs=[
                pl.BlockSpec((LEN, WIDTH), lambda g, *_: (0, g)), group_spec((LEN, WIDTH)),
                whole_spec((D, LEN)), whole_spec((wide, rows_in, D)), group_spec((LEN, WIDTH)),
                group_spec((LEN, WIDTH)), group_spec((LEN, 128)), group_spec((LEN, 128)),
                group_spec((LEN, WIDTH)), group_spec((LEN, WIDTH)),
            ],
            scratch_shapes=[
                pltpu.VMEM((LEN, D), BF16),
                pltpu.VMEM((LEN, 128), BF16), pltpu.VMEM((LEN, 128), BF16),
                pltpu.VMEM((LEN, WIDTH), BF16), pltpu.VMEM((2, LEN, WIDTH), F32),
                pltpu.SMEM((32,), jnp.int32), pltpu.SMEM((32,), jnp.int32),
                pltpu.SMEM((32,), jnp.int32), pltpu.SemaphoreType.DMA((GROUPS, 16)),
            ],
        ),
        out_shape=[
            jax.ShapeDtypeStruct((LEN, D), BF16), out((LEN, WIDTH), F32),
            jax.ShapeDtypeStruct((D, LEN), BF16), jax.ShapeDtypeStruct((wide, rows_in, D), BF16),
            out((LEN, WIDTH), F32), out((LEN, WIDTH), F32), out((LEN, 128), F32),
            out((LEN, 128), F32), out((LEN, WIDTH), F32), out((LEN, WIDTH), F32),
        ],
        compiler_params=pltpu.CompilerParams(
            dimension_semantics=("arbitrary",), vmem_limit_bytes=VMEM_LIMIT
        ),
        cost_estimate=cost(20 * 10**9, 40 * 10**6),
        name="attend",
    )(lengths, place, *pieces, tokens, norm, bias, perm, proj, cosine, sine, onehot)


def attend_back_kernel(
    lengths, place, dmixed_ref, mixed_ref, rden_ref, wq_ref, wk_ref, qf_ref, kf_ref, v_ref,
    a1t_ref, w_ref, perm_ref, proj_ref, cos_ref, sin_ref, onehot_ref, ones_ref,
    keep_ref, send_ref, bias_ref, da1_ref,
    qb, kb, dnb, dnh, lift, dqf, dkf, dv, dqkv, base, first, last,
):
    count = make_blocks(lengths, base, first, last)
    qb[...] = qf_ref[0].astype(BF16)
    kb[...] = kf_ref[0].astype(BF16)
    lane = lax.broadcasted_iota(jnp.int32, (1, 128), 1)
    ones = ones_ref[...]
    def lift_rows(here):
        for pair in range(2):
            lanes = slice(128 * pair, 128 * (pair + 1))
            dnum = dmixed_ref[here, lanes] * rden_ref[0, here, lanes]
            high, low = halves(dnum)
            dnb[here, lanes] = high
            part_high, part_low = halves(dnum * mixed_ref[0, here, lanes])
            dden = -mm(jnp.concatenate([part_high, part_low], axis=1), ones)
            den_high, den_low = halves(dden)
            high, low = high.astype(F32), low.astype(F32)
            den_high = pltpu.roll(den_high.astype(F32), 64, 1)
            den_low = pltpu.roll(den_low.astype(F32), 64, 1)
            low_far = pltpu.roll(low, 64, 1)
            v = v_ref[0, here, lanes]
            v_high, v_low = halves(v)
            v_high, v_low = v_high.astype(F32), v_low.astype(F32)
            v_far = pltpu.roll(v_high, 64, 1)
            for side in range(2):
                own = (lane >= 64 * side) & (lane < 64 * side + 64)
                mark = 64 - 64 * side
                rest = jnp.where(lane == mark, den_high, jnp.where(lane == mark + 1, den_low, 0.0))
                both = ((lane == mark) | (lane == mark + 1)).astype(F32)
                head = 2 * pair + side
                dnh[head, here, :128] = jnp.where(own, high, low_far).astype(BF16)
                dnh[head, here, 128:] = jnp.where(own, high, rest).astype(BF16)
                lift[head, here, :128] = jnp.where(own, v_high, v_far).astype(BF16)
                lift[head, here, 128:] = jnp.where(own, v_low, both).astype(BF16)
    row_blocks(lift_rows)
    dqf[...] = jnp.zeros_like(dqf)
    dkf[...] = jnp.zeros_like(dkf)
    dv[...] = jnp.zeros_like(dv)

    def one_span(index, carry):
        rows = pl.ds(pl.multiple_of(base[index], 16), SPAN)
        mask = span_mask(onehot_ref, rows, first[index], last[index])
        q = qb[rows, :]
        k = kb[rows, :]
        q_total = jnp.zeros((SPAN, 128), F32)
        k_total = jnp.zeros((SPAN, 128), F32)
        for pair in range(2):
            lanes = slice(128 * pair, 128 * (pair + 1))
            dn_pair = dnb[rows, lanes]
            v_total = jnp.zeros((SPAN, 128), F32)
            for side in range(2):
                head = 2 * pair + side
                feats = lane_mask(32 * head, 32 * head + 32, 128, BF16)
                q_head = q * feats
                k_head = k * feats
                lifted = lift[head, rows, :]
                dn_head = dnh[head, rows, :]
                scores = mm_nt(k, q_head).astype(BF16) * mask
                dscores = mm_nt(dn_head, lifted).astype(BF16) * mask
                dscores_t = mm_nt(lifted, dn_head).astype(BF16) * mask
                q_total = q_total + mm(dscores, k_head)
                k_total = k_total + mm(dscores_t, q_head)
                own = lane_mask(64 * side, 64 * side + 64, 128, BF16)
                v_total = v_total + mm(scores, dn_pair * own)
            dv[rows, lanes] += v_total
        dqf[rows, :] += q_total
        dkf[rows, :] += k_total
        return carry

    lax.fori_loop(0, count, one_span, 0)
    proj_low = proj_ref[0, :, 128:]
    proj_high = proj_ref[1]
    square = proj_ref[2]
    perm = perm_ref[...]
    def feature_rows(here):
        for which, (w_in, phi_in, dphi) in enumerate(
            ((wq_ref, qf_ref, dqf), (wk_ref, kf_ref, dkf))
        ):
            r = dphi[here, :] * phi_in[0, here, :]
            high, low = halves(r)
            both = jnp.concatenate([high, low], axis=1)
            spread = mm_nt(both, square)
            dw = mm_nt(both, proj_high) + mm_nt(high, proj_low)
            du = (dw - 2.0 * w_in[0, here, :] * spread) * HD ** (-0.25)
            c = du[:, :128]
            e = du[:, 128:]
            cosine = cos_ref[here, :]
            sine = sin_ref[here, :]
            turned = jnp.concatenate([c * cosine + e * sine, e * cosine - c * sine], axis=1)
            dqkv[here, WIDTH * which : WIDTH * (which + 1)] = mm_nt(
                turned.astype(BF16), perm
            ).astype(BF16)

    row_blocks(feature_rows)
    dqkv[:, 2 * WIDTH :] = dv[...].astype(BF16)
    bias_ref[0] = jnp.sum(dqkv[...].astype(F32), axis=0, keepdims=True)
    grad = mm(a1t_ref[...], dqkv[...]).astype(BF16)
    at = pl.program_id(0)
    store_halves(grad, place[3], keep_ref.at[at], send_ref.at[at])
    w = w_ref[...].reshape(D, D)
    fresh = pl.program_id(0) == 0

    @pl.when(fresh)
    def _():
        da1_ref[...] = mm_nt(dqkv[...], w)

    @pl.when(jnp.logical_not(fresh))
    def _():
        da1_ref[...] += mm_nt(dqkv[...], w)


def store_halves(grad, core, keep_ref, send_ref):
    wide, rows = keep_ref.shape[0], D // keep_ref.shape[0]
    half = rows // 2
    parts = grad.reshape(wide, rows, D)
    for cols in range(3):
        block = parts[:, :, WIDTH * cols : WIDTH * (cols + 1)]
        here = pl.ds(half * cols, half)

        @pl.when(core == 0)
        def _():
            keep_ref[:, here, :] = block[:, :half]
            send_ref[:, here, :] = block[:, half:]

        @pl.when(core == 1)
        def _():
            keep_ref[:, here, :] = block[:, half:]
            send_ref[:, here, :] = block[:, :half]


def attend_back(
    lengths, place, wide, dmixed, saved, a1t, w_in, perm, proj, cosine, sine, onehot, ones
):
    mixed, rden, wq, wk, qf, kf, v = saved

    def by_group(shape):
        return pl.BlockSpec((1,) + shape, lambda g, *_: (g,) + (0,) * len(shape))

    rows_in = D // wide
    half = struct((GROUPS, wide, 3 * rows_in // 2, WIDTH), BF16)
    half_spec = once(half.shape)
    if wide > 1:
        half = pltpu.VMEM(half.shape, BF16)
        half_spec = pl.BlockSpec(memory_space=pltpu.VMEM)
    return pl.pallas_call(
        attend_back_kernel,
        grid_spec=pltpu.PrefetchScalarGridSpec(
            num_scalar_prefetch=2,
            grid=(GROUPS,),
            in_specs=[
                pl.BlockSpec((LEN, WIDTH), lambda g, *_: (0, g)),
                by_group((LEN, WIDTH)), by_group((LEN, WIDTH)), by_group((LEN, WIDTH)),
                by_group((LEN, WIDTH)), by_group((LEN, 128)), by_group((LEN, 128)),
                by_group((LEN, WIDTH)), once((D, LEN)),
                pl.BlockSpec((wide, rows_in, D), lambda g, *_: (0, g, 0)),
                once((WIDTH, WIDTH)), once((3, WIDTH, WIDTH)), once((LEN, 128)),
                once((LEN, 128)), once((LEN, 128)), once((WIDTH, 128)),
            ],
            out_specs=[
                half_spec, half_spec, group_spec((1, D)),
                whole_spec((LEN, D)),
            ],
            scratch_shapes=[
                pltpu.VMEM((LEN, 128), BF16), pltpu.VMEM((LEN, 128), BF16),
                pltpu.VMEM((LEN, WIDTH), BF16), pltpu.VMEM((4, LEN, WIDTH), BF16),
                pltpu.VMEM((4, LEN, WIDTH), BF16), pltpu.VMEM((LEN, 128), F32),
                pltpu.VMEM((LEN, 128), F32), pltpu.VMEM((LEN, WIDTH), F32),
                pltpu.VMEM((LEN, D), BF16),
                pltpu.SMEM((32,), jnp.int32), pltpu.SMEM((32,), jnp.int32),
                pltpu.SMEM((32,), jnp.int32),
            ],
        ),
        out_shape=[
            half, half, struct((GROUPS, 1, D), F32), struct((LEN, D), F32),
        ],
        compiler_params=pltpu.CompilerParams(
            dimension_semantics=("arbitrary",), vmem_limit_bytes=BACK_LIMIT
        ),
        cost_estimate=cost(GROUPS * 12 * 10**9, GROUPS * 20 * 10**6),
        name="attend_back",
    )(
        lengths, place, dmixed, mixed, rden, wq, wk, qf, kf, v, a1t, w_in, perm, proj, cosine,
        sine, onehot, ones,
    )


def chunk_step(
    place, wide, bias_up, dy_ref, a2, a2t, dyt, up, down, act, dhidden, y, back, outs, dbias_ref,
    fresh,
):
    rows_up = D // wide
    rows_down = FFC // wide
    dbias_ref[0] = jnp.zeros((1, FFC), F32)

    def chunk_rows(here):
        hidden = mm(a2[here, :], up[...]) + bias_up
        below, density = normal_parts(hidden)
        act_now = (hidden * below).astype(BF16)
        act[here, :] = act_now
        dact = mm_nt(dy_ref[here, :], down[...])
        dhidden_now = (dact * (below + hidden * density)).astype(BF16)
        dhidden[here, :] = dhidden_now
        dbias_ref[0] += jnp.sum(dhidden_now.astype(F32), axis=0, keepdims=True)
        if fresh:
            y[here, :] = mm(act_now, down[...])
            back[here, :] = mm_nt(dhidden_now, up[...])
        else:
            y[here, :] += mm(act_now, down[...])
            back[here, :] += mm_nt(dhidden_now, up[...])

    row_blocks(chunk_rows, not fresh)
    grad_up = mm(a2t[...], dhidden[...]).astype(BF16).reshape(wide, rows_up, FFC)
    grad_down = mm(dyt[...], act[...]).astype(BF16)
    core = place[3]

    def store_up(ref):
        for cols in range(4):
            ref[:, rows_up * cols : rows_up * (cols + 1), :] = grad_up[
                :, :, WIDTH * cols : WIDTH * (cols + 1)
            ]

    def store_down(ref):
        if wide == 1:
            for cols in range(4):
                ref[0, D * cols : D * (cols + 1), :] = grad_down[
                    :, WIDTH * cols : WIDTH * (cols + 1)
                ]
            return
        for shard in range(wide):
            block = grad_down[:, rows_down * shard : rows_down * (shard + 1)]
            ref[shard, :, :128] = block[: D // 2]
            ref[shard, :, 128:] = block[D // 2 :]

    for when, keep_ref, send_ref in outs:
        for side in range(2):
            now = core == side

            @pl.when(now if when is None else now & when)
            def _():
                store_up(keep_ref if side == 0 else send_ref)
                store_down(send_ref if side == 0 else keep_ref)


def load_up(flat, at, up, wide):
    rows = D // wide
    for cols in range(4):
        here = pl.ds(at + rows * cols, rows)
        up[:, WIDTH * cols : WIDTH * (cols + 1)] = flat[:, here, :].reshape(D, WIDTH)


def load_down(flat, at, down, wide):
    rows = FFC // wide
    for cols in range(3):
        here = pl.ds(at + rows * cols, rows)
        down[:, WIDTH * cols : WIDTH * (cols + 1)] = flat[:, here, :].reshape(FFC, WIDTH)


def middle_first_kernel(wide, count_in, place, *refs):
    pieces = refs[:count_in]
    (
        x_ref, attn_ref, dy_ref, rows_ref, bias_up_ref,
        x1_ref, a2_ref, a2t_ref, dyt_ref, y_ref, back_ref, out_ref, keep_ref, send_ref, dbias_ref,
        flat, up, down, act, dhidden, sems,
    ) = refs[count_in:]
    copies = flat_copies(place, pieces, flat, sems)
    for copy in copies:
        copy.start()
    for cols in range(0, D, 256):
        dyt_ref[cols : cols + 256, :] = transposed(dy_ref[:, cols : cols + 256])
    for copy in copies:
        copy.wait()
    half_out = D // wide // 2
    half_flat = flat.shape[1] // 2
    for cols in range(3):
        upper = flat[:, half_out * cols : half_out * (cols + 1), :]
        lower = flat[:, half_flat + half_out * cols : half_flat + half_out * (cols + 1), :]
        out_ref[:, WIDTH * cols : WIDTH * (cols + 1)] = jnp.concatenate(
            [upper, lower], axis=1
        ).reshape(D, WIDTH)
    def norm_rows(here):
        x1 = x_ref[here, :].astype(F32) + (mm(attn_ref[here, :], out_ref[...]) + rows_ref[7:8, :])
        x1_ref[here, :] = x1
        centre = x1 - jnp.mean(x1, axis=-1, keepdims=True)
        spread = jnp.mean(centre * centre, axis=-1, keepdims=True)
        a2_ref[here, :] = (
            centre * lax.rsqrt(spread + norm_eps) * rows_ref[2:3, :] + rows_ref[3:4, :]
        ).astype(BF16)

    row_blocks(norm_rows)
    for cols in range(0, D, 256):
        a2t_ref[cols : cols + 256, :] = transposed(a2_ref[:, cols : cols + 256])
    load_up(flat, 3 * half_out, up, wide)
    load_down(flat, half_flat + 3 * half_out, down, wide)
    chunk_step(
        place, wide, bias_up_ref[0], dy_ref, a2_ref, a2t_ref, dyt_ref, up, down, act, dhidden,
        y_ref, back_ref, [(None, keep_ref, send_ref)], dbias_ref, True,
    )


def middle_rest_kernel(wide, count_in, place, *refs):
    pieces = refs[:count_in]
    (
        dy_ref, a2_ref, a2t_ref, dyt_ref, bias_up_ref, attn_ref, out_ref, rows_ref,
        y_in, back_in, x1_in,
        block_ref, dx1_ref, dmixed_ref, okeep_ref, osend_ref, vec_ref,
        keep_ref, send_ref, dbias_ref,
        flat, up, down, act, dhidden, back, dbranch, sems, flat_sems,
    ) = refs[count_in:]
    step = pl.program_id(0)
    y_copy = pltpu.make_async_copy(y_in, block_ref, sems.at[0])
    back_copy = pltpu.make_async_copy(back_in, back, sems.at[1])
    x1_copy = pltpu.make_async_copy(x1_in, dx1_ref, sems.at[2])

    def chunk_copies(chunk, side):
        if count_in == 1:
            return [
                pltpu.make_async_copy(
                    pieces[0].at[chunk], flat.at[chunk], flat_sems.at[chunk, 0]
                )
            ]
        copies = []
        for flip in range(2):
            column = place[1] if flip == 0 else 1 - place[1]
            for shift in range(4):
                shard = lax.rem(place[0] + 4 - shift, 4) * 2 + column
                copies.append(
                    pltpu.make_async_copy(
                        pieces[2 * side + flip].at[shift], flat.at[chunk, shard],
                        flat_sems.at[chunk, len(copies)],
                    )
                )
        return copies

    def fetch(chunk):
        for side in range(2):

            @pl.when((place[3] == chunk) if side == 0 else (place[3] != chunk))
            def _():
                if side == 0 or count_in > 1:
                    for copy in chunk_copies(chunk, side):
                        copy.start()

    def arrived(chunk):
        for copy in chunk_copies(chunk, 0):
            copy.wait()

    @pl.when(step == 0)
    def _():
        if count_in == 1:
            for chunk in range(2):
                for copy in chunk_copies(chunk, 0):
                    copy.start()
        else:
            fetch(0)
        y_copy.start()
        back_copy.start()
        if count_in > 1:
            fetch(1)
        x1_copy.start()
        arrived(0)
        y_copy.wait()
        back_copy.wait()

    @pl.when(step == 1)
    def _():
        arrived(1)

    load_up(flat.at[step], 0, up, wide)
    load_down(flat.at[step], 4 * (D // wide), down, wide)
    chunk_step(
        place, wide, bias_up_ref[0], dy_ref, a2_ref, a2t_ref, dyt_ref, up, down, act, dhidden,
        block_ref, back, [(None, keep_ref.at[step], send_ref.at[step])], dbias_ref, False,
    )

    @pl.when(step == 1)
    def _():
        x1_copy.wait()
        vec_ref[...] = jnp.zeros_like(vec_ref)

        def last_rows(here):
            x1 = dx1_ref[here, :]
            block_ref[here, :] = x1 + (block_ref[here, :] + rows_ref[8:9, :])
            dn = back[here, :]
            dy = dy_ref[here, :].astype(F32)
            centre = x1 - jnp.mean(x1, axis=-1, keepdims=True)
            spread = jnp.mean(centre * centre, axis=-1, keepdims=True)
            scale = lax.rsqrt(spread + norm_eps)
            zh = centre * scale
            vec_ref[0:1, :] += jnp.sum(dn * zh, axis=0, keepdims=True)
            vec_ref[1:2, :] += jnp.sum(dn, axis=0, keepdims=True)
            e = dn * rows_ref[2:3, :]
            dz = (
                e
                - jnp.mean(e, axis=-1, keepdims=True)
                - zh * jnp.mean(e * zh, axis=-1, keepdims=True)
            ) * scale
            dx1 = dy + dz
            dx1_ref[here, :] = dx1
            low = dx1.astype(BF16)
            dbranch[here, :] = low
            vec_ref[2:3, :] += jnp.sum(low.astype(F32), axis=0, keepdims=True)
            vec_ref[3:4, :] += jnp.sum(dy, axis=0, keepdims=True)
            dmixed_ref[here, :] = mm_nt(low, out_ref[...])

        row_blocks(last_rows, True)
        for cols in range(0, D, 256):
            up[cols : cols + 256, :] = transposed(attn_ref[:, cols : cols + 256])
        store_halves(mm(up[...], dbranch[...]).astype(BF16), place[3], okeep_ref, osend_ref)


def once(shape):
    return whole_spec(shape, pipeline_mode=pl.Buffered(1))


def struct(shape, dtype):
    return jax.ShapeDtypeStruct(shape, dtype)


def weight_scratch():
    return [
        pltpu.VMEM((D, FFC), BF16), pltpu.VMEM((FFC, D), BF16), pltpu.VMEM((LEN, FFC), BF16),
        pltpu.VMEM((LEN, FFC), BF16),
    ]


def middle_first(place, wide, pieces, tokens, attn, cotangent, vectors, bias_up):
    rows_flat = 3 * D // wide + 2 * FFC * D // (WIDTH * wide)
    half = (wide, FFC * D // (WIDTH * wide), WIDTH)
    outs = [
        struct((LEN, D), F32), struct((LEN, D), BF16), struct((D, LEN), BF16),
        struct((D, LEN), BF16), struct((LEN, D), F32), struct((LEN, D), F32),
        struct((D, D), BF16), struct(half, BF16), struct(half, BF16), struct((1, 1, FFC), F32),
    ]
    return pl.pallas_call(
        functools.partial(middle_first_kernel, wide, len(pieces)),
        grid_spec=pltpu.PrefetchScalarGridSpec(
            num_scalar_prefetch=1,
            grid=(1,),
            in_specs=[any_spec()] * len(pieces)
            + [
                once((LEN, D)), once((LEN, D)), once((LEN, D)), once((13, D)),
                pl.BlockSpec((1, 1, FFC), lambda *_: (0, 0, 0)),
            ],
            out_specs=[once(out.shape) for out in outs],
            scratch_shapes=[pltpu.VMEM((wide, rows_flat, WIDTH), BF16)]
            + weight_scratch()
            + [pltpu.SemaphoreType.DMA((16,))],
        ),
        out_shape=outs,
        compiler_params=pltpu.CompilerParams(
            dimension_semantics=("arbitrary",), vmem_limit_bytes=VMEM_LIMIT
        ),
        cost_estimate=cost(14 * 10**9, 30 * 10**6),
        name="middle_first",
    )(place, *pieces, tokens, attn, cotangent, vectors, bias_up)


def middle_rest(place, wide, pieces, cotangent, state, bias_up, attn, w_out, vectors, sums):
    a2, a2t, dyt = state
    half = (wide, FFC * D // (WIDTH * wide), WIDTH)
    out_half = (wide, 3 * D // (2 * wide), WIDTH)
    outs = [
        struct((LEN, D), F32), struct((LEN, D), F32), struct((LEN, D), F32),
        struct(out_half, BF16), struct(out_half, BF16), struct((8, D), F32),
        struct((2,) + half, BF16), struct((2,) + half, BF16), struct((2, 1, FFC), F32),
    ]
    out_specs = [once(out.shape) for out in outs[:8]] + [group_spec((1, FFC))]
    if wide > 1:
        for index in (3, 4, 6, 7):
            outs[index] = pltpu.VMEM(outs[index].shape, BF16)
            out_specs[index] = pl.BlockSpec(memory_space=pltpu.VMEM)
    rows_flat = 2 * FFC * D // (WIDTH * wide)
    return pl.pallas_call(
        functools.partial(middle_rest_kernel, wide, len(pieces)),
        grid_spec=pltpu.PrefetchScalarGridSpec(
            num_scalar_prefetch=1,
            grid=(2,),
            in_specs=[any_spec()] * len(pieces)
            + [
                once((LEN, D)), once((LEN, D)), once((D, LEN)), once((D, LEN)),
                pl.BlockSpec((1, 1, FFC), lambda j, *_: (j + 1, 0, 0)),
                once((LEN, D)), once((D, D)), once((13, D)),
                any_spec(), any_spec(), any_spec(),
            ],
            out_specs=out_specs,
            scratch_shapes=[pltpu.VMEM((2, wide, rows_flat, WIDTH), BF16)]
            + weight_scratch()
            + [
                pltpu.VMEM((LEN, D), F32), pltpu.VMEM((LEN, D), BF16),
                pltpu.SemaphoreType.DMA((3,)), pltpu.SemaphoreType.DMA((2, 8)),
            ],
        ),
        out_shape=outs,
        compiler_params=pltpu.CompilerParams(
            dimension_semantics=("arbitrary",), vmem_limit_bytes=REST_LIMIT
        ),
        cost_estimate=cost(28 * 10**9, 40 * 10**6),
        name="middle_rest",
    )(place, *pieces, cotangent, a2, a2t, dyt, bias_up, attn, w_out, vectors, *sums)


def input_kernel(
    wide, x_ref, dx1_ref, da1_ref, rows_ref, middle_ref, bias_in_ref, bias_first_ref, bias_rest_ref,
    out_ref, vec_ref,
):
    gain = rows_ref[0:1, :]
    x = x_ref[...].astype(F32)
    dn = da1_ref[...]
    centre = x - jnp.mean(x, axis=-1, keepdims=True)
    spread = jnp.mean(centre * centre, axis=-1, keepdims=True)
    scale = lax.rsqrt(spread + norm_eps)
    zh = centre * scale
    e = dn * gain
    dz = (
        e - jnp.mean(e, axis=-1, keepdims=True) - zh * jnp.mean(e * zh, axis=-1, keepdims=True)
    ) * scale
    out_ref[...] = dx1_ref[...] + dz

    @pl.when(pl.program_id(0) == 0)
    def _():
        vec_ref[...] = jnp.zeros_like(vec_ref)
        vec_ref[2:4, :] = middle_ref[0:2, :]
        vec_ref[7:9, :] = middle_ref[2:4, :]
        for group in range(GROUPS):
            lanes = slice(WIDTH * group, WIDTH * (group + 1))
            for which in range(3):
                vec_ref[4 + which : 5 + which, lanes] = bias_in_ref[
                    group, :, WIDTH * which : WIDTH * (which + 1)
                ]
        for chunk in range(CHUNKS):
            for part in range(8):
                value = (
                    bias_first_ref[0] if chunk == 0 else bias_rest_ref[chunk - 1]
                )[:, 128 * part : 128 * (part + 1)]
                start = FFC * chunk + 128 * part if wide == 1 else 384 * part + 128 * chunk
                row, lane = 9 + start // D, start % D
                vec_ref[row : row + 1, lane : lane + 128] = value

    vec_ref[0:1, :] += jnp.sum(dn * zh, axis=0, keepdims=True)
    vec_ref[1:2, :] += jnp.sum(dn, axis=0, keepdims=True)


def input_side(wide, tokens, dx1, da1, vectors, middle_vec, bias_in, bias_first, bias_rest):
    block = pl.BlockSpec((256, D), lambda i: (i, 0))
    return pl.pallas_call(
        functools.partial(input_kernel, wide),
        grid=(LEN // 256,),
        in_specs=[
            block, block, block, whole_spec((13, D)), whole_spec((8, D)),
            whole_spec((GROUPS, 1, D)), whole_spec((1, 1, FFC)), whole_spec((2, 1, FFC)),
        ],
        out_specs=[block, whole_spec((16, D))],
        out_shape=[struct((LEN, D), F32), struct((16, D), F32)],
        compiler_params=pltpu.CompilerParams(dimension_semantics=("arbitrary",)),
        cost_estimate=cost(10**6, 12 * 10**6),
        name="input_side",
    )(tokens, dx1, da1, vectors, middle_vec, bias_in, bias_first, bias_rest)


def tables(lengths, projection):
    ends = jnp.cumsum(lengths[0])
    starts = ends - lengths[0]
    place = jnp.arange(LEN, dtype=jnp.int32)
    member = (place[:, None] >= starts[None, :]) & (place[:, None] < ends[None, :])
    offset = jnp.sum(jnp.where(member, starts[None, :], 0), axis=1)
    position = (place - offset).astype(F32)
    freq = 10000.0 ** (-jnp.arange(32, dtype=F32) / 32)
    angles = position[:, None] * jnp.tile(freq, 4)[None, :]
    onehot = jnp.pad(member.astype(BF16), ((0, 0), (0, 128 - member.shape[1])))
    eye = jnp.asarray(np.eye(4, dtype=np.float32))
    lifted = jnp.einsum("hif,ab->haibf", projection.reshape(2, 32, FEAT), eye)
    lifted = lifted.reshape(WIDTH, 128)
    rounded = lax.reduce_precision(lifted, 8, 7)
    high, low = rounded.astype(BF16), (lifted - rounded).astype(BF16)
    square = np.zeros((2, 4, 32, 4, 32), np.float32)
    for head in range(4):
        square[:, head, :, head, :] = 0.5
    square = jnp.asarray(square.reshape(WIDTH, 128), BF16)
    proj = jnp.stack(
        [
            jnp.concatenate([high, low], axis=1),
            jnp.concatenate([high, high], axis=1),
            jnp.concatenate([square, square], axis=1),
        ]
    )
    return jnp.cos(angles), jnp.sin(angles), onehot, proj


def wide_perm(shift_z, flip_x):
    pairs = []
    for z in range(4):
        for x in range(2):
            target_x = 1 - x if flip_x else x
            pairs.append((2 * z + x, 2 * ((z + shift_z) % 4) + target_x))
    return pairs


def narrow_perm(flip_y, flip_core):
    pairs = []
    for y in range(2):
        for core in range(2):
            pairs.append(
                (2 * y + core, 2 * (1 - y if flip_y else y) + (1 - core if flip_core else core))
            )
    return pairs


def over_z(values, shift):
    return lax.ppermute(values, "wide", wide_perm(shift, False))


def over_x(values):
    return lax.ppermute(values, "wide", wide_perm(0, True))


def over_far(values, bit):
    return lax.ppermute(values, "wide", [(w, w ^ bit) for w in range(8)])


def over_y(values):
    return lax.ppermute(values, "narrow", narrow_perm(True, False))


def over_core(values):
    return lax.ppermute(values, "narrow", narrow_perm(False, True))


def tie(*values):
    return lax.optimization_barrier(values)


def special():
    return lax.axis_size("wide") == 8 and lax.axis_size("narrow") == 4


def sum_wide(values):
    if not special():
        return lax.psum(values, "wide")
    for perm in (wide_perm(0, True), [(w, w ^ 2) for w in range(8)], [(w, w ^ 4) for w in range(8)]):
        values = values + lax.ppermute(values, "wide", perm)
    return values


def sum_narrow(values):
    if not special():
        return lax.psum(values, "narrow")
    pair = values + over_core(values)
    return pair + over_y(pair)


def along_z(mine):
    return jnp.stack([mine] + [over_z(mine, shift) for shift in (1, 2, 3)])


def small_call(kernel, name, place, operands, outs):
    return pl.pallas_call(
        kernel,
        grid_spec=pltpu.PrefetchScalarGridSpec(
            num_scalar_prefetch=1,
            grid=(1,),
            in_specs=[once(value.shape) for value in operands],
            out_specs=[once(out.shape) for out in outs],
        ),
        out_shape=outs,
        compiler_params=pltpu.CompilerParams(
            dimension_semantics=("arbitrary",), vmem_limit_bytes=VMEM_LIMIT
        ),
        cost_estimate=cost(10**6, sum(4 * math.prod(v.shape) for v in operands + outs)),
        name=name,
    )(place, *operands)


def held_call(kernel, name, place, operands, outs, held=None, flops=10**6):
    here = pl.BlockSpec(memory_space=pltpu.VMEM)
    held = len(outs) if held is None else held
    return pl.pallas_call(
        kernel,
        in_specs=[pl.BlockSpec(memory_space=pltpu.SMEM)] + [here] * len(operands),
        out_specs=[here] * len(outs),
        out_shape=[
            pltpu.VMEM(out.shape, out.dtype) if index < held else out
            for index, out in enumerate(outs)
        ],
        compiler_params=pltpu.CompilerParams(vmem_limit_bytes=24 * 1024 * 1024),
        cost_estimate=pl.CostEstimate(flops=flops, transcendentals=0, bytes_accessed=10**5),
        name=name,
    )(place, *[pltpu.with_memory_space_constraint(value, pltpu.VMEM) for value in operands])


def pick_kernel(
    place, in_ref, out_ref, up_ref, down_ref, near_ref, last_ref, first_ref, rest_ref
):
    core = place[3]
    here = pl.ds(pl.multiple_of(48 * core, 16), 48)
    for group in range(GROUPS):
        ref, index = (near_ref, group) if group < 2 else (last_ref, 0)
        for which in range(3):
            ref[index, :, WIDTH * which : WIDTH * (which + 1)] = in_ref[
                which, here, WIDTH * group : WIDTH * (group + 1)
            ].astype(BF16)
    for cols in range(3):
        first_ref[48 * cols : 48 * (cols + 1), :] = out_ref[
            here, WIDTH * cols : WIDTH * (cols + 1)
        ].astype(BF16)

    def put_up(ref, at, chunk):
        for cols in range(4):
            rows = slice(at + 96 * cols, at + 96 * (cols + 1))
            for side in range(2):
                start = 384 * (2 * cols + side) + 128 * chunk
                ref[rows, 128 * side : 128 * (side + 1)] = up_ref[:, start : start + 128].astype(
                    BF16
                )

    def put_down(ref, at, chunk):
        for cols in range(3):
            ref[at + 128 * cols : at + 128 * (cols + 1), :] = down_ref[
                128 * chunk : 128 * (chunk + 1), WIDTH * cols : WIDTH * (cols + 1)
            ].astype(BF16)

    for side in range(2):

        @pl.when(core == side)
        def _():
            if side == 0:
                put_up(first_ref, 144, 0)
            else:
                put_down(first_ref, 144, 0)

        @pl.when(core == side)
        def _():
            put_up(rest_ref, 0, 1 + side)
            put_down(rest_ref, 384, 1 + side)


def chunk_of(ref, chunk, shard):
    return ref[chunk, shard] if len(ref.shape) == 4 else ref[shard]


def first_sum_kernel(place, *refs):
    send_ref, keep_ref = refs[-2:]
    x = place[1]
    at = 0
    for index in range(0, len(refs) - 2, 2):
        own, got = refs[index], refs[index + 1]
        for part in range(own.shape[0] if len(own.shape) == 4 and own.shape[0] == 3 else 1):
            rows = own.shape[-2]
            here = pl.ds(at, rows)
            for z in range(4):
                for out, side in ((keep_ref, x), (send_ref, 1 - x)):
                    out[z, here, :] = (
                        chunk_of(own, part, 2 * z + side).astype(F32)
                        + chunk_of(got, part, 2 * z + side).astype(F32)
                    ).astype(BF16)
            at += rows


def first_sum(place, pairs):
    rows = sum(
        own.shape[-2] * (own.shape[0] if own.ndim == 4 and own.shape[0] == 3 else 1)
        for own, _ in pairs
    )
    return held_call(
        first_sum_kernel, "first_sum", place, [value for pair in pairs for value in pair],
        [struct((4, rows, WIDTH), BF16)] * 2,
    )


def first_sum_y_kernel(place, own, got, send, keep):
    y = place[2]
    for group in range(GROUPS):
        here = pl.ds(144 * group, 144)
        for shard in range(8):
            total = own[group, shard].astype(F32) + got[group, shard].astype(F32)
            left, right = total[:, :128].astype(BF16), total[:, 128:].astype(BF16)
            keep[shard, here, :] = jnp.where(y == 0, left, right)
            send[shard, here, :] = jnp.where(y == 0, right, left)


def split_x_kernel(place, own, got, send, keep):
    x = place[1]
    for z in range(4):
        for out, side in ((keep, x), (send, 1 - x)):
            out[z] = (own[2 * z + side].astype(F32) + got[2 * z + side].astype(F32)).astype(BF16)


def second_sum_kernel(place, own_ref, got_ref, *outs):
    z = place[0]
    for shift, out in enumerate(outs):
        there = lax.rem(z + shift, 4)
        out[...] = (own_ref[there].astype(F32) + got_ref[there].astype(F32)).astype(BF16)


def second_sum(place, own, got):
    outs = [struct(own.shape[1:], BF16)] * 4
    return held_call(second_sum_kernel, "second_sum", place, [own, got], outs)


def z_sum_kernel(place, *refs):
    total = refs[0][...].astype(F32)
    for ref in refs[1:4]:
        total = total + ref[...].astype(F32)
    rows = refs[0].shape[0]
    refs[-1][:rows, :] = total.astype(refs[-1].dtype)
    if len(refs) == 7:
        refs[-1][rows:, :] = (refs[4][...].astype(F32) + refs[5][...].astype(F32)).astype(BF16)


def z_sum(place, parts, below=(), got=None):
    if got is None:
        got = [over_z(parts[shift], shift) for shift in (1, 2, 3)]
    rows = parts[0].shape[0] + (below[0].shape[0] if below else 0)
    return held_call(
        z_sum_kernel, "z_sum", place, [parts[0]] + got + list(below),
        [struct((rows, parts[0].shape[1]), BF16 if below else F32)],
        flops=3 * 10**10 if below else 10**6,
    )[0]


def first_sum_z_kernel(place, *refs):
    z = place[0]
    outs = refs[-4:]
    for shift, out in enumerate(outs):
        there = lax.rem(z + shift, 4) * 2
        at = 0
        for index in range(0, len(refs) - 4, 2):
            own, got = refs[index], refs[index + 1]
            rows = own.shape[-2]
            for x in range(2):
                out[x, at : at + rows, :] = (
                    chunk_of(own, 1, there + x).astype(F32)
                    + chunk_of(got, 1, there + x).astype(F32)
                ).astype(BF16)
            at += rows


def first_sum_z(place, pairs):
    rows = sum(own.shape[-2] for own, _ in pairs)
    return held_call(
        first_sum_z_kernel, "first_sum_z", place, [value for pair in pairs for value in pair],
        [struct((2, rows, WIDTH), BF16)] * 4,
    )


def split_sum_kernel(place, *refs):
    keep, send = refs[-2:]
    x = place[1]
    for out, at in ((keep, x), (send, 1 - x)):
        total = refs[0][at].astype(F32)
        for ref in refs[1:4]:
            total = total + ref[at].astype(F32)
        out[...] = total.astype(BF16)


def split_sum(place, parts):
    return held_call(
        split_sum_kernel, "split_sum", place, parts, [struct(parts[0].shape[1:], BF16)] * 2
    )


def to_row(column):
    size = column.shape[0]
    eye = lax.broadcasted_iota(jnp.int32, (size, size), 0) == lax.broadcasted_iota(
        jnp.int32, (size, size), 1
    )
    return jnp.sum(jnp.where(eye, column, 0.0), axis=0, keepdims=True)


def to_column(row):
    size = row.shape[1]
    eye = lax.broadcasted_iota(jnp.int32, (size, size), 0) == lax.broadcasted_iota(
        jnp.int32, (size, size), 1
    )
    return jnp.sum(jnp.where(eye, row, 0.0), axis=1, keepdims=True)


DECAY = 1.0 - STEP ** (-0.8)


def lane_values(values):
    lane = lax.broadcasted_iota(jnp.int32, (1, D), 1)
    row = jnp.zeros((1, D), F32)
    for index, value in enumerate(values):
        row = jnp.where(lane == index, value, row)
    return row


def moments(grad, rows_old):
    plain = grad * grad
    squares = plain + square_eps
    mean = jnp.sum(squares, axis=1, keepdims=True) * (1.0 / grad.shape[1])
    rows_new = DECAY * rows_old + (1.0 - DECAY) * to_row(mean)
    total = jnp.sum(rows_new, axis=1, keepdims=True)
    divided = jnp.sum(plain * to_column(1.0 / rows_new), axis=0, keepdims=True)
    return rows_new, total, jnp.sum(squares, axis=0, keepdims=True), divided


def ffn_moments_kernel(
    place, own, got, up_rows, down_rows, out_rows,
    up_grad, down_grad, out_grad, up_rows_new, down_rows_new, out_rows_new, sums,
):
    core = place[3]

    def collect(low, high):
        for chunk in range(CHUNKS):
            at = 384 * chunk
            for cols in range(4):
                for side in range(2):
                    start = 384 * (2 * cols + side) + 128 * chunk
                    up_grad[:, start : start + 128] = low[
                        at + 96 * cols : at + 96 * (cols + 1), 128 * side : 128 * (side + 1)
                    ]
            for side in range(2):
                down_grad[128 * chunk : 128 * (chunk + 1), 384 * side : 384 * (side + 1)] = (
                    jnp.transpose(high[at : at + 384, 128 * side : 128 * (side + 1)])
                )
        for cols in range(3):
            lanes = slice(WIDTH * cols, WIDTH * (cols + 1))
            at = 1152 + 48 * cols
            out_grad[:48, lanes] = low[at : at + 48, :]
            out_grad[48:, lanes] = high[at : at + 48, :]

    @pl.when(core == 0)
    def _():
        collect(own, got)

    @pl.when(core == 1)
    def _():
        collect(got, own)

    up_new, up_total, up_sums, up_divided = moments(up_grad[...], up_rows[...])
    down_new, down_total, down_sums, down_divided = moments(down_grad[...], down_rows[...])
    out_new, out_total, out_sums, out_divided = moments(out_grad[...], out_rows[...])
    up_rows_new[...] = up_new
    down_rows_new[...] = down_new
    out_rows_new[...] = out_new
    for part in range(4):
        lanes = slice(D * part, D * (part + 1))
        sums[part : part + 1, :] = up_sums[:, lanes]
        sums[4 + part : 5 + part, :] = up_divided[:, lanes]
    sums[8:9, :] = down_sums
    sums[9:10, :] = down_divided
    sums[10:11, :] = out_sums
    sums[11:12, :] = out_divided
    sums[12:13, :] = lane_values([up_total, down_total, out_total])
    sums[13:16, :] = jnp.zeros((3, D), F32)


def in_moments_kernel(
    place, own, own_y, other, other_y, rows_old, vector, ffn_sums, grad, rows_new, sums,
):
    def collect(low, high):
        for group in range(GROUPS):
            for which in range(3):
                rows = slice(144 * group + 48 * which, 144 * group + 48 * (which + 1))
                for side in range(2):
                    start = WIDTH * group + 128 * side
                    grad[which, :48, start : start + 128] = low[side][rows, :]
                    grad[which, 48:, start : start + 128] = high[side][rows, :]

    for core in range(2):
        for y in range(2):

            @pl.when((place[3] == core) & (place[2] == y))
            def _():
                mine = (own, own_y) if y == 0 else (own_y, own)
                far = (other, other_y) if y == 0 else (other_y, other)
                collect(mine if core == 0 else far, far if core == 0 else mine)

    totals = []
    for which in range(3):
        new, total, columns, divided = moments(grad[which], rows_old[which : which + 1, :])
        rows_new[which : which + 1, :] = new
        sums[which : which + 1, :] = columns
        sums[3 + which : 4 + which, :] = divided
        totals.append(total)
    sums[6:7, :] = lane_values(totals)
    sums[7:8, :] = jnp.zeros((1, D), F32)
    sums[8:24, :] = vector[...]
    sums[24:40, :] = ffn_sums[...]


def matrix_step(weight, grad, rows, cols, total, col_sums, divided, rows_full, rate):
    cols_new = DECAY * cols + (1.0 - DECAY) * col_sums * (1.0 / rows_full)
    mean = total * (1.0 / rows_full)
    square_sum = mean * jnp.sum(divided / cols_new, axis=1, keepdims=True)
    rms = jnp.sqrt(square_sum * (1.0 / (rows_full * grad.shape[1])))
    factor = to_column(lax.rsqrt(rows / mean)) * (rate / jnp.maximum(1.0, rms / clip_level))
    return cols_new, weight - grad * factor * lax.rsqrt(cols_new)


def finish_kernel(
    place, inward, up, down, out, in_grad, up_grad, down_grad, out_grad, in_rows, up_rows,
    down_rows, out_rows, in_cols, up_cols, down_cols, out_cols, sums, vectors, vector_state,
    in_cols_new, up_cols_new, down_cols_new, out_cols_new, in_next, up_next, down_next, out_next,
    vector_grad, state_next, vectors_next,
):
    base_rate = 0.3 * D ** (-0.5)
    for which in range(3):
        here = slice(which, which + 1)
        in_cols_new[here, :], in_next[which] = matrix_step(
            inward[which], in_grad[which], in_rows[here, :], in_cols[here, :],
            sums[6:7, which : which + 1], sums[here, :], sums[3 + which : 4 + which, :], D,
            base_rate,
        )

    def wide_row(first):
        return jnp.concatenate([sums[first + i : first + i + 1, :] for i in range(4)], axis=1)

    up_cols_new[...], up_next[...] = matrix_step(
        up[...], up_grad[...], up_rows[...], up_cols[...], sums[36:37, 0:1], wide_row(24),
        wide_row(28), D, base_rate,
    )
    down_cols_new[...], down_next[...] = matrix_step(
        down[...], down_grad[...], down_rows[...], down_cols[...], sums[36:37, 1:2],
        sums[32:33, :], sums[33:34, :], FF, 0.3 * FF ** (-0.5),
    )
    out_cols_new[...], out_next[...] = matrix_step(
        out[...], out_grad[...], out_rows[...], out_cols[...], sums[36:37, 2:3],
        sums[34:35, :], sums[35:36, :], D, 1.2 * D ** (-0.5),
    )
    g = sums[8:21, :]
    vector_grad[...] = g
    state = DECAY * vector_state[...] + (1.0 - DECAY) * (g * g + square_eps)
    state_next[...] = state
    update = g * lax.rsqrt(state)
    total = jnp.sum(jnp.sum(update * update, axis=0, keepdims=True), axis=1, keepdims=True)
    rms = jnp.sqrt(total * (1.0 / (13 * D)))
    vectors_next[...] = vectors[...] - update * (0.25 / jnp.maximum(1.0, rms / clip_level))


def shards(
    tokens, cotangent, lengths, projection, inward, outward, expand, shrink, vectors,
    inward_rows, inward_columns, outward_rows, outward_columns, expand_rows, expand_columns,
    shrink_rows, shrink_columns, vector_state,
):
    full = special()
    rows = outward.shape[0]
    wide = 8 if full else 1
    wide_at = lax.axis_index("wide").astype(jnp.int32)
    narrow_at = lax.axis_index("narrow").astype(jnp.int32)
    core = narrow_at % 2 if full else jnp.int32(0)
    place = jnp.stack([wide_at // 2, wide_at % 2, narrow_at // 2, core])
    per = FFC // wide
    cosine, sine, onehot, proj = tables(lengths, projection)
    if full:
        *own_in, own_first, own_rest = small_call(
            pick_kernel, "pick", place, [inward, outward, expand, shrink],
            [
                struct((2, 48, D), BF16), struct((1, 48, D), BF16), struct((528, WIDTH), BF16),
                struct((768, WIDTH), BF16),
            ],
        )
        in_z = [along_z(value) for value in own_in]
        *in_z, own_first, cosine, sine, onehot, proj = tie(
            *in_z, own_first, cosine, sine, onehot, proj
        )
        first_z = along_z(own_first)
        in_x = [over_x(value) for value in in_z]
        pieces_in = []
        *in_z, first_z = tie(*in_z, *in_x, first_z)
        for near, far in zip(in_z[:2], in_z[2:]):
            pieces_in += [near, far, over_core(near), over_core(far)]
        *pieces_in, first_z, own_rest = tie(*pieces_in, first_z, own_rest)
        first_x = over_x(first_z)
        rest_got = [over_z(own_rest, shift) for shift in (1, 2, 3)]
    else:
        in_low = lax.all_gather(inward.astype(BF16), "wide", axis=1, tiled=True)
        out_low = lax.all_gather(outward.astype(BF16), "wide", axis=0, tiled=True)
        up_low = lax.all_gather(expand.astype(BF16), "wide", axis=0, tiled=True)
        down_low = lax.all_gather(shrink.astype(BF16), "wide", axis=0, tiled=True)
        units = jnp.transpose(in_low.reshape(3, D, GROUPS, WIDTH), (2, 1, 0, 3))
        pieces_in = [units.reshape(1, 3 * D, D)]

        def blocks(matrix):
            count = matrix.shape[1] // WIDTH
            return jnp.transpose(matrix.reshape(-1, count, WIDTH), (1, 0, 2)).reshape(-1, WIDTH)

        ups = [blocks(up_low[:, FFC * j : FFC * (j + 1)]) for j in range(CHUNKS)]
        downs = [blocks(down_low[FFC * j : FFC * (j + 1)]) for j in range(CHUNKS)]
        half = D // 2
        pieces_first = [
            jnp.concatenate([blocks(out_low[:half]), ups[0], blocks(out_low[half:]), downs[0]])[
                None
            ]
        ]
        pieces_rest = [
            jnp.stack([jnp.concatenate([ups[j], downs[j]])[None] for j in range(1, CHUNKS)])
        ]
    perm = jnp.asarray(head_perm(), BF16)
    block_ones = np.kron(np.eye(2, dtype=np.float32), np.ones((64, 64), np.float32))
    ones = jnp.asarray(np.concatenate([block_ones, block_ones]), BF16)
    split = vectors[4:6].reshape(2, GROUPS, 4, 2, 32)
    bias_qk = jnp.transpose(split, (0, 1, 3, 2, 4)).reshape(2, GROUPS, WIDTH)
    bias = jnp.concatenate([bias_qk, vectors[6].reshape(1, GROUPS, WIDTH)])
    bias = jnp.transpose(bias, (1, 0, 2))
    bias_up = vectors[9:].reshape(wide, CHUNKS, per)
    bias_up = jnp.transpose(bias_up, (1, 0, 2)).reshape(CHUNKS, 1, FFC)
    attn, mixed, a1t, w_in, wq, wk, qf, kf, v, rden = attend(
        lengths, place, pieces_in, wide, tokens, vectors[:2], bias, perm, proj, cosine, sine,
        onehot,
    )
    if full:
        attn, first_x, *rest_got = tie(attn, first_x, *rest_got)
        rest_z = jnp.stack([own_rest] + rest_got)
        first_cores = [over_core(first_z), over_core(first_x)]
        *first_cores, rest_z = tie(*first_cores, rest_z)
        pieces_first = [first_z, first_x] + first_cores
        rest_x = over_x(rest_z)
    x1, a2, a2t, dyt, y, back, w_out, keep0, send0, dbias0 = middle_first(
        place, wide, pieces_first, tokens, attn, cotangent, vectors, bias_up
    )
    if full:
        rest_core = over_core(rest_z)
        rest_x, rest_core, send0, y = tie(rest_x, rest_core, send0, y)
        pieces_rest = [rest_z, rest_x, rest_core, over_core(rest_x)]
        got0 = over_core(send0)
    (
        block_out, dx1, dmixed, okeep, osend, middle_vec, keep12, send12, dbias12,
    ) = middle_rest(
        place, wide, pieces_rest, cotangent, (a2, a2t, dyt), bias_up, attn, w_out, vectors,
        (y, back, x1),
    )
    if full:
        got0, send12, osend = tie(got0, send12, osend)
        got12 = over_core(send12)
        send_b, keep_b = first_sum(place, [(keep0, got0), (keep12, got12)])
        e_parts = first_sum_z(place, [(keep12, got12), (okeep, over_core(osend))])
        dmixed, send_b, keep_b, *e_parts = tie(dmixed, send_b, keep_b, *e_parts)
        got_b = over_x(send_b)
        e_got = [over_z(e_parts[shift], shift) for shift in (1, 2, 3)]
    saved = (mixed, rden, wq, wk, qf, kf, v)
    in_keep, in_send, in_bias, da1 = attend_back(
        lengths, place, wide, dmixed, saved, a1t, w_in, perm, proj, cosine, sine, onehot, ones
    )
    if full:
        b_parts = list(second_sum(place, keep_b, got_b))
        in_send, da1, *e_got, b_parts[1] = tie(in_send, da1, *e_got, b_parts[1])
        keep_e, send_e = split_sum(place, [e_parts[0]] + e_got)
        send_e, in_send = tie(send_e, in_send)
        got_e = over_x(send_e)
        got_in = over_core(in_send)
        send_c, keep_c = held_call(
            first_sum_y_kernel, "first_sum_y", place, [in_keep, got_in],
            [struct((8, 432, 128), BF16)] * 2,
        )
        da1, send_c = tie(da1, send_c)
        got_c = over_y(send_c)
    input_grad, vector_local = input_side(
        wide, tokens, dx1, da1, vectors, middle_vec, in_bias, dbias0, dbias12
    )
    if full:
        vector_part = sum_narrow(vector_local)

        def pair_sum(mine, got):
            half_sum = mine.astype(F32) + got.astype(F32)
            return half_sum, over_core(half_sum)

        got_c, input_grad, vector_part = tie(got_c, input_grad, vector_part)
        send_c, keep_c = held_call(
            split_x_kernel, "split_x", place, [keep_c, got_c], [struct((4, 432, 128), BF16)] * 2
        )
        got_c = over_x(send_c)
        ffn_mine = z_sum(place, b_parts, (keep_e, got_e))
        ffn_mine, got_c = tie(ffn_mine, got_c)
        c_parts = second_sum(place, keep_c, got_c)
        ffn_mine, *c_parts = tie(ffn_mine, *c_parts)
        ffn_y = over_y(ffn_mine)
        c_got = [over_z(c_parts[shift], shift) for shift in (1, 2, 3)]
        ffn_y, *c_got = tie(ffn_y, *c_got)
        c_mine = z_sum(place, c_parts, (), c_got)
        c_mine, ffn_y = tie(c_mine, ffn_y)
        c_y = over_y(c_mine)
        c_core = over_core(c_mine)
        ffn_own, ffn_got = pair_sum(ffn_mine, ffn_y)
        expand_grad, shrink_grad, outward_grad, up_rows, down_rows, out_rows, sums = held_call(
            ffn_moments_kernel, "ffn_moments", place,
            [
                ffn_own, ffn_got, expand_rows[None], shrink_rows[None], outward_rows[None],
            ],
            [
                struct(expand.shape, F32), struct(shrink.shape, F32), struct(outward.shape, F32),
                struct((1, 96), F32), struct((1, 384), F32), struct((1, 96), F32),
                struct((16, D), F32),
            ],
            0,
        )
        c_y, sums = tie(c_y, sums)
        inward_grad, in_rows, sums = held_call(
            in_moments_kernel, "in_moments", place,
            [c_mine, c_y, c_core, over_core(c_y), inward_rows, vector_part, sums],
            [struct(inward.shape, F32), struct((3, 96), F32), struct((40, D), F32)],
            0,
        )
        sums = sum_wide(sums)
        (
            in_cols, up_cols, down_cols, out_cols, inward_next, expand_next, shrink_next,
            outward_next, vector_grad, vector_state_next, vectors_next,
        ) = small_call(
            finish_kernel, "finish", place,
            [
                inward, expand, shrink, outward, inward_grad, expand_grad, shrink_grad,
                outward_grad, in_rows, up_rows, down_rows, out_rows, inward_columns,
                expand_columns[None], shrink_columns[None], outward_columns[None], sums, vectors,
                vector_state,
            ],
            [
                struct((3, D), F32), struct((1, FF), F32), struct((1, D), F32),
                struct((1, D), F32), struct(inward.shape, F32), struct(expand.shape, F32),
                struct(shrink.shape, F32), struct(outward.shape, F32), struct((13, D), F32),
                struct((13, D), F32), struct((13, D), F32),
            ],
        )
        return (
            block_out, input_grad, inward_grad, outward_grad, expand_grad, shrink_grad,
            vector_grad, in_rows, in_cols, out_rows[0], out_cols[0], up_rows[0], up_cols[0],
            down_rows[0], down_cols[0], vector_state_next, inward_next, outward_next,
            expand_next, shrink_next, vectors_next,
        )
    vector_part = sum_narrow(vector_local[:13])

    def reduced(values, axis):
        part = lax.psum_scatter(values, "wide", scatter_dimension=axis, tiled=True)
        return lax.psum(part.astype(F32), "narrow")

    keeps = [keep0, keep12[0], keep12[1]]
    sends = [send0, send12[0], send12[1]]
    up_grads = [
        jnp.transpose(keep.reshape(4, D, WIDTH), (1, 0, 2)).reshape(D, FFC) for keep in keeps
    ]
    down_grads = [
        jnp.transpose(send.reshape(4, D, WIDTH), (0, 2, 1)).reshape(FFC, D) for send in sends
    ]
    expand_grad = reduced(jnp.concatenate(up_grads, axis=1), 0)
    shrink_grad = reduced(jnp.concatenate(down_grads, axis=0), 0)

    def rebuilt(keep, send):
        return jnp.concatenate(
            [keep.reshape(-1, 3, D // 2, WIDTH), send.reshape(-1, 3, D // 2, WIDTH)], axis=2
        )

    outward_grad = reduced(jnp.transpose(rebuilt(okeep, osend)[0], (1, 0, 2)).reshape(D, D), 0)
    in_units = rebuilt(in_keep, in_send)
    inward_grad = reduced(jnp.transpose(in_units, (1, 2, 0, 3)).reshape(3, D, D), 1)
    decay = 1.0 - STEP ** (-0.8)
    wide_count = lax.axis_size("wide")
    grads_list = [inward_grad, outward_grad[None], expand_grad[None], shrink_grad[None]]
    rows_old = [inward_rows, outward_rows[None], expand_rows[None], shrink_rows[None]]
    columns_old = [
        inward_columns,
        outward_columns[None],
        expand_columns[None],
        shrink_columns[None],
    ]
    weights_old = [inward, outward[None], expand[None], shrink[None]]
    rates = [0.3 * D ** (-0.5), 1.2 * D ** (-0.5), 0.3 * D ** (-0.5), 0.3 * FF ** (-0.5)]
    bounds = [0, 3, 4, 5, 6]
    rows_next = []
    column_parts = []
    for member in range(4):
        squares = grads_list[member] * grads_list[member] + square_eps
        rows_next.append(decay * rows_old[member] + (1.0 - decay) * jnp.mean(squares, axis=-1))
        column_parts.append(jnp.sum(squares, axis=-2))
    row_totals = jnp.concatenate([jnp.sum(entry, axis=-1) for entry in rows_next])
    shapes = [part.shape for part in column_parts] + [row_totals.shape, vector_part.shape]
    flat = jnp.concatenate(
        [part.reshape(-1) for part in column_parts + [row_totals, vector_part]]
    )
    flat = jnp.pad(flat, (0, -flat.shape[0] % 1024)).reshape(-1, 128)
    flat = sum_wide(flat).reshape(-1)
    summed = []
    offset = 0
    for shape in shapes:
        size = 1
        for extent in shape:
            size *= extent
        summed.append(flat[offset : offset + size].reshape(shape))
        offset += size
    column_sums = list(summed[0:4])
    totals_sum = summed[4]
    vector_grad = summed[5]
    columns_next = []
    scaled_list = []
    row_means = []
    sizes_full = []
    for member in range(4):
        grad_now = grads_list[member]
        rows_full = grad_now.shape[-2] * wide_count
        sizes_full.append(rows_full * grad_now.shape[-1])
        columns_next.append(
            decay * columns_old[member] + (1.0 - decay) * column_sums[member] / rows_full
        )
        row_mean = totals_sum[bounds[member] : bounds[member + 1]] / rows_full
        row_means.append(row_mean)
        scaled_list.append(
            grad_now
            * lax.rsqrt(rows_next[member] / row_mean[:, None])[..., None]
            * lax.rsqrt(columns_next[member])[:, None, :]
        )
    partial_squares = jnp.concatenate(
        [jnp.sum(entry * entry, axis=(-2, -1)) for entry in scaled_list]
    )
    total_squares = sum_wide(jnp.pad(partial_squares, (0, 122)).reshape(1, 128))[0, :6]
    rms_list = [
        jnp.sqrt(total_squares[bounds[member] : bounds[member + 1]] / sizes_full[member])
        for member in range(4)
    ]
    weights_next = []
    for member in range(4):
        limiter = jnp.maximum(1.0, rms_list[member] / clip_level)
        weights_next.append(
            weights_old[member] - rates[member] * scaled_list[member] / limiter[:, None, None]
        )
    vector_state_next = decay * vector_state + (1.0 - decay) * (
        vector_grad * vector_grad + square_eps
    )
    vector_update = vector_grad * lax.rsqrt(vector_state_next)
    vector_rms = jnp.sqrt(jnp.mean(vector_update * vector_update))
    vectors_next = vectors - 0.25 * vector_update / jnp.maximum(1.0, vector_rms / clip_level)
    return (
        block_out,
        input_grad,
        inward_grad,
        outward_grad,
        expand_grad,
        shrink_grad,
        vector_grad,
        rows_next[0],
        columns_next[0],
        rows_next[1][0],
        columns_next[1][0],
        rows_next[2][0],
        columns_next[2][0],
        rows_next[3][0],
        columns_next[3][0],
        vector_state_next,
        weights_next[0],
        weights_next[1][0],
        weights_next[2][0],
        weights_next[3][0],
        vectors_next,
    )


def solution(mesh):
    placed = (
        P(("narrow", "wide"), None),
        P(("narrow", "wide"), None),
        P(("narrow", "wide"), None),
        P(),
        P(None, "wide", None),
        P("wide", None),
        P("wide", None),
        P("wide", None),
        P(),
        P(None, "wide"),
        P(),
        P("wide"),
        P(),
        P("wide"),
        P(),
        P("wide"),
        P(),
        P(),
    )
    return jax.shard_map(
        shards,
        mesh=mesh,
        in_specs=placed,
        out_specs=(
            P(("narrow", "wide"), None),
            P(("narrow", "wide"), None),
            P(None, "wide", None),
            P("wide", None),
            P("wide", None),
            P("wide", None),
            P(),
            P(None, "wide"),
            P(),
            P("wide"),
            P(),
            P("wide"),
            P(),
            P("wide"),
            P(),
            P(),
            P(None, "wide", None),
            P("wide", None),
            P("wide", None),
            P("wide", None),
            P(),
        ),
        check_vma=False,
    )
```

```python
import functools
import math

import jax
import jax.numpy as jnp
import numpy as np
from jax import lax
from jax.experimental import pallas as pl
from jax.experimental.pallas import tpu as pltpu
from jax.sharding import PartitionSpec as P

D = 768
HEADS = 12
HD = 64
FF = 3072
FEAT = 32
STEP = 10
LEN = 1024
SPAN = 256
CHUNKS = 3
GROUPS = 3
WIDTH = 256
FFC = FF // CHUNKS

norm_eps = 1e-05
square_eps = 1e-30
clip_level = 1.0

F32 = jnp.float32
BF16 = jnp.bfloat16
VMEM_LIMIT = 60 * 1024 * 1024
REST_LIMIT = 54 * 1024 * 1024
BACK_LIMIT = 46 * 1024 * 1024


def mm(left, right):
    return lax.dot_general(left, right, (((1,), (0,)), ((), ())), preferred_element_type=F32)


def mm_nt(left, right):
    return lax.dot_general(left, right, (((1,), (1,)), ((), ())), preferred_element_type=F32)


def mm_tn(left, right):
    return lax.dot_general(left, right, (((0,), (0,)), ((), ())), preferred_element_type=F32)


def halves(values):
    high = values.astype(BF16)
    return high, (values - high.astype(F32)).astype(BF16)


TAIL = (
    0.1795078068971634,
    0.17978088557720184,
    0.14234966039657593,
    0.06379217654466629,
    0.0434231162071228,
    -0.261725515127182,
    0.20454804599285126,
    -0.05167665705084801,
)


def normal_parts(values):
    size = jnp.abs(values)
    t = 1.0 / (1.0 + 0.45 * size)
    poly = TAIL[-1]
    for coeff in TAIL[-2::-1]:
        poly = poly * t + coeff
    bell = jnp.exp(-0.5 * values * values)
    tail = poly * t * bell
    return jnp.where(values >= 0, 1.0 - tail, tail), bell * 0.3989422804014327


def transposed(values):
    row = lax.broadcasted_iota(jnp.int32, (256, 256), 0)
    col = lax.broadcasted_iota(jnp.int32, (256, 256), 1)
    eye = (row == col).astype(F32).astype(BF16)
    return mm_nt(eye, values).astype(BF16)


def head_perm():
    perm = np.zeros((WIDTH, WIDTH), np.float32)
    for head in range(4):
        for half in range(2):
            for i in range(32):
                perm[head * 64 + half * 32 + i, half * 128 + head * 32 + i] = 1.0
    return perm


def make_blocks(lengths, base, first, last):
    def step(s, carry):
        count, begin, begin_row, end = carry
        new_end = end + lengths[0, s]
        full = new_end - begin_row > SPAN

        @pl.when(full)
        def _():
            base[count] = begin_row
            first[count] = begin
            last[count] = s - 1

        row = jnp.minimum((end // 16) * 16, LEN - SPAN)
        return (
            jnp.where(full, count + 1, count),
            jnp.where(full, s, begin),
            jnp.where(full, row, begin_row),
            new_end,
        )

    segments = lengths.shape[1]
    zero = jnp.int32(0)
    count, begin, begin_row, _ = lax.fori_loop(0, segments, step, (zero, zero, zero, zero))
    base[count] = begin_row
    first[count] = begin
    last[count] = segments - 1
    return count + 1


def lane_mask(lo, hi, width, dtype):
    lane = lax.broadcasted_iota(jnp.int32, (1, width), 1)
    return ((lane >= lo) & (lane < hi)).astype(F32).astype(dtype)


def value_rows(v_pair, head):
    keep = lane_mask(64 * head, 64 * head + 64, 128, BF16)
    return jnp.concatenate([v_pair * keep, jnp.broadcast_to(keep, v_pair.shape)], axis=1)


def span_mask(onehot, rows, lo, hi):
    member = onehot[rows, :]
    lane = lax.broadcasted_iota(jnp.int32, (1, 128), 1)
    inside = ((lane >= lo) & (lane <= hi)).astype(F32).astype(BF16)
    return mm_nt(member * inside, member).astype(BF16)


def cost(flops, size):
    return pl.CostEstimate(flops=10**6, transcendentals=0, bytes_accessed=10**5)


def row_blocks(body, loop=False):
    if not loop:
        for rows in range(0, LEN, 256):
            body(pl.ds(rows, 256))
        return

    def step(index, carry):
        body(pl.ds(pl.multiple_of(index * 256, 256), 256))
        return carry

    lax.fori_loop(0, LEN // 256, step, 0)


def any_spec():
    return pl.BlockSpec(memory_space=pl.ANY)


def in_copies(place, pieces, dst, sems, unit):
    if len(pieces) == 1:
        rows = dst.shape[1] // 3
        here = pl.ds(unit * rows, rows)
        return [pltpu.make_async_copy(pieces[0].at[:, here], dst.at[:, here], sems.at[unit, 0])]
    z, x, core = place[0], place[1], place[3]
    part, index = (0, unit) if unit < 2 else (4, 0)
    copies = []
    for side in range(2):
        half = core if side == 0 else 1 - core
        for flip in range(2):
            column = x if flip == 0 else 1 - x
            for shift in range(4):
                row = lax.rem(z + 4 - shift, 4) * 2 + column
                start = pl.multiple_of(unit * 96 + half * 48, 16)
                copies.append(
                    pltpu.make_async_copy(
                        pieces[part + 2 * side + flip].at[shift, index],
                        dst.at[row, pl.ds(start, 48)],
                        sems.at[unit, len(copies)],
                    )
                )
    return copies


def flat_copies(place, pieces, dst, sems):
    if len(pieces) == 1:
        return [pltpu.make_async_copy(pieces[0], dst, sems.at[0])]
    z, x, core = place[0], place[1], place[3]
    span = dst.shape[1] // 2
    copies = []
    for side in range(2):
        half = core if side == 0 else 1 - core
        for flip in range(2):
            column = x if flip == 0 else 1 - x
            for shift in range(4):
                row = lax.rem(z + 4 - shift, 4) * 2 + column
                start = pl.multiple_of(half * span, 16)
                copies.append(
                    pltpu.make_async_copy(
                        pieces[2 * side + flip].at[shift],
                        dst.at[row, pl.ds(start, span)],
                        sems.at[len(copies)],
                    )
                )
    return copies


def attend_kernel(count_in, lengths, place, *refs):
    pieces = refs[:count_in]
    (
        x_ref, norm_ref, bias_ref, perm_ref, proj_ref, cos_ref, sin_ref, onehot_ref,
        attn_ref, mixed_ref, a1t_ref, w_ref, wq_ref, wk_ref, qf_ref, kf_ref, v_ref, rden_ref,
        a1, qb, kb, vb, parts, base, first, last, sems,
    ) = refs[count_in:]
    group = pl.program_id(0)

    @pl.when(group == 0)
    def _():
        for unit in range(GROUPS):
            for copy in in_copies(place, pieces, w_ref, sems, unit):
                copy.start()
        def norm_rows(here):
            x = x_ref[here, :].astype(F32)
            centre = x - jnp.mean(x, axis=-1, keepdims=True)
            spread = jnp.mean(centre * centre, axis=-1, keepdims=True)
            a1[here, :] = (
                centre * lax.rsqrt(spread + norm_eps) * norm_ref[0:1, :] + norm_ref[1:2, :]
            ).astype(BF16)

        row_blocks(norm_rows)
        for cols in range(0, D, 256):
            a1t_ref[cols : cols + 256, :] = transposed(a1[:, cols : cols + 256])

    for unit in range(GROUPS):

        @pl.when(group == unit)
        def _():
            for copy in in_copies(place, pieces, w_ref, sems, unit):
                copy.wait()

    count = make_blocks(lengths, base, first, last)
    shard = w_ref.shape[1] // 3
    here = pl.ds(pl.multiple_of(group * shard, 16), shard)
    w = w_ref[:, here, :].reshape(D, D)
    perm = perm_ref[...]
    bias = bias_ref[0]
    proj_both = proj_ref[0]
    proj_high = proj_ref[1, :, :128]
    square = proj_ref[2, :, :128]
    weights = [mm(w[:, WIDTH * i : WIDTH * (i + 1)], perm).astype(BF16) for i in range(2)]

    def feature_rows(here):
        for which, (out_w, out_f, low_f) in enumerate(
            ((wq_ref, qf_ref, qb), (wk_ref, kf_ref, kb))
        ):
            u = (mm(a1[here, :], weights[which]) + bias[which : which + 1, :]) * HD ** (-0.25)
            c = u[:, :128]
            e = u[:, 128:]
            cosine = cos_ref[here, :]
            sine = sin_ref[here, :]
            turned = jnp.concatenate([c * cosine - e * sine, e * cosine + c * sine], axis=1)
            out_w[0, here, :] = turned
            high, low = halves(turned)
            sq_high, sq_low = halves(turned * turned)
            both = mm(high, proj_both)
            logits = (
                both[:, :128] + both[:, 128:] + mm(low, proj_high)
                - (mm(sq_high, square) + mm(sq_low, square))
            )
            phi = jnp.exp(logits) * FEAT ** (-0.5)
            out_f[0, here, :] = phi
            low_f[here, :] = phi.astype(BF16)
        v = mm(a1[here, :], w[:, 2 * WIDTH :]) + bias[2:3, :]
        v_ref[0, here, :] = v
        vb[here, :] = v.astype(BF16)

    row_blocks(feature_rows)
    parts[...] = jnp.zeros_like(parts)

    def one_span(index, carry):
        rows = pl.ds(pl.multiple_of(base[index], 16), SPAN)
        mask = span_mask(onehot_ref, rows, first[index], last[index])
        q = qb[rows, :]
        k = kb[rows, :]
        for pair in range(2):
            v_pair = vb[rows, 128 * pair : 128 * (pair + 1)]
            total = jnp.zeros((SPAN, WIDTH), F32)
            for side in range(2):
                head = 2 * pair + side
                scores = mm_nt(q * lane_mask(32 * head, 32 * head + 32, 128, BF16), k)
                total = total + mm(scores.astype(BF16) * mask, value_rows(v_pair, side))
            parts[pair, rows, :] += total
        return carry

    lax.fori_loop(0, count, one_span, 0)
    for pair in range(2):
        lanes = slice(128 * pair, 128 * (pair + 1))
        inverse = 1.0 / parts[pair, :, 128:]
        rden_ref[0, :, lanes] = inverse
        mixed = parts[pair, :, :128] * inverse
        mixed_ref[0, :, lanes] = mixed
        attn_ref[:, lanes] = mixed.astype(BF16)


def whole_spec(shape, **options):
    return pl.BlockSpec(shape, lambda *_: (0,) * len(shape), **options)


def group_spec(shape):
    return pl.BlockSpec((1,) + shape, lambda g, *_: (g,) + (0,) * len(shape))


def attend(lengths, place, pieces, wide, tokens, norm, bias, perm, proj, cosine, sine, onehot):
    def out(shape, dtype):
        return jax.ShapeDtypeStruct((GROUPS,) + shape, dtype)

    rows_in = 3 * D // wide
    return pl.pallas_call(
        functools.partial(attend_kernel, len(pieces)),
        grid_spec=pltpu.PrefetchScalarGridSpec(
            num_scalar_prefetch=2,
            grid=(GROUPS,),
            in_specs=[any_spec()] * len(pieces)
            + [
                whole_spec((LEN, D)), whole_spec((2, D)), group_spec((3, WIDTH)),
                whole_spec((WIDTH, WIDTH)), whole_spec((3, WIDTH, WIDTH)), whole_spec((LEN, 128)),
                whole_spec((LEN, 128)), whole_spec((LEN, 128)),
            ],
            out_specs=[
                pl.BlockSpec((LEN, WIDTH), lambda g, *_: (0, g)), group_spec((LEN, WIDTH)),
                whole_spec((D, LEN)), whole_spec((wide, rows_in, D)), group_spec((LEN, WIDTH)),
                group_spec((LEN, WIDTH)), group_spec((LEN, 128)), group_spec((LEN, 128)),
                group_spec((LEN, WIDTH)), group_spec((LEN, WIDTH)),
            ],
            scratch_shapes=[
                pltpu.VMEM((LEN, D), BF16),
                pltpu.VMEM((LEN, 128), BF16), pltpu.VMEM((LEN, 128), BF16),
                pltpu.VMEM((LEN, WIDTH), BF16), pltpu.VMEM((2, LEN, WIDTH), F32),
                pltpu.SMEM((32,), jnp.int32), pltpu.SMEM((32,), jnp.int32),
                pltpu.SMEM((32,), jnp.int32), pltpu.SemaphoreType.DMA((GROUPS, 16)),
            ],
        ),
        out_shape=[
            jax.ShapeDtypeStruct((LEN, D), BF16), out((LEN, WIDTH), F32),
            jax.ShapeDtypeStruct((D, LEN), BF16), jax.ShapeDtypeStruct((wide, rows_in, D), BF16),
            out((LEN, WIDTH), F32), out((LEN, WIDTH), F32), out((LEN, 128), F32),
            out((LEN, 128), F32), out((LEN, WIDTH), F32), out((LEN, WIDTH), F32),
        ],
        compiler_params=pltpu.CompilerParams(
            dimension_semantics=("arbitrary",), vmem_limit_bytes=VMEM_LIMIT
        ),
        cost_estimate=cost(20 * 10**9, 40 * 10**6),
        name="attend",
    )(lengths, place, *pieces, tokens, norm, bias, perm, proj, cosine, sine, onehot)


def attend_back_kernel(
    lengths, place, dmixed_ref, mixed_ref, rden_ref, wq_ref, wk_ref, qf_ref, kf_ref, v_ref,
    a1t_ref, w_ref, perm_ref, proj_ref, cos_ref, sin_ref, onehot_ref, ones_ref,
    keep_ref, send_ref, bias_ref, da1_ref,
    qb, kb, dnb, dnh, lift, dqf, dkf, dv, dqkv, base, first, last,
):
    count = make_blocks(lengths, base, first, last)
    qb[...] = qf_ref[0].astype(BF16)
    kb[...] = kf_ref[0].astype(BF16)
    lane = lax.broadcasted_iota(jnp.int32, (1, 128), 1)
    ones = ones_ref[...]
    def lift_rows(here):
        for pair in range(2):
            lanes = slice(128 * pair, 128 * (pair + 1))
            dnum = dmixed_ref[here, lanes] * rden_ref[0, here, lanes]
            high, low = halves(dnum)
            dnb[here, lanes] = high
            part_high, part_low = halves(dnum * mixed_ref[0, here, lanes])
            dden = -mm(jnp.concatenate([part_high, part_low], axis=1), ones)
            den_high, den_low = halves(dden)
            high, low = high.astype(F32), low.astype(F32)
            den_high = pltpu.roll(den_high.astype(F32), 64, 1)
            den_low = pltpu.roll(den_low.astype(F32), 64, 1)
            low_far = pltpu.roll(low, 64, 1)
            v = v_ref[0, here, lanes]
            v_high, v_low = halves(v)
            v_high, v_low = v_high.astype(F32), v_low.astype(F32)
            v_far = pltpu.roll(v_high, 64, 1)
            for side in range(2):
                own = (lane >= 64 * side) & (lane < 64 * side + 64)
                mark = 64 - 64 * side
                rest = jnp.where(lane == mark, den_high, jnp.where(lane == mark + 1, den_low, 0.0))
                both = ((lane == mark) | (lane == mark + 1)).astype(F32)
                head = 2 * pair + side
                dnh[head, here, :128] = jnp.where(own, high, low_far).astype(BF16)
                dnh[head, here, 128:] = jnp.where(own, high, rest).astype(BF16)
                lift[head, here, :128] = jnp.where(own, v_high, v_far).astype(BF16)
                lift[head, here, 128:] = jnp.where(own, v_low, both).astype(BF16)
    row_blocks(lift_rows)
    dqf[...] = jnp.zeros_like(dqf)
    dkf[...] = jnp.zeros_like(dkf)
    dv[...] = jnp.zeros_like(dv)

    def one_span(index, carry):
        rows = pl.ds(pl.multiple_of(base[index], 16), SPAN)
        mask = span_mask(onehot_ref, rows, first[index], last[index])
        q = qb[rows, :]
        k = kb[rows, :]
        q_total = jnp.zeros((SPAN, 128), F32)
        k_total = jnp.zeros((SPAN, 128), F32)
        for pair in range(2):
            lanes = slice(128 * pair, 128 * (pair + 1))
            dn_pair = dnb[rows, lanes]
            v_total = jnp.zeros((SPAN, 128), F32)
            for side in range(2):
                head = 2 * pair + side
                feats = lane_mask(32 * head, 32 * head + 32, 128, BF16)
                q_head = q * feats
                k_head = k * feats
                lifted = lift[head, rows, :]
                dn_head = dnh[head, rows, :]
                scores = mm_nt(k, q_head).astype(BF16) * mask
                dscores = mm_nt(dn_head, lifted).astype(BF16) * mask
                dscores_t = mm_nt(lifted, dn_head).astype(BF16) * mask
                q_total = q_total + mm(dscores, k_head)
                k_total = k_total + mm(dscores_t, q_head)
                own = lane_mask(64 * side, 64 * side + 64, 128, BF16)
                v_total = v_total + mm(scores, dn_pair * own)
            dv[rows, lanes] += v_total
        dqf[rows, :] += q_total
        dkf[rows, :] += k_total
        return carry

    lax.fori_loop(0, count, one_span, 0)
    proj_low = proj_ref[0, :, 128:]
    proj_high = proj_ref[1]
    square = proj_ref[2]
    perm = perm_ref[...]
    def feature_rows(here):
        for which, (w_in, phi_in, dphi) in enumerate(
            ((wq_ref, qf_ref, dqf), (wk_ref, kf_ref, dkf))
        ):
            r = dphi[here, :] * phi_in[0, here, :]
            high, low = halves(r)
            both = jnp.concatenate([high, low], axis=1)
            spread = mm_nt(both, square)
            dw = mm_nt(both, proj_high) + mm_nt(high, proj_low)
            du = (dw - 2.0 * w_in[0, here, :] * spread) * HD ** (-0.25)
            c = du[:, :128]
            e = du[:, 128:]
            cosine = cos_ref[here, :]
            sine = sin_ref[here, :]
            turned = jnp.concatenate([c * cosine + e * sine, e * cosine - c * sine], axis=1)
            dqkv[here, WIDTH * which : WIDTH * (which + 1)] = mm_nt(
                turned.astype(BF16), perm
            ).astype(BF16)

    row_blocks(feature_rows)
    dqkv[:, 2 * WIDTH :] = dv[...].astype(BF16)
    bias_ref[0] = jnp.sum(dqkv[...].astype(F32), axis=0, keepdims=True)
    grad = mm(a1t_ref[...], dqkv[...]).astype(BF16)
    at = pl.program_id(0)
    store_halves(grad, place[3], keep_ref.at[at], send_ref.at[at])
    w = w_ref[...].reshape(D, D)
    fresh = pl.program_id(0) == 0

    @pl.when(fresh)
    def _():
        da1_ref[...] = mm_nt(dqkv[...], w)

    @pl.when(jnp.logical_not(fresh))
    def _():
        da1_ref[...] += mm_nt(dqkv[...], w)


def store_halves(grad, core, keep_ref, send_ref):
    wide, rows = keep_ref.shape[0], D // keep_ref.shape[0]
    half = rows // 2
    parts = grad.reshape(wide, rows, D)
    for cols in range(3):
        block = parts[:, :, WIDTH * cols : WIDTH * (cols + 1)]
        here = pl.ds(half * cols, half)

        @pl.when(core == 0)
        def _():
            keep_ref[:, here, :] = block[:, :half]
            send_ref[:, here, :] = block[:, half:]

        @pl.when(core == 1)
        def _():
            keep_ref[:, here, :] = block[:, half:]
            send_ref[:, here, :] = block[:, :half]


def attend_back(
    lengths, place, wide, dmixed, saved, a1t, w_in, perm, proj, cosine, sine, onehot, ones
):
    mixed, rden, wq, wk, qf, kf, v = saved

    def by_group(shape):
        return pl.BlockSpec((1,) + shape, lambda g, *_: (g,) + (0,) * len(shape))

    rows_in = D // wide
    half = struct((GROUPS, wide, 3 * rows_in // 2, WIDTH), BF16)
    half_spec = once(half.shape)
    if wide > 1:
        half = pltpu.VMEM(half.shape, BF16)
        half_spec = pl.BlockSpec(memory_space=pltpu.VMEM)
    return pl.pallas_call(
        attend_back_kernel,
        grid_spec=pltpu.PrefetchScalarGridSpec(
            num_scalar_prefetch=2,
            grid=(GROUPS,),
            in_specs=[
                pl.BlockSpec((LEN, WIDTH), lambda g, *_: (0, g)),
                by_group((LEN, WIDTH)), by_group((LEN, WIDTH)), by_group((LEN, WIDTH)),
                by_group((LEN, WIDTH)), by_group((LEN, 128)), by_group((LEN, 128)),
                by_group((LEN, WIDTH)), once((D, LEN)),
                pl.BlockSpec((wide, rows_in, D), lambda g, *_: (0, g, 0)),
                once((WIDTH, WIDTH)), once((3, WIDTH, WIDTH)), once((LEN, 128)),
                once((LEN, 128)), once((LEN, 128)), once((WIDTH, 128)),
            ],
            out_specs=[
                half_spec, half_spec, group_spec((1, D)),
                whole_spec((LEN, D)),
            ],
            scratch_shapes=[
                pltpu.VMEM((LEN, 128), BF16), pltpu.VMEM((LEN, 128), BF16),
                pltpu.VMEM((LEN, WIDTH), BF16), pltpu.VMEM((4, LEN, WIDTH), BF16),
                pltpu.VMEM((4, LEN, WIDTH), BF16), pltpu.VMEM((LEN, 128), F32),
                pltpu.VMEM((LEN, 128), F32), pltpu.VMEM((LEN, WIDTH), F32),
                pltpu.VMEM((LEN, D), BF16),
                pltpu.SMEM((32,), jnp.int32), pltpu.SMEM((32,), jnp.int32),
                pltpu.SMEM((32,), jnp.int32),
            ],
        ),
        out_shape=[
            half, half, struct((GROUPS, 1, D), F32), struct((LEN, D), F32),
        ],
        compiler_params=pltpu.CompilerParams(
            dimension_semantics=("arbitrary",), vmem_limit_bytes=BACK_LIMIT
        ),
        cost_estimate=cost(GROUPS * 12 * 10**9, GROUPS * 20 * 10**6),
        name="attend_back",
    )(
        lengths, place, dmixed, mixed, rden, wq, wk, qf, kf, v, a1t, w_in, perm, proj, cosine,
        sine, onehot, ones,
    )


def chunk_step(
    place, wide, bias_up, dy_ref, a2, a2t, dyt, up, down, act, dhidden, y, back, outs, dbias_ref,
    fresh,
):
    rows_up = D // wide
    rows_down = FFC // wide
    dbias_ref[0] = jnp.zeros((1, FFC), F32)

    def chunk_rows(here):
        hidden = mm(a2[here, :], up[...]) + bias_up
        below, density = normal_parts(hidden)
        act_now = (hidden * below).astype(BF16)
        act[here, :] = act_now
        dact = mm_nt(dy_ref[here, :], down[...])
        dhidden_now = (dact * (below + hidden * density)).astype(BF16)
        dhidden[here, :] = dhidden_now
        dbias_ref[0] += jnp.sum(dhidden_now.astype(F32), axis=0, keepdims=True)
        if fresh:
            y[here, :] = mm(act_now, down[...])
            back[here, :] = mm_nt(dhidden_now, up[...])
        else:
            y[here, :] += mm(act_now, down[...])
            back[here, :] += mm_nt(dhidden_now, up[...])

    row_blocks(chunk_rows, True)
    grad_up = mm(a2t[...], dhidden[...]).astype(BF16).reshape(wide, rows_up, FFC)
    grad_down = mm(dyt[...], act[...]).astype(BF16)
    core = place[3]

    def store_up(ref):
        for cols in range(4):
            ref[:, rows_up * cols : rows_up * (cols + 1), :] = grad_up[
                :, :, WIDTH * cols : WIDTH * (cols + 1)
            ]

    def store_down(ref):
        if wide == 1:
            for cols in range(4):
                ref[0, D * cols : D * (cols + 1), :] = grad_down[
                    :, WIDTH * cols : WIDTH * (cols + 1)
                ]
            return
        for shard in range(wide):
            block = grad_down[:, rows_down * shard : rows_down * (shard + 1)]
            ref[shard, :, :128] = block[: D // 2]
            ref[shard, :, 128:] = block[D // 2 :]

    for when, keep_ref, send_ref in outs:
        for side in range(2):
            now = core == side

            @pl.when(now if when is None else now & when)
            def _():
                store_up(keep_ref if side == 0 else send_ref)
                store_down(send_ref if side == 0 else keep_ref)


def load_up(flat, at, up, wide):
    rows = D // wide
    for cols in range(4):
        here = pl.ds(at + rows * cols, rows)
        up[:, WIDTH * cols : WIDTH * (cols + 1)] = flat[:, here, :].reshape(D, WIDTH)


def load_down(flat, at, down, wide):
    rows = FFC // wide
    for cols in range(3):
        here = pl.ds(at + rows * cols, rows)
        down[:, WIDTH * cols : WIDTH * (cols + 1)] = flat[:, here, :].reshape(FFC, WIDTH)


def middle_first_kernel(wide, count_in, place, *refs):
    pieces = refs[:count_in]
    (
        x_ref, attn_ref, dy_ref, rows_ref, bias_up_ref,
        x1_ref, a2_ref, a2t_ref, dyt_ref, y_ref, back_ref, out_ref, keep_ref, send_ref, dbias_ref,
        flat, up, down, act, dhidden, sems,
    ) = refs[count_in:]
    copies = flat_copies(place, pieces, flat, sems)
    for copy in copies:
        copy.start()
    for cols in range(0, D, 256):
        dyt_ref[cols : cols + 256, :] = transposed(dy_ref[:, cols : cols + 256])
    for copy in copies:
        copy.wait()
    half_out = D // wide // 2
    half_flat = flat.shape[1] // 2
    for cols in range(3):
        upper = flat[:, half_out * cols : half_out * (cols + 1), :]
        lower = flat[:, half_flat + half_out * cols : half_flat + half_out * (cols + 1), :]
        out_ref[:, WIDTH * cols : WIDTH * (cols + 1)] = jnp.concatenate(
            [upper, lower], axis=1
        ).reshape(D, WIDTH)
    def norm_rows(here):
        x1 = x_ref[here, :].astype(F32) + (mm(attn_ref[here, :], out_ref[...]) + rows_ref[7:8, :])
        x1_ref[here, :] = x1
        centre = x1 - jnp.mean(x1, axis=-1, keepdims=True)
        spread = jnp.mean(centre * centre, axis=-1, keepdims=True)
        a2_ref[here, :] = (
            centre * lax.rsqrt(spread + norm_eps) * rows_ref[2:3, :] + rows_ref[3:4, :]
        ).astype(BF16)

    row_blocks(norm_rows)
    for cols in range(0, D, 256):
        a2t_ref[cols : cols + 256, :] = transposed(a2_ref[:, cols : cols + 256])
    load_up(flat, 3 * half_out, up, wide)
    load_down(flat, half_flat + 3 * half_out, down, wide)
    chunk_step(
        place, wide, bias_up_ref[0], dy_ref, a2_ref, a2t_ref, dyt_ref, up, down, act, dhidden,
        y_ref, back_ref, [(None, keep_ref, send_ref)], dbias_ref, True,
    )


def middle_rest_kernel(wide, count_in, place, *refs):
    pieces = refs[:count_in]
    (
        dy_ref, a2_ref, a2t_ref, dyt_ref, bias_up_ref, attn_ref, out_ref, rows_ref,
        y_in, back_in, x1_in,
        block_ref, dx1_ref, dmixed_ref, okeep_ref, osend_ref, vec_ref,
        keep_ref, send_ref, dbias_ref,
        flat, up, down, act, dhidden, back, dbranch, sems, flat_sems,
    ) = refs[count_in:]
    step = pl.program_id(0)
    y_copy = pltpu.make_async_copy(y_in, block_ref, sems.at[0])
    back_copy = pltpu.make_async_copy(back_in, back, sems.at[1])
    x1_copy = pltpu.make_async_copy(x1_in, dx1_ref, sems.at[2])

    def chunk_copies(chunk, side):
        if count_in == 1:
            return [
                pltpu.make_async_copy(
                    pieces[0].at[chunk], flat.at[chunk], flat_sems.at[chunk, 0]
                )
            ]
        copies = []
        for flip in range(2):
            column = place[1] if flip == 0 else 1 - place[1]
            for shift in range(4):
                shard = lax.rem(place[0] + 4 - shift, 4) * 2 + column
                copies.append(
                    pltpu.make_async_copy(
                        pieces[2 * side + flip].at[shift], flat.at[chunk, shard],
                        flat_sems.at[chunk, len(copies)],
                    )
                )
        return copies

    def fetch(chunk):
        for side in range(2):

            @pl.when((place[3] == chunk) if side == 0 else (place[3] != chunk))
            def _():
                if side == 0 or count_in > 1:
                    for copy in chunk_copies(chunk, side):
                        copy.start()

    def arrived(chunk):
        for copy in chunk_copies(chunk, 0):
            copy.wait()

    @pl.when(step == 0)
    def _():
        if count_in == 1:
            for chunk in range(2):
                for copy in chunk_copies(chunk, 0):
                    copy.start()
        else:
            fetch(0)
        y_copy.start()
        back_copy.start()
        if count_in > 1:
            fetch(1)
        x1_copy.start()
        arrived(0)
        y_copy.wait()
        back_copy.wait()

    @pl.when(step == 1)
    def _():
        arrived(1)

    load_up(flat.at[step], 0, up, wide)
    load_down(flat.at[step], 4 * (D // wide), down, wide)
    chunk_step(
        place, wide, bias_up_ref[0], dy_ref, a2_ref, a2t_ref, dyt_ref, up, down, act, dhidden,
        block_ref, back, [(None, keep_ref.at[step], send_ref.at[step])], dbias_ref, False,
    )

    @pl.when(step == 1)
    def _():
        x1_copy.wait()
        vec_ref[...] = jnp.zeros_like(vec_ref)

        def last_rows(here):
            x1 = dx1_ref[here, :]
            block_ref[here, :] = x1 + (block_ref[here, :] + rows_ref[8:9, :])
            dn = back[here, :]
            dy = dy_ref[here, :].astype(F32)
            centre = x1 - jnp.mean(x1, axis=-1, keepdims=True)
            spread = jnp.mean(centre * centre, axis=-1, keepdims=True)
            scale = lax.rsqrt(spread + norm_eps)
            zh = centre * scale
            vec_ref[0:1, :] += jnp.sum(dn * zh, axis=0, keepdims=True)
            vec_ref[1:2, :] += jnp.sum(dn, axis=0, keepdims=True)
            e = dn * rows_ref[2:3, :]
            dz = (
                e
                - jnp.mean(e, axis=-1, keepdims=True)
                - zh * jnp.mean(e * zh, axis=-1, keepdims=True)
            ) * scale
            dx1 = dy + dz
            dx1_ref[here, :] = dx1
            low = dx1.astype(BF16)
            dbranch[here, :] = low
            vec_ref[2:3, :] += jnp.sum(low.astype(F32), axis=0, keepdims=True)
            vec_ref[3:4, :] += jnp.sum(dy, axis=0, keepdims=True)
            dmixed_ref[here, :] = mm_nt(low, out_ref[...])

        row_blocks(last_rows, True)
        for cols in range(0, D, 256):
            up[cols : cols + 256, :] = transposed(attn_ref[:, cols : cols + 256])
        store_halves(mm(up[...], dbranch[...]).astype(BF16), place[3], okeep_ref, osend_ref)


def once(shape):
    return whole_spec(shape, pipeline_mode=pl.Buffered(1))


def struct(shape, dtype):
    return jax.ShapeDtypeStruct(shape, dtype)


def weight_scratch():
    return [
        pltpu.VMEM((D, FFC), BF16), pltpu.VMEM((FFC, D), BF16), pltpu.VMEM((LEN, FFC), BF16),
        pltpu.VMEM((LEN, FFC), BF16),
    ]


def middle_first(place, wide, pieces, tokens, attn, cotangent, vectors, bias_up):
    rows_flat = 3 * D // wide + 2 * FFC * D // (WIDTH * wide)
    half = (wide, FFC * D // (WIDTH * wide), WIDTH)
    outs = [
        struct((LEN, D), F32), struct((LEN, D), BF16), struct((D, LEN), BF16),
        struct((D, LEN), BF16), struct((LEN, D), F32), struct((LEN, D), F32),
        struct((D, D), BF16), struct(half, BF16), struct(half, BF16), struct((1, 1, FFC), F32),
    ]
    return pl.pallas_call(
        functools.partial(middle_first_kernel, wide, len(pieces)),
        grid_spec=pltpu.PrefetchScalarGridSpec(
            num_scalar_prefetch=1,
            grid=(1,),
            in_specs=[any_spec()] * len(pieces)
            + [
                once((LEN, D)), once((LEN, D)), once((LEN, D)), once((13, D)),
                pl.BlockSpec((1, 1, FFC), lambda *_: (0, 0, 0)),
            ],
            out_specs=[once(out.shape) for out in outs],
            scratch_shapes=[pltpu.VMEM((wide, rows_flat, WIDTH), BF16)]
            + weight_scratch()
            + [pltpu.SemaphoreType.DMA((16,))],
        ),
        out_shape=outs,
        compiler_params=pltpu.CompilerParams(
            dimension_semantics=("arbitrary",), vmem_limit_bytes=VMEM_LIMIT
        ),
        cost_estimate=cost(14 * 10**9, 30 * 10**6),
        name="middle_first",
    )(place, *pieces, tokens, attn, cotangent, vectors, bias_up)


def middle_rest(place, wide, pieces, cotangent, state, bias_up, attn, w_out, vectors, sums):
    a2, a2t, dyt = state
    half = (wide, FFC * D // (WIDTH * wide), WIDTH)
    out_half = (wide, 3 * D // (2 * wide), WIDTH)
    outs = [
        struct((LEN, D), F32), struct((LEN, D), F32), struct((LEN, D), F32),
        struct(out_half, BF16), struct(out_half, BF16), struct((8, D), F32),
        struct((2,) + half, BF16), struct((2,) + half, BF16), struct((2, 1, FFC), F32),
    ]
    out_specs = [once(out.shape) for out in outs[:8]] + [group_spec((1, FFC))]
    if wide > 1:
        for index in (3, 4, 6, 7):
            outs[index] = pltpu.VMEM(outs[index].shape, BF16)
            out_specs[index] = pl.BlockSpec(memory_space=pltpu.VMEM)
    rows_flat = 2 * FFC * D // (WIDTH * wide)
    return pl.pallas_call(
        functools.partial(middle_rest_kernel, wide, len(pieces)),
        grid_spec=pltpu.PrefetchScalarGridSpec(
            num_scalar_prefetch=1,
            grid=(2,),
            in_specs=[any_spec()] * len(pieces)
            + [
                once((LEN, D)), once((LEN, D)), once((D, LEN)), once((D, LEN)),
                pl.BlockSpec((1, 1, FFC), lambda j, *_: (j + 1, 0, 0)),
                once((LEN, D)), once((D, D)), once((13, D)),
                any_spec(), any_spec(), any_spec(),
            ],
            out_specs=out_specs,
            scratch_shapes=[pltpu.VMEM((2, wide, rows_flat, WIDTH), BF16)]
            + weight_scratch()
            + [
                pltpu.VMEM((LEN, D), F32), pltpu.VMEM((LEN, D), BF16),
                pltpu.SemaphoreType.DMA((3,)), pltpu.SemaphoreType.DMA((2, 8)),
            ],
        ),
        out_shape=outs,
        compiler_params=pltpu.CompilerParams(
            dimension_semantics=("arbitrary",), vmem_limit_bytes=REST_LIMIT
        ),
        cost_estimate=cost(28 * 10**9, 40 * 10**6),
        name="middle_rest",
    )(place, *pieces, cotangent, a2, a2t, dyt, bias_up, attn, w_out, vectors, *sums)


def input_kernel(
    wide, x_ref, dx1_ref, da1_ref, rows_ref, middle_ref, bias_in_ref, bias_first_ref, bias_rest_ref,
    out_ref, vec_ref,
):
    gain = rows_ref[0:1, :]
    x = x_ref[...].astype(F32)
    dn = da1_ref[...]
    centre = x - jnp.mean(x, axis=-1, keepdims=True)
    spread = jnp.mean(centre * centre, axis=-1, keepdims=True)
    scale = lax.rsqrt(spread + norm_eps)
    zh = centre * scale
    e = dn * gain
    dz = (
        e - jnp.mean(e, axis=-1, keepdims=True) - zh * jnp.mean(e * zh, axis=-1, keepdims=True)
    ) * scale
    out_ref[...] = dx1_ref[...] + dz

    @pl.when(pl.program_id(0) == 0)
    def _():
        vec_ref[...] = jnp.zeros_like(vec_ref)
        vec_ref[2:4, :] = middle_ref[0:2, :]
        vec_ref[7:9, :] = middle_ref[2:4, :]
        for group in range(GROUPS):
            lanes = slice(WIDTH * group, WIDTH * (group + 1))
            for which in range(3):
                vec_ref[4 + which : 5 + which, lanes] = bias_in_ref[
                    group, :, WIDTH * which : WIDTH * (which + 1)
                ]
        for chunk in range(CHUNKS):
            for part in range(8):
                value = (
                    bias_first_ref[0] if chunk == 0 else bias_rest_ref[chunk - 1]
                )[:, 128 * part : 128 * (part + 1)]
                start = FFC * chunk + 128 * part if wide == 1 else 384 * part + 128 * chunk
                row, lane = 9 + start // D, start % D
                vec_ref[row : row + 1, lane : lane + 128] = value

    vec_ref[0:1, :] += jnp.sum(dn * zh, axis=0, keepdims=True)
    vec_ref[1:2, :] += jnp.sum(dn, axis=0, keepdims=True)


def input_side(wide, tokens, dx1, da1, vectors, middle_vec, bias_in, bias_first, bias_rest):
    block = pl.BlockSpec((256, D), lambda i: (i, 0))
    return pl.pallas_call(
        functools.partial(input_kernel, wide),
        grid=(LEN // 256,),
        in_specs=[
            block, block, block, whole_spec((13, D)), whole_spec((8, D)),
            whole_spec((GROUPS, 1, D)), whole_spec((1, 1, FFC)), whole_spec((2, 1, FFC)),
        ],
        out_specs=[block, whole_spec((16, D))],
        out_shape=[struct((LEN, D), F32), struct((16, D), F32)],
        compiler_params=pltpu.CompilerParams(dimension_semantics=("arbitrary",)),
        cost_estimate=cost(10**6, 12 * 10**6),
        name="input_side",
    )(tokens, dx1, da1, vectors, middle_vec, bias_in, bias_first, bias_rest)


def tables(lengths, projection):
    ends = jnp.cumsum(lengths[0])
    starts = ends - lengths[0]
    place = jnp.arange(LEN, dtype=jnp.int32)
    member = (place[:, None] >= starts[None, :]) & (place[:, None] < ends[None, :])
    offset = jnp.sum(jnp.where(member, starts[None, :], 0), axis=1)
    position = (place - offset).astype(F32)
    freq = 10000.0 ** (-jnp.arange(32, dtype=F32) / 32)
    angles = position[:, None] * jnp.tile(freq, 4)[None, :]
    onehot = jnp.pad(member.astype(BF16), ((0, 0), (0, 128 - member.shape[1])))
    eye = jnp.asarray(np.eye(4, dtype=np.float32))
    lifted = jnp.einsum("hif,ab->haibf", projection.reshape(2, 32, FEAT), eye)
    lifted = lifted.reshape(WIDTH, 128)
    rounded = lax.reduce_precision(lifted, 8, 7)
    high, low = rounded.astype(BF16), (lifted - rounded).astype(BF16)
    square = np.zeros((2, 4, 32, 4, 32), np.float32)
    for head in range(4):
        square[:, head, :, head, :] = 0.5
    square = jnp.asarray(square.reshape(WIDTH, 128), BF16)
    proj = jnp.stack(
        [
            jnp.concatenate([high, low], axis=1),
            jnp.concatenate([high, high], axis=1),
            jnp.concatenate([square, square], axis=1),
        ]
    )
    return jnp.cos(angles), jnp.sin(angles), onehot, proj


def wide_perm(shift_z, flip_x):
    pairs = []
    for z in range(4):
        for x in range(2):
            target_x = 1 - x if flip_x else x
            pairs.append((2 * z + x, 2 * ((z + shift_z) % 4) + target_x))
    return pairs


def narrow_perm(flip_y, flip_core):
    pairs = []
    for y in range(2):
        for core in range(2):
            pairs.append(
                (2 * y + core, 2 * (1 - y if flip_y else y) + (1 - core if flip_core else core))
            )
    return pairs


def over_z(values, shift):
    return lax.ppermute(values, "wide", wide_perm(shift, False))


def over_x(values):
    return lax.ppermute(values, "wide", wide_perm(0, True))


def over_far(values, bit):
    return lax.ppermute(values, "wide", [(w, w ^ bit) for w in range(8)])


def over_y(values):
    return lax.ppermute(values, "narrow", narrow_perm(True, False))


def over_core(values):
    return lax.ppermute(values, "narrow", narrow_perm(False, True))


def tie(*values):
    return lax.optimization_barrier(values)


def special():
    return lax.axis_size("wide") == 8 and lax.axis_size("narrow") == 4


def sum_wide(values):
    if not special():
        return lax.psum(values, "wide")
    for perm in (wide_perm(0, True), [(w, w ^ 2) for w in range(8)], [(w, w ^ 4) for w in range(8)]):
        values = values + lax.ppermute(values, "wide", perm)
    return values


def sum_narrow(values):
    if not special():
        return lax.psum(values, "narrow")
    pair = values + over_core(values)
    return pair + over_y(pair)


def along_z(mine):
    return jnp.stack([mine] + [over_z(mine, shift) for shift in (1, 2, 3)])


def small_call(kernel, name, place, operands, outs):
    return pl.pallas_call(
        kernel,
        grid_spec=pltpu.PrefetchScalarGridSpec(
            num_scalar_prefetch=1,
            grid=(1,),
            in_specs=[once(value.shape) for value in operands],
            out_specs=[once(out.shape) for out in outs],
        ),
        out_shape=outs,
        compiler_params=pltpu.CompilerParams(
            dimension_semantics=("arbitrary",), vmem_limit_bytes=VMEM_LIMIT
        ),
        cost_estimate=cost(10**6, sum(4 * math.prod(v.shape) for v in operands + outs)),
        name=name,
    )(place, *operands)


def held_call(kernel, name, place, operands, outs, held=None, flops=10**6):
    here = pl.BlockSpec(memory_space=pltpu.VMEM)
    held = len(outs) if held is None else held
    return pl.pallas_call(
        kernel,
        in_specs=[pl.BlockSpec(memory_space=pltpu.SMEM)] + [here] * len(operands),
        out_specs=[here] * len(outs),
        out_shape=[
            pltpu.VMEM(out.shape, out.dtype) if index < held else out
            for index, out in enumerate(outs)
        ],
        compiler_params=pltpu.CompilerParams(vmem_limit_bytes=24 * 1024 * 1024),
        cost_estimate=pl.CostEstimate(flops=flops, transcendentals=0, bytes_accessed=10**5),
        name=name,
    )(place, *[pltpu.with_memory_space_constraint(value, pltpu.VMEM) for value in operands])


def pick_kernel(
    place, in_ref, out_ref, up_ref, down_ref, near_ref, last_ref, first_ref, rest_ref
):
    core = place[3]
    here = pl.ds(pl.multiple_of(48 * core, 16), 48)
    for group in range(GROUPS):
        ref, index = (near_ref, group) if group < 2 else (last_ref, 0)
        for which in range(3):
            ref[index, :, WIDTH * which : WIDTH * (which + 1)] = in_ref[
                which, here, WIDTH * group : WIDTH * (group + 1)
            ].astype(BF16)
    for cols in range(3):
        first_ref[48 * cols : 48 * (cols + 1), :] = out_ref[
            here, WIDTH * cols : WIDTH * (cols + 1)
        ].astype(BF16)

    def put_up(ref, at, chunk):
        for cols in range(4):
            rows = slice(at + 96 * cols, at + 96 * (cols + 1))
            for side in range(2):
                start = 384 * (2 * cols + side) + 128 * chunk
                ref[rows, 128 * side : 128 * (side + 1)] = up_ref[:, start : start + 128].astype(
                    BF16
                )

    def put_down(ref, at, chunk):
        for cols in range(3):
            ref[at + 128 * cols : at + 128 * (cols + 1), :] = down_ref[
                128 * chunk : 128 * (chunk + 1), WIDTH * cols : WIDTH * (cols + 1)
            ].astype(BF16)

    for side in range(2):

        @pl.when(core == side)
        def _():
            if side == 0:
                put_up(first_ref, 144, 0)
            else:
                put_down(first_ref, 144, 0)

        @pl.when(core == side)
        def _():
            put_up(rest_ref, 0, 1 + side)
            put_down(rest_ref, 384, 1 + side)


def chunk_of(ref, chunk, shard):
    return ref[chunk, shard] if len(ref.shape) == 4 else ref[shard]


def first_sum_kernel(place, *refs):
    send_ref, keep_ref = refs[-2:]
    x = place[1]
    at = 0
    for index in range(0, len(refs) - 2, 2):
        own, got = refs[index], refs[index + 1]
        for part in range(own.shape[0] if len(own.shape) == 4 and own.shape[0] == 3 else 1):
            rows = own.shape[-2]
            here = pl.ds(at, rows)
            for z in range(4):
                for out, side in ((keep_ref, x), (send_ref, 1 - x)):
                    out[z, here, :] = (
                        chunk_of(own, part, 2 * z + side).astype(F32)
                        + chunk_of(got, part, 2 * z + side).astype(F32)
                    ).astype(BF16)
            at += rows


def first_sum(place, pairs):
    rows = sum(
        own.shape[-2] * (own.shape[0] if own.ndim == 4 and own.shape[0] == 3 else 1)
        for own, _ in pairs
    )
    return held_call(
        first_sum_kernel, "first_sum", place, [value for pair in pairs for value in pair],
        [struct((4, rows, WIDTH), BF16)] * 2,
    )


def first_sum_y_kernel(place, own, got, send, keep):
    y = place[2]
    for group in range(GROUPS):
        here = pl.ds(144 * group, 144)
        for shard in range(8):
            total = own[group, shard].astype(F32) + got[group, shard].astype(F32)
            left, right = total[:, :128].astype(BF16), total[:, 128:].astype(BF16)
            keep[shard, here, :] = jnp.where(y == 0, left, right)
            send[shard, here, :] = jnp.where(y == 0, right, left)


def split_x_kernel(place, own, got, send, keep):
    x = place[1]
    for z in range(4):
        for out, side in ((keep, x), (send, 1 - x)):
            out[z] = (own[2 * z + side].astype(F32) + got[2 * z + side].astype(F32)).astype(BF16)


def second_sum_kernel(place, own_ref, got_ref, *outs):
    z = place[0]
    for shift, out in enumerate(outs):
        there = lax.rem(z + shift, 4)
        out[...] = (own_ref[there].astype(F32) + got_ref[there].astype(F32)).astype(BF16)


def second_sum(place, own, got):
    outs = [struct(own.shape[1:], BF16)] * 4
    return held_call(second_sum_kernel, "second_sum", place, [own, got], outs)


def z_sum_kernel(place, *refs):
    total = refs[0][...].astype(F32)
    for ref in refs[1:4]:
        total = total + ref[...].astype(F32)
    rows = refs[0].shape[0]
    refs[-1][:rows, :] = total.astype(refs[-1].dtype)
    if len(refs) == 7:
        refs[-1][rows:, :] = (refs[4][...].astype(F32) + refs[5][...].astype(F32)).astype(BF16)


def z_sum(place, parts, below=(), got=None):
    if got is None:
        got = [over_z(parts[shift], shift) for shift in (1, 2, 3)]
    rows = parts[0].shape[0] + (below[0].shape[0] if below else 0)
    return held_call(
        z_sum_kernel, "z_sum", place, [parts[0]] + got + list(below),
        [struct((rows, parts[0].shape[1]), BF16 if below else F32)],
        flops=3 * 10**10 if below else 10**6,
    )[0]


def first_sum_z_kernel(place, *refs):
    z = place[0]
    outs = refs[-4:]
    for shift, out in enumerate(outs):
        there = lax.rem(z + shift, 4) * 2
        at = 0
        for index in range(0, len(refs) - 4, 2):
            own, got = refs[index], refs[index + 1]
            rows = own.shape[-2]
            for x in range(2):
                out[x, at : at + rows, :] = (
                    chunk_of(own, 1, there + x).astype(F32)
                    + chunk_of(got, 1, there + x).astype(F32)
                ).astype(BF16)
            at += rows


def first_sum_z(place, pairs):
    rows = sum(own.shape[-2] for own, _ in pairs)
    return held_call(
        first_sum_z_kernel, "first_sum_z", place, [value for pair in pairs for value in pair],
        [struct((2, rows, WIDTH), BF16)] * 4,
    )


def split_sum_kernel(place, *refs):
    keep, send = refs[-2:]
    x = place[1]
    for out, at in ((keep, x), (send, 1 - x)):
        total = refs[0][at].astype(F32)
        for ref in refs[1:4]:
            total = total + ref[at].astype(F32)
        out[...] = total.astype(BF16)


def split_sum(place, parts):
    return held_call(
        split_sum_kernel, "split_sum", place, parts, [struct(parts[0].shape[1:], BF16)] * 2
    )


def to_row(column):
    size = column.shape[0]
    eye = lax.broadcasted_iota(jnp.int32, (size, size), 0) == lax.broadcasted_iota(
        jnp.int32, (size, size), 1
    )
    return jnp.sum(jnp.where(eye, column, 0.0), axis=0, keepdims=True)


def to_column(row):
    size = row.shape[1]
    eye = lax.broadcasted_iota(jnp.int32, (size, size), 0) == lax.broadcasted_iota(
        jnp.int32, (size, size), 1
    )
    return jnp.sum(jnp.where(eye, row, 0.0), axis=1, keepdims=True)


DECAY = 1.0 - STEP ** (-0.8)


def lane_values(values):
    lane = lax.broadcasted_iota(jnp.int32, (1, D), 1)
    row = jnp.zeros((1, D), F32)
    for index, value in enumerate(values):
        row = jnp.where(lane == index, value, row)
    return row


def moments(grad, rows_old):
    plain = grad * grad
    squares = plain + square_eps
    mean = jnp.sum(squares, axis=1, keepdims=True) * (1.0 / grad.shape[1])
    rows_new = DECAY * rows_old + (1.0 - DECAY) * to_row(mean)
    total = jnp.sum(rows_new, axis=1, keepdims=True)
    divided = jnp.sum(plain * to_column(1.0 / rows_new), axis=0, keepdims=True)
    return rows_new, total, jnp.sum(squares, axis=0, keepdims=True), divided


def ffn_moments_kernel(
    place, own, got, up_rows, down_rows, out_rows,
    up_grad, down_grad, out_grad, up_rows_new, down_rows_new, out_rows_new, sums,
):
    core = place[3]

    def collect(low, high):
        for chunk in range(CHUNKS):
            at = 384 * chunk
            for cols in range(4):
                for side in range(2):
                    start = 384 * (2 * cols + side) + 128 * chunk
                    up_grad[:, start : start + 128] = low[
                        at + 96 * cols : at + 96 * (cols + 1), 128 * side : 128 * (side + 1)
                    ]
            for side in range(2):
                down_grad[128 * chunk : 128 * (chunk + 1), 384 * side : 384 * (side + 1)] = (
                    jnp.transpose(high[at : at + 384, 128 * side : 128 * (side + 1)])
                )
        for cols in range(3):
            lanes = slice(WIDTH * cols, WIDTH * (cols + 1))
            at = 1152 + 48 * cols
            out_grad[:48, lanes] = low[at : at + 48, :]
            out_grad[48:, lanes] = high[at : at + 48, :]

    @pl.when(core == 0)
    def _():
        collect(own, got)

    @pl.when(core == 1)
    def _():
        collect(got, own)

    up_new, up_total, up_sums, up_divided = moments(up_grad[...], up_rows[...])
    down_new, down_total, down_sums, down_divided = moments(down_grad[...], down_rows[...])
    out_new, out_total, out_sums, out_divided = moments(out_grad[...], out_rows[...])
    up_rows_new[...] = up_new
    down_rows_new[...] = down_new
    out_rows_new[...] = out_new
    for part in range(4):
        lanes = slice(D * part, D * (part + 1))
        sums[part : part + 1, :] = up_sums[:, lanes]
        sums[4 + part : 5 + part, :] = up_divided[:, lanes]
    sums[8:9, :] = down_sums
    sums[9:10, :] = down_divided
    sums[10:11, :] = out_sums
    sums[11:12, :] = out_divided
    sums[12:13, :] = lane_values([up_total, down_total, out_total])
    sums[13:16, :] = jnp.zeros((3, D), F32)


def in_moments_kernel(
    place, own, own_y, other, other_y, rows_old, vector, vector_far, ffn_sums, grad, rows_new,
    sums,
):
    def collect(low, high):
        for group in range(GROUPS):
            for which in range(3):
                rows = slice(144 * group + 48 * which, 144 * group + 48 * (which + 1))
                for side in range(2):
                    start = WIDTH * group + 128 * side
                    grad[which, :48, start : start + 128] = low[side][rows, :]
                    grad[which, 48:, start : start + 128] = high[side][rows, :]

    for core in range(2):
        for y in range(2):

            @pl.when((place[3] == core) & (place[2] == y))
            def _():
                mine = (own, own_y) if y == 0 else (own_y, own)
                far = (other, other_y) if y == 0 else (other_y, other)
                collect(mine if core == 0 else far, far if core == 0 else mine)

    totals = []
    for which in range(3):
        new, total, columns, divided = moments(grad[which], rows_old[which : which + 1, :])
        rows_new[which : which + 1, :] = new
        sums[which : which + 1, :] = columns
        sums[3 + which : 4 + which, :] = divided
        totals.append(total)
    sums[6:7, :] = lane_values(totals)
    sums[7:8, :] = jnp.zeros((1, D), F32)
    sums[8:24, :] = vector[...] + vector_far[...]
    sums[24:40, :] = ffn_sums[...]


def matrix_step(weight, grad, rows, cols, total, col_sums, divided, rows_full, rate):
    cols_new = DECAY * cols + (1.0 - DECAY) * col_sums * (1.0 / rows_full)
    mean = total * (1.0 / rows_full)
    square_sum = mean * jnp.sum(divided / cols_new, axis=1, keepdims=True)
    rms = jnp.sqrt(square_sum * (1.0 / (rows_full * grad.shape[1])))
    factor = to_column(lax.rsqrt(rows / mean)) * (rate / jnp.maximum(1.0, rms / clip_level))
    return cols_new, weight - grad * factor * lax.rsqrt(cols_new)


def finish_kernel(
    place, inward, up, down, out, in_grad, up_grad, down_grad, out_grad, in_rows, up_rows,
    down_rows, out_rows, in_cols, up_cols, down_cols, out_cols, sums, vectors, vector_state,
    in_cols_new, up_cols_new, down_cols_new, out_cols_new, in_next, up_next, down_next, out_next,
    vector_grad, state_next, vectors_next,
):
    base_rate = 0.3 * D ** (-0.5)
    for which in range(3):
        here = slice(which, which + 1)
        in_cols_new[here, :], in_next[which] = matrix_step(
            inward[which], in_grad[which], in_rows[here, :], in_cols[here, :],
            sums[6:7, which : which + 1], sums[here, :], sums[3 + which : 4 + which, :], D,
            base_rate,
        )

    def wide_row(first):
        return jnp.concatenate([sums[first + i : first + i + 1, :] for i in range(4)], axis=1)

    up_new, up_next[...] = matrix_step(
        up[...], up_grad[...], up_rows[...], up_cols[...], sums[36:37, 0:1], wide_row(24),
        wide_row(28), D, base_rate,
    )
    down_new, down_next[...] = matrix_step(
        down[...], down_grad[...], down_rows[...], down_cols[...], sums[36:37, 1:2],
        sums[32:33, :], sums[33:34, :], FF, 0.3 * FF ** (-0.5),
    )
    out_new, out_next[...] = matrix_step(
        out[...], out_grad[...], out_rows[...], out_cols[...], sums[36:37, 2:3],
        sums[34:35, :], sums[35:36, :], D, 1.2 * D ** (-0.5),
    )
    up_cols_new[...] = up_new.reshape(FF)
    down_cols_new[...] = down_new.reshape(D)
    out_cols_new[...] = out_new.reshape(D)
    g = sums[8:21, :]
    vector_grad[...] = g
    state = DECAY * vector_state[...] + (1.0 - DECAY) * (g * g + square_eps)
    state_next[...] = state
    update = g * lax.rsqrt(state)
    total = jnp.sum(jnp.sum(update * update, axis=0, keepdims=True), axis=1, keepdims=True)
    rms = jnp.sqrt(total * (1.0 / (13 * D)))
    vectors_next[...] = vectors[...] - update * (0.25 / jnp.maximum(1.0, rms / clip_level))


def shards(
    tokens, cotangent, lengths, projection, inward, outward, expand, shrink, vectors,
    inward_rows, inward_columns, outward_rows, outward_columns, expand_rows, expand_columns,
    shrink_rows, shrink_columns, vector_state,
):
    full = special()
    rows = outward.shape[0]
    wide = 8 if full else 1
    wide_at = lax.axis_index("wide").astype(jnp.int32)
    narrow_at = lax.axis_index("narrow").astype(jnp.int32)
    core = narrow_at % 2 if full else jnp.int32(0)
    place = jnp.stack([wide_at // 2, wide_at % 2, narrow_at // 2, core])
    per = FFC // wide
    cosine, sine, onehot, proj = tables(lengths, projection)
    if full:
        *own_in, own_first, own_rest = small_call(
            pick_kernel, "pick", place, [inward, outward, expand, shrink],
            [
                struct((2, 48, D), BF16), struct((1, 48, D), BF16), struct((528, WIDTH), BF16),
                struct((768, WIDTH), BF16),
            ],
        )
        in_z = [along_z(value) for value in own_in]
        *in_z, own_first, cosine, sine, onehot, proj = tie(
            *in_z, own_first, cosine, sine, onehot, proj
        )
        first_z = along_z(own_first)
        in_x = [over_x(value) for value in in_z]
        pieces_in = []
        *in_z, first_z = tie(*in_z, *in_x, first_z)
        for near, far in zip(in_z[:2], in_z[2:]):
            pieces_in += [near, far, over_core(near), over_core(far)]
        *pieces_in, first_z, own_rest = tie(*pieces_in, first_z, own_rest)
        first_x = over_x(first_z)
        rest_got = [over_z(own_rest, shift) for shift in (1, 2, 3)]
    else:
        in_low = lax.all_gather(inward.astype(BF16), "wide", axis=1, tiled=True)
        out_low = lax.all_gather(outward.astype(BF16), "wide", axis=0, tiled=True)
        up_low = lax.all_gather(expand.astype(BF16), "wide", axis=0, tiled=True)
        down_low = lax.all_gather(shrink.astype(BF16), "wide", axis=0, tiled=True)
        units = jnp.transpose(in_low.reshape(3, D, GROUPS, WIDTH), (2, 1, 0, 3))
        pieces_in = [units.reshape(1, 3 * D, D)]

        def blocks(matrix):
            count = matrix.shape[1] // WIDTH
            return jnp.transpose(matrix.reshape(-1, count, WIDTH), (1, 0, 2)).reshape(-1, WIDTH)

        ups = [blocks(up_low[:, FFC * j : FFC * (j + 1)]) for j in range(CHUNKS)]
        downs = [blocks(down_low[FFC * j : FFC * (j + 1)]) for j in range(CHUNKS)]
        half = D // 2
        pieces_first = [
            jnp.concatenate([blocks(out_low[:half]), ups[0], blocks(out_low[half:]), downs[0]])[
                None
            ]
        ]
        pieces_rest = [
            jnp.stack([jnp.concatenate([ups[j], downs[j]])[None] for j in range(1, CHUNKS)])
        ]
    perm = jnp.asarray(head_perm(), BF16)
    block_ones = np.kron(np.eye(2, dtype=np.float32), np.ones((64, 64), np.float32))
    ones = jnp.asarray(np.concatenate([block_ones, block_ones]), BF16)
    split = vectors[4:6].reshape(2, GROUPS, 4, 2, 32)
    bias_qk = jnp.transpose(split, (0, 1, 3, 2, 4)).reshape(2, GROUPS, WIDTH)
    bias = jnp.concatenate([bias_qk, vectors[6].reshape(1, GROUPS, WIDTH)])
    bias = jnp.transpose(bias, (1, 0, 2))
    bias_up = vectors[9:].reshape(wide, CHUNKS, per)
    bias_up = jnp.transpose(bias_up, (1, 0, 2)).reshape(CHUNKS, 1, FFC)
    attn, mixed, a1t, w_in, wq, wk, qf, kf, v, rden = attend(
        lengths, place, pieces_in, wide, tokens, vectors[:2], bias, perm, proj, cosine, sine,
        onehot,
    )
    if full:
        attn, first_x, *rest_got = tie(attn, first_x, *rest_got)
        rest_z = jnp.stack([own_rest] + rest_got)
        first_cores = [over_core(first_z), over_core(first_x)]
        *first_cores, rest_z = tie(*first_cores, rest_z)
        pieces_first = [first_z, first_x] + first_cores
        rest_x = over_x(rest_z)
    x1, a2, a2t, dyt, y, back, w_out, keep0, send0, dbias0 = middle_first(
        place, wide, pieces_first, tokens, attn, cotangent, vectors, bias_up
    )
    if full:
        rest_core = over_core(rest_z)
        rest_x, rest_core, send0, y = tie(rest_x, rest_core, send0, y)
        pieces_rest = [rest_z, rest_x, rest_core, over_core(rest_x)]
        got0 = over_core(send0)
    (
        block_out, dx1, dmixed, okeep, osend, middle_vec, keep12, send12, dbias12,
    ) = middle_rest(
        place, wide, pieces_rest, cotangent, (a2, a2t, dyt), bias_up, attn, w_out, vectors,
        (y, back, x1),
    )
    if full:
        got0, send12, osend = tie(got0, send12, osend)
        got12 = over_core(send12)
        send_b, keep_b = first_sum(place, [(keep0, got0), (keep12, got12)])
        e_parts = first_sum_z(place, [(keep12, got12), (okeep, over_core(osend))])
        dmixed, send_b, keep_b, *e_parts = tie(dmixed, send_b, keep_b, *e_parts)
        got_b = over_x(send_b)
        e_got = [over_z(e_parts[shift], shift) for shift in (1, 2, 3)]
    saved = (mixed, rden, wq, wk, qf, kf, v)
    in_keep, in_send, in_bias, da1 = attend_back(
        lengths, place, wide, dmixed, saved, a1t, w_in, perm, proj, cosine, sine, onehot, ones
    )
    if full:
        b_parts = list(second_sum(place, keep_b, got_b))
        in_send, da1, *e_got, b_parts[1] = tie(in_send, da1, *e_got, b_parts[1])
        keep_e, send_e = split_sum(place, [e_parts[0]] + e_got)
        send_e, in_send = tie(send_e, in_send)
        got_e = over_x(send_e)
        got_in = over_core(in_send)
        send_c, keep_c = held_call(
            first_sum_y_kernel, "first_sum_y", place, [in_keep, got_in],
            [struct((8, 432, 128), BF16)] * 2,
        )
        da1, send_c = tie(da1, send_c)
        got_c = over_y(send_c)
    input_grad, vector_local = input_side(
        wide, tokens, dx1, da1, vectors, middle_vec, in_bias, dbias0, dbias12
    )
    if full:
        def pair_sum(mine, got):
            half_sum = mine.astype(F32) + got.astype(F32)
            return half_sum, over_core(half_sum)

        got_c, input_grad, vector_local = tie(got_c, input_grad, vector_local)
        send_c, keep_c = held_call(
            split_x_kernel, "split_x", place, [keep_c, got_c], [struct((4, 432, 128), BF16)] * 2
        )
        send_c, b_parts[0] = tie(send_c, b_parts[0])
        got_c = over_x(send_c)
        ffn_mine = z_sum(place, b_parts, (keep_e, got_e))
        ffn_mine, got_c = tie(ffn_mine, got_c)
        c_parts = second_sum(place, keep_c, got_c)
        ffn_mine, *c_parts = tie(ffn_mine, *c_parts)
        ffn_y = over_y(ffn_mine)
        c_mine = z_sum(place, c_parts)
        c_mine, vector_local = tie(c_mine, vector_local)
        c_y = over_y(c_mine)
        c_y, vector_y = tie(c_y, over_y(vector_local))
        vector_pair = vector_local + vector_y
        c_core = over_core(c_mine)
        ffn_y, c_mine = tie(ffn_y, c_mine)
        ffn_own, ffn_got = pair_sum(ffn_mine, ffn_y)
        expand_grad, shrink_grad, outward_grad, up_rows, down_rows, out_rows, sums = held_call(
            ffn_moments_kernel, "ffn_moments", place,
            [
                ffn_own, ffn_got, expand_rows[None], shrink_rows[None], outward_rows[None],
            ],
            [
                struct(expand.shape, F32), struct(shrink.shape, F32), struct(outward.shape, F32),
                struct((1, 96), F32), struct((1, 384), F32), struct((1, 96), F32),
                struct((16, D), F32),
            ],
            0,
        )
        c_y, sums = tie(c_y, sums)
        inward_grad, in_rows, sums = held_call(
            in_moments_kernel, "in_moments", place,
            [
                c_mine, c_y, c_core, over_core(c_y), inward_rows, vector_pair,
                over_core(vector_pair), sums,
            ],
            [struct(inward.shape, F32), struct((3, 96), F32), struct((40, D), F32)],
            0,
        )
        sums = sum_wide(sums)
        (
            in_cols, up_cols, down_cols, out_cols, inward_next, expand_next, shrink_next,
            outward_next, vector_grad, vector_state_next, vectors_next,
        ) = small_call(
            finish_kernel, "finish", place,
            [
                inward, expand, shrink, outward, inward_grad, expand_grad, shrink_grad,
                outward_grad, in_rows, up_rows, down_rows, out_rows, inward_columns,
                expand_columns[None], shrink_columns[None], outward_columns[None], sums, vectors,
                vector_state,
            ],
            [
                struct((3, D), F32), struct((FF,), F32), struct((D,), F32),
                struct((D,), F32), struct(inward.shape, F32), struct(expand.shape, F32),
                struct(shrink.shape, F32), struct(outward.shape, F32), struct((13, D), F32),
                struct((13, D), F32), struct((13, D), F32),
            ],
        )
        return (
            block_out, input_grad, inward_grad, outward_grad, expand_grad, shrink_grad,
            vector_grad, in_rows, in_cols, out_rows[0], out_cols, up_rows[0], up_cols,
            down_rows[0], down_cols, vector_state_next, inward_next, outward_next,
            expand_next, shrink_next, vectors_next,
        )
    vector_part = sum_narrow(vector_local[:13])

    def reduced(values, axis):
        part = lax.psum_scatter(values, "wide", scatter_dimension=axis, tiled=True)
        return lax.psum(part.astype(F32), "narrow")

    keeps = [keep0, keep12[0], keep12[1]]
    sends = [send0, send12[0], send12[1]]
    up_grads = [
        jnp.transpose(keep.reshape(4, D, WIDTH), (1, 0, 2)).reshape(D, FFC) for keep in keeps
    ]
    down_grads = [
        jnp.transpose(send.reshape(4, D, WIDTH), (0, 2, 1)).reshape(FFC, D) for send in sends
    ]
    expand_grad = reduced(jnp.concatenate(up_grads, axis=1), 0)
    shrink_grad = reduced(jnp.concatenate(down_grads, axis=0), 0)

    def rebuilt(keep, send):
        return jnp.concatenate(
            [keep.reshape(-1, 3, D // 2, WIDTH), send.reshape(-1, 3, D // 2, WIDTH)], axis=2
        )

    outward_grad = reduced(jnp.transpose(rebuilt(okeep, osend)[0], (1, 0, 2)).reshape(D, D), 0)
    in_units = rebuilt(in_keep, in_send)
    inward_grad = reduced(jnp.transpose(in_units, (1, 2, 0, 3)).reshape(3, D, D), 1)
    decay = 1.0 - STEP ** (-0.8)
    wide_count = lax.axis_size("wide")
    grads_list = [inward_grad, outward_grad[None], expand_grad[None], shrink_grad[None]]
    rows_old = [inward_rows, outward_rows[None], expand_rows[None], shrink_rows[None]]
    columns_old = [
        inward_columns,
        outward_columns[None],
        expand_columns[None],
        shrink_columns[None],
    ]
    weights_old = [inward, outward[None], expand[None], shrink[None]]
    rates = [0.3 * D ** (-0.5), 1.2 * D ** (-0.5), 0.3 * D ** (-0.5), 0.3 * FF ** (-0.5)]
    bounds = [0, 3, 4, 5, 6]
    rows_next = []
    column_parts = []
    for member in range(4):
        squares = grads_list[member] * grads_list[member] + square_eps
        rows_next.append(decay * rows_old[member] + (1.0 - decay) * jnp.mean(squares, axis=-1))
        column_parts.append(jnp.sum(squares, axis=-2))
    row_totals = jnp.concatenate([jnp.sum(entry, axis=-1) for entry in rows_next])
    shapes = [part.shape for part in column_parts] + [row_totals.shape, vector_part.shape]
    flat = jnp.concatenate(
        [part.reshape(-1) for part in column_parts + [row_totals, vector_part]]
    )
    flat = jnp.pad(flat, (0, -flat.shape[0] % 1024)).reshape(-1, 128)
    flat = sum_wide(flat).reshape(-1)
    summed = []
    offset = 0
    for shape in shapes:
        size = 1
        for extent in shape:
            size *= extent
        summed.append(flat[offset : offset + size].reshape(shape))
        offset += size
    column_sums = list(summed[0:4])
    totals_sum = summed[4]
    vector_grad = summed[5]
    columns_next = []
    scaled_list = []
    row_means = []
    sizes_full = []
    for member in range(4):
        grad_now = grads_list[member]
        rows_full = grad_now.shape[-2] * wide_count
        sizes_full.append(rows_full * grad_now.shape[-1])
        columns_next.append(
            decay * columns_old[member] + (1.0 - decay) * column_sums[member] / rows_full
        )
        row_mean = totals_sum[bounds[member] : bounds[member + 1]] / rows_full
        row_means.append(row_mean)
        scaled_list.append(
            grad_now
            * lax.rsqrt(rows_next[member] / row_mean[:, None])[..., None]
            * lax.rsqrt(columns_next[member])[:, None, :]
        )
    partial_squares = jnp.concatenate(
        [jnp.sum(entry * entry, axis=(-2, -1)) for entry in scaled_list]
    )
    total_squares = sum_wide(jnp.pad(partial_squares, (0, 122)).reshape(1, 128))[0, :6]
    rms_list = [
        jnp.sqrt(total_squares[bounds[member] : bounds[member + 1]] / sizes_full[member])
        for member in range(4)
    ]
    weights_next = []
    for member in range(4):
        limiter = jnp.maximum(1.0, rms_list[member] / clip_level)
        weights_next.append(
            weights_old[member] - rates[member] * scaled_list[member] / limiter[:, None, None]
        )
    vector_state_next = decay * vector_state + (1.0 - decay) * (
        vector_grad * vector_grad + square_eps
    )
    vector_update = vector_grad * lax.rsqrt(vector_state_next)
    vector_rms = jnp.sqrt(jnp.mean(vector_update * vector_update))
    vectors_next = vectors - 0.25 * vector_update / jnp.maximum(1.0, vector_rms / clip_level)
    return (
        block_out,
        input_grad,
        inward_grad,
        outward_grad,
        expand_grad,
        shrink_grad,
        vector_grad,
        rows_next[0],
        columns_next[0],
        rows_next[1][0],
        columns_next[1][0],
        rows_next[2][0],
        columns_next[2][0],
        rows_next[3][0],
        columns_next[3][0],
        vector_state_next,
        weights_next[0],
        weights_next[1][0],
        weights_next[2][0],
        weights_next[3][0],
        vectors_next,
    )


def solution(mesh):
    placed = (
        P(("narrow", "wide"), None),
        P(("narrow", "wide"), None),
        P(("narrow", "wide"), None),
        P(),
        P(None, "wide", None),
        P("wide", None),
        P("wide", None),
        P("wide", None),
        P(),
        P(None, "wide"),
        P(),
        P("wide"),
        P(),
        P("wide"),
        P(),
        P("wide"),
        P(),
        P(),
    )
    return jax.shard_map(
        shards,
        mesh=mesh,
        in_specs=placed,
        out_specs=(
            P(("narrow", "wide"), None),
            P(("narrow", "wide"), None),
            P(None, "wide", None),
            P("wide", None),
            P("wide", None),
            P("wide", None),
            P(),
            P(None, "wide"),
            P(),
            P("wide"),
            P(),
            P("wide"),
            P(),
            P("wide"),
            P(),
            P(),
            P(None, "wide", None),
            P("wide", None),
            P("wide", None),
            P("wide", None),
            P(),
        ),
        check_vma=False,
    )
```

```python
import functools
import math

import jax
import jax.numpy as jnp
import numpy as np
from jax import lax
from jax.experimental import pallas as pl
from jax.experimental.pallas import tpu as pltpu
from jax.sharding import PartitionSpec as P

D = 768
HEADS = 12
HD = 64
FF = 3072
FEAT = 32
STEP = 10
LEN = 1024
SPAN = 256
CHUNKS = 3
GROUPS = 3
WIDTH = 256
FFC = FF // CHUNKS

norm_eps = 1e-05
square_eps = 1e-30
clip_level = 1.0

F32 = jnp.float32
BF16 = jnp.bfloat16
VMEM_LIMIT = 60 * 1024 * 1024
REST_LIMIT = 54 * 1024 * 1024
BACK_LIMIT = 46 * 1024 * 1024


def mm(left, right):
    return lax.dot_general(left, right, (((1,), (0,)), ((), ())), preferred_element_type=F32)


def mm_nt(left, right):
    return lax.dot_general(left, right, (((1,), (1,)), ((), ())), preferred_element_type=F32)


def mm_tn(left, right):
    return lax.dot_general(left, right, (((0,), (0,)), ((), ())), preferred_element_type=F32)


def halves(values):
    high = values.astype(BF16)
    return high, (values - high.astype(F32)).astype(BF16)


TAIL = (
    0.1795078068971634,
    0.17978088557720184,
    0.14234966039657593,
    0.06379217654466629,
    0.0434231162071228,
    -0.261725515127182,
    0.20454804599285126,
    -0.05167665705084801,
)


def normal_parts(values):
    size = jnp.abs(values)
    t = 1.0 / (1.0 + 0.45 * size)
    poly = TAIL[-1]
    for coeff in TAIL[-2::-1]:
        poly = poly * t + coeff
    bell = jnp.exp(-0.5 * values * values)
    tail = poly * t * bell
    return jnp.where(values >= 0, 1.0 - tail, tail), bell * 0.3989422804014327


def transposed(values):
    row = lax.broadcasted_iota(jnp.int32, (256, 256), 0)
    col = lax.broadcasted_iota(jnp.int32, (256, 256), 1)
    eye = (row == col).astype(F32).astype(BF16)
    return mm_nt(eye, values).astype(BF16)


def head_perm():
    perm = np.zeros((WIDTH, WIDTH), np.float32)
    for head in range(4):
        for half in range(2):
            for i in range(32):
                perm[head * 64 + half * 32 + i, half * 128 + head * 32 + i] = 1.0
    return perm


def make_blocks(lengths, base, first, last):
    def step(s, carry):
        count, begin, begin_row, end = carry
        new_end = end + lengths[0, s]
        full = new_end - begin_row > SPAN

        @pl.when(full)
        def _():
            base[count] = begin_row
            first[count] = begin
            last[count] = s - 1

        row = jnp.minimum((end // 16) * 16, LEN - SPAN)
        return (
            jnp.where(full, count + 1, count),
            jnp.where(full, s, begin),
            jnp.where(full, row, begin_row),
            new_end,
        )

    segments = lengths.shape[1]
    zero = jnp.int32(0)
    count, begin, begin_row, _ = lax.fori_loop(0, segments, step, (zero, zero, zero, zero))
    base[count] = begin_row
    first[count] = begin
    last[count] = segments - 1
    return count + 1


def lane_mask(lo, hi, width, dtype):
    lane = lax.broadcasted_iota(jnp.int32, (1, width), 1)
    return ((lane >= lo) & (lane < hi)).astype(F32).astype(dtype)


def value_rows(v_pair, head):
    keep = lane_mask(64 * head, 64 * head + 64, 128, BF16)
    return jnp.concatenate([v_pair * keep, jnp.broadcast_to(keep, v_pair.shape)], axis=1)


def span_mask(onehot, rows, lo, hi):
    member = onehot[rows, :]
    lane = lax.broadcasted_iota(jnp.int32, (1, 128), 1)
    inside = ((lane >= lo) & (lane <= hi)).astype(F32).astype(BF16)
    return mm_nt(member * inside, member).astype(BF16)


def cost(flops, size):
    return pl.CostEstimate(flops=10**6, transcendentals=0, bytes_accessed=10**5)


def row_blocks(body, loop=False):
    if not loop:
        for rows in range(0, LEN, 256):
            body(pl.ds(rows, 256))
        return

    def step(index, carry):
        body(pl.ds(pl.multiple_of(index * 256, 256), 256))
        return carry

    lax.fori_loop(0, LEN // 256, step, 0)


def any_spec():
    return pl.BlockSpec(memory_space=pl.ANY)


def in_copies(place, pieces, dst, sems, unit):
    if len(pieces) == 1:
        rows = dst.shape[1] // 3
        here = pl.ds(unit * rows, rows)
        return [pltpu.make_async_copy(pieces[0].at[:, here], dst.at[:, here], sems.at[unit, 0])]
    z, x, core = place[0], place[1], place[3]
    part, index = (0, unit) if unit < 2 else (4, 0)
    copies = []
    for side in range(2):
        half = core if side == 0 else 1 - core
        for flip in range(2):
            column = x if flip == 0 else 1 - x
            for shift in range(4):
                row = lax.rem(z + 4 - shift, 4) * 2 + column
                start = pl.multiple_of(unit * 96 + half * 48, 16)
                copies.append(
                    pltpu.make_async_copy(
                        pieces[part + 2 * side + flip].at[shift, index],
                        dst.at[row, pl.ds(start, 48)],
                        sems.at[unit, len(copies)],
                    )
                )
    return copies


def flat_copies(place, pieces, dst, sems):
    if len(pieces) == 1:
        return [pltpu.make_async_copy(pieces[0], dst, sems.at[0])]
    z, x, core = place[0], place[1], place[3]
    span = dst.shape[1] // 2
    copies = []
    for side in range(2):
        half = core if side == 0 else 1 - core
        for flip in range(2):
            column = x if flip == 0 else 1 - x
            for shift in range(4):
                row = lax.rem(z + 4 - shift, 4) * 2 + column
                start = pl.multiple_of(half * span, 16)
                copies.append(
                    pltpu.make_async_copy(
                        pieces[2 * side + flip].at[shift],
                        dst.at[row, pl.ds(start, span)],
                        sems.at[len(copies)],
                    )
                )
    return copies


def attend_kernel(count_in, lengths, place, *refs):
    pieces = refs[:count_in]
    (
        x_ref, norm_ref, bias_ref, perm_ref, proj_ref, cos_ref, sin_ref, onehot_ref,
        attn_ref, mixed_ref, a1t_ref, w_ref, wq_ref, wk_ref, qf_ref, kf_ref, v_ref, rden_ref,
        a1, qb, kb, vb, parts, base, first, last, sems,
    ) = refs[count_in:]
    group = pl.program_id(0)

    @pl.when(group == 0)
    def _():
        for unit in range(GROUPS):
            for copy in in_copies(place, pieces, w_ref, sems, unit):
                copy.start()
        def norm_rows(here):
            x = x_ref[here, :].astype(F32)
            centre = x - jnp.mean(x, axis=-1, keepdims=True)
            spread = jnp.mean(centre * centre, axis=-1, keepdims=True)
            a1[here, :] = (
                centre * lax.rsqrt(spread + norm_eps) * norm_ref[0:1, :] + norm_ref[1:2, :]
            ).astype(BF16)

        row_blocks(norm_rows)
        for cols in range(0, D, 256):
            a1t_ref[cols : cols + 256, :] = transposed(a1[:, cols : cols + 256])

    for unit in range(GROUPS):

        @pl.when(group == unit)
        def _():
            for copy in in_copies(place, pieces, w_ref, sems, unit):
                copy.wait()

    count = make_blocks(lengths, base, first, last)
    shard = w_ref.shape[1] // 3
    here = pl.ds(pl.multiple_of(group * shard, 16), shard)
    w = w_ref[:, here, :].reshape(D, D)
    perm = perm_ref[...]
    bias = bias_ref[0]
    proj_both = proj_ref[0]
    proj_high = proj_ref[1, :, :128]
    square = proj_ref[2, :, :128]
    weights = [mm(w[:, WIDTH * i : WIDTH * (i + 1)], perm).astype(BF16) for i in range(2)]

    def feature_rows(here):
        for which, (out_w, out_f, low_f) in enumerate(
            ((wq_ref, qf_ref, qb), (wk_ref, kf_ref, kb))
        ):
            u = (mm(a1[here, :], weights[which]) + bias[which : which + 1, :]) * HD ** (-0.25)
            c = u[:, :128]
            e = u[:, 128:]
            cosine = cos_ref[here, :]
            sine = sin_ref[here, :]
            turned = jnp.concatenate([c * cosine - e * sine, e * cosine + c * sine], axis=1)
            out_w[0, here, :] = turned
            high, low = halves(turned)
            sq_high, sq_low = halves(turned * turned)
            both = mm(high, proj_both)
            logits = (
                both[:, :128] + both[:, 128:] + mm(low, proj_high)
                - (mm(sq_high, square) + mm(sq_low, square))
            )
            phi = jnp.exp(logits) * FEAT ** (-0.5)
            out_f[0, here, :] = phi
            low_f[here, :] = phi.astype(BF16)
        v = mm(a1[here, :], w[:, 2 * WIDTH :]) + bias[2:3, :]
        v_ref[0, here, :] = v
        vb[here, :] = v.astype(BF16)

    row_blocks(feature_rows)
    parts[...] = jnp.zeros_like(parts)

    def one_span(index, carry):
        rows = pl.ds(pl.multiple_of(base[index], 16), SPAN)
        mask = span_mask(onehot_ref, rows, first[index], last[index])
        q = qb[rows, :]
        k = kb[rows, :]
        for pair in range(2):
            v_pair = vb[rows, 128 * pair : 128 * (pair + 1)]
            total = jnp.zeros((SPAN, WIDTH), F32)
            for side in range(2):
                head = 2 * pair + side
                scores = mm_nt(q * lane_mask(32 * head, 32 * head + 32, 128, BF16), k)
                total = total + mm(scores.astype(BF16) * mask, value_rows(v_pair, side))
            parts[pair, rows, :] += total
        return carry

    lax.fori_loop(0, count, one_span, 0)
    for pair in range(2):
        lanes = slice(128 * pair, 128 * (pair + 1))
        inverse = 1.0 / parts[pair, :, 128:]
        rden_ref[0, :, lanes] = inverse
        mixed = parts[pair, :, :128] * inverse
        mixed_ref[0, :, lanes] = mixed
        attn_ref[:, lanes] = mixed.astype(BF16)


def whole_spec(shape, **options):
    return pl.BlockSpec(shape, lambda *_: (0,) * len(shape), **options)


def group_spec(shape):
    return pl.BlockSpec((1,) + shape, lambda g, *_: (g,) + (0,) * len(shape))


def attend(lengths, place, pieces, wide, tokens, norm, bias, perm, proj, cosine, sine, onehot):
    def out(shape, dtype):
        return jax.ShapeDtypeStruct((GROUPS,) + shape, dtype)

    rows_in = 3 * D // wide
    return pl.pallas_call(
        functools.partial(attend_kernel, len(pieces)),
        grid_spec=pltpu.PrefetchScalarGridSpec(
            num_scalar_prefetch=2,
            grid=(GROUPS,),
            in_specs=[any_spec()] * len(pieces)
            + [
                whole_spec((LEN, D)), whole_spec((2, D)), group_spec((3, WIDTH)),
                whole_spec((WIDTH, WIDTH)), whole_spec((3, WIDTH, WIDTH)), whole_spec((LEN, 128)),
                whole_spec((LEN, 128)), whole_spec((LEN, 128)),
            ],
            out_specs=[
                pl.BlockSpec((LEN, WIDTH), lambda g, *_: (0, g)), group_spec((LEN, WIDTH)),
                whole_spec((D, LEN)), whole_spec((wide, rows_in, D)), group_spec((LEN, WIDTH)),
                group_spec((LEN, WIDTH)), group_spec((LEN, 128)), group_spec((LEN, 128)),
                group_spec((LEN, WIDTH)), group_spec((LEN, WIDTH)),
            ],
            scratch_shapes=[
                pltpu.VMEM((LEN, D), BF16),
                pltpu.VMEM((LEN, 128), BF16), pltpu.VMEM((LEN, 128), BF16),
                pltpu.VMEM((LEN, WIDTH), BF16), pltpu.VMEM((2, LEN, WIDTH), F32),
                pltpu.SMEM((32,), jnp.int32), pltpu.SMEM((32,), jnp.int32),
                pltpu.SMEM((32,), jnp.int32), pltpu.SemaphoreType.DMA((GROUPS, 16)),
            ],
        ),
        out_shape=[
            jax.ShapeDtypeStruct((LEN, D), BF16), out((LEN, WIDTH), F32),
            jax.ShapeDtypeStruct((D, LEN), BF16), jax.ShapeDtypeStruct((wide, rows_in, D), BF16),
            out((LEN, WIDTH), F32), out((LEN, WIDTH), F32), out((LEN, 128), F32),
            out((LEN, 128), F32), out((LEN, WIDTH), F32), out((LEN, WIDTH), F32),
        ],
        compiler_params=pltpu.CompilerParams(
            dimension_semantics=("arbitrary",), vmem_limit_bytes=VMEM_LIMIT
        ),
        cost_estimate=cost(20 * 10**9, 40 * 10**6),
        name="attend",
    )(lengths, place, *pieces, tokens, norm, bias, perm, proj, cosine, sine, onehot)


def attend_back_kernel(
    lengths, place, dmixed_ref, mixed_ref, rden_ref, wq_ref, wk_ref, qf_ref, kf_ref, v_ref,
    a1t_ref, w_ref, perm_ref, proj_ref, cos_ref, sin_ref, onehot_ref, ones_ref,
    keep_ref, send_ref, bias_ref, da1_ref,
    qb, kb, dnb, dnh, lift, dqf, dkf, dv, dqkv, base, first, last,
):
    count = make_blocks(lengths, base, first, last)
    qb[...] = qf_ref[0].astype(BF16)
    kb[...] = kf_ref[0].astype(BF16)
    lane = lax.broadcasted_iota(jnp.int32, (1, 128), 1)
    ones = ones_ref[...]
    def lift_rows(here):
        for pair in range(2):
            lanes = slice(128 * pair, 128 * (pair + 1))
            dnum = dmixed_ref[here, lanes] * rden_ref[0, here, lanes]
            high, low = halves(dnum)
            dnb[here, lanes] = high
            part_high, part_low = halves(dnum * mixed_ref[0, here, lanes])
            dden = -mm(jnp.concatenate([part_high, part_low], axis=1), ones)
            den_high, den_low = halves(dden)
            high, low = high.astype(F32), low.astype(F32)
            den_high = pltpu.roll(den_high.astype(F32), 64, 1)
            den_low = pltpu.roll(den_low.astype(F32), 64, 1)
            low_far = pltpu.roll(low, 64, 1)
            v = v_ref[0, here, lanes]
            v_high, v_low = halves(v)
            v_high, v_low = v_high.astype(F32), v_low.astype(F32)
            v_far = pltpu.roll(v_high, 64, 1)
            for side in range(2):
                own = (lane >= 64 * side) & (lane < 64 * side + 64)
                mark = 64 - 64 * side
                rest = jnp.where(lane == mark, den_high, jnp.where(lane == mark + 1, den_low, 0.0))
                both = ((lane == mark) | (lane == mark + 1)).astype(F32)
                head = 2 * pair + side
                dnh[head, here, :128] = jnp.where(own, high, low_far).astype(BF16)
                dnh[head, here, 128:] = jnp.where(own, high, rest).astype(BF16)
                lift[head, here, :128] = jnp.where(own, v_high, v_far).astype(BF16)
                lift[head, here, 128:] = jnp.where(own, v_low, both).astype(BF16)
    row_blocks(lift_rows)
    dqf[...] = jnp.zeros_like(dqf)
    dkf[...] = jnp.zeros_like(dkf)
    dv[...] = jnp.zeros_like(dv)

    def one_span(index, carry):
        rows = pl.ds(pl.multiple_of(base[index], 16), SPAN)
        mask = span_mask(onehot_ref, rows, first[index], last[index])
        q = qb[rows, :]
        k = kb[rows, :]
        q_total = jnp.zeros((SPAN, 128), F32)
        k_total = jnp.zeros((SPAN, 128), F32)
        for pair in range(2):
            lanes = slice(128 * pair, 128 * (pair + 1))
            dn_pair = dnb[rows, lanes]
            v_total = jnp.zeros((SPAN, 128), F32)
            for side in range(2):
                head = 2 * pair + side
                feats = lane_mask(32 * head, 32 * head + 32, 128, BF16)
                q_head = q * feats
                k_head = k * feats
                lifted = lift[head, rows, :]
                dn_head = dnh[head, rows, :]
                scores = mm_nt(k, q_head).astype(BF16) * mask
                dscores = mm_nt(dn_head, lifted).astype(BF16) * mask
                dscores_t = mm_nt(lifted, dn_head).astype(BF16) * mask
                q_total = q_total + mm(dscores, k_head)
                k_total = k_total + mm(dscores_t, q_head)
                own = lane_mask(64 * side, 64 * side + 64, 128, BF16)
                v_total = v_total + mm(scores, dn_pair * own)
            dv[rows, lanes] += v_total
        dqf[rows, :] += q_total
        dkf[rows, :] += k_total
        return carry

    lax.fori_loop(0, count, one_span, 0)
    proj_low = proj_ref[0, :, 128:]
    proj_high = proj_ref[1]
    square = proj_ref[2]
    perm = perm_ref[...]
    def feature_rows(here):
        for which, (w_in, phi_in, dphi) in enumerate(
            ((wq_ref, qf_ref, dqf), (wk_ref, kf_ref, dkf))
        ):
            r = dphi[here, :] * phi_in[0, here, :]
            high, low = halves(r)
            both = jnp.concatenate([high, low], axis=1)
            spread = mm_nt(both, square)
            dw = mm_nt(both, proj_high) + mm_nt(high, proj_low)
            du = (dw - 2.0 * w_in[0, here, :] * spread) * HD ** (-0.25)
            c = du[:, :128]
            e = du[:, 128:]
            cosine = cos_ref[here, :]
            sine = sin_ref[here, :]
            turned = jnp.concatenate([c * cosine + e * sine, e * cosine - c * sine], axis=1)
            dqkv[here, WIDTH * which : WIDTH * (which + 1)] = mm_nt(
                turned.astype(BF16), perm
            ).astype(BF16)

    row_blocks(feature_rows)
    dqkv[:, 2 * WIDTH :] = dv[...].astype(BF16)
    bias_ref[0] = jnp.sum(dqkv[...].astype(F32), axis=0, keepdims=True)
    grad = mm(a1t_ref[...], dqkv[...]).astype(BF16)
    at = pl.program_id(0)
    store_halves(grad, place[3], keep_ref.at[at], send_ref.at[at])
    w = w_ref[...].reshape(D, D)
    fresh = pl.program_id(0) == 0

    @pl.when(fresh)
    def _():
        da1_ref[...] = mm_nt(dqkv[...], w)

    @pl.when(jnp.logical_not(fresh))
    def _():
        da1_ref[...] += mm_nt(dqkv[...], w)


def store_halves(grad, core, keep_ref, send_ref):
    wide, rows = keep_ref.shape[0], D // keep_ref.shape[0]
    half = rows // 2
    parts = grad.reshape(wide, rows, D)
    for cols in range(3):
        block = parts[:, :, WIDTH * cols : WIDTH * (cols + 1)]
        here = pl.ds(half * cols, half)

        @pl.when(core == 0)
        def _():
            keep_ref[:, here, :] = block[:, :half]
            send_ref[:, here, :] = block[:, half:]

        @pl.when(core == 1)
        def _():
            keep_ref[:, here, :] = block[:, half:]
            send_ref[:, here, :] = block[:, :half]


def attend_back(
    lengths, place, wide, dmixed, saved, a1t, w_in, perm, proj, cosine, sine, onehot, ones
):
    mixed, rden, wq, wk, qf, kf, v = saved

    def by_group(shape):
        return pl.BlockSpec((1,) + shape, lambda g, *_: (g,) + (0,) * len(shape))

    rows_in = D // wide
    half = struct((GROUPS, wide, 3 * rows_in // 2, WIDTH), BF16)
    half_spec = once(half.shape)
    if wide > 1:
        half = pltpu.VMEM(half.shape, BF16)
        half_spec = pl.BlockSpec(memory_space=pltpu.VMEM)
    return pl.pallas_call(
        attend_back_kernel,
        grid_spec=pltpu.PrefetchScalarGridSpec(
            num_scalar_prefetch=2,
            grid=(GROUPS,),
            in_specs=[
                pl.BlockSpec((LEN, WIDTH), lambda g, *_: (0, g)),
                by_group((LEN, WIDTH)), by_group((LEN, WIDTH)), by_group((LEN, WIDTH)),
                by_group((LEN, WIDTH)), by_group((LEN, 128)), by_group((LEN, 128)),
                by_group((LEN, WIDTH)), once((D, LEN)),
                pl.BlockSpec((wide, rows_in, D), lambda g, *_: (0, g, 0)),
                once((WIDTH, WIDTH)), once((3, WIDTH, WIDTH)), once((LEN, 128)),
                once((LEN, 128)), once((LEN, 128)), once((WIDTH, 128)),
            ],
            out_specs=[
                half_spec, half_spec, group_spec((1, D)),
                whole_spec((LEN, D)),
            ],
            scratch_shapes=[
                pltpu.VMEM((LEN, 128), BF16), pltpu.VMEM((LEN, 128), BF16),
                pltpu.VMEM((LEN, WIDTH), BF16), pltpu.VMEM((4, LEN, WIDTH), BF16),
                pltpu.VMEM((4, LEN, WIDTH), BF16), pltpu.VMEM((LEN, 128), F32),
                pltpu.VMEM((LEN, 128), F32), pltpu.VMEM((LEN, WIDTH), F32),
                pltpu.VMEM((LEN, D), BF16),
                pltpu.SMEM((32,), jnp.int32), pltpu.SMEM((32,), jnp.int32),
                pltpu.SMEM((32,), jnp.int32),
            ],
        ),
        out_shape=[
            half, half, struct((GROUPS, 1, D), F32), struct((LEN, D), F32),
        ],
        compiler_params=pltpu.CompilerParams(
            dimension_semantics=("arbitrary",), vmem_limit_bytes=BACK_LIMIT
        ),
        cost_estimate=cost(GROUPS * 12 * 10**9, GROUPS * 20 * 10**6),
        name="attend_back",
    )(
        lengths, place, dmixed, mixed, rden, wq, wk, qf, kf, v, a1t, w_in, perm, proj, cosine,
        sine, onehot, ones,
    )


def chunk_step(
    place, wide, bias_up, dy_ref, a2, a2t, dyt, up, down, act, dhidden, y, back, outs, dbias_ref,
    fresh,
):
    rows_up = D // wide
    rows_down = FFC // wide
    dbias_ref[0] = jnp.zeros((1, FFC), F32)

    def chunk_rows(here):
        hidden = mm(a2[here, :], up[...]) + bias_up
        below, density = normal_parts(hidden)
        act_now = (hidden * below).astype(BF16)
        act[here, :] = act_now
        dact = mm_nt(dy_ref[here, :], down[...])
        dhidden_now = (dact * (below + hidden * density)).astype(BF16)
        dhidden[here, :] = dhidden_now
        dbias_ref[0] += jnp.sum(dhidden_now.astype(F32), axis=0, keepdims=True)
        if fresh:
            y[here, :] = mm(act_now, down[...])
            back[here, :] = mm_nt(dhidden_now, up[...])
        else:
            y[here, :] += mm(act_now, down[...])
            back[here, :] += mm_nt(dhidden_now, up[...])

    row_blocks(chunk_rows, True)
    grad_up = mm(a2t[...], dhidden[...]).astype(BF16).reshape(wide, rows_up, FFC)
    grad_down = mm(dyt[...], act[...]).astype(BF16)
    core = place[3]

    def store_up(ref):
        for cols in range(4):
            ref[:, rows_up * cols : rows_up * (cols + 1), :] = grad_up[
                :, :, WIDTH * cols : WIDTH * (cols + 1)
            ]

    def store_down(ref):
        if wide == 1:
            for cols in range(4):
                ref[0, D * cols : D * (cols + 1), :] = grad_down[
                    :, WIDTH * cols : WIDTH * (cols + 1)
                ]
            return
        for shard in range(wide):
            block = grad_down[:, rows_down * shard : rows_down * (shard + 1)]
            ref[shard, :, :128] = block[: D // 2]
            ref[shard, :, 128:] = block[D // 2 :]

    for when, keep_ref, send_ref in outs:
        for side in range(2):
            now = core == side

            @pl.when(now if when is None else now & when)
            def _():
                store_up(keep_ref if side == 0 else send_ref)
                store_down(send_ref if side == 0 else keep_ref)


def load_up(flat, at, up, wide):
    rows = D // wide
    for cols in range(4):
        here = pl.ds(at + rows * cols, rows)
        up[:, WIDTH * cols : WIDTH * (cols + 1)] = flat[:, here, :].reshape(D, WIDTH)


def load_down(flat, at, down, wide):
    rows = FFC // wide
    for cols in range(3):
        here = pl.ds(at + rows * cols, rows)
        down[:, WIDTH * cols : WIDTH * (cols + 1)] = flat[:, here, :].reshape(FFC, WIDTH)


def middle_first_kernel(wide, count_in, place, *refs):
    pieces = refs[:count_in]
    (
        x_ref, attn_ref, dy_ref, rows_ref, bias_up_ref,
        x1_ref, a2_ref, a2t_ref, dyt_ref, y_ref, back_ref, out_ref, keep_ref, send_ref, dbias_ref,
        flat, up, down, act, dhidden, sems,
    ) = refs[count_in:]
    copies = flat_copies(place, pieces, flat, sems)
    for copy in copies:
        copy.start()
    for cols in range(0, D, 256):
        dyt_ref[cols : cols + 256, :] = transposed(dy_ref[:, cols : cols + 256])
    for copy in copies:
        copy.wait()
    half_out = D // wide // 2
    half_flat = flat.shape[1] // 2
    for cols in range(3):
        upper = flat[:, half_out * cols : half_out * (cols + 1), :]
        lower = flat[:, half_flat + half_out * cols : half_flat + half_out * (cols + 1), :]
        out_ref[:, WIDTH * cols : WIDTH * (cols + 1)] = jnp.concatenate(
            [upper, lower], axis=1
        ).reshape(D, WIDTH)
    def norm_rows(here):
        x1 = x_ref[here, :].astype(F32) + (mm(attn_ref[here, :], out_ref[...]) + rows_ref[7:8, :])
        x1_ref[here, :] = x1
        centre = x1 - jnp.mean(x1, axis=-1, keepdims=True)
        spread = jnp.mean(centre * centre, axis=-1, keepdims=True)
        a2_ref[here, :] = (
            centre * lax.rsqrt(spread + norm_eps) * rows_ref[2:3, :] + rows_ref[3:4, :]
        ).astype(BF16)

    row_blocks(norm_rows)
    for cols in range(0, D, 256):
        a2t_ref[cols : cols + 256, :] = transposed(a2_ref[:, cols : cols + 256])
    load_up(flat, 3 * half_out, up, wide)
    load_down(flat, half_flat + 3 * half_out, down, wide)
    chunk_step(
        place, wide, bias_up_ref[0], dy_ref, a2_ref, a2t_ref, dyt_ref, up, down, act, dhidden,
        y_ref, back_ref, [(None, keep_ref, send_ref)], dbias_ref, True,
    )


def middle_rest_kernel(wide, count_in, place, *refs):
    pieces = refs[:count_in]
    (
        dy_ref, a2_ref, a2t_ref, dyt_ref, bias_up_ref, attn_ref, out_ref, rows_ref,
        y_in, back_in, x1_in,
        block_ref, dx1_ref, dmixed_ref, okeep_ref, osend_ref, vec_ref,
        keep_ref, send_ref, dbias_ref,
        flat, up, down, act, dhidden, back, dbranch, sems, flat_sems,
    ) = refs[count_in:]
    step = pl.program_id(0)
    y_copy = pltpu.make_async_copy(y_in, block_ref, sems.at[0])
    back_copy = pltpu.make_async_copy(back_in, back, sems.at[1])
    x1_copy = pltpu.make_async_copy(x1_in, dx1_ref, sems.at[2])

    def chunk_copies(chunk, side):
        if count_in == 1:
            return [
                pltpu.make_async_copy(
                    pieces[0].at[chunk], flat.at[chunk], flat_sems.at[chunk, 0]
                )
            ]
        copies = []
        for flip in range(2):
            column = place[1] if flip == 0 else 1 - place[1]
            for shift in range(4):
                shard = lax.rem(place[0] + 4 - shift, 4) * 2 + column
                copies.append(
                    pltpu.make_async_copy(
                        pieces[2 * side + flip].at[shift], flat.at[chunk, shard],
                        flat_sems.at[chunk, len(copies)],
                    )
                )
        return copies

    def fetch(chunk):
        for side in range(2):

            @pl.when((place[3] == chunk) if side == 0 else (place[3] != chunk))
            def _():
                if side == 0 or count_in > 1:
                    for copy in chunk_copies(chunk, side):
                        copy.start()

    def arrived(chunk):
        for copy in chunk_copies(chunk, 0):
            copy.wait()

    @pl.when(step == 0)
    def _():
        if count_in == 1:
            for chunk in range(2):
                for copy in chunk_copies(chunk, 0):
                    copy.start()
        else:
            fetch(0)
        y_copy.start()
        back_copy.start()
        if count_in > 1:
            fetch(1)
        x1_copy.start()
        arrived(0)
        y_copy.wait()
        back_copy.wait()

    @pl.when(step == 1)
    def _():
        arrived(1)

    load_up(flat.at[step], 0, up, wide)
    load_down(flat.at[step], 4 * (D // wide), down, wide)
    chunk_step(
        place, wide, bias_up_ref[0], dy_ref, a2_ref, a2t_ref, dyt_ref, up, down, act, dhidden,
        block_ref, back, [(None, keep_ref.at[step], send_ref.at[step])], dbias_ref, False,
    )

    @pl.when(step == 1)
    def _():
        x1_copy.wait()
        vec_ref[...] = jnp.zeros_like(vec_ref)

        def last_rows(here):
            x1 = dx1_ref[here, :]
            block_ref[here, :] = x1 + (block_ref[here, :] + rows_ref[8:9, :])
            dn = back[here, :]
            dy = dy_ref[here, :].astype(F32)
            centre = x1 - jnp.mean(x1, axis=-1, keepdims=True)
            spread = jnp.mean(centre * centre, axis=-1, keepdims=True)
            scale = lax.rsqrt(spread + norm_eps)
            zh = centre * scale
            vec_ref[0:1, :] += jnp.sum(dn * zh, axis=0, keepdims=True)
            vec_ref[1:2, :] += jnp.sum(dn, axis=0, keepdims=True)
            e = dn * rows_ref[2:3, :]
            dz = (
                e
                - jnp.mean(e, axis=-1, keepdims=True)
                - zh * jnp.mean(e * zh, axis=-1, keepdims=True)
            ) * scale
            dx1 = dy + dz
            dx1_ref[here, :] = dx1
            low = dx1.astype(BF16)
            dbranch[here, :] = low
            vec_ref[2:3, :] += jnp.sum(low.astype(F32), axis=0, keepdims=True)
            vec_ref[3:4, :] += jnp.sum(dy, axis=0, keepdims=True)
            dmixed_ref[here, :] = mm_nt(low, out_ref[...])

        row_blocks(last_rows, True)
        for cols in range(0, D, 256):
            up[cols : cols + 256, :] = transposed(attn_ref[:, cols : cols + 256])
        store_halves(mm(up[...], dbranch[...]).astype(BF16), place[3], okeep_ref, osend_ref)


def once(shape):
    return whole_spec(shape, pipeline_mode=pl.Buffered(1))


def struct(shape, dtype):
    return jax.ShapeDtypeStruct(shape, dtype)


def weight_scratch():
    return [
        pltpu.VMEM((D, FFC), BF16), pltpu.VMEM((FFC, D), BF16), pltpu.VMEM((LEN, FFC), BF16),
        pltpu.VMEM((LEN, FFC), BF16),
    ]


def middle_first(place, wide, pieces, tokens, attn, cotangent, vectors, bias_up):
    rows_flat = 3 * D // wide + 2 * FFC * D // (WIDTH * wide)
    half = (wide, FFC * D // (WIDTH * wide), WIDTH)
    outs = [
        struct((LEN, D), F32), struct((LEN, D), BF16), struct((D, LEN), BF16),
        struct((D, LEN), BF16), struct((LEN, D), F32), struct((LEN, D), F32),
        struct((D, D), BF16), struct(half, BF16), struct(half, BF16), struct((1, 1, FFC), F32),
    ]
    return pl.pallas_call(
        functools.partial(middle_first_kernel, wide, len(pieces)),
        grid_spec=pltpu.PrefetchScalarGridSpec(
            num_scalar_prefetch=1,
            grid=(1,),
            in_specs=[any_spec()] * len(pieces)
            + [
                once((LEN, D)), once((LEN, D)), once((LEN, D)), once((13, D)),
                pl.BlockSpec((1, 1, FFC), lambda *_: (0, 0, 0)),
            ],
            out_specs=[once(out.shape) for out in outs],
            scratch_shapes=[pltpu.VMEM((wide, rows_flat, WIDTH), BF16)]
            + weight_scratch()
            + [pltpu.SemaphoreType.DMA((16,))],
        ),
        out_shape=outs,
        compiler_params=pltpu.CompilerParams(
            dimension_semantics=("arbitrary",), vmem_limit_bytes=VMEM_LIMIT
        ),
        cost_estimate=cost(14 * 10**9, 30 * 10**6),
        name="middle_first",
    )(place, *pieces, tokens, attn, cotangent, vectors, bias_up)


def middle_rest(place, wide, pieces, cotangent, state, bias_up, attn, w_out, vectors, sums):
    a2, a2t, dyt = state
    half = (wide, FFC * D // (WIDTH * wide), WIDTH)
    out_half = (wide, 3 * D // (2 * wide), WIDTH)
    outs = [
        struct((LEN, D), F32), struct((LEN, D), F32), struct((LEN, D), F32),
        struct(out_half, BF16), struct(out_half, BF16), struct((8, D), F32),
        struct((2,) + half, BF16), struct((2,) + half, BF16), struct((2, 1, FFC), F32),
    ]
    out_specs = [once(out.shape) for out in outs[:8]] + [group_spec((1, FFC))]
    if wide > 1:
        for index in (3, 4, 6, 7):
            outs[index] = pltpu.VMEM(outs[index].shape, BF16)
            out_specs[index] = pl.BlockSpec(memory_space=pltpu.VMEM)
    rows_flat = 2 * FFC * D // (WIDTH * wide)
    return pl.pallas_call(
        functools.partial(middle_rest_kernel, wide, len(pieces)),
        grid_spec=pltpu.PrefetchScalarGridSpec(
            num_scalar_prefetch=1,
            grid=(2,),
            in_specs=[any_spec()] * len(pieces)
            + [
                once((LEN, D)), once((LEN, D)), once((D, LEN)), once((D, LEN)),
                pl.BlockSpec((1, 1, FFC), lambda j, *_: (j + 1, 0, 0)),
                once((LEN, D)), once((D, D)), once((13, D)),
                any_spec(), any_spec(), any_spec(),
            ],
            out_specs=out_specs,
            scratch_shapes=[pltpu.VMEM((2, wide, rows_flat, WIDTH), BF16)]
            + weight_scratch()
            + [
                pltpu.VMEM((LEN, D), F32), pltpu.VMEM((LEN, D), BF16),
                pltpu.SemaphoreType.DMA((3,)), pltpu.SemaphoreType.DMA((2, 8)),
            ],
        ),
        out_shape=outs,
        compiler_params=pltpu.CompilerParams(
            dimension_semantics=("arbitrary",), vmem_limit_bytes=REST_LIMIT
        ),
        cost_estimate=cost(28 * 10**9, 40 * 10**6),
        name="middle_rest",
    )(place, *pieces, cotangent, a2, a2t, dyt, bias_up, attn, w_out, vectors, *sums)


def input_kernel(
    wide, x_ref, dx1_ref, da1_ref, rows_ref, middle_ref, bias_in_ref, bias_first_ref, bias_rest_ref,
    out_ref, vec_ref,
):
    gain = rows_ref[0:1, :]
    x = x_ref[...].astype(F32)
    dn = da1_ref[...]
    centre = x - jnp.mean(x, axis=-1, keepdims=True)
    spread = jnp.mean(centre * centre, axis=-1, keepdims=True)
    scale = lax.rsqrt(spread + norm_eps)
    zh = centre * scale
    e = dn * gain
    dz = (
        e - jnp.mean(e, axis=-1, keepdims=True) - zh * jnp.mean(e * zh, axis=-1, keepdims=True)
    ) * scale
    out_ref[...] = dx1_ref[...] + dz

    @pl.when(pl.program_id(0) == 0)
    def _():
        vec_ref[...] = jnp.zeros_like(vec_ref)
        vec_ref[2:4, :] = middle_ref[0:2, :]
        vec_ref[7:9, :] = middle_ref[2:4, :]
        for group in range(GROUPS):
            lanes = slice(WIDTH * group, WIDTH * (group + 1))
            for which in range(3):
                vec_ref[4 + which : 5 + which, lanes] = bias_in_ref[
                    group, :, WIDTH * which : WIDTH * (which + 1)
                ]
        for chunk in range(CHUNKS):
            for part in range(8):
                value = (
                    bias_first_ref[0] if chunk == 0 else bias_rest_ref[chunk - 1]
                )[:, 128 * part : 128 * (part + 1)]
                start = FFC * chunk + 128 * part if wide == 1 else 384 * part + 128 * chunk
                row, lane = 9 + start // D, start % D
                vec_ref[row : row + 1, lane : lane + 128] = value

    vec_ref[0:1, :] += jnp.sum(dn * zh, axis=0, keepdims=True)
    vec_ref[1:2, :] += jnp.sum(dn, axis=0, keepdims=True)


def input_side(wide, tokens, dx1, da1, vectors, middle_vec, bias_in, bias_first, bias_rest):
    block = pl.BlockSpec((256, D), lambda i: (i, 0))
    return pl.pallas_call(
        functools.partial(input_kernel, wide),
        grid=(LEN // 256,),
        in_specs=[
            block, block, block, whole_spec((13, D)), whole_spec((8, D)),
            whole_spec((GROUPS, 1, D)), whole_spec((1, 1, FFC)), whole_spec((2, 1, FFC)),
        ],
        out_specs=[block, whole_spec((16, D))],
        out_shape=[struct((LEN, D), F32), struct((16, D), F32)],
        compiler_params=pltpu.CompilerParams(dimension_semantics=("arbitrary",)),
        cost_estimate=cost(10**6, 12 * 10**6),
        name="input_side",
    )(tokens, dx1, da1, vectors, middle_vec, bias_in, bias_first, bias_rest)


def tables(lengths, projection):
    ends = jnp.cumsum(lengths[0])
    starts = ends - lengths[0]
    place = jnp.arange(LEN, dtype=jnp.int32)
    member = (place[:, None] >= starts[None, :]) & (place[:, None] < ends[None, :])
    offset = jnp.sum(jnp.where(member, starts[None, :], 0), axis=1)
    position = (place - offset).astype(F32)
    freq = 10000.0 ** (-jnp.arange(32, dtype=F32) / 32)
    angles = position[:, None] * jnp.tile(freq, 4)[None, :]
    onehot = jnp.pad(member.astype(BF16), ((0, 0), (0, 128 - member.shape[1])))
    eye = jnp.asarray(np.eye(4, dtype=np.float32))
    lifted = jnp.einsum("hif,ab->haibf", projection.reshape(2, 32, FEAT), eye)
    lifted = lifted.reshape(WIDTH, 128)
    rounded = lax.reduce_precision(lifted, 8, 7)
    high, low = rounded.astype(BF16), (lifted - rounded).astype(BF16)
    square = np.zeros((2, 4, 32, 4, 32), np.float32)
    for head in range(4):
        square[:, head, :, head, :] = 0.5
    square = jnp.asarray(square.reshape(WIDTH, 128), BF16)
    proj = jnp.stack(
        [
            jnp.concatenate([high, low], axis=1),
            jnp.concatenate([high, high], axis=1),
            jnp.concatenate([square, square], axis=1),
        ]
    )
    return jnp.cos(angles), jnp.sin(angles), onehot, proj


def wide_perm(shift_z, flip_x):
    pairs = []
    for z in range(4):
        for x in range(2):
            target_x = 1 - x if flip_x else x
            pairs.append((2 * z + x, 2 * ((z + shift_z) % 4) + target_x))
    return pairs


def narrow_perm(flip_y, flip_core):
    pairs = []
    for y in range(2):
        for core in range(2):
            pairs.append(
                (2 * y + core, 2 * (1 - y if flip_y else y) + (1 - core if flip_core else core))
            )
    return pairs


def over_z(values, shift):
    return lax.ppermute(values, "wide", wide_perm(shift, False))


def over_x(values):
    return lax.ppermute(values, "wide", wide_perm(0, True))


def over_far(values, bit):
    return lax.ppermute(values, "wide", [(w, w ^ bit) for w in range(8)])


def over_y(values):
    return lax.ppermute(values, "narrow", narrow_perm(True, False))


def over_core(values):
    return lax.ppermute(values, "narrow", narrow_perm(False, True))


def tie(*values):
    return lax.optimization_barrier(values)


def special():
    return lax.axis_size("wide") == 8 and lax.axis_size("narrow") == 4


def sum_wide(values):
    if not special():
        return lax.psum(values, "wide")
    for perm in (wide_perm(0, True), [(w, w ^ 2) for w in range(8)], [(w, w ^ 4) for w in range(8)]):
        values = values + lax.ppermute(values, "wide", perm)
    return values


def sum_narrow(values):
    if not special():
        return lax.psum(values, "narrow")
    pair = values + over_core(values)
    return pair + over_y(pair)


def along_z(mine):
    return jnp.stack([mine] + [over_z(mine, shift) for shift in (1, 2, 3)])


def small_call(kernel, name, place, operands, outs):
    return pl.pallas_call(
        kernel,
        grid_spec=pltpu.PrefetchScalarGridSpec(
            num_scalar_prefetch=1,
            grid=(1,),
            in_specs=[once(value.shape) for value in operands],
            out_specs=[once(out.shape) for out in outs],
        ),
        out_shape=outs,
        compiler_params=pltpu.CompilerParams(
            dimension_semantics=("arbitrary",), vmem_limit_bytes=VMEM_LIMIT
        ),
        cost_estimate=cost(10**6, sum(4 * math.prod(v.shape) for v in operands + outs)),
        name=name,
    )(place, *operands)


def held_call(kernel, name, place, operands, outs, held=None, flops=10**6):
    here = pl.BlockSpec(memory_space=pltpu.VMEM)
    held = len(outs) if held is None else held
    return pl.pallas_call(
        kernel,
        in_specs=[pl.BlockSpec(memory_space=pltpu.SMEM)] + [here] * len(operands),
        out_specs=[here] * len(outs),
        out_shape=[
            pltpu.VMEM(out.shape, out.dtype) if index < held else out
            for index, out in enumerate(outs)
        ],
        compiler_params=pltpu.CompilerParams(vmem_limit_bytes=24 * 1024 * 1024),
        cost_estimate=pl.CostEstimate(flops=flops, transcendentals=0, bytes_accessed=10**5),
        name=name,
    )(place, *[pltpu.with_memory_space_constraint(value, pltpu.VMEM) for value in operands])


def pick_kernel(
    place, in_ref, out_ref, up_ref, down_ref, near_ref, last_ref, first_ref, rest_ref
):
    core = place[3]
    here = pl.ds(pl.multiple_of(48 * core, 16), 48)
    for group in range(GROUPS):
        ref, index = (near_ref, group) if group < 2 else (last_ref, 0)
        for which in range(3):
            ref[index, :, WIDTH * which : WIDTH * (which + 1)] = in_ref[
                which, here, WIDTH * group : WIDTH * (group + 1)
            ].astype(BF16)
    for cols in range(3):
        first_ref[48 * cols : 48 * (cols + 1), :] = out_ref[
            here, WIDTH * cols : WIDTH * (cols + 1)
        ].astype(BF16)

    def put_up(ref, at, chunk):
        for cols in range(4):
            rows = slice(at + 96 * cols, at + 96 * (cols + 1))
            for side in range(2):
                start = 384 * (2 * cols + side) + 128 * chunk
                ref[rows, 128 * side : 128 * (side + 1)] = up_ref[:, start : start + 128].astype(
                    BF16
                )

    def put_down(ref, at, chunk):
        for cols in range(3):
            ref[at + 128 * cols : at + 128 * (cols + 1), :] = down_ref[
                128 * chunk : 128 * (chunk + 1), WIDTH * cols : WIDTH * (cols + 1)
            ].astype(BF16)

    for side in range(2):

        @pl.when(core == side)
        def _():
            if side == 0:
                put_up(first_ref, 144, 0)
            else:
                put_down(first_ref, 144, 0)

        @pl.when(core == side)
        def _():
            put_up(rest_ref, 0, 1 + side)
            put_down(rest_ref, 384, 1 + side)


def chunk_of(ref, chunk, shard):
    return ref[chunk, shard] if len(ref.shape) == 4 else ref[shard]


def first_sum_kernel(place, *refs):
    send_ref, keep_ref = refs[-2:]
    x = place[1]
    at = 0
    for index in range(0, len(refs) - 2, 2):
        own, got = refs[index], refs[index + 1]
        for part in range(own.shape[0] if len(own.shape) == 4 and own.shape[0] == 3 else 1):
            rows = own.shape[-2]
            here = pl.ds(at, rows)
            for z in range(4):
                for out, side in ((keep_ref, x), (send_ref, 1 - x)):
                    out[z, here, :] = (
                        chunk_of(own, part, 2 * z + side).astype(F32)
                        + chunk_of(got, part, 2 * z + side).astype(F32)
                    ).astype(BF16)
            at += rows


def first_sum(place, pairs):
    rows = sum(
        own.shape[-2] * (own.shape[0] if own.ndim == 4 and own.shape[0] == 3 else 1)
        for own, _ in pairs
    )
    return held_call(
        first_sum_kernel, "first_sum", place, [value for pair in pairs for value in pair],
        [struct((4, rows, WIDTH), BF16)] * 2,
    )


def first_sum_y_kernel(place, own, got, send, keep):
    y = place[2]
    for group in range(GROUPS):
        here = pl.ds(144 * group, 144)
        for shard in range(8):
            total = own[group, shard].astype(F32) + got[group, shard].astype(F32)
            left, right = total[:, :128].astype(BF16), total[:, 128:].astype(BF16)
            keep[shard, here, :] = jnp.where(y == 0, left, right)
            send[shard, here, :] = jnp.where(y == 0, right, left)


def split_x_kernel(place, own, got, send, keep):
    x = place[1]
    for z in range(4):
        for out, side in ((keep, x), (send, 1 - x)):
            out[z] = (own[2 * z + side].astype(F32) + got[2 * z + side].astype(F32)).astype(BF16)


def second_sum_kernel(place, own_ref, got_ref, *outs):
    z = place[0]
    for shift, out in enumerate(outs):
        there = lax.rem(z + shift, 4)
        out[...] = (own_ref[there].astype(F32) + got_ref[there].astype(F32)).astype(BF16)


def second_sum(place, own, got):
    outs = [struct(own.shape[1:], BF16)] * 4
    return held_call(second_sum_kernel, "second_sum", place, [own, got], outs)


def z_sum_kernel(place, *refs):
    total = refs[0][...].astype(F32)
    for ref in refs[1:4]:
        total = total + ref[...].astype(F32)
    rows = refs[0].shape[0]
    refs[-1][:rows, :] = total.astype(refs[-1].dtype)
    if len(refs) == 7:
        refs[-1][rows:, :] = (refs[4][...].astype(F32) + refs[5][...].astype(F32)).astype(BF16)


def z_sum(place, parts, below=(), got=None):
    if got is None:
        got = [over_z(parts[shift], shift) for shift in (1, 2, 3)]
    rows = parts[0].shape[0] + (below[0].shape[0] if below else 0)
    return held_call(
        z_sum_kernel, "z_sum", place, [parts[0]] + got + list(below),
        [struct((rows, parts[0].shape[1]), BF16 if below else F32)],
        flops=3 * 10**10 if below else 10**6,
    )[0]


def first_sum_z_kernel(place, *refs):
    z = place[0]
    outs = refs[-4:]
    for shift, out in enumerate(outs):
        there = lax.rem(z + shift, 4) * 2
        at = 0
        for index in range(0, len(refs) - 4, 2):
            own, got = refs[index], refs[index + 1]
            rows = own.shape[-2]
            for x in range(2):
                out[x, at : at + rows, :] = (
                    chunk_of(own, 1, there + x).astype(F32)
                    + chunk_of(got, 1, there + x).astype(F32)
                ).astype(BF16)
            at += rows


def first_sum_z(place, pairs):
    rows = sum(own.shape[-2] for own, _ in pairs)
    return held_call(
        first_sum_z_kernel, "first_sum_z", place, [value for pair in pairs for value in pair],
        [struct((2, rows, WIDTH), BF16)] * 4,
    )


def split_sum_kernel(place, *refs):
    keep, send = refs[-2:]
    x = place[1]
    for out, at in ((keep, x), (send, 1 - x)):
        total = refs[0][at].astype(F32)
        for ref in refs[1:4]:
            total = total + ref[at].astype(F32)
        out[...] = total.astype(BF16)


def split_sum(place, parts):
    return held_call(
        split_sum_kernel, "split_sum", place, parts, [struct(parts[0].shape[1:], BF16)] * 2
    )


def to_row(column):
    size = column.shape[0]
    eye = lax.broadcasted_iota(jnp.int32, (size, size), 0) == lax.broadcasted_iota(
        jnp.int32, (size, size), 1
    )
    return jnp.sum(jnp.where(eye, column, 0.0), axis=0, keepdims=True)


def to_column(row):
    size = row.shape[1]
    eye = lax.broadcasted_iota(jnp.int32, (size, size), 0) == lax.broadcasted_iota(
        jnp.int32, (size, size), 1
    )
    return jnp.sum(jnp.where(eye, row, 0.0), axis=1, keepdims=True)


DECAY = 1.0 - STEP ** (-0.8)


def lane_values(values):
    lane = lax.broadcasted_iota(jnp.int32, (1, D), 1)
    row = jnp.zeros((1, D), F32)
    for index, value in enumerate(values):
        row = jnp.where(lane == index, value, row)
    return row


def moments(grad, rows_old):
    plain = grad * grad
    squares = plain + square_eps
    mean = jnp.sum(squares, axis=1, keepdims=True) * (1.0 / grad.shape[1])
    rows_new = DECAY * rows_old + (1.0 - DECAY) * to_row(mean)
    total = jnp.sum(rows_new, axis=1, keepdims=True)
    divided = jnp.sum(plain * to_column(1.0 / rows_new), axis=0, keepdims=True)
    return rows_new, total, jnp.sum(squares, axis=0, keepdims=True), divided


def ffn_moments_kernel(
    place, own, got, up_rows, down_rows, out_rows,
    up_grad, down_grad, out_grad, up_rows_new, down_rows_new, out_rows_new, sums,
):
    core = place[3]

    def collect(low, high):
        for chunk in range(CHUNKS):
            at = 384 * chunk
            for cols in range(4):
                for side in range(2):
                    start = 384 * (2 * cols + side) + 128 * chunk
                    up_grad[:, start : start + 128] = low[
                        at + 96 * cols : at + 96 * (cols + 1), 128 * side : 128 * (side + 1)
                    ]
            for side in range(2):
                down_grad[128 * chunk : 128 * (chunk + 1), 384 * side : 384 * (side + 1)] = (
                    jnp.transpose(high[at : at + 384, 128 * side : 128 * (side + 1)])
                )
        for cols in range(3):
            lanes = slice(WIDTH * cols, WIDTH * (cols + 1))
            at = 1152 + 48 * cols
            out_grad[:48, lanes] = low[at : at + 48, :]
            out_grad[48:, lanes] = high[at : at + 48, :]

    @pl.when(core == 0)
    def _():
        collect(own, got)

    @pl.when(core == 1)
    def _():
        collect(got, own)

    up_new, up_total, up_sums, up_divided = moments(up_grad[...], up_rows[...])
    down_new, down_total, down_sums, down_divided = moments(down_grad[...], down_rows[...])
    out_new, out_total, out_sums, out_divided = moments(out_grad[...], out_rows[...])
    up_rows_new[...] = up_new
    down_rows_new[...] = down_new
    out_rows_new[...] = out_new
    for part in range(4):
        lanes = slice(D * part, D * (part + 1))
        sums[part : part + 1, :] = up_sums[:, lanes]
        sums[4 + part : 5 + part, :] = up_divided[:, lanes]
    sums[8:9, :] = down_sums
    sums[9:10, :] = down_divided
    sums[10:11, :] = out_sums
    sums[11:12, :] = out_divided
    sums[12:13, :] = lane_values([up_total, down_total, out_total])
    sums[13:16, :] = jnp.zeros((3, D), F32)


def in_moments_kernel(
    place, own, own_y, other, other_y, rows_old, vector, vector_far, ffn_sums, grad, rows_new,
    sums,
):
    def collect(low, high):
        for group in range(GROUPS):
            for which in range(3):
                rows = slice(144 * group + 48 * which, 144 * group + 48 * (which + 1))
                for side in range(2):
                    start = WIDTH * group + 128 * side
                    grad[which, :48, start : start + 128] = low[side][rows, :]
                    grad[which, 48:, start : start + 128] = high[side][rows, :]

    for core in range(2):
        for y in range(2):

            @pl.when((place[3] == core) & (place[2] == y))
            def _():
                mine = (own, own_y) if y == 0 else (own_y, own)
                far = (other, other_y) if y == 0 else (other_y, other)
                collect(mine if core == 0 else far, far if core == 0 else mine)

    totals = []
    for which in range(3):
        new, total, columns, divided = moments(grad[which], rows_old[which : which + 1, :])
        rows_new[which : which + 1, :] = new
        sums[which : which + 1, :] = columns
        sums[3 + which : 4 + which, :] = divided
        totals.append(total)
    sums[6:7, :] = lane_values(totals)
    sums[7:8, :] = jnp.zeros((1, D), F32)
    sums[8:24, :] = vector[...] + vector_far[...]
    sums[24:40, :] = ffn_sums[...]


def matrix_step(weight, grad, rows, cols, total, col_sums, divided, rows_full, rate):
    cols_new = DECAY * cols + (1.0 - DECAY) * col_sums * (1.0 / rows_full)
    mean = total * (1.0 / rows_full)
    square_sum = mean * jnp.sum(divided / cols_new, axis=1, keepdims=True)
    rms = jnp.sqrt(square_sum * (1.0 / (rows_full * grad.shape[1])))
    factor = to_column(lax.rsqrt(rows / mean)) * (rate / jnp.maximum(1.0, rms / clip_level))
    return cols_new, weight - grad * factor * lax.rsqrt(cols_new)


def finish_kernel(
    place, inward, up, down, out, in_grad, up_grad, down_grad, out_grad, in_rows, up_rows,
    down_rows, out_rows, in_cols, up_cols, down_cols, out_cols, sums, vectors, vector_state,
    in_cols_new, up_cols_new, down_cols_new, out_cols_new, in_next, up_next, down_next, out_next,
    vector_grad, state_next, vectors_next,
):
    base_rate = 0.3 * D ** (-0.5)
    for which in range(3):
        here = slice(which, which + 1)
        in_cols_new[here, :], in_next[which] = matrix_step(
            inward[which], in_grad[which], in_rows[here, :], in_cols[here, :],
            sums[6:7, which : which + 1], sums[here, :], sums[3 + which : 4 + which, :], D,
            base_rate,
        )

    def wide_row(first):
        return jnp.concatenate([sums[first + i : first + i + 1, :] for i in range(4)], axis=1)

    up_new, up_next[...] = matrix_step(
        up[...], up_grad[...], up_rows[...], up_cols[...], sums[36:37, 0:1], wide_row(24),
        wide_row(28), D, base_rate,
    )
    down_new, down_next[...] = matrix_step(
        down[...], down_grad[...], down_rows[...], down_cols[...], sums[36:37, 1:2],
        sums[32:33, :], sums[33:34, :], FF, 0.3 * FF ** (-0.5),
    )
    out_new, out_next[...] = matrix_step(
        out[...], out_grad[...], out_rows[...], out_cols[...], sums[36:37, 2:3],
        sums[34:35, :], sums[35:36, :], D, 1.2 * D ** (-0.5),
    )
    up_cols_new[...] = up_new.reshape(FF)
    down_cols_new[...] = down_new.reshape(D)
    out_cols_new[...] = out_new.reshape(D)
    g = sums[8:21, :]
    vector_grad[...] = g
    state = DECAY * vector_state[...] + (1.0 - DECAY) * (g * g + square_eps)
    state_next[...] = state
    update = g * lax.rsqrt(state)
    total = jnp.sum(jnp.sum(update * update, axis=0, keepdims=True), axis=1, keepdims=True)
    rms = jnp.sqrt(total * (1.0 / (13 * D)))
    vectors_next[...] = vectors[...] - update * (0.25 / jnp.maximum(1.0, rms / clip_level))


def shards(
    tokens, cotangent, lengths, projection, inward, outward, expand, shrink, vectors,
    inward_rows, inward_columns, outward_rows, outward_columns, expand_rows, expand_columns,
    shrink_rows, shrink_columns, vector_state,
):
    full = special()
    rows = outward.shape[0]
    wide = 8 if full else 1
    wide_at = lax.axis_index("wide").astype(jnp.int32)
    narrow_at = lax.axis_index("narrow").astype(jnp.int32)
    core = narrow_at % 2 if full else jnp.int32(0)
    place = jnp.stack([wide_at // 2, wide_at % 2, narrow_at // 2, core])
    per = FFC // wide
    cosine, sine, onehot, proj = tables(lengths, projection)
    if full:
        *own_in, own_first, own_rest = small_call(
            pick_kernel, "pick", place, [inward, outward, expand, shrink],
            [
                struct((2, 48, D), BF16), struct((1, 48, D), BF16), struct((528, WIDTH), BF16),
                struct((768, WIDTH), BF16),
            ],
        )
        in_z = [along_z(value) for value in own_in]
        *in_z, own_first, cosine, sine, onehot, proj = tie(
            *in_z, own_first, cosine, sine, onehot, proj
        )
        first_z = along_z(own_first)
        in_x = [over_x(value) for value in in_z]
        pieces_in = []
        *in_z, first_z = tie(*in_z, *in_x, first_z)
        for near, far in zip(in_z[:2], in_z[2:]):
            pieces_in += [near, far, over_core(near), over_core(far)]
        *pieces_in, first_z, own_rest = tie(*pieces_in, first_z, own_rest)
        first_x = over_x(first_z)
        rest_got = [over_z(own_rest, shift) for shift in (1, 2, 3)]
    else:
        in_low = lax.all_gather(inward.astype(BF16), "wide", axis=1, tiled=True)
        out_low = lax.all_gather(outward.astype(BF16), "wide", axis=0, tiled=True)
        up_low = lax.all_gather(expand.astype(BF16), "wide", axis=0, tiled=True)
        down_low = lax.all_gather(shrink.astype(BF16), "wide", axis=0, tiled=True)
        units = jnp.transpose(in_low.reshape(3, D, GROUPS, WIDTH), (2, 1, 0, 3))
        pieces_in = [units.reshape(1, 3 * D, D)]

        def blocks(matrix):
            count = matrix.shape[1] // WIDTH
            return jnp.transpose(matrix.reshape(-1, count, WIDTH), (1, 0, 2)).reshape(-1, WIDTH)

        ups = [blocks(up_low[:, FFC * j : FFC * (j + 1)]) for j in range(CHUNKS)]
        downs = [blocks(down_low[FFC * j : FFC * (j + 1)]) for j in range(CHUNKS)]
        half = D // 2
        pieces_first = [
            jnp.concatenate([blocks(out_low[:half]), ups[0], blocks(out_low[half:]), downs[0]])[
                None
            ]
        ]
        pieces_rest = [
            jnp.stack([jnp.concatenate([ups[j], downs[j]])[None] for j in range(1, CHUNKS)])
        ]
    perm = jnp.asarray(head_perm(), BF16)
    block_ones = np.kron(np.eye(2, dtype=np.float32), np.ones((64, 64), np.float32))
    ones = jnp.asarray(np.concatenate([block_ones, block_ones]), BF16)
    split = vectors[4:6].reshape(2, GROUPS, 4, 2, 32)
    bias_qk = jnp.transpose(split, (0, 1, 3, 2, 4)).reshape(2, GROUPS, WIDTH)
    bias = jnp.concatenate([bias_qk, vectors[6].reshape(1, GROUPS, WIDTH)])
    bias = jnp.transpose(bias, (1, 0, 2))
    bias_up = vectors[9:].reshape(wide, CHUNKS, per)
    bias_up = jnp.transpose(bias_up, (1, 0, 2)).reshape(CHUNKS, 1, FFC)
    attn, mixed, a1t, w_in, wq, wk, qf, kf, v, rden = attend(
        lengths, place, pieces_in, wide, tokens, vectors[:2], bias, perm, proj, cosine, sine,
        onehot,
    )
    if full:
        attn, first_x, *rest_got = tie(attn, first_x, *rest_got)
        rest_z = jnp.stack([own_rest] + rest_got)
        first_cores = [over_core(first_z), over_core(first_x)]
        *first_cores, rest_z = tie(*first_cores, rest_z)
        pieces_first = [first_z, first_x] + first_cores
        rest_x = over_x(rest_z)
    x1, a2, a2t, dyt, y, back, w_out, keep0, send0, dbias0 = middle_first(
        place, wide, pieces_first, tokens, attn, cotangent, vectors, bias_up
    )
    if full:
        rest_core = over_core(rest_z)
        rest_x, rest_core, send0, y = tie(rest_x, rest_core, send0, y)
        pieces_rest = [rest_z, rest_x, rest_core, over_core(rest_x)]
        got0 = over_core(send0)
    (
        block_out, dx1, dmixed, okeep, osend, middle_vec, keep12, send12, dbias12,
    ) = middle_rest(
        place, wide, pieces_rest, cotangent, (a2, a2t, dyt), bias_up, attn, w_out, vectors,
        (y, back, x1),
    )
    if full:
        got0, send12, osend = tie(got0, send12, osend)
        got12 = over_core(send12)
        send_b, keep_b = first_sum(place, [(keep0, got0), (keep12, got12)])
        e_parts = first_sum_z(place, [(keep12, got12), (okeep, over_core(osend))])
        dmixed, send_b, keep_b, *e_parts = tie(dmixed, send_b, keep_b, *e_parts)
        got_b = over_x(send_b)
        e_got = [over_z(e_parts[shift], shift) for shift in (1, 2, 3)]
    saved = (mixed, rden, wq, wk, qf, kf, v)
    in_keep, in_send, in_bias, da1 = attend_back(
        lengths, place, wide, dmixed, saved, a1t, w_in, perm, proj, cosine, sine, onehot, ones
    )
    if full:
        in_send, da1, got_b, *e_got = tie(in_send, da1, got_b, *e_got)
        b_parts = list(second_sum(place, keep_b, got_b))
        got_in = over_core(in_send)
        got_in, *e_got, b_parts[1] = tie(got_in, *e_got, b_parts[1])
        keep_e, send_e = split_sum(place, [e_parts[0]] + e_got)
        got_e = over_x(send_e)
        send_c, keep_c = held_call(
            first_sum_y_kernel, "first_sum_y", place, [in_keep, got_in],
            [struct((8, 432, 128), BF16)] * 2,
        )
        da1, send_c = tie(da1, send_c)
        got_c = over_y(send_c)
    input_grad, vector_local = input_side(
        wide, tokens, dx1, da1, vectors, middle_vec, in_bias, dbias0, dbias12
    )
    if full:
        def pair_sum(mine, got):
            half_sum = mine.astype(F32) + got.astype(F32)
            return half_sum, over_core(half_sum)

        got_c, input_grad, vector_local = tie(got_c, input_grad, vector_local)
        send_c, keep_c = held_call(
            split_x_kernel, "split_x", place, [keep_c, got_c], [struct((4, 432, 128), BF16)] * 2
        )
        send_c, b_parts[0] = tie(send_c, b_parts[0])
        got_c = over_x(send_c)
        ffn_mine = z_sum(place, b_parts, (keep_e, got_e))
        ffn_mine, got_c = tie(ffn_mine, got_c)
        c_parts = second_sum(place, keep_c, got_c)
        ffn_mine, *c_parts = tie(ffn_mine, *c_parts)
        ffn_y = over_y(ffn_mine)
        c_mine = z_sum(place, c_parts)
        c_mine, vector_local = tie(c_mine, vector_local)
        c_y = over_y(c_mine)
        vector_y = over_y(vector_local)
        c_core = over_core(c_mine)
        ffn_y, c_mine = tie(ffn_y, c_mine)
        ffn_own, ffn_got = pair_sum(ffn_mine, ffn_y)
        expand_grad, shrink_grad, outward_grad, up_rows, down_rows, out_rows, sums = held_call(
            ffn_moments_kernel, "ffn_moments", place,
            [
                ffn_own, ffn_got, expand_rows[None], shrink_rows[None], outward_rows[None],
            ],
            [
                struct(expand.shape, F32), struct(shrink.shape, F32), struct(outward.shape, F32),
                struct((1, 96), F32), struct((1, 384), F32), struct((1, 96), F32),
                struct((16, D), F32),
            ],
            0,
        )
        c_y, vector_y, sums = tie(c_y, vector_y, sums)
        vector_pair = vector_local + vector_y
        inward_grad, in_rows, sums = held_call(
            in_moments_kernel, "in_moments", place,
            [
                c_mine, c_y, c_core, over_core(c_y), inward_rows, vector_pair,
                over_core(vector_pair), sums,
            ],
            [struct(inward.shape, F32), struct((3, 96), F32), struct((40, D), F32)],
            0,
        )
        sums = sum_wide(sums)
        (
            in_cols, up_cols, down_cols, out_cols, inward_next, expand_next, shrink_next,
            outward_next, vector_grad, vector_state_next, vectors_next,
        ) = small_call(
            finish_kernel, "finish", place,
            [
                inward, expand, shrink, outward, inward_grad, expand_grad, shrink_grad,
                outward_grad, in_rows, up_rows, down_rows, out_rows, inward_columns,
                expand_columns[None], shrink_columns[None], outward_columns[None], sums, vectors,
                vector_state,
            ],
            [
                struct((3, D), F32), struct((FF,), F32), struct((D,), F32),
                struct((D,), F32), struct(inward.shape, F32), struct(expand.shape, F32),
                struct(shrink.shape, F32), struct(outward.shape, F32), struct((13, D), F32),
                struct((13, D), F32), struct((13, D), F32),
            ],
        )
        return (
            block_out, input_grad, inward_grad, outward_grad, expand_grad, shrink_grad,
            vector_grad, in_rows, in_cols, out_rows[0], out_cols, up_rows[0], up_cols,
            down_rows[0], down_cols, vector_state_next, inward_next, outward_next,
            expand_next, shrink_next, vectors_next,
        )
    vector_part = sum_narrow(vector_local[:13])

    def reduced(values, axis):
        part = lax.psum_scatter(values, "wide", scatter_dimension=axis, tiled=True)
        return lax.psum(part.astype(F32), "narrow")

    keeps = [keep0, keep12[0], keep12[1]]
    sends = [send0, send12[0], send12[1]]
    up_grads = [
        jnp.transpose(keep.reshape(4, D, WIDTH), (1, 0, 2)).reshape(D, FFC) for keep in keeps
    ]
    down_grads = [
        jnp.transpose(send.reshape(4, D, WIDTH), (0, 2, 1)).reshape(FFC, D) for send in sends
    ]
    expand_grad = reduced(jnp.concatenate(up_grads, axis=1), 0)
    shrink_grad = reduced(jnp.concatenate(down_grads, axis=0), 0)

    def rebuilt(keep, send):
        return jnp.concatenate(
            [keep.reshape(-1, 3, D // 2, WIDTH), send.reshape(-1, 3, D // 2, WIDTH)], axis=2
        )

    outward_grad = reduced(jnp.transpose(rebuilt(okeep, osend)[0], (1, 0, 2)).reshape(D, D), 0)
    in_units = rebuilt(in_keep, in_send)
    inward_grad = reduced(jnp.transpose(in_units, (1, 2, 0, 3)).reshape(3, D, D), 1)
    decay = 1.0 - STEP ** (-0.8)
    wide_count = lax.axis_size("wide")
    grads_list = [inward_grad, outward_grad[None], expand_grad[None], shrink_grad[None]]
    rows_old = [inward_rows, outward_rows[None], expand_rows[None], shrink_rows[None]]
    columns_old = [
        inward_columns,
        outward_columns[None],
        expand_columns[None],
        shrink_columns[None],
    ]
    weights_old = [inward, outward[None], expand[None], shrink[None]]
    rates = [0.3 * D ** (-0.5), 1.2 * D ** (-0.5), 0.3 * D ** (-0.5), 0.3 * FF ** (-0.5)]
    bounds = [0, 3, 4, 5, 6]
    rows_next = []
    column_parts = []
    for member in range(4):
        squares = grads_list[member] * grads_list[member] + square_eps
        rows_next.append(decay * rows_old[member] + (1.0 - decay) * jnp.mean(squares, axis=-1))
        column_parts.append(jnp.sum(squares, axis=-2))
    row_totals = jnp.concatenate([jnp.sum(entry, axis=-1) for entry in rows_next])
    shapes = [part.shape for part in column_parts] + [row_totals.shape, vector_part.shape]
    flat = jnp.concatenate(
        [part.reshape(-1) for part in column_parts + [row_totals, vector_part]]
    )
    flat = jnp.pad(flat, (0, -flat.shape[0] % 1024)).reshape(-1, 128)
    flat = sum_wide(flat).reshape(-1)
    summed = []
    offset = 0
    for shape in shapes:
        size = 1
        for extent in shape:
            size *= extent
        summed.append(flat[offset : offset + size].reshape(shape))
        offset += size
    column_sums = list(summed[0:4])
    totals_sum = summed[4]
    vector_grad = summed[5]
    columns_next = []
    scaled_list = []
    row_means = []
    sizes_full = []
    for member in range(4):
        grad_now = grads_list[member]
        rows_full = grad_now.shape[-2] * wide_count
        sizes_full.append(rows_full * grad_now.shape[-1])
        columns_next.append(
            decay * columns_old[member] + (1.0 - decay) * column_sums[member] / rows_full
        )
        row_mean = totals_sum[bounds[member] : bounds[member + 1]] / rows_full
        row_means.append(row_mean)
        scaled_list.append(
            grad_now
            * lax.rsqrt(rows_next[member] / row_mean[:, None])[..., None]
            * lax.rsqrt(columns_next[member])[:, None, :]
        )
    partial_squares = jnp.concatenate(
        [jnp.sum(entry * entry, axis=(-2, -1)) for entry in scaled_list]
    )
    total_squares = sum_wide(jnp.pad(partial_squares, (0, 122)).reshape(1, 128))[0, :6]
    rms_list = [
        jnp.sqrt(total_squares[bounds[member] : bounds[member + 1]] / sizes_full[member])
        for member in range(4)
    ]
    weights_next = []
    for member in range(4):
        limiter = jnp.maximum(1.0, rms_list[member] / clip_level)
        weights_next.append(
            weights_old[member] - rates[member] * scaled_list[member] / limiter[:, None, None]
        )
    vector_state_next = decay * vector_state + (1.0 - decay) * (
        vector_grad * vector_grad + square_eps
    )
    vector_update = vector_grad * lax.rsqrt(vector_state_next)
    vector_rms = jnp.sqrt(jnp.mean(vector_update * vector_update))
    vectors_next = vectors - 0.25 * vector_update / jnp.maximum(1.0, vector_rms / clip_level)
    return (
        block_out,
        input_grad,
        inward_grad,
        outward_grad,
        expand_grad,
        shrink_grad,
        vector_grad,
        rows_next[0],
        columns_next[0],
        rows_next[1][0],
        columns_next[1][0],
        rows_next[2][0],
        columns_next[2][0],
        rows_next[3][0],
        columns_next[3][0],
        vector_state_next,
        weights_next[0],
        weights_next[1][0],
        weights_next[2][0],
        weights_next[3][0],
        vectors_next,
    )


def solution(mesh):
    placed = (
        P(("narrow", "wide"), None),
        P(("narrow", "wide"), None),
        P(("narrow", "wide"), None),
        P(),
        P(None, "wide", None),
        P("wide", None),
        P("wide", None),
        P("wide", None),
        P(),
        P(None, "wide"),
        P(),
        P("wide"),
        P(),
        P("wide"),
        P(),
        P("wide"),
        P(),
        P(),
    )
    return jax.shard_map(
        shards,
        mesh=mesh,
        in_specs=placed,
        out_specs=(
            P(("narrow", "wide"), None),
            P(("narrow", "wide"), None),
            P(None, "wide", None),
            P("wide", None),
            P("wide", None),
            P("wide", None),
            P(),
            P(None, "wide"),
            P(),
            P("wide"),
            P(),
            P("wide"),
            P(),
            P("wide"),
            P(),
            P(),
            P(None, "wide", None),
            P("wide", None),
            P("wide", None),
            P("wide", None),
            P(),
        ),
        check_vma=False,
    )
```

```python
import functools
import math

import jax
import jax.numpy as jnp
import numpy as np
from jax import lax
from jax.experimental import pallas as pl
from jax.experimental.pallas import tpu as pltpu
from jax.sharding import PartitionSpec as P

D = 768
HEADS = 12
HD = 64
FF = 3072
FEAT = 32
STEP = 10
LEN = 1024
SPAN = 256
CHUNKS = 3
GROUPS = 3
WIDTH = 256
FFC = FF // CHUNKS

norm_eps = 1e-05
square_eps = 1e-30
clip_level = 1.0

F32 = jnp.float32
BF16 = jnp.bfloat16
VMEM_LIMIT = 60 * 1024 * 1024
REST_LIMIT = 54 * 1024 * 1024
BACK_LIMIT = 46 * 1024 * 1024


def mm(left, right):
    return lax.dot_general(left, right, (((1,), (0,)), ((), ())), preferred_element_type=F32)


def mm_nt(left, right):
    return lax.dot_general(left, right, (((1,), (1,)), ((), ())), preferred_element_type=F32)


def mm_tn(left, right):
    return lax.dot_general(left, right, (((0,), (0,)), ((), ())), preferred_element_type=F32)


def halves(values):
    high = values.astype(BF16)
    return high, (values - high.astype(F32)).astype(BF16)


TAIL = (
    0.1795078068971634,
    0.17978088557720184,
    0.14234966039657593,
    0.06379217654466629,
    0.0434231162071228,
    -0.261725515127182,
    0.20454804599285126,
    -0.05167665705084801,
)


def normal_parts(values):
    size = jnp.abs(values)
    t = 1.0 / (1.0 + 0.45 * size)
    poly = TAIL[-1]
    for coeff in TAIL[-2::-1]:
        poly = poly * t + coeff
    bell = jnp.exp(-0.5 * values * values)
    tail = poly * t * bell
    return jnp.where(values >= 0, 1.0 - tail, tail), bell * 0.3989422804014327


def transposed(values):
    row = lax.broadcasted_iota(jnp.int32, (256, 256), 0)
    col = lax.broadcasted_iota(jnp.int32, (256, 256), 1)
    eye = (row == col).astype(F32).astype(BF16)
    return mm_nt(eye, values).astype(BF16)


def head_perm():
    perm = np.zeros((WIDTH, WIDTH), np.float32)
    for head in range(4):
        for half in range(2):
            for i in range(32):
                perm[head * 64 + half * 32 + i, half * 128 + head * 32 + i] = 1.0
    return perm


def make_blocks(lengths, base, first, last):
    def step(s, carry):
        count, begin, begin_row, end = carry
        new_end = end + lengths[0, s]
        full = new_end - begin_row > SPAN

        @pl.when(full)
        def _():
            base[count] = begin_row
            first[count] = begin
            last[count] = s - 1

        row = jnp.minimum((end // 16) * 16, LEN - SPAN)
        return (
            jnp.where(full, count + 1, count),
            jnp.where(full, s, begin),
            jnp.where(full, row, begin_row),
            new_end,
        )

    segments = lengths.shape[1]
    zero = jnp.int32(0)
    count, begin, begin_row, _ = lax.fori_loop(0, segments, step, (zero, zero, zero, zero))
    base[count] = begin_row
    first[count] = begin
    last[count] = segments - 1
    return count + 1


def lane_mask(lo, hi, width, dtype):
    lane = lax.broadcasted_iota(jnp.int32, (1, width), 1)
    return ((lane >= lo) & (lane < hi)).astype(F32).astype(dtype)


def value_rows(v_pair, head):
    keep = lane_mask(64 * head, 64 * head + 64, 128, BF16)
    return jnp.concatenate([v_pair * keep, jnp.broadcast_to(keep, v_pair.shape)], axis=1)


def span_mask(onehot, rows, lo, hi):
    member = onehot[rows, :]
    lane = lax.broadcasted_iota(jnp.int32, (1, 128), 1)
    inside = ((lane >= lo) & (lane <= hi)).astype(F32).astype(BF16)
    return mm_nt(member * inside, member).astype(BF16)


def cost(flops, size):
    return pl.CostEstimate(flops=10**6, transcendentals=0, bytes_accessed=10**5)


def row_blocks(body, loop=False):
    if not loop:
        for rows in range(0, LEN, 256):
            body(pl.ds(rows, 256))
        return

    def step(index, carry):
        body(pl.ds(pl.multiple_of(index * 256, 256), 256))
        return carry

    lax.fori_loop(0, LEN // 256, step, 0)


def any_spec():
    return pl.BlockSpec(memory_space=pl.ANY)


def in_copies(place, pieces, dst, sems, unit):
    if len(pieces) == 1:
        rows = dst.shape[1] // 3
        here = pl.ds(unit * rows, rows)
        return [pltpu.make_async_copy(pieces[0].at[:, here], dst.at[:, here], sems.at[unit, 0])]
    z, x, core = place[0], place[1], place[3]
    part, index = (0, unit) if unit < 2 else (4, 0)
    copies = []
    for side in range(2):
        half = core if side == 0 else 1 - core
        for flip in range(2):
            column = x if flip == 0 else 1 - x
            for shift in range(4):
                row = lax.rem(z + 4 - shift, 4) * 2 + column
                start = pl.multiple_of(unit * 96 + half * 48, 16)
                copies.append(
                    pltpu.make_async_copy(
                        pieces[part + 2 * side + flip].at[shift, index],
                        dst.at[row, pl.ds(start, 48)],
                        sems.at[unit, len(copies)],
                    )
                )
    return copies


def flat_copies(place, pieces, dst, sems):
    if len(pieces) == 1:
        return [pltpu.make_async_copy(pieces[0], dst, sems.at[0])]
    z, x, core = place[0], place[1], place[3]
    span = dst.shape[1] // 2
    copies = []
    for side in range(2):
        half = core if side == 0 else 1 - core
        for flip in range(2):
            column = x if flip == 0 else 1 - x
            for shift in range(4):
                row = lax.rem(z + 4 - shift, 4) * 2 + column
                start = pl.multiple_of(half * span, 16)
                copies.append(
                    pltpu.make_async_copy(
                        pieces[2 * side + flip].at[shift],
                        dst.at[row, pl.ds(start, span)],
                        sems.at[len(copies)],
                    )
                )
    return copies


def attend_kernel(count_in, lengths, place, *refs):
    pieces = refs[:count_in]
    (
        x_ref, norm_ref, bias_ref, perm_ref, proj_ref, cos_ref, sin_ref, onehot_ref,
        attn_ref, mixed_ref, a1t_ref, w_ref, wq_ref, wk_ref, qf_ref, kf_ref, v_ref, rden_ref,
        a1, qb, kb, vb, parts, base, first, last, sems,
    ) = refs[count_in:]
    group = pl.program_id(0)

    @pl.when(group == 0)
    def _():
        for unit in range(GROUPS):
            for copy in in_copies(place, pieces, w_ref, sems, unit):
                copy.start()
        def norm_rows(here):
            x = x_ref[here, :].astype(F32)
            centre = x - jnp.mean(x, axis=-1, keepdims=True)
            spread = jnp.mean(centre * centre, axis=-1, keepdims=True)
            a1[here, :] = (
                centre * lax.rsqrt(spread + norm_eps) * norm_ref[0:1, :] + norm_ref[1:2, :]
            ).astype(BF16)

        row_blocks(norm_rows)
        for cols in range(0, D, 256):
            a1t_ref[cols : cols + 256, :] = transposed(a1[:, cols : cols + 256])

    for unit in range(GROUPS):

        @pl.when(group == unit)
        def _():
            for copy in in_copies(place, pieces, w_ref, sems, unit):
                copy.wait()

    count = make_blocks(lengths, base, first, last)
    shard = w_ref.shape[1] // 3
    here = pl.ds(pl.multiple_of(group * shard, 16), shard)
    w = w_ref[:, here, :].reshape(D, D)
    perm = perm_ref[...]
    bias = bias_ref[0]
    proj_both = proj_ref[0]
    proj_high = proj_ref[1, :, :128]
    square = proj_ref[2, :, :128]
    weights = [mm(w[:, WIDTH * i : WIDTH * (i + 1)], perm).astype(BF16) for i in range(2)]

    def feature_rows(here):
        for which, (out_w, out_f, low_f) in enumerate(
            ((wq_ref, qf_ref, qb), (wk_ref, kf_ref, kb))
        ):
            u = (mm(a1[here, :], weights[which]) + bias[which : which + 1, :]) * HD ** (-0.25)
            c = u[:, :128]
            e = u[:, 128:]
            cosine = cos_ref[here, :]
            sine = sin_ref[here, :]
            turned = jnp.concatenate([c * cosine - e * sine, e * cosine + c * sine], axis=1)
            out_w[0, here, :] = turned
            high, low = halves(turned)
            sq_high, sq_low = halves(turned * turned)
            both = mm(high, proj_both)
            logits = (
                both[:, :128] + both[:, 128:] + mm(low, proj_high)
                - (mm(sq_high, square) + mm(sq_low, square))
            )
            phi = jnp.exp(logits) * FEAT ** (-0.5)
            out_f[0, here, :] = phi
            low_f[here, :] = phi.astype(BF16)
        v = mm(a1[here, :], w[:, 2 * WIDTH :]) + bias[2:3, :]
        v_ref[0, here, :] = v
        vb[here, :] = v.astype(BF16)

    row_blocks(feature_rows)
    parts[...] = jnp.zeros_like(parts)

    def one_span(index, carry):
        rows = pl.ds(pl.multiple_of(base[index], 16), SPAN)
        mask = span_mask(onehot_ref, rows, first[index], last[index])
        q = qb[rows, :]
        k = kb[rows, :]
        for pair in range(2):
            v_pair = vb[rows, 128 * pair : 128 * (pair + 1)]
            total = jnp.zeros((SPAN, WIDTH), F32)
            for side in range(2):
                head = 2 * pair + side
                scores = mm_nt(q * lane_mask(32 * head, 32 * head + 32, 128, BF16), k)
                total = total + mm(scores.astype(BF16) * mask, value_rows(v_pair, side))
            parts[pair, rows, :] += total
        return carry

    lax.fori_loop(0, count, one_span, 0)
    for pair in range(2):
        lanes = slice(128 * pair, 128 * (pair + 1))
        inverse = 1.0 / parts[pair, :, 128:]
        rden_ref[0, :, lanes] = inverse
        mixed = parts[pair, :, :128] * inverse
        mixed_ref[0, :, lanes] = mixed
        attn_ref[:, lanes] = mixed.astype(BF16)


def whole_spec(shape, **options):
    return pl.BlockSpec(shape, lambda *_: (0,) * len(shape), **options)


def group_spec(shape):
    return pl.BlockSpec((1,) + shape, lambda g, *_: (g,) + (0,) * len(shape))


def attend(lengths, place, pieces, wide, tokens, norm, bias, perm, proj, cosine, sine, onehot):
    def out(shape, dtype):
        return jax.ShapeDtypeStruct((GROUPS,) + shape, dtype)

    rows_in = 3 * D // wide
    return pl.pallas_call(
        functools.partial(attend_kernel, len(pieces)),
        grid_spec=pltpu.PrefetchScalarGridSpec(
            num_scalar_prefetch=2,
            grid=(GROUPS,),
            in_specs=[any_spec()] * len(pieces)
            + [
                whole_spec((LEN, D)), whole_spec((2, D)), group_spec((3, WIDTH)),
                whole_spec((WIDTH, WIDTH)), whole_spec((3, WIDTH, WIDTH)), whole_spec((LEN, 128)),
                whole_spec((LEN, 128)), whole_spec((LEN, 128)),
            ],
            out_specs=[
                pl.BlockSpec((LEN, WIDTH), lambda g, *_: (0, g)), group_spec((LEN, WIDTH)),
                whole_spec((D, LEN)), whole_spec((wide, rows_in, D)), group_spec((LEN, WIDTH)),
                group_spec((LEN, WIDTH)), group_spec((LEN, 128)), group_spec((LEN, 128)),
                group_spec((LEN, WIDTH)), group_spec((LEN, WIDTH)),
            ],
            scratch_shapes=[
                pltpu.VMEM((LEN, D), BF16),
                pltpu.VMEM((LEN, 128), BF16), pltpu.VMEM((LEN, 128), BF16),
                pltpu.VMEM((LEN, WIDTH), BF16), pltpu.VMEM((2, LEN, WIDTH), F32),
                pltpu.SMEM((32,), jnp.int32), pltpu.SMEM((32,), jnp.int32),
                pltpu.SMEM((32,), jnp.int32), pltpu.SemaphoreType.DMA((GROUPS, 16)),
            ],
        ),
        out_shape=[
            jax.ShapeDtypeStruct((LEN, D), BF16), out((LEN, WIDTH), F32),
            jax.ShapeDtypeStruct((D, LEN), BF16), jax.ShapeDtypeStruct((wide, rows_in, D), BF16),
            out((LEN, WIDTH), F32), out((LEN, WIDTH), F32), out((LEN, 128), F32),
            out((LEN, 128), F32), out((LEN, WIDTH), F32), out((LEN, WIDTH), F32),
        ],
        compiler_params=pltpu.CompilerParams(
            dimension_semantics=("arbitrary",), vmem_limit_bytes=VMEM_LIMIT
        ),
        cost_estimate=cost(20 * 10**9, 40 * 10**6),
        name="attend",
    )(lengths, place, *pieces, tokens, norm, bias, perm, proj, cosine, sine, onehot)


def attend_back_kernel(
    lengths, place, dmixed_ref, mixed_ref, rden_ref, wq_ref, wk_ref, qf_ref, kf_ref, v_ref,
    a1t_ref, w_ref, perm_ref, proj_ref, cos_ref, sin_ref, onehot_ref, ones_ref,
    keep_ref, send_ref, bias_ref, da1_ref,
    qb, kb, dnb, dnh, lift, dqf, dkf, dv, dqkv, base, first, last,
):
    count = make_blocks(lengths, base, first, last)
    qb[...] = qf_ref[0].astype(BF16)
    kb[...] = kf_ref[0].astype(BF16)
    lane = lax.broadcasted_iota(jnp.int32, (1, 128), 1)
    ones = ones_ref[...]
    def lift_rows(here):
        for pair in range(2):
            lanes = slice(128 * pair, 128 * (pair + 1))
            dnum = dmixed_ref[here, lanes] * rden_ref[0, here, lanes]
            high, low = halves(dnum)
            dnb[here, lanes] = high
            part_high, part_low = halves(dnum * mixed_ref[0, here, lanes])
            dden = -mm(jnp.concatenate([part_high, part_low], axis=1), ones)
            den_high, den_low = halves(dden)
            high, low = high.astype(F32), low.astype(F32)
            den_high = pltpu.roll(den_high.astype(F32), 64, 1)
            den_low = pltpu.roll(den_low.astype(F32), 64, 1)
            low_far = pltpu.roll(low, 64, 1)
            v = v_ref[0, here, lanes]
            v_high, v_low = halves(v)
            v_high, v_low = v_high.astype(F32), v_low.astype(F32)
            v_far = pltpu.roll(v_high, 64, 1)
            for side in range(2):
                own = (lane >= 64 * side) & (lane < 64 * side + 64)
                mark = 64 - 64 * side
                rest = jnp.where(lane == mark, den_high, jnp.where(lane == mark + 1, den_low, 0.0))
                both = ((lane == mark) | (lane == mark + 1)).astype(F32)
                head = 2 * pair + side
                dnh[head, here, :128] = jnp.where(own, high, low_far).astype(BF16)
                dnh[head, here, 128:] = jnp.where(own, high, rest).astype(BF16)
                lift[head, here, :128] = jnp.where(own, v_high, v_far).astype(BF16)
                lift[head, here, 128:] = jnp.where(own, v_low, both).astype(BF16)
    row_blocks(lift_rows)
    dqf[...] = jnp.zeros_like(dqf)
    dkf[...] = jnp.zeros_like(dkf)
    dv[...] = jnp.zeros_like(dv)

    def one_span(index, carry):
        rows = pl.ds(pl.multiple_of(base[index], 16), SPAN)
        mask = span_mask(onehot_ref, rows, first[index], last[index])
        q = qb[rows, :]
        k = kb[rows, :]
        q_total = jnp.zeros((SPAN, 128), F32)
        k_total = jnp.zeros((SPAN, 128), F32)
        for pair in range(2):
            lanes = slice(128 * pair, 128 * (pair + 1))
            dn_pair = dnb[rows, lanes]
            v_total = jnp.zeros((SPAN, 128), F32)
            for side in range(2):
                head = 2 * pair + side
                feats = lane_mask(32 * head, 32 * head + 32, 128, BF16)
                q_head = q * feats
                k_head = k * feats
                lifted = lift[head, rows, :]
                dn_head = dnh[head, rows, :]
                scores = mm_nt(k, q_head).astype(BF16) * mask
                dscores = mm_nt(dn_head, lifted).astype(BF16) * mask
                dscores_t = mm_nt(lifted, dn_head).astype(BF16) * mask
                q_total = q_total + mm(dscores, k_head)
                k_total = k_total + mm(dscores_t, q_head)
                own = lane_mask(64 * side, 64 * side + 64, 128, BF16)
                v_total = v_total + mm(scores, dn_pair * own)
            dv[rows, lanes] += v_total
        dqf[rows, :] += q_total
        dkf[rows, :] += k_total
        return carry

    lax.fori_loop(0, count, one_span, 0)
    proj_low = proj_ref[0, :, 128:]
    proj_high = proj_ref[1]
    square = proj_ref[2]
    perm = perm_ref[...]
    def feature_rows(here):
        for which, (w_in, phi_in, dphi) in enumerate(
            ((wq_ref, qf_ref, dqf), (wk_ref, kf_ref, dkf))
        ):
            r = dphi[here, :] * phi_in[0, here, :]
            high, low = halves(r)
            both = jnp.concatenate([high, low], axis=1)
            spread = mm_nt(both, square)
            dw = mm_nt(both, proj_high) + mm_nt(high, proj_low)
            du = (dw - 2.0 * w_in[0, here, :] * spread) * HD ** (-0.25)
            c = du[:, :128]
            e = du[:, 128:]
            cosine = cos_ref[here, :]
            sine = sin_ref[here, :]
            turned = jnp.concatenate([c * cosine + e * sine, e * cosine - c * sine], axis=1)
            dqkv[here, WIDTH * which : WIDTH * (which + 1)] = mm_nt(
                turned.astype(BF16), perm
            ).astype(BF16)

    row_blocks(feature_rows)
    dqkv[:, 2 * WIDTH :] = dv[...].astype(BF16)
    bias_ref[0] = jnp.sum(dqkv[...].astype(F32), axis=0, keepdims=True)
    grad = mm(a1t_ref[...], dqkv[...]).astype(BF16)
    at = pl.program_id(0)
    store_halves(grad, place[3], keep_ref.at[at], send_ref.at[at])
    w = w_ref[...].reshape(D, D)
    fresh = pl.program_id(0) == 0

    @pl.when(fresh)
    def _():
        da1_ref[...] = mm_nt(dqkv[...], w)

    @pl.when(jnp.logical_not(fresh))
    def _():
        da1_ref[...] += mm_nt(dqkv[...], w)


def store_halves(grad, core, keep_ref, send_ref):
    wide, rows = keep_ref.shape[0], D // keep_ref.shape[0]
    half = rows // 2
    parts = grad.reshape(wide, rows, D)
    for cols in range(3):
        block = parts[:, :, WIDTH * cols : WIDTH * (cols + 1)]
        here = pl.ds(half * cols, half)

        @pl.when(core == 0)
        def _():
            keep_ref[:, here, :] = block[:, :half]
            send_ref[:, here, :] = block[:, half:]

        @pl.when(core == 1)
        def _():
            keep_ref[:, here, :] = block[:, half:]
            send_ref[:, here, :] = block[:, :half]


def attend_back(
    lengths, place, wide, dmixed, saved, a1t, w_in, perm, proj, cosine, sine, onehot, ones
):
    mixed, rden, wq, wk, qf, kf, v = saved

    def by_group(shape):
        return pl.BlockSpec((1,) + shape, lambda g, *_: (g,) + (0,) * len(shape))

    rows_in = D // wide
    half = struct((GROUPS, wide, 3 * rows_in // 2, WIDTH), BF16)
    half_spec = once(half.shape)
    if wide > 1:
        half = pltpu.VMEM(half.shape, BF16)
        half_spec = pl.BlockSpec(memory_space=pltpu.VMEM)
    return pl.pallas_call(
        attend_back_kernel,
        grid_spec=pltpu.PrefetchScalarGridSpec(
            num_scalar_prefetch=2,
            grid=(GROUPS,),
            in_specs=[
                pl.BlockSpec((LEN, WIDTH), lambda g, *_: (0, g)),
                by_group((LEN, WIDTH)), by_group((LEN, WIDTH)), by_group((LEN, WIDTH)),
                by_group((LEN, WIDTH)), by_group((LEN, 128)), by_group((LEN, 128)),
                by_group((LEN, WIDTH)), once((D, LEN)),
                pl.BlockSpec((wide, rows_in, D), lambda g, *_: (0, g, 0)),
                once((WIDTH, WIDTH)), once((3, WIDTH, WIDTH)), once((LEN, 128)),
                once((LEN, 128)), once((LEN, 128)), once((WIDTH, 128)),
            ],
            out_specs=[
                half_spec, half_spec, group_spec((1, D)),
                whole_spec((LEN, D)),
            ],
            scratch_shapes=[
                pltpu.VMEM((LEN, 128), BF16), pltpu.VMEM((LEN, 128), BF16),
                pltpu.VMEM((LEN, WIDTH), BF16), pltpu.VMEM((4, LEN, WIDTH), BF16),
                pltpu.VMEM((4, LEN, WIDTH), BF16), pltpu.VMEM((LEN, 128), F32),
                pltpu.VMEM((LEN, 128), F32), pltpu.VMEM((LEN, WIDTH), F32),
                pltpu.VMEM((LEN, D), BF16),
                pltpu.SMEM((32,), jnp.int32), pltpu.SMEM((32,), jnp.int32),
                pltpu.SMEM((32,), jnp.int32),
            ],
        ),
        out_shape=[
            half, half, struct((GROUPS, 1, D), F32), struct((LEN, D), F32),
        ],
        compiler_params=pltpu.CompilerParams(
            dimension_semantics=("arbitrary",), vmem_limit_bytes=BACK_LIMIT
        ),
        cost_estimate=cost(GROUPS * 12 * 10**9, GROUPS * 20 * 10**6),
        name="attend_back",
    )(
        lengths, place, dmixed, mixed, rden, wq, wk, qf, kf, v, a1t, w_in, perm, proj, cosine,
        sine, onehot, ones,
    )


def chunk_step(
    place, wide, bias_up, dy_ref, a2, a2t, dyt, up, down, act, dhidden, y, back, outs, dbias_ref,
    fresh,
):
    rows_up = D // wide
    rows_down = FFC // wide
    dbias_ref[0] = jnp.zeros((1, FFC), F32)

    def chunk_rows(here):
        hidden = mm(a2[here, :], up[...]) + bias_up
        below, density = normal_parts(hidden)
        act_now = (hidden * below).astype(BF16)
        act[here, :] = act_now
        dact = mm_nt(dy_ref[here, :], down[...])
        dhidden_now = (dact * (below + hidden * density)).astype(BF16)
        dhidden[here, :] = dhidden_now
        dbias_ref[0] += jnp.sum(dhidden_now.astype(F32), axis=0, keepdims=True)
        if fresh:
            y[here, :] = mm(act_now, down[...])
            back[here, :] = mm_nt(dhidden_now, up[...])
        else:
            y[here, :] += mm(act_now, down[...])
            back[here, :] += mm_nt(dhidden_now, up[...])

    row_blocks(chunk_rows, True)
    grad_up = mm(a2t[...], dhidden[...]).astype(BF16).reshape(wide, rows_up, FFC)
    grad_down = mm(dyt[...], act[...]).astype(BF16)
    core = place[3]

    def store_up(ref):
        for cols in range(4):
            ref[:, rows_up * cols : rows_up * (cols + 1), :] = grad_up[
                :, :, WIDTH * cols : WIDTH * (cols + 1)
            ]

    def store_down(ref):
        if wide == 1:
            for cols in range(4):
                ref[0, D * cols : D * (cols + 1), :] = grad_down[
                    :, WIDTH * cols : WIDTH * (cols + 1)
                ]
            return
        for shard in range(wide):
            block = grad_down[:, rows_down * shard : rows_down * (shard + 1)]
            ref[shard, :, :128] = block[: D // 2]
            ref[shard, :, 128:] = block[D // 2 :]

    for when, keep_ref, send_ref in outs:
        for side in range(2):
            now = core == side

            @pl.when(now if when is None else now & when)
            def _():
                store_up(keep_ref if side == 0 else send_ref)
                store_down(send_ref if side == 0 else keep_ref)


def load_up(flat, at, up, wide):
    rows = D // wide
    for cols in range(4):
        here = pl.ds(at + rows * cols, rows)
        up[:, WIDTH * cols : WIDTH * (cols + 1)] = flat[:, here, :].reshape(D, WIDTH)


def load_down(flat, at, down, wide):
    rows = FFC // wide
    for cols in range(3):
        here = pl.ds(at + rows * cols, rows)
        down[:, WIDTH * cols : WIDTH * (cols + 1)] = flat[:, here, :].reshape(FFC, WIDTH)


def middle_first_kernel(wide, count_in, place, *refs):
    pieces = refs[:count_in]
    (
        x_ref, attn_ref, dy_ref, rows_ref, bias_up_ref,
        x1_ref, a2_ref, a2t_ref, dyt_ref, y_ref, back_ref, out_ref, keep_ref, send_ref, dbias_ref,
        flat, up, down, act, dhidden, sems,
    ) = refs[count_in:]
    copies = flat_copies(place, pieces, flat, sems)
    for copy in copies:
        copy.start()
    for cols in range(0, D, 256):
        dyt_ref[cols : cols + 256, :] = transposed(dy_ref[:, cols : cols + 256])
    for copy in copies:
        copy.wait()
    half_out = D // wide // 2
    half_flat = flat.shape[1] // 2
    for cols in range(3):
        upper = flat[:, half_out * cols : half_out * (cols + 1), :]
        lower = flat[:, half_flat + half_out * cols : half_flat + half_out * (cols + 1), :]
        out_ref[:, WIDTH * cols : WIDTH * (cols + 1)] = jnp.concatenate(
            [upper, lower], axis=1
        ).reshape(D, WIDTH)
    def norm_rows(here):
        x1 = x_ref[here, :].astype(F32) + (mm(attn_ref[here, :], out_ref[...]) + rows_ref[7:8, :])
        x1_ref[here, :] = x1
        centre = x1 - jnp.mean(x1, axis=-1, keepdims=True)
        spread = jnp.mean(centre * centre, axis=-1, keepdims=True)
        a2_ref[here, :] = (
            centre * lax.rsqrt(spread + norm_eps) * rows_ref[2:3, :] + rows_ref[3:4, :]
        ).astype(BF16)

    row_blocks(norm_rows)
    for cols in range(0, D, 256):
        a2t_ref[cols : cols + 256, :] = transposed(a2_ref[:, cols : cols + 256])
    load_up(flat, 3 * half_out, up, wide)
    load_down(flat, half_flat + 3 * half_out, down, wide)
    chunk_step(
        place, wide, bias_up_ref[0], dy_ref, a2_ref, a2t_ref, dyt_ref, up, down, act, dhidden,
        y_ref, back_ref, [(None, keep_ref, send_ref)], dbias_ref, True,
    )


def middle_rest_kernel(wide, count_in, place, *refs):
    pieces = refs[:count_in]
    (
        dy_ref, a2_ref, a2t_ref, dyt_ref, bias_up_ref, attn_ref, out_ref, rows_ref,
        y_in, back_in, x1_in,
        block_ref, dx1_ref, dmixed_ref, okeep_ref, osend_ref, vec_ref,
        keep_ref, send_ref, dbias_ref,
        flat, up, down, act, dhidden, back, dbranch, sems, flat_sems,
    ) = refs[count_in:]
    step = pl.program_id(0)
    y_copy = pltpu.make_async_copy(y_in, block_ref, sems.at[0])
    back_copy = pltpu.make_async_copy(back_in, back, sems.at[1])
    x1_copy = pltpu.make_async_copy(x1_in, dx1_ref, sems.at[2])

    def chunk_copies(chunk, side):
        if count_in == 1:
            return [
                pltpu.make_async_copy(
                    pieces[0].at[chunk], flat.at[chunk], flat_sems.at[chunk, 0]
                )
            ]
        copies = []
        for flip in range(2):
            column = place[1] if flip == 0 else 1 - place[1]
            for shift in range(4):
                shard = lax.rem(place[0] + 4 - shift, 4) * 2 + column
                copies.append(
                    pltpu.make_async_copy(
                        pieces[2 * side + flip].at[shift], flat.at[chunk, shard],
                        flat_sems.at[chunk, len(copies)],
                    )
                )
        return copies

    def fetch(chunk):
        for side in range(2):

            @pl.when((place[3] == chunk) if side == 0 else (place[3] != chunk))
            def _():
                if side == 0 or count_in > 1:
                    for copy in chunk_copies(chunk, side):
                        copy.start()

    def arrived(chunk):
        for copy in chunk_copies(chunk, 0):
            copy.wait()

    @pl.when(step == 0)
    def _():
        if count_in == 1:
            for chunk in range(2):
                for copy in chunk_copies(chunk, 0):
                    copy.start()
        else:
            fetch(0)
        y_copy.start()
        back_copy.start()
        if count_in > 1:
            fetch(1)
        x1_copy.start()
        arrived(0)
        y_copy.wait()
        back_copy.wait()

    @pl.when(step == 1)
    def _():
        arrived(1)

    load_up(flat.at[step], 0, up, wide)
    load_down(flat.at[step], 4 * (D // wide), down, wide)
    chunk_step(
        place, wide, bias_up_ref[0], dy_ref, a2_ref, a2t_ref, dyt_ref, up, down, act, dhidden,
        block_ref, back, [(None, keep_ref.at[step], send_ref.at[step])], dbias_ref, False,
    )

    @pl.when(step == 1)
    def _():
        x1_copy.wait()
        vec_ref[...] = jnp.zeros_like(vec_ref)

        def last_rows(here):
            x1 = dx1_ref[here, :]
            block_ref[here, :] = x1 + (block_ref[here, :] + rows_ref[8:9, :])
            dn = back[here, :]
            dy = dy_ref[here, :].astype(F32)
            centre = x1 - jnp.mean(x1, axis=-1, keepdims=True)
            spread = jnp.mean(centre * centre, axis=-1, keepdims=True)
            scale = lax.rsqrt(spread + norm_eps)
            zh = centre * scale
            vec_ref[0:1, :] += jnp.sum(dn * zh, axis=0, keepdims=True)
            vec_ref[1:2, :] += jnp.sum(dn, axis=0, keepdims=True)
            e = dn * rows_ref[2:3, :]
            dz = (
                e
                - jnp.mean(e, axis=-1, keepdims=True)
                - zh * jnp.mean(e * zh, axis=-1, keepdims=True)
            ) * scale
            dx1 = dy + dz
            dx1_ref[here, :] = dx1
            low = dx1.astype(BF16)
            dbranch[here, :] = low
            vec_ref[2:3, :] += jnp.sum(low.astype(F32), axis=0, keepdims=True)
            vec_ref[3:4, :] += jnp.sum(dy, axis=0, keepdims=True)
            dmixed_ref[here, :] = mm_nt(low, out_ref[...])

        row_blocks(last_rows)
        for cols in range(0, D, 256):
            up[cols : cols + 256, :] = transposed(attn_ref[:, cols : cols + 256])
        store_halves(mm(up[...], dbranch[...]).astype(BF16), place[3], okeep_ref, osend_ref)


def once(shape):
    return whole_spec(shape, pipeline_mode=pl.Buffered(1))


def struct(shape, dtype):
    return jax.ShapeDtypeStruct(shape, dtype)


def weight_scratch():
    return [
        pltpu.VMEM((D, FFC), BF16), pltpu.VMEM((FFC, D), BF16), pltpu.VMEM((LEN, FFC), BF16),
        pltpu.VMEM((LEN, FFC), BF16),
    ]


def middle_first(place, wide, pieces, tokens, attn, cotangent, vectors, bias_up):
    rows_flat = 3 * D // wide + 2 * FFC * D // (WIDTH * wide)
    half = (wide, FFC * D // (WIDTH * wide), WIDTH)
    outs = [
        struct((LEN, D), F32), struct((LEN, D), BF16), struct((D, LEN), BF16),
        struct((D, LEN), BF16), struct((LEN, D), F32), struct((LEN, D), F32),
        struct((D, D), BF16), struct(half, BF16), struct(half, BF16), struct((1, 1, FFC), F32),
    ]
    return pl.pallas_call(
        functools.partial(middle_first_kernel, wide, len(pieces)),
        grid_spec=pltpu.PrefetchScalarGridSpec(
            num_scalar_prefetch=1,
            grid=(1,),
            in_specs=[any_spec()] * len(pieces)
            + [
                once((LEN, D)), once((LEN, D)), once((LEN, D)), once((13, D)),
                pl.BlockSpec((1, 1, FFC), lambda *_: (0, 0, 0)),
            ],
            out_specs=[once(out.shape) for out in outs],
            scratch_shapes=[pltpu.VMEM((wide, rows_flat, WIDTH), BF16)]
            + weight_scratch()
            + [pltpu.SemaphoreType.DMA((16,))],
        ),
        out_shape=outs,
        compiler_params=pltpu.CompilerParams(
            dimension_semantics=("arbitrary",), vmem_limit_bytes=VMEM_LIMIT
        ),
        cost_estimate=cost(14 * 10**9, 30 * 10**6),
        name="middle_first",
    )(place, *pieces, tokens, attn, cotangent, vectors, bias_up)


def middle_rest(place, wide, pieces, cotangent, state, bias_up, attn, w_out, vectors, sums):
    a2, a2t, dyt = state
    half = (wide, FFC * D // (WIDTH * wide), WIDTH)
    out_half = (wide, 3 * D // (2 * wide), WIDTH)
    outs = [
        struct((LEN, D), F32), struct((LEN, D), F32), struct((LEN, D), F32),
        struct(out_half, BF16), struct(out_half, BF16), struct((8, D), F32),
        struct((2,) + half, BF16), struct((2,) + half, BF16), struct((2, 1, FFC), F32),
    ]
    out_specs = [once(out.shape) for out in outs[:8]] + [group_spec((1, FFC))]
    if wide > 1:
        for index in (3, 4, 6, 7):
            outs[index] = pltpu.VMEM(outs[index].shape, BF16)
            out_specs[index] = pl.BlockSpec(memory_space=pltpu.VMEM)
    rows_flat = 2 * FFC * D // (WIDTH * wide)
    return pl.pallas_call(
        functools.partial(middle_rest_kernel, wide, len(pieces)),
        grid_spec=pltpu.PrefetchScalarGridSpec(
            num_scalar_prefetch=1,
            grid=(2,),
            in_specs=[any_spec()] * len(pieces)
            + [
                once((LEN, D)), once((LEN, D)), once((D, LEN)), once((D, LEN)),
                pl.BlockSpec((1, 1, FFC), lambda j, *_: (j + 1, 0, 0)),
                once((LEN, D)), once((D, D)), once((13, D)),
                any_spec(), any_spec(), any_spec(),
            ],
            out_specs=out_specs,
            scratch_shapes=[pltpu.VMEM((2, wide, rows_flat, WIDTH), BF16)]
            + weight_scratch()
            + [
                pltpu.VMEM((LEN, D), F32), pltpu.VMEM((LEN, D), BF16),
                pltpu.SemaphoreType.DMA((3,)), pltpu.SemaphoreType.DMA((2, 8)),
            ],
        ),
        out_shape=outs,
        compiler_params=pltpu.CompilerParams(
            dimension_semantics=("arbitrary",), vmem_limit_bytes=REST_LIMIT
        ),
        cost_estimate=cost(28 * 10**9, 40 * 10**6),
        name="middle_rest",
    )(place, *pieces, cotangent, a2, a2t, dyt, bias_up, attn, w_out, vectors, *sums)


def input_kernel(
    wide, x_ref, dx1_ref, da1_ref, rows_ref, middle_ref, bias_in_ref, bias_first_ref, bias_rest_ref,
    out_ref, vec_ref,
):
    gain = rows_ref[0:1, :]
    x = x_ref[...].astype(F32)
    dn = da1_ref[...]
    centre = x - jnp.mean(x, axis=-1, keepdims=True)
    spread = jnp.mean(centre * centre, axis=-1, keepdims=True)
    scale = lax.rsqrt(spread + norm_eps)
    zh = centre * scale
    e = dn * gain
    dz = (
        e - jnp.mean(e, axis=-1, keepdims=True) - zh * jnp.mean(e * zh, axis=-1, keepdims=True)
    ) * scale
    out_ref[...] = dx1_ref[...] + dz

    @pl.when(pl.program_id(0) == 0)
    def _():
        vec_ref[...] = jnp.zeros_like(vec_ref)
        vec_ref[2:4, :] = middle_ref[0:2, :]
        vec_ref[7:9, :] = middle_ref[2:4, :]
        for group in range(GROUPS):
            lanes = slice(WIDTH * group, WIDTH * (group + 1))
            for which in range(3):
                vec_ref[4 + which : 5 + which, lanes] = bias_in_ref[
                    group, :, WIDTH * which : WIDTH * (which + 1)
                ]
        for chunk in range(CHUNKS):
            for part in range(8):
                value = (
                    bias_first_ref[0] if chunk == 0 else bias_rest_ref[chunk - 1]
                )[:, 128 * part : 128 * (part + 1)]
                start = FFC * chunk + 128 * part if wide == 1 else 384 * part + 128 * chunk
                row, lane = 9 + start // D, start % D
                vec_ref[row : row + 1, lane : lane + 128] = value

    vec_ref[0:1, :] += jnp.sum(dn * zh, axis=0, keepdims=True)
    vec_ref[1:2, :] += jnp.sum(dn, axis=0, keepdims=True)


def input_side(wide, tokens, dx1, da1, vectors, middle_vec, bias_in, bias_first, bias_rest):
    block = pl.BlockSpec((256, D), lambda i: (i, 0))
    return pl.pallas_call(
        functools.partial(input_kernel, wide),
        grid=(LEN // 256,),
        in_specs=[
            block, block, block, whole_spec((13, D)), whole_spec((8, D)),
            whole_spec((GROUPS, 1, D)), whole_spec((1, 1, FFC)), whole_spec((2, 1, FFC)),
        ],
        out_specs=[block, whole_spec((16, D))],
        out_shape=[struct((LEN, D), F32), struct((16, D), F32)],
        compiler_params=pltpu.CompilerParams(dimension_semantics=("arbitrary",)),
        cost_estimate=cost(10**6, 12 * 10**6),
        name="input_side",
    )(tokens, dx1, da1, vectors, middle_vec, bias_in, bias_first, bias_rest)


def tables(lengths, projection):
    ends = jnp.cumsum(lengths[0])
    starts = ends - lengths[0]
    place = jnp.arange(LEN, dtype=jnp.int32)
    member = (place[:, None] >= starts[None, :]) & (place[:, None] < ends[None, :])
    offset = jnp.sum(jnp.where(member, starts[None, :], 0), axis=1)
    position = (place - offset).astype(F32)
    freq = 10000.0 ** (-jnp.arange(32, dtype=F32) / 32)
    angles = position[:, None] * jnp.tile(freq, 4)[None, :]
    onehot = jnp.pad(member.astype(BF16), ((0, 0), (0, 128 - member.shape[1])))
    eye = jnp.asarray(np.eye(4, dtype=np.float32))
    lifted = jnp.einsum("hif,ab->haibf", projection.reshape(2, 32, FEAT), eye)
    lifted = lifted.reshape(WIDTH, 128)
    rounded = lax.reduce_precision(lifted, 8, 7)
    high, low = rounded.astype(BF16), (lifted - rounded).astype(BF16)
    square = np.zeros((2, 4, 32, 4, 32), np.float32)
    for head in range(4):
        square[:, head, :, head, :] = 0.5
    square = jnp.asarray(square.reshape(WIDTH, 128), BF16)
    proj = jnp.stack(
        [
            jnp.concatenate([high, low], axis=1),
            jnp.concatenate([high, high], axis=1),
            jnp.concatenate([square, square], axis=1),
        ]
    )
    return jnp.cos(angles), jnp.sin(angles), onehot, proj


def wide_perm(shift_z, flip_x):
    pairs = []
    for z in range(4):
        for x in range(2):
            target_x = 1 - x if flip_x else x
            pairs.append((2 * z + x, 2 * ((z + shift_z) % 4) + target_x))
    return pairs


def narrow_perm(flip_y, flip_core):
    pairs = []
    for y in range(2):
        for core in range(2):
            pairs.append(
                (2 * y + core, 2 * (1 - y if flip_y else y) + (1 - core if flip_core else core))
            )
    return pairs


def over_z(values, shift):
    return lax.ppermute(values, "wide", wide_perm(shift, False))


def over_x(values):
    return lax.ppermute(values, "wide", wide_perm(0, True))


def over_far(values, bit):
    return lax.ppermute(values, "wide", [(w, w ^ bit) for w in range(8)])


def over_y(values):
    return lax.ppermute(values, "narrow", narrow_perm(True, False))


def over_core(values):
    return lax.ppermute(values, "narrow", narrow_perm(False, True))


def tie(*values):
    return lax.optimization_barrier(values)


def special():
    return lax.axis_size("wide") == 8 and lax.axis_size("narrow") == 4


def sum_wide(values):
    if not special():
        return lax.psum(values, "wide")
    for perm in (wide_perm(0, True), [(w, w ^ 2) for w in range(8)], [(w, w ^ 4) for w in range(8)]):
        values = values + lax.ppermute(values, "wide", perm)
    return values


def sum_narrow(values):
    if not special():
        return lax.psum(values, "narrow")
    pair = values + over_core(values)
    return pair + over_y(pair)


def along_z(mine):
    return jnp.stack([mine] + [over_z(mine, shift) for shift in (1, 2, 3)])


def small_call(kernel, name, place, operands, outs):
    return pl.pallas_call(
        kernel,
        grid_spec=pltpu.PrefetchScalarGridSpec(
            num_scalar_prefetch=1,
            grid=(1,),
            in_specs=[once(value.shape) for value in operands],
            out_specs=[once(out.shape) for out in outs],
        ),
        out_shape=outs,
        compiler_params=pltpu.CompilerParams(
            dimension_semantics=("arbitrary",), vmem_limit_bytes=VMEM_LIMIT
        ),
        cost_estimate=cost(10**6, sum(4 * math.prod(v.shape) for v in operands + outs)),
        name=name,
    )(place, *operands)


def held_call(kernel, name, place, operands, outs, held=None, flops=10**6):
    here = pl.BlockSpec(memory_space=pltpu.VMEM)
    held = len(outs) if held is None else held
    return pl.pallas_call(
        kernel,
        in_specs=[pl.BlockSpec(memory_space=pltpu.SMEM)] + [here] * len(operands),
        out_specs=[here] * len(outs),
        out_shape=[
            pltpu.VMEM(out.shape, out.dtype) if index < held else out
            for index, out in enumerate(outs)
        ],
        compiler_params=pltpu.CompilerParams(vmem_limit_bytes=24 * 1024 * 1024),
        cost_estimate=pl.CostEstimate(flops=flops, transcendentals=0, bytes_accessed=10**5),
        name=name,
    )(place, *[pltpu.with_memory_space_constraint(value, pltpu.VMEM) for value in operands])


def pick_kernel(
    place, in_ref, out_ref, up_ref, down_ref, near_ref, last_ref, first_ref, rest_ref
):
    core = place[3]
    here = pl.ds(pl.multiple_of(48 * core, 16), 48)
    for group in range(GROUPS):
        ref, index = (near_ref, group) if group < 2 else (last_ref, 0)
        for which in range(3):
            ref[index, :, WIDTH * which : WIDTH * (which + 1)] = in_ref[
                which, here, WIDTH * group : WIDTH * (group + 1)
            ].astype(BF16)
    for cols in range(3):
        first_ref[48 * cols : 48 * (cols + 1), :] = out_ref[
            here, WIDTH * cols : WIDTH * (cols + 1)
        ].astype(BF16)

    def put_up(ref, at, chunk):
        for cols in range(4):
            rows = slice(at + 96 * cols, at + 96 * (cols + 1))
            for side in range(2):
                start = 384 * (2 * cols + side) + 128 * chunk
                ref[rows, 128 * side : 128 * (side + 1)] = up_ref[:, start : start + 128].astype(
                    BF16
                )

    def put_down(ref, at, chunk):
        for cols in range(3):
            ref[at + 128 * cols : at + 128 * (cols + 1), :] = down_ref[
                128 * chunk : 128 * (chunk + 1), WIDTH * cols : WIDTH * (cols + 1)
            ].astype(BF16)

    for side in range(2):

        @pl.when(core == side)
        def _():
            if side == 0:
                put_up(first_ref, 144, 0)
            else:
                put_down(first_ref, 144, 0)

        @pl.when(core == side)
        def _():
            put_up(rest_ref, 0, 1 + side)
            put_down(rest_ref, 384, 1 + side)


def chunk_of(ref, chunk, shard):
    return ref[chunk, shard] if len(ref.shape) == 4 else ref[shard]


def first_sum_kernel(place, *refs):
    send_ref, keep_ref = refs[-2:]
    x = place[1]
    at = 0
    for index in range(0, len(refs) - 2, 2):
        own, got = refs[index], refs[index + 1]
        for part in range(own.shape[0] if len(own.shape) == 4 and own.shape[0] == 3 else 1):
            rows = own.shape[-2]
            here = pl.ds(at, rows)
            for z in range(4):
                for out, side in ((keep_ref, x), (send_ref, 1 - x)):
                    out[z, here, :] = (
                        chunk_of(own, part, 2 * z + side).astype(F32)
                        + chunk_of(got, part, 2 * z + side).astype(F32)
                    ).astype(BF16)
            at += rows


def first_sum(place, pairs):
    rows = sum(
        own.shape[-2] * (own.shape[0] if own.ndim == 4 and own.shape[0] == 3 else 1)
        for own, _ in pairs
    )
    return held_call(
        first_sum_kernel, "first_sum", place, [value for pair in pairs for value in pair],
        [struct((4, rows, WIDTH), BF16)] * 2,
    )


def first_sum_y_kernel(place, own, got, send, keep):
    y = place[2]
    for group in range(GROUPS):
        here = pl.ds(144 * group, 144)
        for shard in range(8):
            total = own[group, shard].astype(F32) + got[group, shard].astype(F32)
            left, right = total[:, :128].astype(BF16), total[:, 128:].astype(BF16)
            keep[shard, here, :] = jnp.where(y == 0, left, right)
            send[shard, here, :] = jnp.where(y == 0, right, left)


def split_x_kernel(place, own, got, send, keep):
    x = place[1]
    for z in range(4):
        for out, side in ((keep, x), (send, 1 - x)):
            out[z] = (own[2 * z + side].astype(F32) + got[2 * z + side].astype(F32)).astype(BF16)


def second_sum_kernel(place, own_ref, got_ref, *outs):
    z = place[0]
    for shift, out in enumerate(outs):
        there = lax.rem(z + shift, 4)
        out[...] = (own_ref[there].astype(F32) + got_ref[there].astype(F32)).astype(BF16)


def second_sum(place, own, got):
    outs = [struct(own.shape[1:], BF16)] * 4
    return held_call(second_sum_kernel, "second_sum", place, [own, got], outs)


def z_sum_kernel(place, *refs):
    total = refs[0][...].astype(F32)
    for ref in refs[1:4]:
        total = total + ref[...].astype(F32)
    rows = refs[0].shape[0]
    refs[-1][:rows, :] = total.astype(refs[-1].dtype)
    if len(refs) == 7:
        refs[-1][rows:, :] = (refs[4][...].astype(F32) + refs[5][...].astype(F32)).astype(BF16)


def z_sum(place, parts, below=(), got=None):
    if got is None:
        got = [over_z(parts[shift], shift) for shift in (1, 2, 3)]
    rows = parts[0].shape[0] + (below[0].shape[0] if below else 0)
    return held_call(
        z_sum_kernel, "z_sum", place, [parts[0]] + got + list(below),
        [struct((rows, parts[0].shape[1]), BF16 if below else F32)],
        flops=3 * 10**10 if below else 10**6,
    )[0]


def first_sum_z_kernel(place, *refs):
    z = place[0]
    outs = refs[-4:]
    for shift, out in enumerate(outs):
        there = lax.rem(z + shift, 4) * 2
        at = 0
        for index in range(0, len(refs) - 4, 2):
            own, got = refs[index], refs[index + 1]
            rows = own.shape[-2]
            for x in range(2):
                out[x, at : at + rows, :] = (
                    chunk_of(own, 1, there + x).astype(F32)
                    + chunk_of(got, 1, there + x).astype(F32)
                ).astype(BF16)
            at += rows


def first_sum_z(place, pairs):
    rows = sum(own.shape[-2] for own, _ in pairs)
    return held_call(
        first_sum_z_kernel, "first_sum_z", place, [value for pair in pairs for value in pair],
        [struct((2, rows, WIDTH), BF16)] * 4,
    )


def split_sum_kernel(place, *refs):
    keep, send = refs[-2:]
    x = place[1]
    for out, at in ((keep, x), (send, 1 - x)):
        total = refs[0][at].astype(F32)
        for ref in refs[1:4]:
            total = total + ref[at].astype(F32)
        out[...] = total.astype(BF16)


def split_sum(place, parts):
    return held_call(
        split_sum_kernel, "split_sum", place, parts, [struct(parts[0].shape[1:], BF16)] * 2
    )


def to_row(column):
    size = column.shape[0]
    eye = lax.broadcasted_iota(jnp.int32, (size, size), 0) == lax.broadcasted_iota(
        jnp.int32, (size, size), 1
    )
    return jnp.sum(jnp.where(eye, column, 0.0), axis=0, keepdims=True)


def to_column(row):
    size = row.shape[1]
    eye = lax.broadcasted_iota(jnp.int32, (size, size), 0) == lax.broadcasted_iota(
        jnp.int32, (size, size), 1
    )
    return jnp.sum(jnp.where(eye, row, 0.0), axis=1, keepdims=True)


DECAY = 1.0 - STEP ** (-0.8)


def lane_values(values):
    lane = lax.broadcasted_iota(jnp.int32, (1, D), 1)
    row = jnp.zeros((1, D), F32)
    for index, value in enumerate(values):
        row = jnp.where(lane == index, value, row)
    return row


def moments(grad, rows_old):
    plain = grad * grad
    squares = plain + square_eps
    mean = jnp.sum(squares, axis=1, keepdims=True) * (1.0 / grad.shape[1])
    rows_new = DECAY * rows_old + (1.0 - DECAY) * to_row(mean)
    total = jnp.sum(rows_new, axis=1, keepdims=True)
    divided = jnp.sum(plain * to_column(1.0 / rows_new), axis=0, keepdims=True)
    return rows_new, total, jnp.sum(squares, axis=0, keepdims=True), divided


def ffn_moments_kernel(
    place, own, got, up_rows, down_rows, out_rows,
    up_grad, down_grad, out_grad, up_rows_new, down_rows_new, out_rows_new, sums,
):
    core = place[3]

    def collect(low, high):
        for chunk in range(CHUNKS):
            at = 384 * chunk
            for cols in range(4):
                for side in range(2):
                    start = 384 * (2 * cols + side) + 128 * chunk
                    up_grad[:, start : start + 128] = low[
                        at + 96 * cols : at + 96 * (cols + 1), 128 * side : 128 * (side + 1)
                    ]
            for side in range(2):
                down_grad[128 * chunk : 128 * (chunk + 1), 384 * side : 384 * (side + 1)] = (
                    jnp.transpose(high[at : at + 384, 128 * side : 128 * (side + 1)])
                )
        for cols in range(3):
            lanes = slice(WIDTH * cols, WIDTH * (cols + 1))
            at = 1152 + 48 * cols
            out_grad[:48, lanes] = low[at : at + 48, :]
            out_grad[48:, lanes] = high[at : at + 48, :]

    @pl.when(core == 0)
    def _():
        collect(own, got)

    @pl.when(core == 1)
    def _():
        collect(got, own)

    up_new, up_total, up_sums, up_divided = moments(up_grad[...], up_rows[...])
    down_new, down_total, down_sums, down_divided = moments(down_grad[...], down_rows[...])
    out_new, out_total, out_sums, out_divided = moments(out_grad[...], out_rows[...])
    up_rows_new[...] = up_new
    down_rows_new[...] = down_new
    out_rows_new[...] = out_new
    for part in range(4):
        lanes = slice(D * part, D * (part + 1))
        sums[part : part + 1, :] = up_sums[:, lanes]
        sums[4 + part : 5 + part, :] = up_divided[:, lanes]
    sums[8:9, :] = down_sums
    sums[9:10, :] = down_divided
    sums[10:11, :] = out_sums
    sums[11:12, :] = out_divided
    sums[12:13, :] = lane_values([up_total, down_total, out_total])
    sums[13:16, :] = jnp.zeros((3, D), F32)


def in_moments_kernel(
    place, own, own_y, other, other_y, rows_old, vector, vector_far, ffn_sums, grad, rows_new,
    sums,
):
    def collect(low, high):
        for group in range(GROUPS):
            for which in range(3):
                rows = slice(144 * group + 48 * which, 144 * group + 48 * (which + 1))
                for side in range(2):
                    start = WIDTH * group + 128 * side
                    grad[which, :48, start : start + 128] = low[side][rows, :]
                    grad[which, 48:, start : start + 128] = high[side][rows, :]

    for core in range(2):
        for y in range(2):

            @pl.when((place[3] == core) & (place[2] == y))
            def _():
                mine = (own, own_y) if y == 0 else (own_y, own)
                far = (other, other_y) if y == 0 else (other_y, other)
                collect(mine if core == 0 else far, far if core == 0 else mine)

    totals = []
    for which in range(3):
        new, total, columns, divided = moments(grad[which], rows_old[which : which + 1, :])
        rows_new[which : which + 1, :] = new
        sums[which : which + 1, :] = columns
        sums[3 + which : 4 + which, :] = divided
        totals.append(total)
    sums[6:7, :] = lane_values(totals)
    sums[7:8, :] = jnp.zeros((1, D), F32)
    sums[8:24, :] = vector[...] + vector_far[...]
    sums[24:40, :] = ffn_sums[...]


def matrix_step(weight, grad, rows, cols, total, col_sums, divided, rows_full, rate):
    cols_new = DECAY * cols + (1.0 - DECAY) * col_sums * (1.0 / rows_full)
    mean = total * (1.0 / rows_full)
    square_sum = mean * jnp.sum(divided / cols_new, axis=1, keepdims=True)
    rms = jnp.sqrt(square_sum * (1.0 / (rows_full * grad.shape[1])))
    factor = to_column(lax.rsqrt(rows / mean)) * (rate / jnp.maximum(1.0, rms / clip_level))
    return cols_new, weight - grad * factor * lax.rsqrt(cols_new)


def finish_kernel(
    place, inward, up, down, out, in_grad, up_grad, down_grad, out_grad, in_rows, up_rows,
    down_rows, out_rows, in_cols, up_cols, down_cols, out_cols, sums, vectors, vector_state,
    in_cols_new, up_cols_new, down_cols_new, out_cols_new, in_next, up_next, down_next, out_next,
    vector_grad, state_next, vectors_next,
):
    base_rate = 0.3 * D ** (-0.5)
    for which in range(3):
        here = slice(which, which + 1)
        in_cols_new[here, :], in_next[which] = matrix_step(
            inward[which], in_grad[which], in_rows[here, :], in_cols[here, :],
            sums[6:7, which : which + 1], sums[here, :], sums[3 + which : 4 + which, :], D,
            base_rate,
        )

    def wide_row(first):
        return jnp.concatenate([sums[first + i : first + i + 1, :] for i in range(4)], axis=1)

    up_new, up_next[...] = matrix_step(
        up[...], up_grad[...], up_rows[...], up_cols[...], sums[36:37, 0:1], wide_row(24),
        wide_row(28), D, base_rate,
    )
    down_new, down_next[...] = matrix_step(
        down[...], down_grad[...], down_rows[...], down_cols[...], sums[36:37, 1:2],
        sums[32:33, :], sums[33:34, :], FF, 0.3 * FF ** (-0.5),
    )
    out_new, out_next[...] = matrix_step(
        out[...], out_grad[...], out_rows[...], out_cols[...], sums[36:37, 2:3],
        sums[34:35, :], sums[35:36, :], D, 1.2 * D ** (-0.5),
    )
    up_cols_new[...] = up_new.reshape(FF)
    down_cols_new[...] = down_new.reshape(D)
    out_cols_new[...] = out_new.reshape(D)
    g = sums[8:21, :]
    vector_grad[...] = g
    state = DECAY * vector_state[...] + (1.0 - DECAY) * (g * g + square_eps)
    state_next[...] = state
    update = g * lax.rsqrt(state)
    total = jnp.sum(jnp.sum(update * update, axis=0, keepdims=True), axis=1, keepdims=True)
    rms = jnp.sqrt(total * (1.0 / (13 * D)))
    vectors_next[...] = vectors[...] - update * (0.25 / jnp.maximum(1.0, rms / clip_level))


def shards(
    tokens, cotangent, lengths, projection, inward, outward, expand, shrink, vectors,
    inward_rows, inward_columns, outward_rows, outward_columns, expand_rows, expand_columns,
    shrink_rows, shrink_columns, vector_state,
):
    full = special()
    rows = outward.shape[0]
    wide = 8 if full else 1
    wide_at = lax.axis_index("wide").astype(jnp.int32)
    narrow_at = lax.axis_index("narrow").astype(jnp.int32)
    core = narrow_at % 2 if full else jnp.int32(0)
    place = jnp.stack([wide_at // 2, wide_at % 2, narrow_at // 2, core])
    per = FFC // wide
    cosine, sine, onehot, proj = tables(lengths, projection)
    if full:
        *own_in, own_first, own_rest = small_call(
            pick_kernel, "pick", place, [inward, outward, expand, shrink],
            [
                struct((2, 48, D), BF16), struct((1, 48, D), BF16), struct((528, WIDTH), BF16),
                struct((768, WIDTH), BF16),
            ],
        )
        in_z = [along_z(value) for value in own_in]
        *in_z, own_first, cosine, sine, onehot, proj = tie(
            *in_z, own_first, cosine, sine, onehot, proj
        )
        first_z = along_z(own_first)
        in_x = [over_x(value) for value in in_z]
        pieces_in = []
        *in_z, first_z = tie(*in_z, *in_x, first_z)
        for near, far in zip(in_z[:2], in_z[2:]):
            pieces_in += [near, far, over_core(near), over_core(far)]
        *pieces_in, first_z, own_rest = tie(*pieces_in, first_z, own_rest)
        first_x = over_x(first_z)
        rest_got = [over_z(own_rest, shift) for shift in (1, 2, 3)]
    else:
        in_low = lax.all_gather(inward.astype(BF16), "wide", axis=1, tiled=True)
        out_low = lax.all_gather(outward.astype(BF16), "wide", axis=0, tiled=True)
        up_low = lax.all_gather(expand.astype(BF16), "wide", axis=0, tiled=True)
        down_low = lax.all_gather(shrink.astype(BF16), "wide", axis=0, tiled=True)
        units = jnp.transpose(in_low.reshape(3, D, GROUPS, WIDTH), (2, 1, 0, 3))
        pieces_in = [units.reshape(1, 3 * D, D)]

        def blocks(matrix):
            count = matrix.shape[1] // WIDTH
            return jnp.transpose(matrix.reshape(-1, count, WIDTH), (1, 0, 2)).reshape(-1, WIDTH)

        ups = [blocks(up_low[:, FFC * j : FFC * (j + 1)]) for j in range(CHUNKS)]
        downs = [blocks(down_low[FFC * j : FFC * (j + 1)]) for j in range(CHUNKS)]
        half = D // 2
        pieces_first = [
            jnp.concatenate([blocks(out_low[:half]), ups[0], blocks(out_low[half:]), downs[0]])[
                None
            ]
        ]
        pieces_rest = [
            jnp.stack([jnp.concatenate([ups[j], downs[j]])[None] for j in range(1, CHUNKS)])
        ]
    perm = jnp.asarray(head_perm(), BF16)
    block_ones = np.kron(np.eye(2, dtype=np.float32), np.ones((64, 64), np.float32))
    ones = jnp.asarray(np.concatenate([block_ones, block_ones]), BF16)
    split = vectors[4:6].reshape(2, GROUPS, 4, 2, 32)
    bias_qk = jnp.transpose(split, (0, 1, 3, 2, 4)).reshape(2, GROUPS, WIDTH)
    bias = jnp.concatenate([bias_qk, vectors[6].reshape(1, GROUPS, WIDTH)])
    bias = jnp.transpose(bias, (1, 0, 2))
    bias_up = vectors[9:].reshape(wide, CHUNKS, per)
    bias_up = jnp.transpose(bias_up, (1, 0, 2)).reshape(CHUNKS, 1, FFC)
    attn, mixed, a1t, w_in, wq, wk, qf, kf, v, rden = attend(
        lengths, place, pieces_in, wide, tokens, vectors[:2], bias, perm, proj, cosine, sine,
        onehot,
    )
    if full:
        attn, first_x, *rest_got = tie(attn, first_x, *rest_got)
        rest_z = jnp.stack([own_rest] + rest_got)
        first_cores = [over_core(first_z), over_core(first_x)]
        *first_cores, rest_z = tie(*first_cores, rest_z)
        pieces_first = [first_z, first_x] + first_cores
        rest_x = over_x(rest_z)
    x1, a2, a2t, dyt, y, back, w_out, keep0, send0, dbias0 = middle_first(
        place, wide, pieces_first, tokens, attn, cotangent, vectors, bias_up
    )
    if full:
        rest_core = over_core(rest_z)
        rest_x, rest_core, send0, y = tie(rest_x, rest_core, send0, y)
        pieces_rest = [rest_z, rest_x, rest_core, over_core(rest_x)]
        got0 = over_core(send0)
    (
        block_out, dx1, dmixed, okeep, osend, middle_vec, keep12, send12, dbias12,
    ) = middle_rest(
        place, wide, pieces_rest, cotangent, (a2, a2t, dyt), bias_up, attn, w_out, vectors,
        (y, back, x1),
    )
    if full:
        got0, send12, osend = tie(got0, send12, osend)
        got12 = over_core(send12)
        send_b, keep_b = first_sum(place, [(keep0, got0), (keep12, got12)])
        e_parts = first_sum_z(place, [(keep12, got12), (okeep, over_core(osend))])
        dmixed, send_b, keep_b, *e_parts = tie(dmixed, send_b, keep_b, *e_parts)
        got_b = over_x(send_b)
        e_got = [over_z(e_parts[shift], shift) for shift in (1, 2, 3)]
    saved = (mixed, rden, wq, wk, qf, kf, v)
    in_keep, in_send, in_bias, da1 = attend_back(
        lengths, place, wide, dmixed, saved, a1t, w_in, perm, proj, cosine, sine, onehot, ones
    )
    if full:
        in_send, da1, got_b, *e_got = tie(in_send, da1, got_b, *e_got)
        b_parts = list(second_sum(place, keep_b, got_b))
        got_in = over_core(in_send)
        got_in, *e_got, b_parts[1] = tie(got_in, *e_got, b_parts[1])
        keep_e, send_e = split_sum(place, [e_parts[0]] + e_got)
        got_e = over_x(send_e)
        send_c, keep_c = held_call(
            first_sum_y_kernel, "first_sum_y", place, [in_keep, got_in],
            [struct((8, 432, 128), BF16)] * 2,
        )
        da1, send_c = tie(da1, send_c)
        got_c = over_y(send_c)
    input_grad, vector_local = input_side(
        wide, tokens, dx1, da1, vectors, middle_vec, in_bias, dbias0, dbias12
    )
    if full:
        def pair_sum(mine, got):
            half_sum = mine.astype(F32) + got.astype(F32)
            return half_sum, over_core(half_sum)

        got_c, input_grad, vector_local = tie(got_c, input_grad, vector_local)
        send_c, keep_c = held_call(
            split_x_kernel, "split_x", place, [keep_c, got_c], [struct((4, 432, 128), BF16)] * 2
        )
        send_c, b_parts[0] = tie(send_c, b_parts[0])
        got_c = over_x(send_c)
        ffn_mine = z_sum(place, b_parts, (keep_e, got_e))
        ffn_mine, got_c = tie(ffn_mine, got_c)
        c_parts = second_sum(place, keep_c, got_c)
        ffn_mine, *c_parts = tie(ffn_mine, *c_parts)
        ffn_y = over_y(ffn_mine)
        c_mine = z_sum(place, c_parts)
        c_mine, vector_local = tie(c_mine, vector_local)
        c_y = over_y(c_mine)
        vector_y = over_y(vector_local)
        c_core = over_core(c_mine)
        ffn_y, c_mine = tie(ffn_y, c_mine)
        ffn_own, ffn_got = pair_sum(ffn_mine, ffn_y)
        expand_grad, shrink_grad, outward_grad, up_rows, down_rows, out_rows, sums = held_call(
            ffn_moments_kernel, "ffn_moments", place,
            [
                ffn_own, ffn_got, expand_rows[None], shrink_rows[None], outward_rows[None],
            ],
            [
                struct(expand.shape, F32), struct(shrink.shape, F32), struct(outward.shape, F32),
                struct((1, 96), F32), struct((1, 384), F32), struct((1, 96), F32),
                struct((16, D), F32),
            ],
            0,
        )
        c_y, vector_y, sums = tie(c_y, vector_y, sums)
        vector_pair = vector_local + vector_y
        inward_grad, in_rows, sums = held_call(
            in_moments_kernel, "in_moments", place,
            [
                c_mine, c_y, c_core, over_core(c_y), inward_rows, vector_pair,
                over_core(vector_pair), sums,
            ],
            [struct(inward.shape, F32), struct((3, 96), F32), struct((40, D), F32)],
            0,
        )
        sums = sum_wide(sums)
        (
            in_cols, up_cols, down_cols, out_cols, inward_next, expand_next, shrink_next,
            outward_next, vector_grad, vector_state_next, vectors_next,
        ) = small_call(
            finish_kernel, "finish", place,
            [
                inward, expand, shrink, outward, inward_grad, expand_grad, shrink_grad,
                outward_grad, in_rows, up_rows, down_rows, out_rows, inward_columns,
                expand_columns[None], shrink_columns[None], outward_columns[None], sums, vectors,
                vector_state,
            ],
            [
                struct((3, D), F32), struct((FF,), F32), struct((D,), F32),
                struct((D,), F32), struct(inward.shape, F32), struct(expand.shape, F32),
                struct(shrink.shape, F32), struct(outward.shape, F32), struct((13, D), F32),
                struct((13, D), F32), struct((13, D), F32),
            ],
        )
        return (
            block_out, input_grad, inward_grad, outward_grad, expand_grad, shrink_grad,
            vector_grad, in_rows, in_cols, out_rows[0], out_cols, up_rows[0], up_cols,
            down_rows[0], down_cols, vector_state_next, inward_next, outward_next,
            expand_next, shrink_next, vectors_next,
        )
    vector_part = sum_narrow(vector_local[:13])

    def reduced(values, axis):
        part = lax.psum_scatter(values, "wide", scatter_dimension=axis, tiled=True)
        return lax.psum(part.astype(F32), "narrow")

    keeps = [keep0, keep12[0], keep12[1]]
    sends = [send0, send12[0], send12[1]]
    up_grads = [
        jnp.transpose(keep.reshape(4, D, WIDTH), (1, 0, 2)).reshape(D, FFC) for keep in keeps
    ]
    down_grads = [
        jnp.transpose(send.reshape(4, D, WIDTH), (0, 2, 1)).reshape(FFC, D) for send in sends
    ]
    expand_grad = reduced(jnp.concatenate(up_grads, axis=1), 0)
    shrink_grad = reduced(jnp.concatenate(down_grads, axis=0), 0)

    def rebuilt(keep, send):
        return jnp.concatenate(
            [keep.reshape(-1, 3, D // 2, WIDTH), send.reshape(-1, 3, D // 2, WIDTH)], axis=2
        )

    outward_grad = reduced(jnp.transpose(rebuilt(okeep, osend)[0], (1, 0, 2)).reshape(D, D), 0)
    in_units = rebuilt(in_keep, in_send)
    inward_grad = reduced(jnp.transpose(in_units, (1, 2, 0, 3)).reshape(3, D, D), 1)
    decay = 1.0 - STEP ** (-0.8)
    wide_count = lax.axis_size("wide")
    grads_list = [inward_grad, outward_grad[None], expand_grad[None], shrink_grad[None]]
    rows_old = [inward_rows, outward_rows[None], expand_rows[None], shrink_rows[None]]
    columns_old = [
        inward_columns,
        outward_columns[None],
        expand_columns[None],
        shrink_columns[None],
    ]
    weights_old = [inward, outward[None], expand[None], shrink[None]]
    rates = [0.3 * D ** (-0.5), 1.2 * D ** (-0.5), 0.3 * D ** (-0.5), 0.3 * FF ** (-0.5)]
    bounds = [0, 3, 4, 5, 6]
    rows_next = []
    column_parts = []
    for member in range(4):
        squares = grads_list[member] * grads_list[member] + square_eps
        rows_next.append(decay * rows_old[member] + (1.0 - decay) * jnp.mean(squares, axis=-1))
        column_parts.append(jnp.sum(squares, axis=-2))
    row_totals = jnp.concatenate([jnp.sum(entry, axis=-1) for entry in rows_next])
    shapes = [part.shape for part in column_parts] + [row_totals.shape, vector_part.shape]
    flat = jnp.concatenate(
        [part.reshape(-1) for part in column_parts + [row_totals, vector_part]]
    )
    flat = jnp.pad(flat, (0, -flat.shape[0] % 1024)).reshape(-1, 128)
    flat = sum_wide(flat).reshape(-1)
    summed = []
    offset = 0
    for shape in shapes:
        size = 1
        for extent in shape:
            size *= extent
        summed.append(flat[offset : offset + size].reshape(shape))
        offset += size
    column_sums = list(summed[0:4])
    totals_sum = summed[4]
    vector_grad = summed[5]
    columns_next = []
    scaled_list = []
    row_means = []
    sizes_full = []
    for member in range(4):
        grad_now = grads_list[member]
        rows_full = grad_now.shape[-2] * wide_count
        sizes_full.append(rows_full * grad_now.shape[-1])
        columns_next.append(
            decay * columns_old[member] + (1.0 - decay) * column_sums[member] / rows_full
        )
        row_mean = totals_sum[bounds[member] : bounds[member + 1]] / rows_full
        row_means.append(row_mean)
        scaled_list.append(
            grad_now
            * lax.rsqrt(rows_next[member] / row_mean[:, None])[..., None]
            * lax.rsqrt(columns_next[member])[:, None, :]
        )
    partial_squares = jnp.concatenate(
        [jnp.sum(entry * entry, axis=(-2, -1)) for entry in scaled_list]
    )
    total_squares = sum_wide(jnp.pad(partial_squares, (0, 122)).reshape(1, 128))[0, :6]
    rms_list = [
        jnp.sqrt(total_squares[bounds[member] : bounds[member + 1]] / sizes_full[member])
        for member in range(4)
    ]
    weights_next = []
    for member in range(4):
        limiter = jnp.maximum(1.0, rms_list[member] / clip_level)
        weights_next.append(
            weights_old[member] - rates[member] * scaled_list[member] / limiter[:, None, None]
        )
    vector_state_next = decay * vector_state + (1.0 - decay) * (
        vector_grad * vector_grad + square_eps
    )
    vector_update = vector_grad * lax.rsqrt(vector_state_next)
    vector_rms = jnp.sqrt(jnp.mean(vector_update * vector_update))
    vectors_next = vectors - 0.25 * vector_update / jnp.maximum(1.0, vector_rms / clip_level)
    return (
        block_out,
        input_grad,
        inward_grad,
        outward_grad,
        expand_grad,
        shrink_grad,
        vector_grad,
        rows_next[0],
        columns_next[0],
        rows_next[1][0],
        columns_next[1][0],
        rows_next[2][0],
        columns_next[2][0],
        rows_next[3][0],
        columns_next[3][0],
        vector_state_next,
        weights_next[0],
        weights_next[1][0],
        weights_next[2][0],
        weights_next[3][0],
        vectors_next,
    )


def solution(mesh):
    placed = (
        P(("narrow", "wide"), None),
        P(("narrow", "wide"), None),
        P(("narrow", "wide"), None),
        P(),
        P(None, "wide", None),
        P("wide", None),
        P("wide", None),
        P("wide", None),
        P(),
        P(None, "wide"),
        P(),
        P("wide"),
        P(),
        P("wide"),
        P(),
        P("wide"),
        P(),
        P(),
    )
    return jax.shard_map(
        shards,
        mesh=mesh,
        in_specs=placed,
        out_specs=(
            P(("narrow", "wide"), None),
            P(("narrow", "wide"), None),
            P(None, "wide", None),
            P("wide", None),
            P("wide", None),
            P("wide", None),
            P(),
            P(None, "wide"),
            P(),
            P("wide"),
            P(),
            P("wide"),
            P(),
            P("wide"),
            P(),
            P(),
            P(None, "wide", None),
            P("wide", None),
            P("wide", None),
            P("wide", None),
            P(),
        ),
        check_vma=False,
    )
```
